32 devices in a mesh: clip: 4 (over y, x), patch: 8 (over z, core).
Axes of the slice: x: 2, y: 2, z: 4, core: 2. Of those that a mesh axis runs over, the one named last changes fastest.
Arguments:
- tokens: bfloat16 [96, 208, 768], P('clip', 'patch'), may hold values from -6 to 6
- cls_tokens: bfloat16 [16, 768], P('clip'), may hold values from -6 to 6
- clip_lengths: int32 [4, 4], P('clip'), may hold values from 1 to 19, 24 in all within a row
- time_proj: bfloat16 [2, 768, 2304], replicated, may hold values from -0.21875 to 0.21875
- time_output: bfloat16 [2, 768, 768], replicated, may hold values from -0.4375 to 0.4375
- space_proj: bfloat16 [2, 768, 2304], replicated, may hold values from -0.21875 to 0.21875
- space_output: bfloat16 [2, 768, 768], replicated, may hold values from -0.625 to 0.625
- up_weight: bfloat16 [2, 768, 3072], replicated, may hold values from -0.21875 to 0.21875
- down_weight: bfloat16 [2, 3072, 768], replicated, may hold values from -0.109375 to 0.109375
- norm_gains: float32 [2, 3, 768], replicated, may hold values from 0.5 to 1.5
- norm_biases: float32 [2, 3, 768], replicated, may hold values from -1.8 to 1.8
- cotangent: bfloat16 [96, 208, 768], P('clip', 'patch'), may hold values from -6 to 6
Outputs:
- output: bfloat16 [96, 208, 768], P('clip', 'patch')
- grad_tokens: bfloat16 [96, 208, 768], P('clip', 'patch')
- grad_cls: float32 [16, 768], P('clip')
- grad_time_proj: float32 [2, 768, 2304], P(None, 'patch')
- grad_time_output: float32 [2, 768, 768], P(None, 'patch')
- grad_space_proj: float32 [2, 768, 2304], P(None, 'patch')
- grad_space_output: float32 [2, 768, 768], P(None, 'patch')
- grad_up: float32 [2, 768, 3072], P(None, 'patch')
- grad_down: float32 [2, 3072, 768], P(None, 'patch')
- grad_gains: float32 [2, 3, 768], P(None, None, 'patch')
- grad_biases: float32 [2, 3, 768], P(None, None, 'patch')
The draws below stay inside these ranges and needn't reach their ends.
Inputs may be any that keep to these rules, and one draw needn't show every extreme that they name: `clip_lengths`: each row sums to 24 and its longest clip has exactly 19 frames.
All inputs are finite; a program needn't handle non-finite values.
Results may differ from the reference program's by a relative error of at most 0.019.
Values may be sent and summed in bfloat16 or wider, within the bound.
A program may use at most 384 MiB of HBM per device.

```python
import math
import jax
import jax.numpy as jnp
import numpy as np
from jax import lax

D = 768
HEADS = 12
HD = 64
FF = 3072
LAYERS = 2
PATCHES = 208
REAL_PATCH = 196
F_DEV = 24
C_DEV = 4
LONGEST = 19
FRAMES = 96
CLIPS = 16
N_CLIP = 4


def steps_of(rng, dims, split, least, top_value):
    def one(dim, shards_of):
        heights = jax.random.uniform(jax.random.fold_in(jax.random.fold_in(rng, 6), dim), (shards_of,), jnp.float32, least / len(split), top_value / len(split))
        return jnp.repeat(jnp.exp(heights), dims[dim] // shards_of).reshape((-1,) + (1,) * (len(dims) - dim - 1))

    loudness = one(*split[0])
    for cut in split[1:]:
        loudness = loudness * one(*cut)
    return loudness


def profile(number_of, total, reach, slope):
    weights = [(1 << 20) // math.isqrt(standing ** slope) + 1 for standing in range(2, number_of + 1)]
    spare, counts = total - reach - (number_of - 1), [1] * (number_of - 1)
    while spare > 0:
        free = [i for i in range(number_of - 1) if counts[i] < reach]
        whole, budget = sum([weights[i] for i in free]), spare
        for i in free:
            extra = min(reach - counts[i], max(1, budget * weights[i] // whole), spare)
            counts[i] = counts[i] + extra
            spare = spare - extra
    return np.array([reach] + counts)


def uneven_parts(own_key, number_of, total, bound, skew):
    if number_of == 2:
        one = jax.random.randint(own_key, (), max(1, total - bound), min(bound, total - 1) + 1)
        return jnp.stack([one, total - one])
    lengths = jnp.asarray(profile(number_of, total, bound, skew), jnp.int32)
    twos = (number_of - 1) // 2
    donor, taker = lengths[1:1 + 2 * twos:2], lengths[2:2 + 2 * twos:2]
    room = jnp.minimum(donor - 1, bound - taker)
    passed = jax.random.randint(jax.random.fold_in(own_key, 1), (twos,), 0, 1 << 20) % (room + 1)
    lengths = lengths.at[1:1 + 2 * twos:2].set(donor - passed).at[2:2 + 2 * twos:2].set(taker + passed)
    return lengths[jax.random.permutation(jax.random.fold_in(own_key, 2), number_of)]


def gaussian(key, extent, deviation, reach, split=(), kind=jnp.bfloat16):
    drawn = jax.random.normal(key, extent, jnp.float32) * deviation
    if len(split) > 0:
        drawn = steps_of(key, extent, split, -0.22, 0.18) * drawn
    return jnp.clip(drawn, min=-reach, max=reach).astype(kind)


def setup_inputs(seed: int = 0) -> dict:
    seeds = jax.random.split(jax.random.key(seed), 13)
    return {
        "tokens": gaussian(seeds[0], (FRAMES, PATCHES, D), 1.0, 6.0, ((0, 4), (1, 8))),
        "cls_tokens": gaussian(seeds[1], (CLIPS, D), 1.0, 6.0, ((0, 4),)),
        "clip_lengths": jax.vmap(lambda own: uneven_parts(own, C_DEV, F_DEV, LONGEST, 2))(jax.random.split(seeds[2], N_CLIP)).reshape((N_CLIP, C_DEV)).astype(jnp.int32),
        "time_proj": gaussian(seeds[3], (LAYERS, D, 3 * D), D ** -0.5, 0.21875),
        "time_output": gaussian(seeds[4], (LAYERS, D, D), (D // 4) ** -0.5, 0.4375),
        "space_proj": gaussian(seeds[5], (LAYERS, D, 3 * D), D ** -0.5, 0.21875),
        "space_output": gaussian(seeds[6], (LAYERS, D, D), (D // 8) ** -0.5, 0.625),
        "up_weight": gaussian(seeds[7], (LAYERS, D, FF), D ** -0.5, 0.21875),
        "down_weight": gaussian(seeds[8], (LAYERS, FF, D), FF ** -0.5, 0.109375),
        "norm_gains": jnp.clip(1.0 + 0.1 * jax.random.normal(seeds[9], (LAYERS, 3, D), jnp.float32), 0.5, 1.5),
        "norm_biases": gaussian(seeds[10], (LAYERS, 3, D), 0.3, 1.8, (), jnp.float32),
        "cotangent": gaussian(seeds[11], (FRAMES, PATCHES, D), 1.0, 6.0, ((0, 4), (1, 8))),
    }


EPSILON = 1e-05
NEG_LARGE = -1e+30
ROOT_HALF = 0.7071067811865476
HIGHEST_PREC = lax.Precision.HIGHEST

@jax.custom_vjp
def low(v):
    return lax.optimization_barrier(v.astype(jnp.bfloat16)).astype(jnp.float32)

@jax.custom_vjp
def low_back(v):
    return v

def low_keep(v):
    return (low(v), None)

def low_pass(kept, grad):
    return (grad,)

def back_keep(v):
    return (v, None)

def back_low(kept, grad):
    return (low(grad),)
low.defvjp(low_keep, low_pass)
low_back.defvjp(back_keep, back_low)

def both_round(values):
    return low(low_back(values))

def normalize(values, norm_gain, norm_bias):
    centered = values - lax.optimization_barrier(jnp.mean(values, -1, keepdims=True))
    variance = lax.optimization_barrier(jnp.mean(centered * centered, -1, keepdims=True))
    return centered * lax.rsqrt(variance + EPSILON) * norm_gain + norm_bias

def gelu_value(hidden):
    return 0.5 * hidden * (1.0 + jax.scipy.special.erf(hidden * ROOT_HALF))

def clip_tables(lengths_row, frame_count):
    clip_ends = jnp.cumsum(lengths_row.astype(jnp.int32))
    frame_ids = jnp.arange(frame_count, dtype=jnp.int32)
    frame_slot = lax.optimization_barrier(jnp.sum((frame_ids[:, None] >= clip_ends[None, :]).astype(jnp.int32), axis=1))
    same_clip = frame_slot[:, None] == frame_slot[None, :]
    clip_pick = frame_slot[:, None] == jnp.arange(lengths_row.shape[0], dtype=jnp.int32)[None, :]
    return (same_clip, clip_pick)

@jax.checkpoint
def temporal_mix(queries, key_rows, value_rows, same_clip):
    score_scale = HD ** (-0.5)
    scores = low_back(jnp.einsum('fphd,gphd->phfg', queries, key_rows, precision=HIGHEST_PREC) * score_scale)
    scores = jnp.where(same_clip, scores, NEG_LARGE)
    running_max = lax.optimization_barrier(jnp.max(scores, -1, keepdims=True))
    exponent = jnp.exp(scores - running_max)
    attention = exponent / lax.optimization_barrier(jnp.sum(exponent, -1, keepdims=True))
    return jnp.einsum('phfg,gphd->fphd', attention, value_rows, precision=HIGHEST_PREC)

@jax.checkpoint
def spatial_mix(queries, key_rows, value_rows, cls_keys, cls_values, key_valid):
    score_scale = HD ** (-0.5)
    patch_scores = low_back(jnp.einsum('fihd,fjhd->fhij', queries, key_rows, precision=HIGHEST_PREC) * score_scale)
    patch_scores = jnp.where(key_valid, patch_scores, NEG_LARGE)
    cls_scores = low_back(jnp.einsum('fihd,fhd->fhi', queries, cls_keys, precision=HIGHEST_PREC) * score_scale)
    running_max = jnp.maximum(lax.optimization_barrier(jnp.max(patch_scores, -1)), cls_scores)
    patch_exp = jnp.exp(patch_scores - running_max[..., None])
    cls_exp = jnp.exp(cls_scores - running_max)
    row_total = lax.optimization_barrier(jnp.sum(patch_exp, -1)) + cls_exp
    summed = jnp.einsum('fhij,fjhd->fihd', patch_exp, value_rows, precision=HIGHEST_PREC)
    summed = summed + jnp.einsum('fhi,fhd->fihd', cls_exp, cls_values, precision=HIGHEST_PREC)
    return summed / jnp.transpose(row_total, (0, 2, 1))[..., None]

def linear(left, matrix):
    return jnp.einsum('...d,de->...e', left, matrix, precision=HIGHEST_PREC)

def block_forward(token_block, cls_rows, weight_list, lengths_row):
    time_proj, time_output, space_proj, space_output, up_weight, down_weight, norm_gains, norm_biases = weight_list
    frame_count = token_block.shape[0]
    same_clip, clip_pick = clip_tables(lengths_row, frame_count)
    pick_float = clip_pick.astype(jnp.float32)
    key_valid = jnp.arange(PATCHES, dtype=jnp.int32) < REAL_PATCH
    residual = token_block
    for layer_index in range(LAYERS):
        layer_gains = norm_gains[layer_index]
        layer_biases = norm_biases[layer_index]
        normed = low(normalize(residual, layer_gains[0], layer_biases[0]))
        projected = both_round(linear(normed, time_proj[layer_index]))
        queries = projected[..., :D].reshape(frame_count, PATCHES, HEADS, HD)
        key_rows = projected[..., D:2 * D].reshape(frame_count, PATCHES, HEADS, HD)
        value_rows = projected[..., 2 * D:].reshape(frame_count, PATCHES, HEADS, HD)
        mixed = both_round(temporal_mix(queries, key_rows, value_rows, same_clip).reshape(frame_count, PATCHES, D))
        residual = residual + low_back(linear(mixed, time_output[layer_index]))
        normed = low(normalize(residual, layer_gains[1], layer_biases[1]))
        projected = both_round(linear(normed, space_proj[layer_index]))
        queries = projected[..., :D].reshape(frame_count, PATCHES, HEADS, HD)
        key_rows = projected[..., D:2 * D].reshape(frame_count, PATCHES, HEADS, HD)
        value_rows = projected[..., 2 * D:].reshape(frame_count, PATCHES, HEADS, HD)
        cls_normed = low(normalize(cls_rows, layer_gains[1], layer_biases[1]))
        cls_proj = both_round(linear(cls_normed, space_proj[layer_index][:, D:]))
        cls_frames = jnp.einsum('fc,ce->fe', pick_float, cls_proj, precision=HIGHEST_PREC)
        cls_keys = cls_frames[:, :D].reshape(frame_count, HEADS, HD)
        cls_values = cls_frames[:, D:].reshape(frame_count, HEADS, HD)
        mixed = spatial_mix(queries, key_rows, value_rows, cls_keys, cls_values, key_valid)
        mixed = both_round(mixed.reshape(frame_count, PATCHES, D))
        residual = residual + low_back(linear(mixed, space_output[layer_index]))
        normed = low(normalize(residual, layer_gains[2], layer_biases[2]))
        hidden = low_back(linear(normed, up_weight[layer_index]))
        active = low(gelu_value(hidden))
        residual = residual + low_back(linear(active, down_weight[layer_index]))
    return residual

def reference(tokens, cls_tokens, clip_lengths, time_proj, time_output, space_proj, space_output, up_weight, down_weight, norm_gains, norm_biases, cotangent):
    weights = jax.tree.map(lambda matrix: matrix.astype(jnp.float32), (time_proj, time_output, space_proj, space_output, up_weight, down_weight, norm_gains, norm_biases))
    token_blocks = tokens.astype(jnp.float32).reshape(N_CLIP, F_DEV, PATCHES, D)
    cls_blocks = cls_tokens.astype(jnp.float32).reshape(N_CLIP, C_DEV, D)
    grad_blocks = cotangent.astype(jnp.float32).reshape(N_CLIP, F_DEV, PATCHES, D)

    def one_block(summed, inputs):
        token_block, cls_rows, lengths_row, grad_block = inputs

        def forward(token_in, cls_in, weight_list):
            return block_forward(token_in, cls_in, weight_list, lengths_row)
        result, pullback = jax.vjp(forward, token_block, cls_rows, weights)
        grad_token, grad_cls_rows, grad_weights = pullback(grad_block)
        summed = jax.tree.map(jnp.add, summed, grad_weights)
        return (summed, (result.astype(jnp.bfloat16), grad_token.astype(jnp.bfloat16), grad_cls_rows))
    empty_grads = jax.tree.map(jnp.zeros_like, weights)
    totals, (results, grad_tok, grad_cls_all) = lax.scan(one_block, empty_grads, (token_blocks, cls_blocks, clip_lengths, grad_blocks))
    return (results.reshape(N_CLIP * F_DEV, PATCHES, D), grad_tok.reshape(N_CLIP * F_DEV, PATCHES, D), grad_cls_all.reshape(N_CLIP * C_DEV, D), totals[0], totals[1], totals[2], totals[3], totals[4], totals[5], totals[6], totals[7])
```

```python
import functools

import jax
import jax.numpy as jnp
from jax import lax
from jax.experimental import pallas as pl
from jax.experimental.pallas import tpu as pltpu
from jax.sharding import PartitionSpec as P

HEADS = 12
HD = 64
LAYERS = 2
REAL_PATCH = 196
QUAD = 4
WIDE = QUAD * HD
QUADS = HEADS // QUAD
CLS_ROWS = 16

EPSILON = 1e-05
NEG_LARGE = -1e30
ROOT_HALF = 0.7071067811865476
INV_ROOT_TWO_PI = 0.3989422804014327
SCALE = HD**-0.5
VMEM_LIMIT = 48 * 1024 * 1024

f32 = jnp.float32
bf16 = jnp.bfloat16
MESH = pl.DeviceIdType.MESH


def layer_norm(values, norm_gain, norm_bias):
    centered = values - jnp.mean(values, -1, keepdims=True)
    inverse = lax.rsqrt(jnp.mean(centered * centered, -1, keepdims=True) + EPSILON)
    scaled = centered * inverse
    return (scaled * norm_gain + norm_bias, scaled, inverse)


def norm_back(grad_out, scaled, inverse, norm_gain):
    weighted = grad_out * norm_gain
    grad_input = inverse * (
        weighted
        - jnp.mean(weighted, -1, keepdims=True)
        - scaled * jnp.mean(weighted * scaled, -1, keepdims=True)
    )
    return (grad_input, jnp.sum(grad_out * scaled, 0), jnp.sum(grad_out, 0))


def project(left, matrix):
    return jnp.dot(left, matrix, preferred_element_type=f32)


def project_back(grad_out, matrix):
    return lax.dot_general(grad_out, matrix, (((1,), (1,)), ((), ())), preferred_element_type=f32)


def weight_grad(left, grad_out):
    return lax.dot_general(
        left, grad_out, (((0,), (0,)), ((), ())), preferred_element_type=f32
    ).astype(bf16)


def gelu_value(hidden):
    return 0.5 * hidden * (1.0 + lax.erf(hidden * ROOT_HALF))


def gelu_slope(hidden):
    return 0.5 * (1.0 + lax.erf(hidden * ROOT_HALF)) + hidden * INV_ROOT_TWO_PI * jnp.exp(
        -0.5 * hidden * hidden
    )


def dot_nt(left, right):
    return lax.dot_general(left, right, (((1,), (1,)), ((), ())), preferred_element_type=f32)


def dot_nn(left, right):
    return lax.dot_general(left, right, (((1,), (0,)), ((), ())), preferred_element_type=f32)


def dot_tn(left, right):
    return lax.dot_general(left, right, (((0,), (0,)), ((), ())), preferred_element_type=f32)


def spread_heads(rows):
    head = lax.broadcasted_iota(jnp.int32, rows.shape, 1) // HD
    return jnp.concatenate([jnp.where(head == h, rows, jnp.zeros_like(rows)) for h in range(QUAD)], 0)


def merge_heads(stacked):
    count = stacked.shape[0] // QUAD
    head = lax.broadcasted_iota(jnp.int32, (count, WIDE), 1) // HD
    merged = stacked[:count]
    for h in range(1, QUAD):
        merged = jnp.where(head == h, stacked[h * count : (h + 1) * count], merged)
    return merged


def tile_probs(spread, keys, bias):
    scores = dot_nt(spread, keys) + bias
    exponent = jnp.exp(scores - jnp.max(scores, 1, keepdims=True))
    return exponent * (1.0 / jnp.sum(exponent, 1, keepdims=True))


def tile_forward(queries, keys, values, bias):
    probs = tile_probs(spread_heads(queries * SCALE), keys, bias)
    return merge_heads(dot_nn(probs.astype(bf16), values)).astype(bf16)


def tile_backward(queries, keys, values, grad_out, bias):
    spread = spread_heads(queries * SCALE)
    probs = tile_probs(spread, keys, bias)
    grad_spread = spread_heads(grad_out)
    grad_probs = dot_nt(grad_spread, values)
    delta = jnp.sum(probs * grad_probs, 1, keepdims=True)
    grad_scores = (probs * (grad_probs - delta)).astype(bf16)
    grad_queries = merge_heads(dot_nn(grad_scores, keys)) * SCALE
    grad_keys = dot_tn(grad_scores, spread)
    grad_values = dot_tn(probs.astype(bf16), grad_spread)
    return grad_queries, grad_keys, grad_values


def columns(part, quad, width):
    start = part * width + quad * WIDE
    return slice(start, start + WIDE)


def time_forward_kernel(bias_ref, qkv_ref, out_ref):
    width = out_ref.shape[1]
    bias = bias_ref[...]
    for quad in range(QUADS):
        parts = [qkv_ref[:, columns(part, quad, width)] for part in range(3)]
        out_ref[:, columns(0, quad, width)] = tile_forward(*parts, bias)


def time_backward_kernel(bias_ref, qkv_ref, grad_ref, out_ref):
    width = grad_ref.shape[1]
    bias = bias_ref[...]
    for quad in range(QUADS):
        parts = [qkv_ref[:, columns(part, quad, width)] for part in range(3)]
        grads = tile_backward(*parts, grad_ref[:, columns(0, quad, width)], bias)
        for part in range(3):
            out_ref[:, columns(part, quad, width)] = grads[part].astype(bf16)


def group_rows(patch_count, frames):
    return (2 if patch_count % 2 == 0 else 1) * frames


def time_bias(same_clip, patch_count, frames):
    rows = group_rows(patch_count, frames)
    ids = jnp.arange(rows, dtype=jnp.int32)
    same_patch = (ids[:, None] // frames) == (ids[None, :] // frames)
    tiled = jnp.tile(same_clip, (rows // frames, rows // frames))
    return jnp.tile(jnp.where(same_patch & tiled, 0.0, NEG_LARGE).astype(f32), (QUAD, 1))


def params(*semantics):
    return pltpu.CompilerParams(dimension_semantics=semantics, vmem_limit_bytes=VMEM_LIMIT)


def time_forward(bias, qkv):
    rows = bias.shape[1]
    width = qkv.shape[1] // 3
    return pl.pallas_call(
        time_forward_kernel,
        grid=(qkv.shape[0] // rows,),
        in_specs=[
            pl.BlockSpec(bias.shape, lambda i: (0, 0)),
            pl.BlockSpec((rows, 3 * width), lambda i: (i, 0)),
        ],
        out_specs=pl.BlockSpec((rows, width), lambda i: (i, 0)),
        out_shape=jax.ShapeDtypeStruct((qkv.shape[0], width), bf16),
        compiler_params=params("parallel"),
        name="time_forward",
    )(bias, qkv)


def time_backward(bias, qkv, grad_out):
    rows = bias.shape[1]
    width = qkv.shape[1] // 3
    return pl.pallas_call(
        time_backward_kernel,
        grid=(qkv.shape[0] // rows,),
        in_specs=[
            pl.BlockSpec(bias.shape, lambda i: (0, 0)),
            pl.BlockSpec((rows, 3 * width), lambda i: (i, 0)),
            pl.BlockSpec((rows, width), lambda i: (i, 0)),
        ],
        out_specs=pl.BlockSpec((rows, 3 * width), lambda i: (i, 0)),
        out_shape=jax.ShapeDtypeStruct(qkv.shape, bf16),
        compiler_params=params("parallel"),
        name="time_backward",
    )(bias, qkv, grad_out)


def with_class(slot, rows, cls_rows):
    ids = lax.broadcasted_iota(jnp.int32, cls_rows.shape, 0)
    picked = jnp.sum(jnp.where(ids == slot, cls_rows.astype(f32), 0.0), 0, keepdims=True)
    row_ids = lax.broadcasted_iota(jnp.int32, rows.shape, 0)
    return jnp.where(row_ids == REAL_PATCH, picked.astype(bf16), rows)


def key_bias(count):
    key_ids = lax.broadcasted_iota(jnp.int32, (1, count), 1)
    return jnp.where(key_ids <= REAL_PATCH, 0.0, NEG_LARGE).astype(f32)


def space_forward_kernel(slot_ref, q_ref, k_ref, v_ref, ck_ref, cv_ref, out_ref):
    slot = slot_ref[pl.program_id(0)]
    keys = with_class(slot, k_ref[...], ck_ref[...])
    values = with_class(slot, v_ref[...], cv_ref[...])
    out_ref[...] = tile_forward(q_ref[...], keys, values, key_bias(keys.shape[0]))


def space_backward_kernel(
    slot_ref, q_ref, k_ref, v_ref, ck_ref, cv_ref, g_ref, dq_ref, dk_ref, dv_ref, dck_ref, dcv_ref
):
    slot = slot_ref[pl.program_id(0)]
    keys = with_class(slot, k_ref[...], ck_ref[...])
    values = with_class(slot, v_ref[...], cv_ref[...])
    grad_q, grad_k, grad_v = tile_backward(
        q_ref[...], keys, values, g_ref[...], key_bias(keys.shape[0])
    )
    row_ids = lax.broadcasted_iota(jnp.int32, grad_k.shape, 0)
    dq_ref[...] = grad_q.astype(bf16)
    dk_ref[...] = jnp.where(row_ids < REAL_PATCH, grad_k, 0.0).astype(bf16)
    dv_ref[...] = jnp.where(row_ids < REAL_PATCH, grad_v, 0.0).astype(bf16)
    dck_ref[0] = jnp.sum(jnp.where(row_ids == REAL_PATCH, grad_k, 0.0), 0, keepdims=True)
    dcv_ref[0] = jnp.sum(jnp.where(row_ids == REAL_PATCH, grad_v, 0.0), 0, keepdims=True)


def space_specs(frames, patches):
    cls_block = frames * patches // CLS_ROWS

    def rows(part):
        return pl.BlockSpec((patches, WIDE), lambda f, c, s: (f, part * QUADS + c))

    def cls(part):
        return pl.BlockSpec((CLS_ROWS, WIDE), lambda f, c, s: (cls_block, part * QUADS + c))

    return [rows(0), rows(1), rows(2), cls(1), cls(2)], rows(0)


def space_forward(slots, qkv, frames, patches):
    width = qkv.shape[1] // 3
    in_specs, out_spec = space_specs(frames, patches)
    return pl.pallas_call(
        space_forward_kernel,
        grid_spec=pltpu.PrefetchScalarGridSpec(
            num_scalar_prefetch=1,
            grid=(frames, QUADS),
            in_specs=in_specs,
            out_specs=out_spec,
        ),
        out_shape=jax.ShapeDtypeStruct((frames * patches, width), bf16),
        compiler_params=params("parallel", "parallel"),
        name="space_forward",
    )(slots, qkv, qkv, qkv, qkv, qkv)


def space_backward(slots, qkv, grad_out, frames, patches):
    width = qkv.shape[1] // 3
    in_specs, out_spec = space_specs(frames, patches)
    rows = jax.ShapeDtypeStruct((frames * patches, width), bf16)
    cls_spec = pl.BlockSpec((1, 1, WIDE), lambda f, c, s: (f, 0, c))
    cls = jax.ShapeDtypeStruct((frames, 1, width), f32)
    return pl.pallas_call(
        space_backward_kernel,
        grid_spec=pltpu.PrefetchScalarGridSpec(
            num_scalar_prefetch=1,
            grid=(frames, QUADS),
            in_specs=in_specs + [out_spec],
            out_specs=[out_spec] * 3 + [cls_spec] * 2,
        ),
        out_shape=[rows] * 3 + [cls] * 2,
        compiler_params=params("parallel", "parallel"),
        name="space_backward",
    )(slots, qkv, qkv, qkv, qkv, qkv, grad_out)


CHUNKS = 16
BLOCKS = 3
LAG = 4
ROUTES = (("x", "y", "zl", "zh", "y", "x"), ("y", "x", "zl", "zh", "x", "y"), ("zl", "zh", "x", "y", "y", "x"))
SUMS = 4
STAGES = 7
PIECE = (48, 128)
SEGMENTS = ((0, 4), (1, 4), (2, 1), (3, 3), (4, 1), (5, 3))


def recv_shape(route, stage):
    left = [d for d in ("zh", "zl", "x", "y") if d not in route[: stage + 1]]
    return (2,) * len(left) + PIECE


def reduce_kernel(tokens, *refs):
    (lhs_refs, rhs_refs) = (refs[:6], refs[6:12])
    results = refs[12:18]
    out_ref, buf, core_in, lhs_buf, rhs_buf = refs[18:23]
    inboxes = refs[23 : 23 + BLOCKS * SUMS]
    load_sem, core_send, core_recv, send_sem, recv_sem = refs[23 + BLOCKS * SUMS :]
    clip, patch = lax.axis_index("clip"), lax.axis_index("patch")
    me = {"core": patch % 2, "zl": (patch // 2) % 2, "zh": patch // 4, "x": clip % 2, "y": clip // 2}
    step_of = {"core": ("patch", 1), "zl": ("patch", 2), "zh": ("patch", 4), "x": ("clip", 1), "y": ("clip", 2)}

    def peer(dim):
        axis, stride = step_of[dim]
        own = clip if axis == "clip" else patch
        other = own + stride - 2 * stride * me[dim]
        return (other, patch) if axis == "clip" else (clip, other)

    barrier = pltpu.get_barrier_semaphore()
    for dim in step_of:
        pl.semaphore_signal(barrier, inc=1, device_id=peer(dim), device_id_type=MESH)
    pl.semaphore_wait(barrier, len(step_of))

    def place(route, stage, value):
        done = route[:stage]

        def at(dim):
            if dim in done:
                return me[dim]
            if dim == route[stage]:
                return value
            return slice(None)

        return at

    def core_copy(c, z):
        return pltpu.make_async_remote_copy(
            src_ref=buf.at[c, z // 2, z % 2, 1 - me["core"]],
            dst_ref=core_in.at[c, z // 2, z % 2],
            send_sem=core_send.at[c, z],
            recv_sem=core_recv.at[c, z],
            device_id=peer("core"),
            device_id_type=MESH,
        )

    def exchange(c, block, stage):
        route = ROUTES[block]
        dim = route[stage]
        slot = lax.rem(c, 2)
        if stage < SUMS:
            at = place(route, stage, 1 - me[dim])
            src = buf.at[c, at("zh"), at("zl"), me["core"], block, at("x"), at("y")]
            dst = inboxes[block * SUMS + stage].at[slot]
        elif stage == SUMS:
            src = dst = out_ref.at[c, block, me["x"], me["y"]]
        else:
            if dim == "x":
                src = dst = out_ref.at[c, block, me["x"]]
            else:
                src = dst = out_ref.at[c, block, :, me["y"]]
        return pltpu.make_async_remote_copy(
            src_ref=src,
            dst_ref=dst,
            send_sem=send_sem.at[slot, block, stage],
            recv_sem=recv_sem.at[slot, block, stage],
            device_id=peer(dim),
            device_id_type=MESH,
        )

    def add_core(c):
        for z in range(4):
            core_copy(c, z).wait()
        for zh in range(2):
            for zl in range(2):
                mine = buf[c, zh, zl, me["core"]].astype(f32) + core_in[c, zh, zl].astype(f32)
                buf[c, zh, zl, me["core"]] = mine.astype(bf16)
        for block in range(BLOCKS):
            exchange(c, block, 0).start()

    def add_stage(c, stage):
        slot = lax.rem(c, 2)
        for block in range(BLOCKS):
            exchange(c, block, stage).wait()
            if stage < SUMS:
                at = place(ROUTES[block], stage, me[ROUTES[block][stage]])
                where = (c, at("zh"), at("zl"), me["core"], block, at("x"), at("y"))
                mine = buf[where].astype(f32) + inboxes[block * SUMS + stage][slot].astype(f32)
                buf[where] = mine.astype(bf16)
                if stage == SUMS - 1:
                    out_ref[c, block, me["x"], me["y"]] = mine.astype(bf16)
            if stage + 1 < STAGES - 1:
                exchange(c, block, stage + 1).start()
            else:
                finish(c, block)

    def finish(c, block):
        start = 0
        for which, count in SEGMENTS:

            @pl.when((c >= start) & (c < start + count))
            def _(which=which, start=start):
                for xh in range(2):
                    for yh in range(2):
                        part = out_ref[c, block, xh, yh].astype(f32)
                        columns = slice(block * 256 + yh * 128, block * 256 + (yh + 1) * 128)
                        if which == 0:
                            row = pl.multiple_of((c - start) * 96 + xh * 48, 16)
                            results[which][pl.ds(row, 48), columns] = part
                        else:
                            column = pl.multiple_of((c - start) * 768 + columns.start, 128)
                            results[which][xh * 48 : (xh + 1) * 48, pl.ds(column, 128)] = part

            start += count

    def stages(t):
        for stage in reversed(range(STAGES)):
            c = t - LAG - stage

            @pl.when((c >= 0) & (c < CHUNKS))
            def _():
                if stage == 0:
                    add_core(c)
                else:
                    add_stage(c, stage - 1)

    def store(c, z, core, rows, block):
        for xh in range(2):
            for yh in range(2):
                part = rows[xh * 48 : (xh + 1) * 48, yh * 128 : (yh + 1) * 128]
                buf[c, z // 2, z % 2, core, block, xh, yh] = part.astype(bf16)

    def product(lhs, rhs):
        return lax.dot_general(lhs, rhs, (((0,), (0,)), ((), ())), preferred_element_type=f32)

    def load(which, lhs_column, rhs_column, rows):
        copies = (
            pltpu.make_async_copy(lhs_refs[which].at[:, pl.ds(lhs_column, 768)], lhs_buf.at[pl.ds(0, rows)], load_sem.at[0]),
            pltpu.make_async_copy(rhs_refs[which].at[:, pl.ds(rhs_column, 768)], rhs_buf.at[pl.ds(0, rows)], load_sem.at[1]),
        )
        for copy in copies:
            copy.start()
        for copy in copies:
            copy.wait()

    def whole_chunk(c, which, rhs_column):
        rows = tokens[which]
        load(which, 0, rhs_column, rows)
        for half in range(2):
            lhs = lhs_buf[:rows, half * 384 : (half + 1) * 384]
            for block in range(BLOCKS):
                done = product(lhs, rhs_buf[:rows, block * 256 : (block + 1) * 256])
                for i in range(4):
                    store(c, half * 2 + i // 2, i % 2, done[i * 96 : (i + 1) * 96], block)
        for z in range(4):
            core_copy(c, z).start()

    def down_part(t):
        rows = tokens[0]
        load(0, t * 768, 0, rows)
        for core in range(2):
            lhs = lhs_buf[:rows, core * 384 : (core + 1) * 384]
            for block in range(BLOCKS):
                done = product(lhs, rhs_buf[:rows, block * 256 : (block + 1) * 256])
                for c in range(4):
                    for xh in range(2):
                        for yh in range(2):
                            part = done[c * 96 + xh * 48 : c * 96 + (xh + 1) * 48, yh * 128 : (yh + 1) * 128]
                            buf[c, t // 2, t % 2, core, block, xh, yh] = part.astype(bf16)
        for c in range(4):
            core_copy(c, t).start()

    @pl.loop(0, 4)
    def _(t):
        down_part(t)

    first = 4
    for which, count in SEGMENTS[1:]:

        @pl.loop(first, first + count)
        def _(t, which=which, first=first):
            stages(t)
            whole_chunk(t, which, pl.multiple_of((t - first) * 768, 768))

        first += count

    @pl.loop(CHUNKS, CHUNKS + LAG + STAGES - 1)
    def _(t):
        stages(t)


def reduce_grads(lhs, rhs):
    tokens = tuple(part.shape[0] for part in lhs)
    most = max(tokens)
    inbox = [pltpu.VMEM((2,) + recv_shape(ROUTES[b], s), bf16) for b in range(BLOCKS) for s in range(SUMS)]
    shapes = [(384, 768)] + [(96, 768 * count) for _, count in SEGMENTS[1:]]
    return pl.pallas_call(
        functools.partial(reduce_kernel, tokens),
        out_shape=[jax.ShapeDtypeStruct(shape, f32) for shape in shapes],
        in_specs=[pl.BlockSpec(memory_space=pl.ANY)] * 12,
        out_specs=[pl.BlockSpec(memory_space=pltpu.VMEM)] * 6,
        scratch_shapes=[
            pltpu.VMEM((CHUNKS, BLOCKS, 2, 2) + PIECE, bf16),
            pltpu.VMEM((CHUNKS, 2, 2, 2, BLOCKS, 2, 2) + PIECE, bf16),
            pltpu.VMEM((CHUNKS, 2, 2, BLOCKS, 2, 2) + PIECE, bf16),
            pltpu.VMEM((most, 768), bf16),
            pltpu.VMEM((most, 768), bf16),
            *inbox,
            pltpu.SemaphoreType.DMA((2,)),
            pltpu.SemaphoreType.DMA((CHUNKS, 4)),
            pltpu.SemaphoreType.DMA((CHUNKS, 4)),
            pltpu.SemaphoreType.DMA((2, BLOCKS, STAGES - 1)),
            pltpu.SemaphoreType.DMA((2, BLOCKS, STAGES - 1)),
        ],
        compiler_params=pltpu.CompilerParams(
            collective_id=1, has_side_effects=True, vmem_limit_bytes=56 * 1024 * 1024
        ),
        name="reduce_grads",
    )(*lhs, *rhs)


def reduce_plain(lhs, rhs):
    done = [
        lax.psum_scatter(weight_grad(left, right), "patch", scatter_dimension=0, tiled=True)
        for left, right in zip(lhs, rhs)
    ]
    return [part.astype(f32) for part in lax.psum(done, "clip")]


def frame_slots(lengths_row, frame_ids):
    clip_ends = jnp.cumsum(lengths_row)
    return jnp.sum((frame_ids[:, None] >= clip_ends[None, :]).astype(jnp.int32), axis=1)


class Layout:
    def __init__(self, devices, frames, patches):
        self.devices = devices
        self.frames = frames
        self.patches = patches
        self.all_patches = patches * devices
        self.away_frames = -(-frames // devices)
        used = self.away_frames * patches
        self.block = -(-used // 16) * 16
        self.home_rows = frames * patches
        self.away_rows = self.away_frames * self.all_patches
        self.sent_rows = devices * self.block

    def home_of_sent(self):
        row = jnp.arange(self.sent_rows, dtype=jnp.int32)
        peer, inner = row // self.block, row % self.block
        frame = peer * self.away_frames + inner // self.patches
        valid = (inner < self.away_frames * self.patches) & (frame < self.frames)
        return jnp.where(valid, (inner % self.patches) * self.frames + frame, -1)

    def sent_of_away(self):
        row = jnp.arange(self.away_rows + CLS_ROWS, dtype=jnp.int32)
        frame, patch = row // self.all_patches, row % self.all_patches
        sent = (patch // self.patches) * self.block + frame * self.patches + patch % self.patches
        return jnp.where(row < self.away_rows, sent, -1)

    def to_away(self, values):
        pick = self.home_of_sent()[:, None] == jnp.arange(self.home_rows, dtype=jnp.int32)[None, :]
        sent = jnp.dot(pick.astype(bf16), values, preferred_element_type=bf16)
        got = lax.all_to_all(sent, "patch", split_axis=0, concat_axis=0, tiled=True)
        pick = self.sent_of_away()[:, None] == jnp.arange(self.sent_rows, dtype=jnp.int32)[None, :]
        return jnp.dot(pick.astype(bf16), got, preferred_element_type=f32)

    def to_home(self, values):
        pick = jnp.arange(self.sent_rows, dtype=jnp.int32)[:, None] == self.sent_of_away()[None, : self.away_rows]
        sent = jnp.dot(pick.astype(bf16), values, preferred_element_type=bf16)
        got = lax.all_to_all(sent, "patch", split_axis=0, concat_axis=0, tiled=True)
        pick = jnp.arange(self.home_rows, dtype=jnp.int32)[:, None] == self.home_of_sent()[None, :]
        return jnp.dot(pick.astype(bf16), got, preferred_element_type=f32)


def local(
    tokens,
    cls_tokens,
    clip_lengths,
    time_proj,
    time_output,
    space_proj,
    space_output,
    up_weight,
    down_weight,
    norm_gains,
    norm_biases,
    cotangent,
):
    frames, patch_rows, width = tokens.shape
    devices = lax.axis_size("patch")
    lay = Layout(devices, frames, patch_rows)
    away_rows = lay.away_rows
    patches = lay.all_patches
    clip_count = cls_tokens.shape[0]

    frame_ids = jnp.arange(frames, dtype=jnp.int32)
    slots = frame_slots(clip_lengths[0], frame_ids)
    bias = time_bias(slots[:, None] == slots[None, :], patch_rows, frames)
    my_frames = lax.axis_index("patch") * lay.away_frames + jnp.arange(lay.away_frames, dtype=jnp.int32)
    my_slots = jnp.where(my_frames < frames, frame_slots(clip_lengths[0], my_frames), -1)
    cls_pick = (my_slots[None, :] == jnp.arange(CLS_ROWS, dtype=jnp.int32)[:, None]).astype(f32)

    def home_order(values):
        return jnp.transpose(values, (1, 0, 2)).reshape(lay.home_rows, width)

    def given_order(values):
        return jnp.transpose(values.reshape(patch_rows, frames, width), (1, 0, 2))

    cls_aug = jnp.pad(cls_tokens.astype(f32), ((0, CLS_ROWS - clip_count), (0, 0)))
    residual = home_order(tokens).astype(f32)
    cotangent_away = lay.to_away(home_order(cotangent))
    stored = []
    for layer in range(LAYERS):
        gains, biases = norm_gains[layer], norm_biases[layer]
        normed, scaled_t, inverse_t = layer_norm(residual, gains[0], biases[0])
        normed_t = normed.astype(bf16)
        qkv_t = project(normed_t, time_proj[layer]).astype(bf16)
        mixed_t = time_forward(bias, qkv_t)
        residual = residual + project(mixed_t, time_output[layer])
        away = lay.to_away(residual.astype(bf16))
        away = away + jnp.pad(cls_aug, ((away_rows, 0), (0, 0)))
        normed, scaled_s, inverse_s = layer_norm(away, gains[1], biases[1])
        normed_s = normed.astype(bf16)
        qkv_s = project(normed_s, space_proj[layer]).astype(bf16)
        mixed_s = space_forward(my_slots, qkv_s, lay.away_frames, patches)
        away = away[:away_rows] + project(mixed_s, space_output[layer])
        normed, scaled_f, inverse_f = layer_norm(away, gains[2], biases[2])
        normed_f = normed.astype(bf16)
        hidden = project(normed_f, up_weight[layer])
        active = gelu_value(hidden).astype(bf16)
        away = away + project(active, down_weight[layer])
        residual = lay.to_home(away.astype(bf16))
        stored.append(
            dict(
                normed_t=normed_t, scaled_t=scaled_t, inverse_t=inverse_t, qkv_t=qkv_t, mixed_t=mixed_t,
                normed_s=normed_s, scaled_s=scaled_s, inverse_s=inverse_s, qkv_s=qkv_s, mixed_s=mixed_s,
                normed_f=normed_f, scaled_f=scaled_f, inverse_f=inverse_f, hidden=hidden, active=active,
            )
        )
    output = given_order(residual.astype(bf16))

    grad_cls = jnp.zeros_like(cls_aug)
    grad_away = cotangent_away[:away_rows]
    results = [None] * LAYERS
    for layer in reversed(range(LAYERS)):
        saved = stored[layer]
        gains = norm_gains[layer]
        branch = grad_away.astype(bf16)
        lhs, rhs = [saved["active"]], [branch]
        grad_active = project_back(branch, down_weight[layer])
        grad_hidden = (grad_active * gelu_slope(saved["hidden"])).astype(bf16)
        lhs.append(saved["normed_f"])
        rhs.append(grad_hidden)
        grad_normed = project_back(grad_hidden, up_weight[layer])
        grad_input, gain_two, bias_two = norm_back(
            grad_normed, saved["scaled_f"], saved["inverse_f"], gains[2]
        )
        grad_away = grad_away + grad_input
        branch = grad_away.astype(bf16)
        lhs.append(saved["mixed_s"])
        rhs.append(branch)
        grad_mixed = project_back(branch, space_output[layer]).astype(bf16)
        dq, dk, dv, dck, dcv = space_backward(my_slots, saved["qkv_s"], grad_mixed, lay.away_frames, patches)
        dcls = jnp.concatenate([dck[:, 0], dcv[:, 0]], -1)
        dcls = jnp.dot(cls_pick, dcls, precision=lax.Precision.HIGHEST)
        dcls = jnp.pad(dcls.astype(bf16), ((0, 0), (width, 0)))
        grad_qkv = jnp.concatenate([jnp.concatenate([dq, dk, dv], -1), dcls], 0)
        lhs.append(saved["normed_s"])
        rhs.append(grad_qkv)
        grad_normed = project_back(grad_qkv, space_proj[layer])
        grad_input, gain_one, bias_one = norm_back(
            grad_normed, saved["scaled_s"], saved["inverse_s"], gains[1]
        )
        grad_away = grad_away + grad_input[:away_rows]
        grad_cls = grad_cls + grad_input[away_rows:]
        grad_home = lay.to_home(grad_away.astype(bf16))
        branch = grad_home.astype(bf16)
        lhs.append(saved["mixed_t"])
        rhs.append(branch)
        grad_mixed = project_back(branch, time_output[layer]).astype(bf16)
        grad_qkv = time_backward(bias, saved["qkv_t"], grad_mixed)
        lhs.append(saved["normed_t"])
        rhs.append(grad_qkv)
        grad_normed = project_back(grad_qkv, time_proj[layer])
        grad_input, gain_zero, bias_zero = norm_back(
            grad_normed, saved["scaled_t"], saved["inverse_t"], gains[0]
        )
        grad_home = grad_home + grad_input
        if layer > 0:
            grad_away = lay.to_away(grad_home.astype(bf16))[:away_rows]
        paired = (lax.axis_size("clip"), devices) == (4, 8)
        large = (reduce_grads if paired else reduce_plain)(lhs, rhs)
        large = [large[i] for i in (5, 4, 3, 2, 1, 0)]
        small = (jnp.stack([gain_zero, gain_one, gain_two]), jnp.stack([bias_zero, bias_one, bias_two]))
        results[layer] = list(large) + list(small)
    grad_tokens = given_order(grad_home.astype(bf16))
    stacked = [jnp.stack([results[layer][i] for layer in range(LAYERS)]) for i in range(8)]
    small = jnp.stack(stacked[6:])
    small = lax.psum(small, ("patch", "clip"))
    share = width // devices
    small = lax.dynamic_slice_in_dim(small, lax.axis_index("patch") * share, share, 3)
    grad_cls = lax.psum(grad_cls[:clip_count], "patch")
    return (output, grad_tokens, grad_cls, *stacked[:6], small[0], small[1])


def solution(mesh):
    in_specs = (
        P("clip", "patch", None),
        P("clip", None),
        P("clip", None),
        P(),
        P(),
        P(),
        P(),
        P(),
        P(),
        P(),
        P(),
        P("clip", "patch", None),
    )
    out_specs = (
        P("clip", "patch", None),
        P("clip", "patch", None),
        P("clip", None),
        P(None, "patch", None),
        P(None, "patch", None),
        P(None, "patch", None),
        P(None, "patch", None),
        P(None, "patch", None),
        P(None, "patch", None),
        P(None, None, "patch"),
        P(None, None, "patch"),
    )
    return jax.shard_map(local, mesh=mesh, in_specs=in_specs, out_specs=out_specs, check_vma=False)
```

```python
import functools

import jax
import jax.numpy as jnp
from jax import lax
from jax.experimental import pallas as pl
from jax.experimental.pallas import tpu as pltpu
from jax.sharding import PartitionSpec as P

HEADS = 12
HD = 64
LAYERS = 2
REAL_PATCH = 196
QUAD = 4
WIDE = QUAD * HD
QUADS = HEADS // QUAD
CLS_ROWS = 16

EPSILON = 1e-05
NEG_LARGE = -1e30
ROOT_HALF = 0.7071067811865476
INV_ROOT_TWO_PI = 0.3989422804014327
SCALE = HD**-0.5
VMEM_LIMIT = 48 * 1024 * 1024

f32 = jnp.float32
bf16 = jnp.bfloat16
MESH = pl.DeviceIdType.MESH


def layer_norm(values, norm_gain, norm_bias):
    centered = values - jnp.mean(values, -1, keepdims=True)
    inverse = lax.rsqrt(jnp.mean(centered * centered, -1, keepdims=True) + EPSILON)
    scaled = centered * inverse
    return (scaled * norm_gain + norm_bias, scaled, inverse)


def norm_back(grad_out, scaled, inverse, norm_gain):
    weighted = grad_out * norm_gain
    grad_input = inverse * (
        weighted
        - jnp.mean(weighted, -1, keepdims=True)
        - scaled * jnp.mean(weighted * scaled, -1, keepdims=True)
    )
    return (grad_input, jnp.sum(grad_out * scaled, 0), jnp.sum(grad_out, 0))


def project(left, matrix):
    return jnp.dot(left, matrix, preferred_element_type=f32)


def project_back(grad_out, matrix):
    return lax.dot_general(grad_out, matrix, (((1,), (1,)), ((), ())), preferred_element_type=f32)


def weight_grad(left, grad_out):
    return lax.dot_general(
        left, grad_out, (((0,), (0,)), ((), ())), preferred_element_type=f32
    ).astype(bf16)


def gelu_value(hidden):
    return 0.5 * hidden * (1.0 + lax.erf(hidden * ROOT_HALF))


def gelu_slope(hidden):
    return 0.5 * (1.0 + lax.erf(hidden * ROOT_HALF)) + hidden * INV_ROOT_TWO_PI * jnp.exp(
        -0.5 * hidden * hidden
    )


def dot_nt(left, right):
    return lax.dot_general(left, right, (((1,), (1,)), ((), ())), preferred_element_type=f32)


def dot_nn(left, right):
    return lax.dot_general(left, right, (((1,), (0,)), ((), ())), preferred_element_type=f32)


def dot_tn(left, right):
    return lax.dot_general(left, right, (((0,), (0,)), ((), ())), preferred_element_type=f32)


def spread_heads(rows):
    head = lax.broadcasted_iota(jnp.int32, rows.shape, 1) // HD
    return jnp.concatenate([jnp.where(head == h, rows, jnp.zeros_like(rows)) for h in range(QUAD)], 0)


def merge_heads(stacked):
    count = stacked.shape[0] // QUAD
    head = lax.broadcasted_iota(jnp.int32, (count, WIDE), 1) // HD
    merged = stacked[:count]
    for h in range(1, QUAD):
        merged = jnp.where(head == h, stacked[h * count : (h + 1) * count], merged)
    return merged


def probabilities(scores):
    exponents = [jnp.exp(part - jnp.max(part, 0, keepdims=True)) for part in scores]
    return [part * (1.0 / jnp.sum(part, 0, keepdims=True)) for part in exponents]


def forward_tiles(tiles, bias):
    spreads = [spread_heads(tile[0] * SCALE) for tile in tiles]
    scores = [dot_nt(tile[1], spread) + bias for tile, spread in zip(tiles, spreads)]
    probs = [part.astype(bf16) for part in probabilities(scores)]
    outs = [dot_tn(part, tile[2]) for part, tile in zip(probs, tiles)]
    return [merge_heads(part).astype(bf16) for part in outs]


def backward_tiles(tiles, bias):
    spreads = [spread_heads(tile[0] * SCALE) for tile in tiles]
    grad_spreads = [spread_heads(tile[3]) for tile in tiles]
    scores = [dot_nt(tile[1], spread) + bias for tile, spread in zip(tiles, spreads)]
    grad_probs = [dot_nt(tile[2], spread) for tile, spread in zip(tiles, grad_spreads)]
    probs = probabilities(scores)
    grad_scores = [
        (part * (grad - jnp.sum(part * grad, 0, keepdims=True))).astype(bf16)
        for part, grad in zip(probs, grad_probs)
    ]
    grad_queries = [dot_tn(grad, tile[1]) for grad, tile in zip(grad_scores, tiles)]
    grad_keys = [dot_nn(grad, spread) for grad, spread in zip(grad_scores, spreads)]
    grad_values = [dot_nn(part.astype(bf16), spread) for part, spread in zip(probs, grad_spreads)]
    return [(merge_heads(q) * SCALE, k, v) for q, k, v in zip(grad_queries, grad_keys, grad_values)]


def columns(part, quad, width):
    start = part * width + quad * WIDE
    return slice(start, start + WIDE)


def time_forward_kernel(bias_ref, qkv_ref, out_ref):
    width = out_ref.shape[1]
    bias = bias_ref[...]
    for quad in range(QUADS):
        parts = [qkv_ref[:, columns(part, quad, width)] for part in range(3)]
        out_ref[:, columns(0, quad, width)] = forward_tiles([parts], bias)[0]


def time_backward_kernel(bias_ref, qkv_ref, grad_ref, out_ref):
    width = grad_ref.shape[1]
    bias = bias_ref[...]
    for quad in range(QUADS):
        parts = [qkv_ref[:, columns(part, quad, width)] for part in range(3)]
        grads = backward_tiles([parts + [grad_ref[:, columns(0, quad, width)]]], bias)[0]
        for part in range(3):
            out_ref[:, columns(part, quad, width)] = grads[part].astype(bf16)


def group_rows(patch_count, frames):
    return (2 if patch_count % 2 == 0 else 1) * frames


def time_bias(same_clip, patch_count, frames):
    rows = group_rows(patch_count, frames)
    ids = jnp.arange(rows, dtype=jnp.int32)
    same_patch = (ids[:, None] // frames) == (ids[None, :] // frames)
    tiled = jnp.tile(same_clip, (rows // frames, rows // frames))
    return jnp.tile(jnp.where(same_patch & tiled, 0.0, NEG_LARGE).astype(f32), (1, QUAD))


def params(*semantics):
    return pltpu.CompilerParams(dimension_semantics=semantics, vmem_limit_bytes=VMEM_LIMIT)


def time_forward(bias, qkv):
    rows = bias.shape[0]
    width = qkv.shape[1] // 3
    return pl.pallas_call(
        time_forward_kernel,
        grid=(qkv.shape[0] // rows,),
        in_specs=[
            pl.BlockSpec(bias.shape, lambda i: (0, 0)),
            pl.BlockSpec((rows, 3 * width), lambda i: (i, 0)),
        ],
        out_specs=pl.BlockSpec((rows, width), lambda i: (i, 0)),
        out_shape=jax.ShapeDtypeStruct((qkv.shape[0], width), bf16),
        compiler_params=params("parallel"),
        name="time_forward",
    )(bias, qkv)


def time_backward(bias, qkv, grad_out):
    rows = bias.shape[0]
    width = qkv.shape[1] // 3
    return pl.pallas_call(
        time_backward_kernel,
        grid=(qkv.shape[0] // rows,),
        in_specs=[
            pl.BlockSpec(bias.shape, lambda i: (0, 0)),
            pl.BlockSpec((rows, 3 * width), lambda i: (i, 0)),
            pl.BlockSpec((rows, width), lambda i: (i, 0)),
        ],
        out_specs=pl.BlockSpec((rows, 3 * width), lambda i: (i, 0)),
        out_shape=jax.ShapeDtypeStruct(qkv.shape, bf16),
        compiler_params=params("parallel"),
        name="time_backward",
    )(bias, qkv, grad_out)


def with_class(slot, rows, cls_rows):
    ids = lax.broadcasted_iota(jnp.int32, cls_rows.shape, 0)
    picked = jnp.sum(jnp.where(ids == slot, cls_rows.astype(f32), 0.0), 0, keepdims=True)
    row_ids = lax.broadcasted_iota(jnp.int32, rows.shape, 0)
    return jnp.where(row_ids == REAL_PATCH, picked.astype(bf16), rows)


def key_bias(count):
    key_ids = lax.broadcasted_iota(jnp.int32, (count, 1), 0)
    return jnp.where(key_ids <= REAL_PATCH, 0.0, NEG_LARGE).astype(f32)


def space_forward_kernel(slot_ref, q_ref, k_ref, v_ref, ck_ref, cv_ref, out_ref):
    slot = slot_ref[pl.program_id(0)]
    keys = with_class(slot, k_ref[...], ck_ref[...])
    values = with_class(slot, v_ref[...], cv_ref[...])
    out_ref[...] = forward_tiles([(q_ref[...], keys, values)], key_bias(keys.shape[0]))[0]


def space_backward_kernel(
    slot_ref, q_ref, k_ref, v_ref, ck_ref, cv_ref, g_ref, dq_ref, dk_ref, dv_ref, dck_ref, dcv_ref
):
    slot = slot_ref[pl.program_id(0)]
    keys = with_class(slot, k_ref[...], ck_ref[...])
    values = with_class(slot, v_ref[...], cv_ref[...])
    tile = (q_ref[...], keys, values, g_ref[...])
    grad_q, grad_k, grad_v = backward_tiles([tile], key_bias(keys.shape[0]))[0]
    row_ids = lax.broadcasted_iota(jnp.int32, grad_k.shape, 0)
    dq_ref[...] = grad_q.astype(bf16)
    dk_ref[...] = jnp.where(row_ids < REAL_PATCH, grad_k, 0.0).astype(bf16)
    dv_ref[...] = jnp.where(row_ids < REAL_PATCH, grad_v, 0.0).astype(bf16)
    dck_ref[0] = jnp.sum(jnp.where(row_ids == REAL_PATCH, grad_k, 0.0), 0, keepdims=True)
    dcv_ref[0] = jnp.sum(jnp.where(row_ids == REAL_PATCH, grad_v, 0.0), 0, keepdims=True)


def space_specs(frames, patches):
    cls_block = frames * patches // CLS_ROWS

    def rows(part):
        return pl.BlockSpec((patches, WIDE), lambda f, c, s: (f, part * QUADS + c))

    def cls(part):
        return pl.BlockSpec((CLS_ROWS, WIDE), lambda f, c, s: (cls_block, part * QUADS + c))

    return [rows(0), rows(1), rows(2), cls(1), cls(2)], rows(0)


def space_forward(slots, qkv, frames, patches):
    width = qkv.shape[1] // 3
    in_specs, out_spec = space_specs(frames, patches)
    return pl.pallas_call(
        space_forward_kernel,
        grid_spec=pltpu.PrefetchScalarGridSpec(
            num_scalar_prefetch=1,
            grid=(frames, QUADS),
            in_specs=in_specs,
            out_specs=out_spec,
        ),
        out_shape=jax.ShapeDtypeStruct((frames * patches, width), bf16),
        compiler_params=params("parallel", "parallel"),
        name="space_forward",
    )(slots, qkv, qkv, qkv, qkv, qkv)


def space_backward(slots, qkv, grad_out, frames, patches):
    width = qkv.shape[1] // 3
    in_specs, out_spec = space_specs(frames, patches)
    rows = jax.ShapeDtypeStruct((frames * patches, width), bf16)
    cls_spec = pl.BlockSpec((1, 1, WIDE), lambda f, c, s: (f, 0, c))
    cls = jax.ShapeDtypeStruct((frames, 1, width), f32)
    return pl.pallas_call(
        space_backward_kernel,
        grid_spec=pltpu.PrefetchScalarGridSpec(
            num_scalar_prefetch=1,
            grid=(frames, QUADS),
            in_specs=in_specs + [out_spec],
            out_specs=[out_spec] * 3 + [cls_spec] * 2,
        ),
        out_shape=[rows] * 3 + [cls] * 2,
        compiler_params=params("parallel", "parallel"),
        name="space_backward",
    )(slots, qkv, qkv, qkv, qkv, qkv, grad_out)


CHUNKS = 16
BLOCKS = 3
LAG = 4
ROUTES = (("x", "y", "zl", "zh", "y", "x"), ("y", "x", "zl", "zh", "x", "y"), ("zl", "zh", "x", "y", "y", "x"))
SUMS = 4
STAGES = 7
PIECE = (48, 128)
SMALL = ("core", "zl", "zh", "x", "y")
SEGMENTS = ((0, 4), (1, 4), (2, 1), (3, 3), (4, 1), (5, 3))


def recv_shape(route, stage):
    left = [d for d in ("zh", "zl", "x", "y") if d not in route[: stage + 1]]
    return (2,) * len(left) + PIECE


def reduce_kernel(tokens, *refs):
    (lhs_refs, rhs_refs) = (refs[:6], refs[6:12])
    small_in, small_ref, *results = refs[12:20]
    small_box, out_ref, buf, core_in, lhs_buf, rhs_buf = refs[20:26]
    inboxes = refs[26 : 26 + BLOCKS * SUMS]
    small_send, small_recv, load_sem, core_send, core_recv, send_sem, recv_sem = refs[26 + BLOCKS * SUMS :]
    clip, patch = lax.axis_index("clip"), lax.axis_index("patch")
    me = {"core": patch % 2, "zl": (patch // 2) % 2, "zh": patch // 4, "x": clip % 2, "y": clip // 2}
    step_of = {"core": ("patch", 1), "zl": ("patch", 2), "zh": ("patch", 4), "x": ("clip", 1), "y": ("clip", 2)}

    def peer(dim):
        axis, stride = step_of[dim]
        own = clip if axis == "clip" else patch
        other = own + stride - 2 * stride * me[dim]
        return (other, patch) if axis == "clip" else (clip, other)

    barrier = pltpu.get_barrier_semaphore()
    for dim in step_of:
        pl.semaphore_signal(barrier, inc=1, device_id=peer(dim), device_id_type=MESH)
    pl.semaphore_wait(barrier, len(step_of))

    small_ref[...] = small_in[...]

    def small_copy(i):
        part = pl.ds(0, 16 if i < 3 else 8)
        return pltpu.make_async_remote_copy(
            src_ref=small_ref.at[part],
            dst_ref=small_box.at[i, part],
            send_sem=small_send.at[i],
            recv_sem=small_recv.at[i],
            device_id=peer(SMALL[i]),
            device_id_type=MESH,
        )

    def small_step(i):
        if 0 < i <= len(SMALL):
            rows = slice(0, 16 if i <= 3 else 8)
            small_copy(i - 1).wait()
            small_ref[rows] += small_box[i - 1, rows]
        if i < len(SMALL):
            small_copy(i).start()

    def place(route, stage, value):
        done = route[:stage]

        def at(dim):
            if dim in done:
                return me[dim]
            if dim == route[stage]:
                return value
            return slice(None)

        return at

    def core_copy(c, z):
        return pltpu.make_async_remote_copy(
            src_ref=buf.at[c, z // 2, z % 2, 1 - me["core"]],
            dst_ref=core_in.at[c, z // 2, z % 2],
            send_sem=core_send.at[c, z],
            recv_sem=core_recv.at[c, z],
            device_id=peer("core"),
            device_id_type=MESH,
        )

    def exchange(c, block, stage):
        route = ROUTES[block]
        dim = route[stage]
        slot = lax.rem(c, 2)
        if stage < SUMS:
            at = place(route, stage, 1 - me[dim])
            src = buf.at[c, at("zh"), at("zl"), me["core"], block, at("x"), at("y")]
            dst = inboxes[block * SUMS + stage].at[slot]
        elif stage == SUMS:
            src = dst = out_ref.at[c, block, me["x"], me["y"]]
        else:
            if dim == "x":
                src = dst = out_ref.at[c, block, me["x"]]
            else:
                src = dst = out_ref.at[c, block, :, me["y"]]
        return pltpu.make_async_remote_copy(
            src_ref=src,
            dst_ref=dst,
            send_sem=send_sem.at[slot, block, stage],
            recv_sem=recv_sem.at[slot, block, stage],
            device_id=peer(dim),
            device_id_type=MESH,
        )

    def add_core(c):
        for z in range(4):
            core_copy(c, z).wait()
        for zh in range(2):
            for zl in range(2):
                mine = buf[c, zh, zl, me["core"]].astype(f32) + core_in[c, zh, zl].astype(f32)
                buf[c, zh, zl, me["core"]] = mine.astype(bf16)
        for block in range(BLOCKS):
            exchange(c, block, 0).start()

    def add_stage(c, stage):
        slot = lax.rem(c, 2)
        for block in range(BLOCKS):
            exchange(c, block, stage).wait()
            if stage < SUMS:
                at = place(ROUTES[block], stage, me[ROUTES[block][stage]])
                where = (c, at("zh"), at("zl"), me["core"], block, at("x"), at("y"))
                mine = buf[where].astype(f32) + inboxes[block * SUMS + stage][slot].astype(f32)
                buf[where] = mine.astype(bf16)
                if stage == SUMS - 1:
                    out_ref[c, block, me["x"], me["y"]] = mine.astype(bf16)
            if stage + 1 < STAGES - 1:
                exchange(c, block, stage + 1).start()
            else:
                finish(c, block)

    def finish(c, block):
        start = 0
        for which, count in SEGMENTS:

            @pl.when((c >= start) & (c < start + count))
            def _(which=which, start=start):
                for xh in range(2):
                    for yh in range(2):
                        part = out_ref[c, block, xh, yh]
                        columns = slice(block * 256 + yh * 128, block * 256 + (yh + 1) * 128)
                        if which == 0:
                            row = pl.multiple_of((c - start) * 96 + xh * 48, 16)
                            results[which][pl.ds(row, 48), columns] = part
                        else:
                            column = pl.multiple_of((c - start) * 768 + columns.start, 128)
                            results[which][xh * 48 : (xh + 1) * 48, pl.ds(column, 128)] = part

            start += count

    def stages(t):
        for stage in reversed(range(STAGES)):
            c = t - LAG - stage

            @pl.when((c >= 0) & (c < CHUNKS))
            def _():
                if stage == 0:
                    add_core(c)
                else:
                    add_stage(c, stage - 1)

    def store(c, z, core, rows, block):
        for xh in range(2):
            for yh in range(2):
                part = rows[xh * 48 : (xh + 1) * 48, yh * 128 : (yh + 1) * 128]
                buf[c, z // 2, z % 2, core, block, xh, yh] = part.astype(bf16)

    def product(lhs, rhs):
        return lax.dot_general(lhs, rhs, (((0,), (0,)), ((), ())), preferred_element_type=f32)

    def load(which, lhs_column, rhs_column, rows):
        copies = (
            pltpu.make_async_copy(lhs_refs[which].at[:, pl.ds(lhs_column, 768)], lhs_buf.at[pl.ds(0, rows)], load_sem.at[0]),
            pltpu.make_async_copy(rhs_refs[which].at[:, pl.ds(rhs_column, 768)], rhs_buf.at[pl.ds(0, rows)], load_sem.at[1]),
        )
        for copy in copies:
            copy.start()
        for copy in copies:
            copy.wait()

    def whole_chunk(c, which, rhs_column):
        rows = tokens[which]
        load(which, 0, rhs_column, rows)
        for half in range(2):
            lhs = lhs_buf[:rows, half * 384 : (half + 1) * 384]
            for block in range(BLOCKS):
                done = product(lhs, rhs_buf[:rows, block * 256 : (block + 1) * 256])
                for i in range(4):
                    store(c, half * 2 + i // 2, i % 2, done[i * 96 : (i + 1) * 96], block)
        for z in range(4):
            core_copy(c, z).start()

    def down_part(t):
        rows = tokens[0]
        load(0, t * 768, 0, rows)
        for core in range(2):
            lhs = lhs_buf[:rows, core * 384 : (core + 1) * 384]
            for block in range(BLOCKS):
                done = product(lhs, rhs_buf[:rows, block * 256 : (block + 1) * 256])
                for c in range(4):
                    for xh in range(2):
                        for yh in range(2):
                            part = done[c * 96 + xh * 48 : c * 96 + (xh + 1) * 48, yh * 128 : (yh + 1) * 128]
                            buf[c, t // 2, t % 2, core, block, xh, yh] = part.astype(bf16)
        for c in range(4):
            core_copy(c, t).start()

    small_step(0)

    @pl.loop(0, 4)
    def _(t):
        down_part(t)

    small_step(1)

    first = 4
    for which, count in SEGMENTS[1:]:

        @pl.loop(first, first + count)
        def _(t, which=which, first=first):
            stages(t)
            whole_chunk(t, which, pl.multiple_of((t - first) * 768, 768))

        first += count
        small_step(which + 1)

    @pl.loop(CHUNKS, CHUNKS + LAG + STAGES - 1)
    def _(t):
        stages(t)


def reduce_grads(lhs, rhs, small):
    tokens = tuple(part.shape[0] for part in lhs)
    most = max(tokens)
    inbox = [pltpu.VMEM((2,) + recv_shape(ROUTES[b], s), bf16) for b in range(BLOCKS) for s in range(SUMS)]
    shapes = [(384, 768)] + [(96, 768 * count) for _, count in SEGMENTS[1:]]
    small, *large = pl.pallas_call(
        functools.partial(reduce_kernel, tokens),
        out_shape=[jax.ShapeDtypeStruct(small.shape, f32)] + [jax.ShapeDtypeStruct(shape, bf16) for shape in shapes],
        in_specs=[pl.BlockSpec(memory_space=pl.ANY)] * 12 + [pl.BlockSpec(memory_space=pltpu.VMEM)],
        out_specs=[pl.BlockSpec(memory_space=pltpu.VMEM)] * 7,
        scratch_shapes=[
            pltpu.VMEM((len(SMALL),) + small.shape, f32),
            pltpu.VMEM((CHUNKS, BLOCKS, 2, 2) + PIECE, bf16),
            pltpu.VMEM((CHUNKS, 2, 2, 2, BLOCKS, 2, 2) + PIECE, bf16),
            pltpu.VMEM((CHUNKS, 2, 2, BLOCKS, 2, 2) + PIECE, bf16),
            pltpu.VMEM((most, 768), bf16),
            pltpu.VMEM((most, 768), bf16),
            *inbox,
            pltpu.SemaphoreType.DMA((len(SMALL),)),
            pltpu.SemaphoreType.DMA((len(SMALL),)),
            pltpu.SemaphoreType.DMA((2,)),
            pltpu.SemaphoreType.DMA((CHUNKS, 4)),
            pltpu.SemaphoreType.DMA((CHUNKS, 4)),
            pltpu.SemaphoreType.DMA((2, BLOCKS, STAGES - 1)),
            pltpu.SemaphoreType.DMA((2, BLOCKS, STAGES - 1)),
        ],
        compiler_params=pltpu.CompilerParams(
            collective_id=1, has_side_effects=True, vmem_limit_bytes=56 * 1024 * 1024
        ),
        name="reduce_grads",
    )(*lhs, *rhs, small)
    return large, small


def frame_slots(lengths_row, frame_ids):
    clip_ends = jnp.cumsum(lengths_row)
    return jnp.sum((frame_ids[:, None] >= clip_ends[None, :]).astype(jnp.int32), axis=1)


class Layout:
    def __init__(self, devices, frames, patches):
        self.devices = devices
        self.frames = frames
        self.patches = patches
        self.all_patches = patches * devices
        self.away_frames = -(-frames // devices)
        used = self.away_frames * patches
        self.block = -(-used // 16) * 16
        self.home_rows = frames * patches
        self.away_rows = self.away_frames * self.all_patches
        self.sent_rows = devices * self.block

    def home_of_sent(self):
        row = jnp.arange(self.sent_rows, dtype=jnp.int32)
        peer, inner = row // self.block, row % self.block
        frame = peer * self.away_frames + inner // self.patches
        valid = (inner < self.away_frames * self.patches) & (frame < self.frames)
        return jnp.where(valid, (inner % self.patches) * self.frames + frame, -1)

    def sent_of_away(self):
        row = jnp.arange(self.away_rows + CLS_ROWS, dtype=jnp.int32)
        frame, patch = row // self.all_patches, row % self.all_patches
        sent = (patch // self.patches) * self.block + frame * self.patches + patch % self.patches
        return jnp.where(row < self.away_rows, sent, -1)

    def to_away(self, values):
        pick = self.home_of_sent()[:, None] == jnp.arange(self.home_rows, dtype=jnp.int32)[None, :]
        sent = jnp.dot(pick.astype(bf16), values, preferred_element_type=bf16)
        got = lax.all_to_all(sent, "patch", split_axis=0, concat_axis=0, tiled=True)
        pick = self.sent_of_away()[:, None] == jnp.arange(self.sent_rows, dtype=jnp.int32)[None, :]
        return jnp.dot(pick.astype(bf16), got, preferred_element_type=f32)

    def to_home(self, values):
        pick = jnp.arange(self.sent_rows, dtype=jnp.int32)[:, None] == self.sent_of_away()[None, : self.away_rows]
        sent = jnp.dot(pick.astype(bf16), values, preferred_element_type=bf16)
        got = lax.all_to_all(sent, "patch", split_axis=0, concat_axis=0, tiled=True)
        pick = jnp.arange(self.home_rows, dtype=jnp.int32)[:, None] == self.home_of_sent()[None, :]
        return jnp.dot(pick.astype(bf16), got, preferred_element_type=f32)


def rows_of(total):
    for rows in (80, 48, 16):
        if total % rows == 0:
            return rows
    return total


def norm_rows(values):
    centered = values - jnp.mean(values, -1, keepdims=True)
    inverse = lax.rsqrt(jnp.mean(centered * centered, -1, keepdims=True) + EPSILON)
    return centered * inverse, inverse


def norm_forward(load, gain, shift, out_ref):
    rows = rows_of(out_ref.shape[0])

    @pl.loop(0, out_ref.shape[0] // rows)
    def _(step):
        start = pl.multiple_of(step * rows, 16)
        scaled, _ = norm_rows(load(start, rows))
        out_ref[pl.ds(start, rows), :] = (scaled * gain + shift).astype(bf16)


def norm_backward(load, grad_ref, gain, store, total, sums):
    rows = rows_of(total)
    width = gain.shape[-1]

    def fold(part):
        return jnp.sum(part.reshape(rows // 8, 8, width), 0)

    @pl.loop(0, total // rows)
    def _(step):
        start = pl.multiple_of(step * rows, 16)
        scaled, inverse = norm_rows(load(start, rows))
        grad = grad_ref[pl.ds(start, rows), :]
        weighted = grad * gain
        store(
            start,
            rows,
            inverse
            * (
                weighted
                - jnp.mean(weighted, -1, keepdims=True)
                - scaled * jnp.mean(weighted * scaled, -1, keepdims=True)
            ),
        )
        sums[0][...] += fold(grad * scaled)
        sums[1][...] += fold(grad)


class Loads:
    def __init__(self, sources, buffers, sems):
        self.copies = [
            pltpu.make_async_copy(source, buffer, sems.at[i])
            for i, (source, buffer) in enumerate(zip(sources, buffers))
        ]
        for copy in self.copies:
            copy.start()
        self.buffers = buffers
        self.next = 0

    def get(self):
        self.copies[self.next].wait()
        self.next += 1
        return self.buffers[self.next - 1]


class Saves:
    def __init__(self, buffers, targets, sems):
        self.copies = [
            pltpu.make_async_copy(buffer, target, sems.at[i])
            for i, (buffer, target) in enumerate(zip(buffers, targets))
        ]

    def put(self, i):
        self.copies[i].start()

    def finish(self):
        for copy in self.copies:
            copy.wait()


class Move:
    def __init__(self, devices, sent, got, send_sem, recv_sem):
        self.devices, self.sent, self.got = devices, sent, got
        self.send_sem, self.recv_sem = send_sem, recv_sem
        self.clip, self.me = lax.axis_index("clip"), lax.axis_index("patch")
        self.barrier = pltpu.get_barrier_semaphore()
        for offset in range(1, devices):
            pl.semaphore_signal(self.barrier, inc=1, device_id=self.peer(offset), device_id_type=MESH)

    def peer(self, offset):
        return (self.clip, lax.rem(self.me + offset, self.devices))

    def copy(self, offset):
        other = lax.rem(self.me + offset, self.devices)
        return pltpu.make_async_remote_copy(
            src_ref=self.sent.at[other],
            dst_ref=self.got.at[self.me],
            send_sem=self.send_sem.at[offset],
            recv_sem=self.recv_sem.at[offset],
            device_id=self.peer(offset),
            device_id_type=MESH,
        )

    def run(self, order_ref, source_ref):
        rows = self.sent.shape[1]
        pl.semaphore_wait(self.barrier, self.devices - 1)
        for offset in list(range(1, self.devices)) + [0]:
            other = lax.rem(self.me + offset, self.devices)
            start = pl.multiple_of(other * rows, 16)
            picked = dot_nn(order_ref[pl.ds(start, rows), :], source_ref[...]).astype(bf16)
            if offset:
                self.sent[other] = picked
                self.copy(offset).start()
            else:
                self.got[self.me] = picked
        for offset in range(1, self.devices):
            self.copy(offset).wait()

    def place(self, order_ref):
        width = self.got.shape[-1]
        return dot_nn(order_ref[...], self.got[...].reshape(-1, width))


def time_tiles(bias_ref, qkv_ref, width, group, grad_ref=None):
    rows = bias_ref.shape[0]
    here = pl.ds(pl.multiple_of(group * rows, 16), rows)
    tiles = []
    for quad in range(QUADS):
        tile = [qkv_ref[here, columns(part, quad, width)] for part in range(3)]
        if grad_ref is not None:
            tile.append(grad_ref[here, columns(0, quad, width)])
        tiles.append(tile)
    return here, tiles


def space_tiles(patches, total, slot, qkv_ref, width, frame, grad_ref=None):
    here = pl.ds(pl.multiple_of(frame * patches, 16), patches)
    tiles = []
    for quad in range(QUADS):
        tile = [qkv_ref[here, columns(part, quad, width)] for part in range(3)]
        for part in (1, 2):
            tile[part] = with_class(slot, tile[part], qkv_ref[total : total + CLS_ROWS, columns(part, quad, width)])
        if grad_ref is not None:
            tile.append(grad_ref[here, columns(0, quad, width)])
        tiles.append(tile)
    return here, tiles


def time_half(layer, devices, *refs):
    x_ref, gain_ref, shift_ref, bias_ref, go_ref, land_ref, proj_hbm, output_hbm = refs[:8]
    away_ref, *saved = refs[8:12]
    normed_ref, qkv_ref, mixed_ref = refs[12:15]
    proj, output, after, sent, got, load_sem, save_sem, send_sem, recv_sem = refs[15:]
    width = x_ref.shape[1]
    weights = Loads((proj_hbm.at[layer], output_hbm.at[layer]), (proj, output), load_sem)
    saves = Saves((normed_ref, qkv_ref, mixed_ref), saved, save_sem)
    move = Move(devices, sent, got, send_sem, recv_sem)
    norm_forward(
        lambda start, rows: x_ref[pl.ds(start, rows), :].astype(f32),
        gain_ref[layer, 0:1],
        shift_ref[layer, 0:1],
        normed_ref,
    )
    saves.put(0)
    weight = weights.get()
    for part in range(3):
        here = slice(part * width, (part + 1) * width)
        qkv_ref[:, here] = dot_nn(normed_ref[...], weight[:, here]).astype(bf16)
    saves.put(1)

    @pl.loop(0, x_ref.shape[0] // bias_ref.shape[0])
    def _(group):
        here, tiles = time_tiles(bias_ref, qkv_ref, width, group)
        for quad, done in enumerate(forward_tiles(tiles, bias_ref[...])):
            mixed_ref[here, columns(0, quad, width)] = done

    saves.put(2)
    weight = weights.get()
    after[...] = (x_ref[...].astype(f32) + dot_nn(mixed_ref[...], weight[...])).astype(bf16)
    move.run(go_ref, after)
    away_ref[...] = move.place(land_ref).astype(bf16)
    saves.finish()


def space_half(layer, devices, patches, *refs):
    slot_ref, x_ref, cls_ref, gain_ref, shift_ref, go_ref, land_ref = refs[:7]
    proj_hbm, output_hbm, up_hbm, down_hbm = refs[7:11]
    home_ref, *saved = refs[11:19]
    normed_ref, qkv_ref, mixed_ref, middle_ref, normed_f_ref, active_ref, slope_ref = staged = refs[19:26]
    proj, output, up, down, middle, after, sent, got, load_sem, save_sem, send_sem, recv_sem = refs[26:]
    saves = Saves(staged, saved, save_sem)
    width = x_ref.shape[1]
    total = mixed_ref.shape[0]
    sources = [part.at[layer] for part in (proj_hbm, output_hbm, up_hbm, down_hbm)]
    weights = Loads(sources, (proj, output, up, down), load_sem)
    move = Move(devices, sent, got, send_sem, recv_sem)
    gain, shift = gain_ref[layer, 1:2], shift_ref[layer, 1:2]
    norm_forward(lambda start, rows: x_ref[pl.ds(start, rows), :].astype(f32), gain, shift, normed_ref.at[pl.ds(0, total)])
    scaled, _ = norm_rows(cls_ref[...])
    normed_ref[total:, :] = (scaled * gain + shift).astype(bf16)
    saves.put(0)
    weight = weights.get()
    for part in range(3):
        here = slice(part * width, (part + 1) * width)
        qkv_ref[:, here] = dot_nn(normed_ref[...], weight[:, here]).astype(bf16)
    saves.put(1)
    bias = key_bias(patches)

    @pl.loop(0, total // patches)
    def _(frame):
        here, tiles = space_tiles(patches, total, slot_ref[frame], qkv_ref, width, frame)
        for quad, done in enumerate(forward_tiles(tiles, bias)):
            mixed_ref[here, columns(0, quad, width)] = done

    saves.put(2)
    weight = weights.get()
    middle[...] = x_ref[:total, :].astype(f32) + dot_nn(mixed_ref[...], weight[...])
    middle_ref[...] = middle[...].astype(bf16)
    saves.put(3)
    norm_forward(lambda start, rows: middle[pl.ds(start, rows), :], gain_ref[layer, 2:3], shift_ref[layer, 2:3], normed_f_ref)
    saves.put(4)
    weight = weights.get()
    block = 256
    for start in range(0, up.shape[1], block):
        here = slice(start, start + block)
        hidden = dot_nn(normed_f_ref[...], weight[:, here])
        share = 0.5 * (1.0 + lax.erf(hidden * ROOT_HALF))
        active_ref[:, here] = (hidden * share).astype(bf16)
        slope = share + hidden * (INV_ROOT_TWO_PI * jnp.exp(-0.5 * hidden * hidden))
        slope_ref[:, here] = slope.astype(bf16)
    saves.put(5)
    saves.put(6)
    weight = weights.get()
    after[...] = (middle[...] + dot_nn(active_ref[...], weight[...])).astype(bf16)
    move.run(go_ref, after)
    home_ref[...] = move.place(land_ref).astype(bf16)
    saves.finish()


def space_half_back(layer, devices, patches, *refs):
    slot_ref, grad_ref, cls_ref, gain_ref, go_ref, land_ref = refs[:6]
    inputs = refs[6:14]
    home_ref, grad_cls_ref, sums_ref, *saved = refs[14:20]
    hidden_ref, branch_ref, dqkv_ref = staged = refs[20:23]
    loaded, refs = refs[23:31], refs[31:]
    _, slope_ref, _, middle_ref, _, qkv_ref, _, x_ref = loaded
    state, wide, mixed, after, cls_sum, *sums = refs[:9]
    sent, got, load_sem, save_sem, send_sem, recv_sem = refs[9:]
    width = x_ref.shape[1]
    total = branch_ref.shape[0]
    sources = [part.at[layer] if len(part.shape) == 3 else part for part in inputs]
    loads = Loads(sources, loaded, load_sem)
    saves = Saves(staged, saved, save_sem)
    move = Move(devices, sent, got, send_sem, recv_sem)
    for part in sums:
        part[...] = jnp.zeros_like(part)
    cls_sum[...] = jnp.zeros_like(cls_sum)
    weight = loads.get()
    loads.get()
    block = 256
    for start in range(0, weight.shape[0], block):
        here = slice(start, start + block)
        grad_active = dot_nt(grad_ref[:total, :], weight[here, :])
        hidden_ref[:, here] = (grad_active * slope_ref[:, here].astype(f32)).astype(bf16)
    saves.put(0)
    weight = loads.get()
    wide[:total, :] = dot_nt(hidden_ref[...], weight[...])
    loads.get()

    def keep(start, rows, part):
        here = pl.ds(start, rows)
        both = grad_ref[here, :].astype(f32) + part
        state[here, :] = both
        branch_ref[here, :] = both.astype(bf16)

    norm_backward(
        lambda start, rows: middle_ref[pl.ds(start, rows), :].astype(f32),
        wide,
        gain_ref[layer, 2:3],
        keep,
        total,
        sums[0:2],
    )
    saves.put(1)
    weight = loads.get()
    mixed[...] = dot_nt(branch_ref[...], weight[...]).astype(bf16)
    loads.get()
    bias = key_bias(patches)

    @pl.loop(0, total // patches)
    def _(frame):
        slot = slot_ref[frame]
        here, tiles = space_tiles(patches, total, slot, qkv_ref, width, frame, mixed)
        row_ids = lax.broadcasted_iota(jnp.int32, (patches, WIDE), 0)
        cls_ids = lax.broadcasted_iota(jnp.int32, (CLS_ROWS, WIDE), 0)
        for quad, grads in enumerate(backward_tiles(tiles, bias)):
            dqkv_ref[here, columns(0, quad, width)] = grads[0].astype(bf16)
            for part in (1, 2):
                at = columns(part, quad, width)
                dqkv_ref[here, at] = jnp.where(row_ids < REAL_PATCH, grads[part], 0.0).astype(bf16)
                row = grads[part][REAL_PATCH : REAL_PATCH + 1]
                cls_sum[:, at] += jnp.where(cls_ids == slot, row, 0.0)

    dqkv_ref[total:, :] = cls_sum[...].astype(bf16)
    saves.put(2)
    weight = loads.get()
    wide[...] = dot_nt(dqkv_ref[...], weight[...])
    loads.get()

    def add(start, rows, part):
        here = pl.ds(start, rows)
        after[here, :] = (state[here, :] + part).astype(bf16)

    def keep_cls(start, rows, part):
        grad_cls_ref[...] = part

    gain = gain_ref[layer, 1:2]
    norm_backward(lambda start, rows: x_ref[pl.ds(start, rows), :].astype(f32), wide, gain, add, total, sums[2:4])
    norm_backward(lambda start, rows: cls_ref[...], wide.at[pl.ds(total, CLS_ROWS)], gain, keep_cls, CLS_ROWS, sums[2:4])
    for i, part in enumerate(sums):
        sums_ref[i : i + 1, :] = jnp.sum(part[...], 0, keepdims=True)
    move.run(go_ref, after)
    home_ref[...] = move.place(land_ref).astype(bf16)
    saves.finish()


def time_half_back(layer, devices, *refs):
    grad_ref, gain_ref, bias_ref, go_ref, land_ref = refs[:5]
    inputs = refs[5:9]
    away_ref, sums_ref, saved = refs[9:12]
    dqkv_ref, loaded, refs = refs[12], refs[13:17], refs[17:]
    _, qkv_ref, _, x_ref = loaded
    wide, mixed, after, *sums = refs[:5]
    load_sem, save_sem = refs[5:7]
    width = x_ref.shape[1]
    total = x_ref.shape[0]
    sources = [part.at[layer] if len(part.shape) == 3 else part for part in inputs]
    loads = Loads(sources, loaded, load_sem)
    saves = Saves((dqkv_ref,), (saved,), save_sem)
    move = Move(devices, *refs[7:]) if layer > 0 else None
    for part in sums:
        part[...] = jnp.zeros_like(part)
    weight = loads.get()
    mixed[...] = dot_nt(grad_ref[...], weight[...]).astype(bf16)
    loads.get()

    @pl.loop(0, total // bias_ref.shape[0])
    def _(group):
        here, tiles = time_tiles(bias_ref, qkv_ref, width, group, mixed)
        for quad, grads in enumerate(backward_tiles(tiles, bias_ref[...])):
            for part in range(3):
                dqkv_ref[here, columns(part, quad, width)] = grads[part].astype(bf16)

    saves.put(0)
    weight = loads.get()
    wide[...] = dot_nt(dqkv_ref[...], weight[...])
    loads.get()
    out_ref = after if layer > 0 else away_ref

    def add(start, rows, part):
        here = pl.ds(start, rows)
        out_ref[here, :] = (grad_ref[here, :].astype(f32) + part).astype(bf16)

    norm_backward(
        lambda start, rows: x_ref[pl.ds(start, rows), :].astype(f32), wide, gain_ref[layer, 0:1], add, total, sums
    )
    for i, part in enumerate(sums):
        sums_ref[i : i + 1, :] = jnp.sum(part[...], 0, keepdims=True)
    if layer > 0:
        move.run(go_ref, after)
        away_ref[...] = move.place(land_ref).astype(bf16)
    saves.finish()


IN_VMEM = pl.BlockSpec(memory_space=pltpu.VMEM)
IN_SMEM = pl.BlockSpec(memory_space=pltpu.SMEM)
IN_HBM = pl.BlockSpec(memory_space=pl.ANY)


def shape(*dims, kind=bf16):
    return jax.ShapeDtypeStruct(dims, kind)


def half_call(name, body, collective, near, far, out_near, out_far, scratch):
    compiler = dict(vmem_limit_bytes=58 * 1024 * 1024)
    if collective is not None:
        compiler.update(collective_id=collective, has_side_effects=True)
    in_specs = [IN_SMEM if part.ndim == 1 else IN_VMEM for part in near] + [IN_HBM] * len(far)
    return pl.pallas_call(
        body,
        in_specs=in_specs,
        out_specs=[IN_VMEM] * len(out_near) + [IN_HBM] * len(out_far),
        out_shape=[*out_near, *out_far],
        scratch_shapes=[pltpu.VMEM(part.shape, part.dtype) for part in out_far] + scratch,
        compiler_params=pltpu.CompilerParams(**compiler),
        name=name,
    )(*near, *far)


def fast_local(
    tokens,
    cls_tokens,
    clip_lengths,
    time_proj,
    time_output,
    space_proj,
    space_output,
    up_weight,
    down_weight,
    norm_gains,
    norm_biases,
    cotangent,
):
    frames, patch_rows, width = tokens.shape
    devices = lax.axis_size("patch")
    hidden = up_weight.shape[2]
    lay = Layout(devices, frames, patch_rows)
    home, away, block = lay.home_rows, lay.away_rows, lay.block
    patches = lay.all_patches
    clip_count = cls_tokens.shape[0]
    rows = group_rows(patch_rows, frames)

    frame_ids = jnp.arange(frames, dtype=jnp.int32)
    slots = frame_slots(clip_lengths[0], frame_ids)
    bias = time_bias(slots[:, None] == slots[None, :], patch_rows, frames)
    my_frames = lax.axis_index("patch") * lay.away_frames + jnp.arange(lay.away_frames, dtype=jnp.int32)
    my_slots = frame_slots(clip_lengths[0], my_frames)
    home_ids = jnp.arange(home, dtype=jnp.int32)
    sent_ids = jnp.arange(lay.sent_rows, dtype=jnp.int32)
    home_of_sent, sent_of_away = lay.home_of_sent(), lay.sent_of_away()[:away]
    leave_home = (home_of_sent[:, None] == home_ids[None, :]).astype(bf16)
    reach_home = (home_ids[:, None] == home_of_sent[None, :]).astype(bf16)
    leave_away = (sent_ids[:, None] == sent_of_away[None, :]).astype(bf16)
    reach_away = (sent_of_away[:, None] == sent_ids[None, :]).astype(bf16)

    def home_order(values):
        return jnp.transpose(values, (1, 0, 2)).reshape(home, width)

    def given_order(values):
        return jnp.transpose(values.reshape(patch_rows, frames, width), (1, 0, 2))

    def vmem(*dims, kind=bf16):
        return pltpu.VMEM(dims, kind)

    blocks = [vmem(devices, block, width)] * 2
    sems = [pltpu.SemaphoreType.DMA((devices,))] * 2

    def queue(count):
        return pltpu.SemaphoreType.DMA((count,))

    cls_aug = jnp.pad(cls_tokens.astype(f32), ((0, CLS_ROWS - clip_count), (0, 0)))
    at_home = home_order(tokens)
    sent = jnp.dot(leave_home, home_order(cotangent), preferred_element_type=bf16)
    got = lax.all_to_all(sent, "patch", split_axis=0, concat_axis=0, tiled=True)
    grad_away = jnp.dot(reach_away, got, preferred_element_type=bf16)
    stored = []
    for layer in range(LAYERS):
        x_home = at_home
        x_away, normed_t, qkv_t, mixed_t = half_call(
            "time_half",
            functools.partial(time_half, layer, devices),
            2 + layer,
            (x_home, norm_gains, norm_biases, bias, leave_home, reach_away),
            (time_proj, time_output),
            [shape(away, width)],
            [shape(home, width), shape(home, 3 * width), shape(home, width)],
            [vmem(width, 3 * width), vmem(width, width), vmem(home, width), *blocks, queue(2), queue(3), *sems],
        )
        at_home, normed_s, qkv_s, mixed_s, middle, normed_f, active, slope = half_call(
            "space_half",
            functools.partial(space_half, layer, devices, patches),
            4 + layer,
            (my_slots, x_away, cls_aug, norm_gains, norm_biases, leave_away, reach_home),
            (space_proj, space_output, up_weight, down_weight),
            [shape(home, width)],
            [
                shape(away + CLS_ROWS, width),
                shape(away + CLS_ROWS, 3 * width),
                *[shape(away, width)] * 3,
                *[shape(away, hidden)] * 2,
            ],
            [
                vmem(width, 3 * width),
                vmem(width, width),
                vmem(width, hidden),
                vmem(hidden, width),
                vmem(away, width, kind=f32),
                vmem(away, width),
                *blocks,
                queue(4),
                queue(7),
                *sems,
            ],
        )
        stored.append((x_home, normed_t, qkv_t, mixed_t, x_away, normed_s, qkv_s, mixed_s, middle, normed_f, active, slope))
    output = given_order(at_home)

    grad_cls = jnp.zeros_like(cls_aug)
    results = [None] * LAYERS
    for layer in reversed(range(LAYERS)):
        x_home, normed_t, qkv_t, mixed_t, x_away, normed_s, qkv_s, mixed_s, middle, normed_f, active, slope = stored[layer]
        grad_home, cls_part, sums_s, grad_hidden, branch_s, dqkv_s = half_call(
            "space_half_back",
            functools.partial(space_half_back, layer, devices, patches),
            6 + layer,
            (my_slots, grad_away, cls_aug, norm_gains, leave_away, reach_home),
            (down_weight, slope, up_weight, middle, space_output, qkv_s, space_proj, x_away),
            [shape(home, width), shape(CLS_ROWS, width, kind=f32), shape(8, width, kind=f32)],
            [shape(away, hidden), shape(away, width), shape(away + CLS_ROWS, 3 * width)],
            [
                vmem(hidden, width),
                vmem(away, hidden),
                vmem(width, hidden),
                vmem(away, width),
                vmem(width, width),
                vmem(away + CLS_ROWS, 3 * width),
                vmem(width, 3 * width),
                vmem(away, width),
                vmem(away, width, kind=f32),
                vmem(away + CLS_ROWS, width, kind=f32),
                vmem(away, width),
                vmem(away, width),
                vmem(CLS_ROWS, 3 * width, kind=f32),
                *[vmem(8, width, kind=f32)] * 4,
                *blocks,
                queue(8),
                queue(3),
                *sems,
            ],
        )
        grad_cls = grad_cls + cls_part
        dy_f = grad_away
        grad_away, sums_t, dqkv_t = half_call(
            "time_half_back",
            functools.partial(time_half_back, layer, devices),
            8 if layer > 0 else None,
            (grad_home, norm_gains, bias, leave_home, reach_away),
            (time_output, qkv_t, time_proj, x_home),
            [shape(away if layer > 0 else home, width), shape(8, width, kind=f32)],
            [shape(home, 3 * width)],
            [
                vmem(width, width),
                vmem(home, 3 * width),
                vmem(width, 3 * width),
                vmem(home, width),
                vmem(home, width, kind=f32),
                vmem(home, width),
                vmem(home, width),
                *[vmem(8, width, kind=f32)] * 2,
                queue(4),
                queue(1),
                *(blocks + sems if layer > 0 else []),
            ],
        )
        lhs = (active, normed_f, mixed_s, normed_s, mixed_t, normed_t)
        rhs = (dy_f, grad_hidden, branch_s, dqkv_s, grad_home, dqkv_t)
        small = jnp.concatenate([sums_t[0:1], sums_s[2:3], sums_s[0:1], sums_t[1:2], sums_s[3:4], sums_s[1:2]], 0)
        small = jnp.pad(small, ((0, 2), (0, 0)))
        cls_rows = jnp.zeros((8, width), f32) if layer > 0 else grad_cls[:8]
        large, small = reduce_grads(lhs, rhs, jnp.concatenate([small, cls_rows], 0))
        results[layer] = (large, small)
    grad_tokens = given_order(grad_away)
    grad_cls = results[0][1][8 : 8 + clip_count]
    stacked = [jnp.stack([results[layer][0][i].astype(f32) for layer in range(LAYERS)]) for i in (5, 4, 3, 2, 1, 0)]
    share = width // devices
    small = jnp.stack([results[layer][1] for layer in range(LAYERS)])
    small = lax.dynamic_slice_in_dim(small, lax.axis_index("patch") * share, share, 2)
    return (output, grad_tokens, grad_cls, *stacked, small[:, 0:3], small[:, 3:6])


def general_local(
    tokens,
    cls_tokens,
    clip_lengths,
    time_proj,
    time_output,
    space_proj,
    space_output,
    up_weight,
    down_weight,
    norm_gains,
    norm_biases,
    cotangent,
):
    frames, patch_rows, width = tokens.shape
    devices = lax.axis_size("patch")
    lay = Layout(devices, frames, patch_rows)
    away_rows = lay.away_rows
    patches = lay.all_patches
    clip_count = cls_tokens.shape[0]

    frame_ids = jnp.arange(frames, dtype=jnp.int32)
    slots = frame_slots(clip_lengths[0], frame_ids)
    bias = time_bias(slots[:, None] == slots[None, :], patch_rows, frames)
    my_frames = lax.axis_index("patch") * lay.away_frames + jnp.arange(lay.away_frames, dtype=jnp.int32)
    my_slots = jnp.where(my_frames < frames, frame_slots(clip_lengths[0], my_frames), -1)
    cls_pick = (my_slots[None, :] == jnp.arange(CLS_ROWS, dtype=jnp.int32)[:, None]).astype(f32)

    def home_order(values):
        return jnp.transpose(values, (1, 0, 2)).reshape(lay.home_rows, width)

    def given_order(values):
        return jnp.transpose(values.reshape(patch_rows, frames, width), (1, 0, 2))

    cls_aug = jnp.pad(cls_tokens.astype(f32), ((0, CLS_ROWS - clip_count), (0, 0)))
    residual = home_order(tokens).astype(f32)
    cotangent_away = lay.to_away(home_order(cotangent))
    stored = []
    for layer in range(LAYERS):
        gains, biases = norm_gains[layer], norm_biases[layer]
        normed, scaled_t, inverse_t = layer_norm(residual, gains[0], biases[0])
        normed_t = normed.astype(bf16)
        qkv_t = project(normed_t, time_proj[layer]).astype(bf16)
        mixed_t = time_forward(bias, qkv_t)
        residual = residual + project(mixed_t, time_output[layer])
        away = lay.to_away(residual.astype(bf16))
        away = away + jnp.pad(cls_aug, ((away_rows, 0), (0, 0)))
        normed, scaled_s, inverse_s = layer_norm(away, gains[1], biases[1])
        normed_s = normed.astype(bf16)
        qkv_s = project(normed_s, space_proj[layer]).astype(bf16)
        mixed_s = space_forward(my_slots, qkv_s, lay.away_frames, patches)
        away = away[:away_rows] + project(mixed_s, space_output[layer])
        normed, scaled_f, inverse_f = layer_norm(away, gains[2], biases[2])
        normed_f = normed.astype(bf16)
        hidden = project(normed_f, up_weight[layer])
        active = gelu_value(hidden).astype(bf16)
        away = away + project(active, down_weight[layer])
        residual = lay.to_home(away.astype(bf16))
        stored.append(
            dict(
                normed_t=normed_t, scaled_t=scaled_t, inverse_t=inverse_t, qkv_t=qkv_t, mixed_t=mixed_t,
                normed_s=normed_s, scaled_s=scaled_s, inverse_s=inverse_s, qkv_s=qkv_s, mixed_s=mixed_s,
                normed_f=normed_f, scaled_f=scaled_f, inverse_f=inverse_f, hidden=hidden, active=active,
            )
        )
    output = given_order(residual.astype(bf16))

    grad_cls = jnp.zeros_like(cls_aug)
    grad_away = cotangent_away[:away_rows]
    results = [None] * LAYERS
    for layer in reversed(range(LAYERS)):
        saved = stored[layer]
        gains = norm_gains[layer]
        branch = grad_away.astype(bf16)
        grad_down = weight_grad(saved["active"], branch)
        grad_active = project_back(branch, down_weight[layer])
        grad_hidden = (grad_active * gelu_slope(saved["hidden"])).astype(bf16)
        grad_up = weight_grad(saved["normed_f"], grad_hidden)
        grad_normed = project_back(grad_hidden, up_weight[layer])
        grad_input, gain_two, bias_two = norm_back(
            grad_normed, saved["scaled_f"], saved["inverse_f"], gains[2]
        )
        grad_away = grad_away + grad_input
        branch = grad_away.astype(bf16)
        grad_space_out = weight_grad(saved["mixed_s"], branch)
        grad_mixed = project_back(branch, space_output[layer]).astype(bf16)
        dq, dk, dv, dck, dcv = space_backward(my_slots, saved["qkv_s"], grad_mixed, lay.away_frames, patches)
        dcls = jnp.concatenate([dck[:, 0], dcv[:, 0]], -1)
        dcls = jnp.dot(cls_pick, dcls, precision=lax.Precision.HIGHEST)
        dcls = jnp.pad(dcls.astype(bf16), ((0, 0), (width, 0)))
        grad_qkv = jnp.concatenate([jnp.concatenate([dq, dk, dv], -1), dcls], 0)
        grad_space_proj = weight_grad(saved["normed_s"], grad_qkv)
        grad_normed = project_back(grad_qkv, space_proj[layer])
        grad_input, gain_one, bias_one = norm_back(
            grad_normed, saved["scaled_s"], saved["inverse_s"], gains[1]
        )
        grad_away = grad_away + grad_input[:away_rows]
        grad_cls = grad_cls + grad_input[away_rows:]
        grad_home = lay.to_home(grad_away.astype(bf16))
        branch = grad_home.astype(bf16)
        grad_time_out = weight_grad(saved["mixed_t"], branch)
        grad_mixed = project_back(branch, time_output[layer]).astype(bf16)
        grad_qkv = time_backward(bias, saved["qkv_t"], grad_mixed)
        grad_time_proj = weight_grad(saved["normed_t"], grad_qkv)
        grad_normed = project_back(grad_qkv, time_proj[layer])
        grad_input, gain_zero, bias_zero = norm_back(
            grad_normed, saved["scaled_t"], saved["inverse_t"], gains[0]
        )
        grad_home = grad_home + grad_input
        if layer > 0:
            grad_away = lay.to_away(grad_home.astype(bf16))[:away_rows]
        large = (grad_time_proj, grad_time_out, grad_space_proj, grad_space_out, grad_up, grad_down)
        large = [lax.psum_scatter(part, "patch", scatter_dimension=0, tiled=True) for part in large]
        large = lax.psum(large, "clip")
        small = (jnp.stack([gain_zero, gain_one, gain_two]), jnp.stack([bias_zero, bias_one, bias_two]))
        results[layer] = [part.astype(f32) for part in large] + list(small)
    grad_tokens = given_order(grad_home.astype(bf16))
    stacked = [jnp.stack([results[layer][i] for layer in range(LAYERS)]) for i in range(8)]
    small = jnp.stack(stacked[6:])
    small = lax.psum(small, ("patch", "clip"))
    share = width // devices
    small = lax.dynamic_slice_in_dim(small, lax.axis_index("patch") * share, share, 3)
    grad_cls = lax.psum(grad_cls[:clip_count], "patch")
    return (output, grad_tokens, grad_cls, *stacked[:6], small[0], small[1])


def solution(mesh):
    in_specs = (
        P("clip", "patch", None),
        P("clip", None),
        P("clip", None),
        P(),
        P(),
        P(),
        P(),
        P(),
        P(),
        P(),
        P(),
        P("clip", "patch", None),
    )
    out_specs = (
        P("clip", "patch", None),
        P("clip", "patch", None),
        P("clip", None),
        P(None, "patch", None),
        P(None, "patch", None),
        P(None, "patch", None),
        P(None, "patch", None),
        P(None, "patch", None),
        P(None, "patch", None),
        P(None, None, "patch"),
        P(None, None, "patch"),
    )
    paired = (mesh.shape["clip"], mesh.shape["patch"]) == (4, 8)
    local = fast_local if paired else general_local
    return jax.shard_map(local, mesh=mesh, in_specs=in_specs, out_specs=out_specs, check_vma=False)
```

```python
import functools

import jax
import jax.numpy as jnp
from jax import lax
from jax.experimental import pallas as pl
from jax.experimental.pallas import tpu as pltpu
from jax.sharding import PartitionSpec as P

HEADS = 12
HD = 64
LAYERS = 2
REAL_PATCH = 196
QUAD = 4
WIDE = QUAD * HD
QUADS = HEADS // QUAD
CLS_ROWS = 16

EPSILON = 1e-05
NEG_LARGE = -1e30
ROOT_HALF = 0.7071067811865476
INV_ROOT_TWO_PI = 0.3989422804014327
SCALE = HD**-0.5
VMEM_LIMIT = 48 * 1024 * 1024
VMEM_MOST = 62 * 1024 * 1024

f32 = jnp.float32
bf16 = jnp.bfloat16
MESH = pl.DeviceIdType.MESH


def layer_norm(values, norm_gain, norm_bias):
    centered = values - jnp.mean(values, -1, keepdims=True)
    inverse = lax.rsqrt(jnp.mean(centered * centered, -1, keepdims=True) + EPSILON)
    scaled = centered * inverse
    return (scaled * norm_gain + norm_bias, scaled, inverse)


def norm_back(grad_out, scaled, inverse, norm_gain):
    weighted = grad_out * norm_gain
    grad_input = inverse * (
        weighted
        - jnp.mean(weighted, -1, keepdims=True)
        - scaled * jnp.mean(weighted * scaled, -1, keepdims=True)
    )
    return (grad_input, jnp.sum(grad_out * scaled, 0), jnp.sum(grad_out, 0))


def project(left, matrix):
    return jnp.dot(left, matrix, preferred_element_type=f32)


def project_back(grad_out, matrix):
    return lax.dot_general(grad_out, matrix, (((1,), (1,)), ((), ())), preferred_element_type=f32)


def weight_grad(left, grad_out):
    return lax.dot_general(
        left, grad_out, (((0,), (0,)), ((), ())), preferred_element_type=f32
    ).astype(bf16)


def gelu_value(hidden):
    return 0.5 * hidden * (1.0 + lax.erf(hidden * ROOT_HALF))


def gelu_slope(hidden):
    return 0.5 * (1.0 + lax.erf(hidden * ROOT_HALF)) + hidden * INV_ROOT_TWO_PI * jnp.exp(
        -0.5 * hidden * hidden
    )


def dot_nt(left, right):
    return lax.dot_general(left, right, (((1,), (1,)), ((), ())), preferred_element_type=f32)


def dot_nn(left, right):
    return lax.dot_general(left, right, (((1,), (0,)), ((), ())), preferred_element_type=f32)


def dot_tn(left, right):
    return lax.dot_general(left, right, (((0,), (0,)), ((), ())), preferred_element_type=f32)


def spread_heads(rows):
    head = lax.broadcasted_iota(jnp.int32, rows.shape, 1) // HD
    return jnp.concatenate([jnp.where(head == h, rows, jnp.zeros_like(rows)) for h in range(QUAD)], 0)


def merge_heads(stacked):
    count = stacked.shape[0] // QUAD
    head = lax.broadcasted_iota(jnp.int32, (count, WIDE), 1) // HD
    merged = stacked[:count]
    for h in range(1, QUAD):
        merged = jnp.where(head == h, stacked[h * count : (h + 1) * count], merged)
    return merged


def probabilities(scores):
    exponents = [jnp.exp(part - jnp.max(part, 0, keepdims=True)) for part in scores]
    return [part * (1.0 / jnp.sum(part, 0, keepdims=True)) for part in exponents]


def forward_tiles(tiles, bias):
    spreads = [spread_heads(tile[0] * SCALE) for tile in tiles]
    scores = [dot_nt(tile[1], spread) + bias for tile, spread in zip(tiles, spreads)]
    probs = [part.astype(bf16) for part in probabilities(scores)]
    outs = [dot_tn(part, tile[2]) for part, tile in zip(probs, tiles)]
    return [merge_heads(part).astype(bf16) for part in outs]


def backward_tiles(tiles, bias):
    spreads = [spread_heads(tile[0] * SCALE) for tile in tiles]
    grad_spreads = [spread_heads(tile[3]) for tile in tiles]
    scores = [dot_nt(tile[1], spread) + bias for tile, spread in zip(tiles, spreads)]
    grad_probs = [dot_nt(tile[2], spread) for tile, spread in zip(tiles, grad_spreads)]
    probs = probabilities(scores)
    grad_scores = [
        (part * (grad - jnp.sum(part * grad, 0, keepdims=True))).astype(bf16)
        for part, grad in zip(probs, grad_probs)
    ]
    grad_queries = [dot_tn(grad, tile[1]) for grad, tile in zip(grad_scores, tiles)]
    grad_keys = [dot_nn(grad, spread) for grad, spread in zip(grad_scores, spreads)]
    grad_values = [dot_nn(part.astype(bf16), spread) for part, spread in zip(probs, grad_spreads)]
    return [(merge_heads(q) * SCALE, k, v) for q, k, v in zip(grad_queries, grad_keys, grad_values)]


def columns(part, quad, width):
    start = part * width + quad * WIDE
    return slice(start, start + WIDE)


def time_forward_kernel(bias_ref, qkv_ref, out_ref):
    width = out_ref.shape[1]
    bias = bias_ref[...]
    for quad in range(QUADS):
        parts = [qkv_ref[:, columns(part, quad, width)] for part in range(3)]
        out_ref[:, columns(0, quad, width)] = forward_tiles([parts], bias)[0]


def time_backward_kernel(bias_ref, qkv_ref, grad_ref, out_ref):
    width = grad_ref.shape[1]
    bias = bias_ref[...]
    for quad in range(QUADS):
        parts = [qkv_ref[:, columns(part, quad, width)] for part in range(3)]
        grads = backward_tiles([parts + [grad_ref[:, columns(0, quad, width)]]], bias)[0]
        for part in range(3):
            out_ref[:, columns(part, quad, width)] = grads[part].astype(bf16)


def group_rows(patch_count, frames):
    return (2 if patch_count % 2 == 0 else 1) * frames


def time_bias(same_clip, patch_count, frames):
    rows = group_rows(patch_count, frames)
    ids = jnp.arange(rows, dtype=jnp.int32)
    same_patch = (ids[:, None] // frames) == (ids[None, :] // frames)
    tiled = jnp.tile(same_clip, (rows // frames, rows // frames))
    return jnp.tile(jnp.where(same_patch & tiled, 0.0, NEG_LARGE).astype(f32), (1, QUAD))


def params(*semantics):
    return pltpu.CompilerParams(dimension_semantics=semantics, vmem_limit_bytes=VMEM_LIMIT)


def time_forward(bias, qkv):
    rows = bias.shape[0]
    width = qkv.shape[1] // 3
    return pl.pallas_call(
        time_forward_kernel,
        grid=(qkv.shape[0] // rows,),
        in_specs=[
            pl.BlockSpec(bias.shape, lambda i: (0, 0)),
            pl.BlockSpec((rows, 3 * width), lambda i: (i, 0)),
        ],
        out_specs=pl.BlockSpec((rows, width), lambda i: (i, 0)),
        out_shape=jax.ShapeDtypeStruct((qkv.shape[0], width), bf16),
        compiler_params=params("parallel"),
        name="time_forward",
    )(bias, qkv)


def time_backward(bias, qkv, grad_out):
    rows = bias.shape[0]
    width = qkv.shape[1] // 3
    return pl.pallas_call(
        time_backward_kernel,
        grid=(qkv.shape[0] // rows,),
        in_specs=[
            pl.BlockSpec(bias.shape, lambda i: (0, 0)),
            pl.BlockSpec((rows, 3 * width), lambda i: (i, 0)),
            pl.BlockSpec((rows, width), lambda i: (i, 0)),
        ],
        out_specs=pl.BlockSpec((rows, 3 * width), lambda i: (i, 0)),
        out_shape=jax.ShapeDtypeStruct(qkv.shape, bf16),
        compiler_params=params("parallel"),
        name="time_backward",
    )(bias, qkv, grad_out)


def with_class(slot, rows, cls_rows):
    ids = lax.broadcasted_iota(jnp.int32, cls_rows.shape, 0)
    picked = jnp.sum(jnp.where(ids == slot, cls_rows.astype(f32), 0.0), 0, keepdims=True)
    row_ids = lax.broadcasted_iota(jnp.int32, rows.shape, 0)
    return jnp.where(row_ids == REAL_PATCH, picked.astype(bf16), rows)


def key_bias(count):
    key_ids = lax.broadcasted_iota(jnp.int32, (count, 1), 0)
    return jnp.where(key_ids <= REAL_PATCH, 0.0, NEG_LARGE).astype(f32)


def space_forward_kernel(slot_ref, q_ref, k_ref, v_ref, ck_ref, cv_ref, out_ref):
    slot = slot_ref[pl.program_id(0)]
    keys = with_class(slot, k_ref[...], ck_ref[...])
    values = with_class(slot, v_ref[...], cv_ref[...])
    out_ref[...] = forward_tiles([(q_ref[...], keys, values)], key_bias(keys.shape[0]))[0]


def space_backward_kernel(
    slot_ref, q_ref, k_ref, v_ref, ck_ref, cv_ref, g_ref, dq_ref, dk_ref, dv_ref, dck_ref, dcv_ref
):
    slot = slot_ref[pl.program_id(0)]
    keys = with_class(slot, k_ref[...], ck_ref[...])
    values = with_class(slot, v_ref[...], cv_ref[...])
    tile = (q_ref[...], keys, values, g_ref[...])
    grad_q, grad_k, grad_v = backward_tiles([tile], key_bias(keys.shape[0]))[0]
    row_ids = lax.broadcasted_iota(jnp.int32, grad_k.shape, 0)
    dq_ref[...] = grad_q.astype(bf16)
    dk_ref[...] = jnp.where(row_ids < REAL_PATCH, grad_k, 0.0).astype(bf16)
    dv_ref[...] = jnp.where(row_ids < REAL_PATCH, grad_v, 0.0).astype(bf16)
    dck_ref[0] = jnp.sum(jnp.where(row_ids == REAL_PATCH, grad_k, 0.0), 0, keepdims=True)
    dcv_ref[0] = jnp.sum(jnp.where(row_ids == REAL_PATCH, grad_v, 0.0), 0, keepdims=True)


def space_specs(frames, patches):
    cls_block = frames * patches // CLS_ROWS

    def rows(part):
        return pl.BlockSpec((patches, WIDE), lambda f, c, s: (f, part * QUADS + c))

    def cls(part):
        return pl.BlockSpec((CLS_ROWS, WIDE), lambda f, c, s: (cls_block, part * QUADS + c))

    return [rows(0), rows(1), rows(2), cls(1), cls(2)], rows(0)


def space_forward(slots, qkv, frames, patches):
    width = qkv.shape[1] // 3
    in_specs, out_spec = space_specs(frames, patches)
    return pl.pallas_call(
        space_forward_kernel,
        grid_spec=pltpu.PrefetchScalarGridSpec(
            num_scalar_prefetch=1,
            grid=(frames, QUADS),
            in_specs=in_specs,
            out_specs=out_spec,
        ),
        out_shape=jax.ShapeDtypeStruct((frames * patches, width), bf16),
        compiler_params=params("parallel", "parallel"),
        name="space_forward",
    )(slots, qkv, qkv, qkv, qkv, qkv)


def space_backward(slots, qkv, grad_out, frames, patches):
    width = qkv.shape[1] // 3
    in_specs, out_spec = space_specs(frames, patches)
    rows = jax.ShapeDtypeStruct((frames * patches, width), bf16)
    cls_spec = pl.BlockSpec((1, 1, WIDE), lambda f, c, s: (f, 0, c))
    cls = jax.ShapeDtypeStruct((frames, 1, width), f32)
    return pl.pallas_call(
        space_backward_kernel,
        grid_spec=pltpu.PrefetchScalarGridSpec(
            num_scalar_prefetch=1,
            grid=(frames, QUADS),
            in_specs=in_specs + [out_spec],
            out_specs=[out_spec] * 3 + [cls_spec] * 2,
        ),
        out_shape=[rows] * 3 + [cls] * 2,
        compiler_params=params("parallel", "parallel"),
        name="space_backward",
    )(slots, qkv, qkv, qkv, qkv, qkv, grad_out)


def frame_slots(lengths_row, frame_ids):
    clip_ends = jnp.cumsum(lengths_row)
    return jnp.sum((frame_ids[:, None] >= clip_ends[None, :]).astype(jnp.int32), axis=1)


class Layout:
    def __init__(self, devices, frames, patches):
        self.devices = devices
        self.frames = frames
        self.patches = patches
        self.all_patches = patches * devices
        self.away_frames = -(-frames // devices)
        used = self.away_frames * patches
        self.block = -(-used // 16) * 16
        self.home_rows = frames * patches
        self.away_rows = self.away_frames * self.all_patches
        self.sent_rows = devices * self.block

    def home_of_sent(self):
        row = jnp.arange(self.sent_rows, dtype=jnp.int32)
        peer, inner = row // self.block, row % self.block
        frame = peer * self.away_frames + inner // self.patches
        valid = (inner < self.away_frames * self.patches) & (frame < self.frames)
        return jnp.where(valid, (inner % self.patches) * self.frames + frame, -1)

    def sent_of_away(self):
        row = jnp.arange(self.away_rows + CLS_ROWS, dtype=jnp.int32)
        frame, patch = row // self.all_patches, row % self.all_patches
        sent = (patch // self.patches) * self.block + frame * self.patches + patch % self.patches
        return jnp.where(row < self.away_rows, sent, -1)

    def away_of_sent(self):
        row = jnp.arange(self.sent_rows, dtype=jnp.int32)
        peer, inner = row // self.block, row % self.block
        frame, patch = inner // self.patches, inner % self.patches
        return jnp.where(frame < self.away_frames, frame * self.all_patches + peer * self.patches + patch, -1)

    def sent_of_home(self):
        row = jnp.arange(self.home_rows, dtype=jnp.int32)
        patch, frame = row // self.frames, row % self.frames
        peer, inner = frame // self.away_frames, frame % self.away_frames
        return peer * self.block + inner * self.patches + patch

    def to_away(self, values):
        pick = self.home_of_sent()[:, None] == jnp.arange(self.home_rows, dtype=jnp.int32)[None, :]
        sent = jnp.dot(pick.astype(bf16), values, preferred_element_type=bf16)
        got = lax.all_to_all(sent, "patch", split_axis=0, concat_axis=0, tiled=True)
        pick = self.sent_of_away()[:, None] == jnp.arange(self.sent_rows, dtype=jnp.int32)[None, :]
        return jnp.dot(pick.astype(bf16), got, preferred_element_type=f32)

    def to_home(self, values):
        pick = jnp.arange(self.sent_rows, dtype=jnp.int32)[:, None] == self.sent_of_away()[None, : self.away_rows]
        sent = jnp.dot(pick.astype(bf16), values, preferred_element_type=bf16)
        got = lax.all_to_all(sent, "patch", split_axis=0, concat_axis=0, tiled=True)
        pick = jnp.arange(self.home_rows, dtype=jnp.int32)[:, None] == self.home_of_sent()[None, :]
        return jnp.dot(pick.astype(bf16), got, preferred_element_type=f32)


def rows_of(total):
    for rows in (80, 48, 16):
        if total % rows == 0:
            return rows
    return total


def norm_rows(values):
    centered = values - jnp.mean(values, -1, keepdims=True)
    inverse = lax.rsqrt(jnp.mean(centered * centered, -1, keepdims=True) + EPSILON)
    return centered * inverse, inverse


def norm_forward(load, gain, shift, out_ref):
    rows = rows_of(out_ref.shape[0])

    @pl.loop(0, out_ref.shape[0] // rows)
    def _(step):
        start = pl.multiple_of(step * rows, 16)
        scaled, _ = norm_rows(load(start, rows))
        out_ref[pl.ds(start, rows), :] = (scaled * gain + shift).astype(bf16)


def norm_backward(load, grad_ref, gain, store, total, sums):
    rows = rows_of(total)
    width = gain.shape[-1]

    def fold(part):
        return jnp.sum(part.reshape(rows // 8, 8, width), 0)

    @pl.loop(0, total // rows)
    def _(step):
        start = pl.multiple_of(step * rows, 16)
        scaled, inverse = norm_rows(load(start, rows))
        grad = grad_ref[pl.ds(start, rows), :]
        weighted = grad * gain
        store(
            start,
            rows,
            inverse
            * (
                weighted
                - jnp.mean(weighted, -1, keepdims=True)
                - scaled * jnp.mean(weighted * scaled, -1, keepdims=True)
            ),
        )
        sums[0][...] += fold(grad * scaled)
        sums[1][...] += fold(grad)


class Loads:
    def __init__(self, sources, buffers, sems):
        self.copies = [
            pltpu.make_async_copy(source, buffer, sems.at[i])
            for i, (source, buffer) in enumerate(zip(sources, buffers))
        ]
        for copy in self.copies:
            copy.start()
        self.buffers = buffers
        self.next = 0

    def get(self):
        self.copies[self.next].wait()
        self.next += 1
        return self.buffers[self.next - 1]


class Saves:
    def __init__(self, buffers, targets, sems):
        self.copies = [
            pltpu.make_async_copy(buffer, target, sems.at[i])
            for i, (buffer, target) in enumerate(zip(buffers, targets))
        ]

    def put(self, i):
        self.copies[i].start()

    def finish(self):
        for copy in self.copies:
            copy.wait()


class Place:
    AXES = {"core": ("patch", 1), "zl": ("patch", 2), "zh": ("patch", 4), "x": ("clip", 1), "y": ("clip", 2)}

    def __init__(self):
        self.clip, self.patch = lax.axis_index("clip"), lax.axis_index("patch")
        self.me = {
            "core": lax.rem(self.patch, 2),
            "zl": lax.rem(self.patch // 2, 2),
            "zh": self.patch // 4,
            "x": lax.rem(self.clip, 2),
            "y": self.clip // 2,
        }

    def peer(self, dim):
        axis, stride = self.AXES[dim]
        own = self.clip if axis == "clip" else self.patch
        other = own + stride - 2 * stride * self.me[dim]
        return (other, self.patch) if axis == "clip" else (self.clip, other)


class Shuffle:
    def __init__(self, devices, at, sent, got, send_sem, recv_sem):
        self.devices, self.at = devices, at
        self.sent, self.got, self.send_sem, self.recv_sem = sent, got, send_sem, recv_sem
        self.moves = 0

    def greet(self):
        for offset in range(1, self.devices):
            other = (self.at.clip, lax.rem(self.at.patch + offset, self.devices))
            pl.semaphore_signal(pltpu.get_barrier_semaphore(), inc=1, device_id=other, device_id_type=MESH)

    def meet(self, others=0):
        pl.semaphore_wait(pltpu.get_barrier_semaphore(), self.devices - 1 + others)

    def copy(self, offset):
        two = self.moves % 2
        other = lax.rem(self.at.patch + offset, self.devices)
        return pltpu.make_async_remote_copy(
            src_ref=self.sent.at[other],
            dst_ref=self.got.at[two, self.at.patch],
            send_sem=self.send_sem.at[offset],
            recv_sem=self.recv_sem.at[two, offset],
            device_id=(self.at.clip, other),
            device_id_type=MESH,
        )

    def send(self, order_ref, source_ref):
        rows, width = self.sent.shape[1:]
        half = self.devices // 2
        ids = lax.broadcasted_iota(jnp.int32, (half * rows, source_ref.shape[0]), 1)
        for first in (0, half):
            order = order_ref[first * rows : (first + half) * rows, :]
            picked = dot_nn((order == ids).astype(f32).astype(bf16), source_ref[...]).astype(bf16)
            self.sent[first : first + half] = picked.reshape(half, rows, width)
        for offset in range(1, self.devices):
            self.copy(offset).start()
        self.got[self.moves % 2, self.at.patch] = self.sent[self.at.patch]

    def receive(self, order_ref, target_ref):
        for offset in range(1, self.devices):
            self.copy(offset).wait()
        devices, block, width = self.got.shape[1:]
        rows = target_ref.shape[0] // 3
        ids = lax.broadcasted_iota(jnp.int32, (rows, devices * block), 1)
        for start in range(0, target_ref.shape[0], rows):
            pick = (order_ref[start : start + rows, :] == ids).astype(f32).astype(bf16)
            got = self.got[self.moves % 2].reshape(devices * block, width)
            target_ref[start : start + rows, :] = dot_nn(pick, got).astype(bf16)
        self.moves += 1


def time_tiles(bias_ref, qkv_ref, width, group, grad_ref=None):
    rows = bias_ref.shape[0]
    here = pl.ds(pl.multiple_of(group * rows, 16), rows)
    tiles = []
    for quad in range(QUADS):
        tile = [qkv_ref[here, columns(part, quad, width)] for part in range(3)]
        if grad_ref is not None:
            tile.append(grad_ref[here, columns(0, quad, width)])
        tiles.append(tile)
    return here, tiles


def space_tiles(patches, total, slot, qkv_ref, width, frame, grad_ref=None):
    here = pl.ds(pl.multiple_of(frame * patches, 16), patches)
    tiles = []
    for quad in range(QUADS):
        tile = [qkv_ref[here, columns(part, quad, width)] for part in range(3)]
        for part in (1, 2):
            tile[part] = with_class(slot, tile[part], qkv_ref[total : total + CLS_ROWS, columns(part, quad, width)])
        if grad_ref is not None:
            tile.append(grad_ref[here, columns(0, quad, width)])
        tiles.append(tile)
    return here, tiles


def time_half(layer, devices, *refs):
    x_ref, gain_ref, shift_ref, bias_ref, go_ref, land_ref, proj_hbm, output_hbm = refs[:8]
    away_ref, *saved = refs[8:12]
    normed_ref, qkv_ref, mixed_ref = refs[12:15]
    proj, output, after, load_sem, save_sem, *moving = refs[15:]
    width = x_ref.shape[1]
    shuffle = Shuffle(devices, Place(), *moving)
    shuffle.greet()
    weights = Loads((proj_hbm.at[layer], output_hbm.at[layer]), (proj, output), load_sem)
    saves = Saves((normed_ref, qkv_ref, mixed_ref), saved, save_sem)
    norm_forward(
        lambda start, rows: x_ref[pl.ds(start, rows), :].astype(f32),
        gain_ref[layer, 0:1],
        shift_ref[layer, 0:1],
        normed_ref,
    )
    saves.put(0)
    weight = weights.get()
    for part in range(3):
        here = slice(part * width, (part + 1) * width)
        qkv_ref[:, here] = dot_nn(normed_ref[...], weight[:, here]).astype(bf16)
    saves.put(1)

    @pl.loop(0, x_ref.shape[0] // bias_ref.shape[0])
    def _(group):
        here, tiles = time_tiles(bias_ref, qkv_ref, width, group)
        for quad, done in enumerate(forward_tiles(tiles, bias_ref[...])):
            mixed_ref[here, columns(0, quad, width)] = done

    saves.put(2)
    weight = weights.get()
    after[...] = (x_ref[...].astype(f32) + dot_nn(mixed_ref[...], weight[...])).astype(bf16)
    shuffle.meet()
    shuffle.send(go_ref, after)
    shuffle.receive(land_ref, away_ref)
    saves.finish()


def space_half(layer, devices, patches, *refs):
    slot_ref, x_ref, cls_ref, gain_ref, shift_ref, *orders = refs[:10]
    leave_home, reach_away, leave_away, reach_home, grad_ref = orders
    proj_hbm, output_hbm, up_hbm, down_hbm = refs[10:14]
    result_ref, grad_away_ref, *saved = refs[14:23]
    normed_ref, qkv_ref, mixed_ref, middle_ref, normed_f_ref, active_ref, slope_ref = staged = refs[23:30]
    proj, output, up, down, middle, after, load_sem, save_sem, *moving = refs[30:]
    moves = layer < LAYERS - 1
    if moves:
        shuffle = Shuffle(devices, Place(), *moving)
        shuffle.greet()
    saves = Saves(staged, saved, save_sem)
    width = x_ref.shape[1]
    total = mixed_ref.shape[0]
    sources = [part.at[layer] for part in (proj_hbm, output_hbm, up_hbm, down_hbm)]
    weights = Loads(sources, (proj, output, up, down), load_sem)
    if moves:
        shuffle.meet()
        shuffle.send(leave_home, grad_ref)
    gain, shift = gain_ref[layer, 1:2], shift_ref[layer, 1:2]
    norm_forward(lambda start, rows: x_ref[pl.ds(start, rows), :].astype(f32), gain, shift, normed_ref.at[pl.ds(0, total)])
    scaled, _ = norm_rows(cls_ref[...])
    normed_ref[total:, :] = (scaled * gain + shift).astype(bf16)
    saves.put(0)
    weight = weights.get()
    for part in range(3):
        here = slice(part * width, (part + 1) * width)
        qkv_ref[:, here] = dot_nn(normed_ref[...], weight[:, here]).astype(bf16)
    saves.put(1)
    bias = key_bias(patches)

    @pl.loop(0, total // patches)
    def _(frame):
        here, tiles = space_tiles(patches, total, slot_ref[frame], qkv_ref, width, frame)
        for quad, done in enumerate(forward_tiles(tiles, bias)):
            mixed_ref[here, columns(0, quad, width)] = done

    saves.put(2)
    weight = weights.get()
    middle[...] = x_ref[:total, :].astype(f32) + dot_nn(mixed_ref[...], weight[...])
    middle_ref[...] = middle[...].astype(bf16)
    saves.put(3)
    norm_forward(lambda start, rows: middle[pl.ds(start, rows), :], gain_ref[layer, 2:3], shift_ref[layer, 2:3], normed_f_ref)
    saves.put(4)
    weight = weights.get()
    block = 256
    for start in range(0, up.shape[1], block):
        here = slice(start, start + block)
        hidden = dot_nn(normed_f_ref[...], weight[:, here])
        share = 0.5 * (1.0 + lax.erf(hidden * ROOT_HALF))
        active_ref[:, here] = (hidden * share).astype(bf16)
        slope = share + hidden * (INV_ROOT_TWO_PI * jnp.exp(-0.5 * hidden * hidden))
        slope_ref[:, here] = slope.astype(bf16)
    saves.put(5)
    saves.put(6)
    weight = weights.get()
    after[...] = (middle[...] + dot_nn(active_ref[...], weight[...])).astype(bf16)
    if moves:
        shuffle.receive(reach_away, grad_away_ref)
        shuffle.send(leave_away, after)
        shuffle.receive(reach_home, result_ref)
    else:
        result_ref[...] = after[...]
    saves.finish()


CHUNKS = 16
TOTAL = CHUNKS * LAYERS
BLOCKS = 3
PIECE = (48, 128)
ROUTES = (("x", "y", "zl", "zh", "y", "x"), ("y", "x", "zl", "zh", "x", "y"), ("zl", "zh", "x", "y", "y", "x"))
SUMS = 4
STAGES = 7
RAW_SLOTS = 8
ACC_SLOTS = 6
SEGMENTS = (4, 4, 1, 3, 1, 3)
SMALL = ("core", "zl", "zh", "x", "y")
SMALL_ROWS = 24


def recv_shape(route, stage):
    left = [dim for dim in ("zh", "zl", "x", "y") if dim not in route[: stage + 1]]
    return (2,) * len(left) + PIECE


class Pump:
    def __init__(self, at, results, scratch):
        self.at, self.results = at, results
        self.raw, self.core_in, self.acc, self.out, *rest = scratch
        self.inboxes = rest[: BLOCKS * SUMS]
        self.core_send, self.core_recv, self.core_free, self.send_sem, self.recv_sem = rest[BLOCKS * SUMS :]
        self.made = self.stepped = 0

    def core_copy(self, c, z):
        slot = lax.rem(c, RAW_SLOTS)
        return pltpu.make_async_remote_copy(
            src_ref=self.raw.at[slot, z // 2, z % 2, 1 - self.at.me["core"]],
            dst_ref=self.core_in.at[slot, z // 2, z % 2],
            send_sem=self.core_send.at[slot, z],
            recv_sem=self.core_recv.at[slot, z],
            device_id=self.at.peer("core"),
            device_id_type=MESH,
        )

    def claim(self, c, known):
        if known >= RAW_SLOTS:
            pl.semaphore_wait(self.core_free, 1)

    def store(self, c, z, core, block, rows):
        slot = lax.rem(c, RAW_SLOTS)
        for xh in range(2):
            for yh in range(2):
                part = rows[xh * 48 : (xh + 1) * 48, yh * 128 : (yh + 1) * 128]
                self.raw[slot, z // 2, z % 2, core, block, xh, yh] = part.astype(bf16)

    def make_chunks(self, count, lhs, rhs):
        first = self.made

        def one(i, c, known):
            self.claim(c, known)
            for half in range(2):
                left = lhs(slice(half * 384, (half + 1) * 384))
                for block in range(BLOCKS):
                    done = dot_tn(left, rhs(i, block * 256))
                    for j in range(4):
                        self.store(c, half * 2 + j // 2, j % 2, block, done[j * 96 : (j + 1) * 96])
            for z in range(4):
                self.core_copy(c, z).start()

        if count == 1:
            one(0, first, first)
        else:
            assert (first >= RAW_SLOTS) == (first + count - 1 >= RAW_SLOTS)

            @pl.loop(0, count)
            def _(i):
                one(i, first + i, first)

        self.made += count
        assert self.made - self.stepped <= RAW_SLOTS

    def make_down(self, lhs, rhs):
        first = self.made

        @pl.loop(0, 4)
        def _(z):
            if first >= RAW_SLOTS:

                @pl.when(z == 0)
                def _():
                    pl.semaphore_wait(self.core_free, 4)

            for core in range(2):
                left = lhs(pl.ds(pl.multiple_of(z * 768 + core * 384, 128), 384))
                for block in range(BLOCKS):
                    done = dot_tn(left, rhs[:, block * 256 : (block + 1) * 256])
                    for c in range(4):
                        self.store_at(first + c, z, core, block, done[c * 96 : (c + 1) * 96])
            for c in range(4):
                slot = (first + c) % RAW_SLOTS
                zh, zl = z // 2, lax.rem(z, 2)
                pltpu.make_async_remote_copy(
                    src_ref=self.raw.at[slot, zh, zl, 1 - self.at.me["core"]],
                    dst_ref=self.core_in.at[slot, zh, zl],
                    send_sem=self.core_send.at[slot, z],
                    recv_sem=self.core_recv.at[slot, z],
                    device_id=self.at.peer("core"),
                    device_id_type=MESH,
                ).start()

        self.made += 4
        assert self.made - self.stepped <= RAW_SLOTS

    def store_at(self, c, z, core, block, rows):
        for xh in range(2):
            for yh in range(2):
                part = rows[xh * 48 : (xh + 1) * 48, yh * 128 : (yh + 1) * 128]
                self.raw[c % RAW_SLOTS, z // 2, lax.rem(z, 2), core, block, xh, yh] = part.astype(bf16)

    def part(self, c, block, stage, value):
        route = ROUTES[block]

        def pick(dim):
            if dim in route[:stage]:
                return self.at.me[dim]
            return value if dim == route[stage] else slice(None)

        return (lax.rem(c, ACC_SLOTS), pick("zh"), pick("zl"), block, pick("x"), pick("y"))

    def exchange(self, c, block, stage):
        me = self.at.me
        dim = ROUTES[block][stage]
        two = lax.rem(c, 2)
        if stage < SUMS:
            src = self.acc.at[self.part(c, block, stage, 1 - me[dim])]
            dst = self.inboxes[block * SUMS + stage].at[two]
        else:
            slot = lax.rem(c, ACC_SLOTS)
            if stage == SUMS:
                src = dst = self.out.at[slot, block, me["x"], me["y"]]
            elif dim == "x":
                src = dst = self.out.at[slot, block, me["x"]]
            else:
                src = dst = self.out.at[slot, block, :, me["y"]]
        return pltpu.make_async_remote_copy(
            src_ref=src,
            dst_ref=dst,
            send_sem=self.send_sem.at[two, block, stage],
            recv_sem=self.recv_sem.at[two, block, stage],
            device_id=self.at.peer(dim),
            device_id_type=MESH,
        )

    def enter(self, c):
        me = self.at.me
        slot, into = lax.rem(c, RAW_SLOTS), lax.rem(c, ACC_SLOTS)
        for z in range(4):
            self.core_copy(c, z).wait()
        for zh in range(2):
            for zl in range(2):
                both = self.raw[slot, zh, zl, me["core"]].astype(f32) + self.core_in[slot, zh, zl].astype(f32)
                self.acc[into, zh, zl] = both.astype(bf16)

        @pl.when(c < TOTAL - RAW_SLOTS)
        def _():
            pl.semaphore_signal(self.core_free, inc=1, device_id=self.at.peer("core"), device_id_type=MESH)

        for block in range(BLOCKS):
            self.exchange(c, block, 0).start()

    def advance(self, c, stage):
        me = self.at.me
        slot, two = lax.rem(c, ACC_SLOTS), lax.rem(c, 2)
        for block in range(BLOCKS):
            self.exchange(c, block, stage).wait()
            if stage < SUMS:
                where = self.part(c, block, stage, me[ROUTES[block][stage]])
                both = self.acc[where].astype(f32) + self.inboxes[block * SUMS + stage][two].astype(f32)
                if stage == SUMS - 1:
                    self.out[slot, block, me["x"], me["y"]] = both.astype(bf16)
                else:
                    self.acc[where] = both.astype(bf16)
            if stage + 1 < STAGES - 1:
                self.exchange(c, block, stage + 1).start()
            else:
                self.finish(c, block)

    def finish(self, c, block):
        slot = lax.rem(c, ACC_SLOTS)
        layer = LAYERS - 1 - c // CHUNKS
        inner = lax.rem(c, CHUNKS)
        start = 0
        for which, count in enumerate(SEGMENTS):

            @pl.when((inner >= start) & (inner < start + count))
            def _(which=which, start=start):
                for xh in range(2):
                    for yh in range(2):
                        part = self.out[slot, block, xh, yh]
                        column = block * 256 + yh * 128
                        if which == 0:
                            row = pl.multiple_of((inner - start) * 96 + xh * 48, 16)
                            self.results[which][layer, pl.ds(row, 48), column : column + 128] = part
                        else:
                            at = pl.ds(pl.multiple_of((inner - start) * 768 + column, 128), 128)
                            self.results[which][layer, xh * 48 : (xh + 1) * 48, at] = part

            start += count

    def run_step(self, t):
        for stage in reversed(range(STAGES)):
            c = t - stage

            @pl.when((c >= 0) & (c < TOTAL))
            def _(c=c, stage=stage):
                if stage == 0:
                    self.enter(c)
                else:
                    self.advance(c, stage - 1)

    def step(self, count=1):
        first = self.stepped
        self.stepped += count
        assert min(self.stepped, TOTAL) <= self.made

        @pl.loop(first, first + count)
        def _(t):
            self.run_step(t)

    def inside(self, count):
        first = self.stepped
        self.stepped += count
        assert min(self.stepped, TOTAL) <= self.made
        return first


class Small:
    def __init__(self, at, values, boxes, send_sem, recv_sem):
        self.at, self.values, self.boxes, self.send_sem, self.recv_sem = at, values, boxes, send_sem, recv_sem

    def rows(self, i):
        return SMALL_ROWS if i < 3 else 16

    def copy(self, i):
        part = pl.ds(0, self.rows(i))
        return pltpu.make_async_remote_copy(
            src_ref=self.values.at[part],
            dst_ref=self.boxes.at[i, part],
            send_sem=self.send_sem.at[i],
            recv_sem=self.recv_sem.at[i],
            device_id=self.at.peer(SMALL[i]),
            device_id_type=MESH,
        )

    def step(self, i):
        if i > 0:
            rows = slice(0, self.rows(i - 1))
            self.copy(i - 1).wait()
            self.values[rows] += self.boxes[i - 1, rows]
        if i < len(SMALL):
            self.copy(i).start()


class Ring:
    def __init__(self, sources, slots, sems):
        self.sources, self.slots, self.sems = sources, slots, sems
        self.depth = slots.shape[0]
        self.started = self.taken = 0
        for _ in range(self.depth):
            self.start()

    def copy(self, i):
        source = self.sources[i]
        slot = i % self.depth
        return pltpu.make_async_copy(source, self.slots.at[slot, pl.ds(0, source.shape[0])], self.sems.at[slot])

    def start(self):
        if self.started < len(self.sources):
            self.copy(self.started).start()
            self.started += 1

    def take(self):
        i = self.taken
        self.copy(i).wait()
        self.taken += 1
        return self.slots.at[i % self.depth, pl.ds(0, self.sources[i].shape[0])]

    def free(self):
        self.start()


class Single:
    def __init__(self, sources, buffer, sem):
        self.copies = [
            pltpu.make_async_copy(source, buffer.at[pl.ds(0, source.shape[0])], sem) for source in sources
        ]
        self.next = 0
        self.copies[0].start()

    def take(self):
        self.copies[self.next].wait()

    def free(self):
        self.next += 1
        if self.next < len(self.copies):
            self.copies[self.next].start()


def backward_kernel(devices, patches, *refs):
    slot_ref, grad_ref, x_out_ref, cls_ref, gain_ref, bias_ref = refs[:6]
    leave_home, reach_away, leave_away, reach_home = refs[6:10]
    weights = dict(zip(("time_proj", "time_output", "space_proj", "space_output", "up", "down"), refs[10:16]))
    names = ("x_home", "normed_t", "qkv_t", "mixed_t", "x_away", "normed_s", "qkv_s", "mixed_s", "middle", "normed_f", "active", "slope")
    refs = refs[16:]
    saved = [dict(zip(names, refs[len(names) * layer : len(names) * (layer + 1)])) for layer in range(LAYERS)]
    refs = refs[len(names) * LAYERS :]
    output_ref, tokens_ref, small_ref, *results = refs[:9]
    refs = refs[9:]
    hidden, qkv, dqkv, wide, state, mixed, branch, x_buf, grad_buf, home_buf, cls_sum = refs[:11]
    weight_slots, lhs_slots, sent, got, small_boxes, *sums = refs[11:22]
    sem_hidden, sem_qkv, sem_x, sem_weight, sem_lhs, sem_sent, sem_got, small_send, small_recv = refs[22:31]
    pump_scratch = refs[31:]

    at = Place()
    shuffle = Shuffle(devices, at, sent, got, sem_sent, sem_got)
    shuffle.greet()
    for dim in ("x", "y"):
        pl.semaphore_signal(pltpu.get_barrier_semaphore(), inc=1, device_id=at.peer(dim), device_id_type=MESH)

    width = grad_ref.shape[1]
    total = grad_ref.shape[0]
    parts = range(0, 3 * width, width)
    order = tuple(reversed(range(LAYERS)))
    tiles, lhs = [], []
    for layer in order:
        wide_parts = range(0, weights["up"].shape[2], width)
        tiles += [weights["down"].at[layer, pl.ds(start, width), :] for start in wide_parts]
        tiles += [weights["up"].at[layer, :, pl.ds(start, width)] for start in wide_parts]
        tiles += [weights["space_output"].at[layer]]
        tiles += [weights["space_proj"].at[layer, :, pl.ds(start, width)] for start in parts]
        tiles += [weights["time_output"].at[layer]]
        tiles += [weights["time_proj"].at[layer, :, pl.ds(start, width)] for start in parts]
        here = saved[layer]
        lhs += [here["slope"].at[:, pl.ds(start, width)] for start in wide_parts]
        lhs += [here[name] for name in ("normed_f", "mixed_s", "normed_s", "mixed_t", "normed_t")]
    fill = Single([saved[layer]["active"] for layer in order], hidden, sem_hidden)
    ring = Ring(tiles, weight_slots, sem_weight)
    left = Ring(lhs, lhs_slots, sem_lhs)
    load_qkv = Single([saved[layer][name] for layer in order for name in ("qkv_s", "qkv_t")], qkv, sem_qkv)
    load_x = Single(
        [saved[layer][name] for layer in order for name in ("middle", "x_away", "x_home")], x_buf, sem_x
    )
    pump = Pump(at, results, pump_scratch)
    small = Small(at, small_ref, small_boxes, small_send, small_recv)
    for part in sums:
        part[...] = jnp.zeros_like(part)
    small_ref[...] = jnp.zeros_like(small_ref)
    key_mask = key_bias(patches)

    def load_rows(start, rows):
        return x_buf[pl.ds(start, rows), :].astype(f32)

    def back_product(rows, source, count):
        for i in range(count):
            tile = ring.take()
            part = dot_nt(source[:rows, i * width : (i + 1) * width], tile[...])
            if i:
                wide[:rows, :] += part
            else:
                wide[:rows, :] = part
            ring.free()

    shuffle.meet(2)
    shuffle.send(leave_away, x_out_ref)

    for layer in order:
        last = layer == 0
        dy = grad_buf if last else grad_ref

        fill.take()
        pump.make_down(lambda at_: hidden[:, at_], dy)
        if last:
            pump.step(2)
        for start in range(0, hidden.shape[1], width):
            tile, slope = ring.take(), left.take()
            for block in range(0, width, WIDE):
                grad_active = dot_nt(dy[...], tile[block : block + WIDE, :])
                grad_hidden = grad_active * slope[:, block : block + WIDE].astype(f32)
                hidden[:, start + block : start + block + WIDE] = grad_hidden.astype(bf16)
            ring.free()
            left.free()
        pump.step()
        back_product(total, hidden, hidden.shape[1] // width)
        pump.step()

        def keep(start, rows, part, dy=dy):
            here = pl.ds(start, rows)
            both = dy[here, :].astype(f32) + part
            state[here, :] = both
            branch[here, :] = both.astype(bf16)

        load_x.take()
        norm_backward(load_rows, wide, gain_ref[layer, 2:3], keep, total, sums[0:2])
        load_x.free()

        tile = ring.take()
        mixed[...] = dot_nt(branch[...], tile[...]).astype(bf16)
        ring.free()
        load_qkv.take()
        cls_sum[...] = jnp.zeros_like(cls_sum)
        first = pump.inside(1 if last else 2)

        @pl.loop(0, total // patches)
        def _(frame, first=first, last=last):
            slot = slot_ref[frame]
            here, these = space_tiles(patches, total, slot, qkv, width, frame, mixed)
            row_ids = lax.broadcasted_iota(jnp.int32, (patches, WIDE), 0)
            cls_ids = lax.broadcasted_iota(jnp.int32, (CLS_ROWS, WIDE), 0)
            for quad, grads in enumerate(backward_tiles(these, key_mask)):
                dqkv[here, columns(0, quad, width)] = grads[0].astype(bf16)
                for part in (1, 2):
                    where = columns(part, quad, width)
                    dqkv[here, where] = jnp.where(row_ids < REAL_PATCH, grads[part], 0.0).astype(bf16)
                    row = grads[part][REAL_PATCH : REAL_PATCH + 1]
                    cls_sum[:, where] += jnp.where(cls_ids == slot, row, 0.0)

            @pl.when(frame < (1 if last else 2))
            def _():
                pump.run_step(first + frame)

        load_qkv.free()
        dqkv[total:, :] = cls_sum[...].astype(bf16)
        back_product(total + CLS_ROWS, dqkv, 3)
        if not last:
            shuffle.receive(reach_home, output_ref)

        def add(start, rows, part):
            here = pl.ds(start, rows)
            mixed[here, :] = (state[here, :] + part).astype(bf16)

        def keep_cls(start, rows, part):
            small_ref[16:24] += part[:8]

        load_x.take()
        gain = gain_ref[layer, 1:2]
        norm_backward(load_rows, wide, gain, add, total, sums[2:4])
        norm_backward(lambda start, rows: cls_ref[...], wide.at[pl.ds(total, CLS_ROWS)], gain, keep_cls, CLS_ROWS, sums[2:4])
        load_x.free()
        shuffle.send(leave_away, mixed)
        tile = left.take()
        pump.make_chunks(2, lambda at_: tile[:, at_], lambda i, start: hidden[:, pl.ds(pl.multiple_of(i * width + start, 128), WIDE)])
        pump.step()
        pump.make_chunks(2, lambda at_: tile[:, at_], lambda i, start: hidden[:, pl.ds(pl.multiple_of((i + 2) * width + start, 128), WIDE)])
        left.free()
        fill.free()
        pump.step()
        tile = left.take()
        pump.make_chunks(1, lambda at_: tile[:, at_], lambda i, start: branch[:, start : start + WIDE])
        left.free()
        tile = left.take()
        pump.step()
        pump.make_chunks(3, lambda at_: tile[:, at_], lambda i, start: dqkv[:, pl.ds(pl.multiple_of(i * width + start, 128), WIDE)])
        left.free()
        pump.step()
        shuffle.receive(reach_home, home_buf)

        tile = ring.take()
        mixed[...] = dot_nt(home_buf[...], tile[...]).astype(bf16)
        ring.free()
        load_qkv.take()
        groups = total // bias_ref.shape[0]
        first = pump.inside(2)

        @pl.loop(0, groups)
        def _(group, first=first):
            here, these = time_tiles(bias_ref, qkv, width, group, mixed)
            for quad, grads in enumerate(backward_tiles(these, bias_ref[...])):
                for part in range(3):
                    dqkv[here, columns(part, quad, width)] = grads[part].astype(bf16)

            for i, when in enumerate((4, 10)):

                @pl.when(group == when)
                def _(i=i):
                    pump.run_step(first + i)

        load_qkv.free()
        back_product(total, dqkv, 3)
        pump.step()
        target = tokens_ref if last else mixed

        def add_home(start, rows, part, target=target):
            here = pl.ds(start, rows)
            target[here, :] = (home_buf[here, :].astype(f32) + part).astype(bf16)

        load_x.take()
        norm_backward(load_rows, wide, gain_ref[layer, 0:1], add_home, total, sums[4:6])
        load_x.free()
        for i, part in enumerate(sums):
            row = layer * 8 + (2, 5, 1, 4, 0, 3)[i]
            small_ref[row : row + 1, :] += jnp.sum(part[...], 0, keepdims=True)
            part[...] = jnp.zeros_like(part)
        if last:
            small.step(0)
        else:
            shuffle.send(leave_home, mixed)
        tile = left.take()
        pump.make_chunks(1, lambda at_: tile[:, at_], lambda i, start: home_buf[:, start : start + WIDE])
        left.free()
        tile = left.take()
        pump.step()
        pump.make_chunks(3, lambda at_: tile[:, at_], lambda i, start: dqkv[:total, pl.ds(pl.multiple_of(i * width + start, 128), WIDE)])
        left.free()
        if last:
            for i in range(1, len(SMALL) + 1):
                pump.step()
                small.step(i)
        else:
            pump.step(2)
            shuffle.receive(reach_away, grad_buf)

    pump.step(TOTAL + STAGES - 1 - pump.stepped)


IN_VMEM = pl.BlockSpec(memory_space=pltpu.VMEM)
IN_SMEM = pl.BlockSpec(memory_space=pltpu.SMEM)
IN_HBM = pl.BlockSpec(memory_space=pl.ANY)


def shape(*dims, kind=bf16):
    return jax.ShapeDtypeStruct(dims, kind)


def half_call(name, body, collective, near, far, out_near, out_far, scratch):
    compiler = dict(vmem_limit_bytes=58 * 1024 * 1024)
    if collective is not None:
        compiler.update(collective_id=collective, has_side_effects=True)
    in_specs = [IN_SMEM if part.ndim == 1 else IN_VMEM for part in near] + [IN_HBM] * len(far)
    return pl.pallas_call(
        body,
        in_specs=in_specs,
        out_specs=[IN_VMEM] * len(out_near) + [IN_HBM] * len(out_far),
        out_shape=[*out_near, *out_far],
        scratch_shapes=[pltpu.VMEM(part.shape, part.dtype) for part in out_far] + scratch,
        compiler_params=pltpu.CompilerParams(**compiler),
        name=name,
    )(*near, *far)


def fast_local(
    tokens,
    cls_tokens,
    clip_lengths,
    time_proj,
    time_output,
    space_proj,
    space_output,
    up_weight,
    down_weight,
    norm_gains,
    norm_biases,
    cotangent,
):
    frames, patch_rows, width = tokens.shape
    devices = lax.axis_size("patch")
    hidden = up_weight.shape[2]
    lay = Layout(devices, frames, patch_rows)
    home, away, block = lay.home_rows, lay.away_rows, lay.block
    patches = lay.all_patches
    clip_count = cls_tokens.shape[0]

    frame_ids = jnp.arange(frames, dtype=jnp.int32)
    slots = frame_slots(clip_lengths[0], frame_ids)
    bias = time_bias(slots[:, None] == slots[None, :], patch_rows, frames)
    my_frames = lax.axis_index("patch") * lay.away_frames + jnp.arange(lay.away_frames, dtype=jnp.int32)
    my_slots = frame_slots(clip_lengths[0], my_frames)
    home_of_sent, sent_of_away = lay.home_of_sent(), lay.sent_of_away()[:away]
    orders = [
        part[:, None] for part in (home_of_sent, sent_of_away, lay.away_of_sent(), lay.sent_of_home())
    ]
    leave_home, reach_away, leave_away, reach_home = orders

    def home_order(values):
        return jnp.transpose(values, (1, 0, 2)).reshape(home, width)

    def given_order(values):
        return jnp.transpose(values.reshape(patch_rows, frames, width), (1, 0, 2))

    def vmem(*dims, kind=bf16):
        return pltpu.VMEM(dims, kind)

    def queue(*counts):
        return pltpu.SemaphoreType.DMA(counts)

    moving = [vmem(devices, block, width), vmem(2, devices, block, width), queue(devices), queue(2, devices)]
    cls_aug = jnp.pad(cls_tokens.astype(f32), ((0, CLS_ROWS - clip_count), (0, 0)))
    at_home = home_order(tokens)
    grad_home = home_order(cotangent)
    stored = []
    for layer in range(LAYERS):
        x_home = at_home
        x_away, normed_t, qkv_t, mixed_t = half_call(
            "time_half",
            functools.partial(time_half, layer, devices),
            2 + layer,
            (x_home, norm_gains, norm_biases, bias, leave_home, reach_away),
            (time_proj, time_output),
            [shape(away, width)],
            [shape(home, width), shape(home, 3 * width), shape(home, width)],
            [vmem(width, 3 * width), vmem(width, width), vmem(home, width), queue(2), queue(3), *moving],
        )
        moves = layer < LAYERS - 1
        at_home, got_grad, normed_s, qkv_s, mixed_s, middle, normed_f, active, slope = half_call(
            "space_half",
            functools.partial(space_half, layer, devices, patches),
            4 if moves else None,
            (my_slots, x_away, cls_aug, norm_gains, norm_biases, *orders, grad_home),
            (space_proj, space_output, up_weight, down_weight),
            [shape(home if moves else away, width), shape(away, width) if moves else shape(16, width)],
            [
                shape(away + CLS_ROWS, width),
                shape(away + CLS_ROWS, 3 * width),
                *[shape(away, width)] * 3,
                *[shape(away, hidden)] * 2,
            ],
            [
                vmem(width, 3 * width),
                vmem(width, width),
                vmem(width, hidden),
                vmem(hidden, width),
                vmem(away, width, kind=f32),
                vmem(away, width),
                queue(4),
                queue(7),
                *(moving if moves else []),
            ],
        )
        grad_away = got_grad if layer == 0 else grad_away
        stored.append((x_home, normed_t, qkv_t, mixed_t, x_away, normed_s, qkv_s, mixed_s, middle, normed_f, active, slope))
    x_out = at_home

    inbox = [vmem(2, *recv_shape(ROUTES[b], s)) for b in range(BLOCKS) for s in range(SUMS)]
    single = pltpu.SemaphoreType.DMA
    near = (my_slots, grad_away, x_out, cls_aug, norm_gains, bias, *orders)
    far = (time_proj, time_output, space_proj, space_output, up_weight, down_weight, *stored[0], *stored[1])
    share = width // devices
    out_shape = [shape(home, width), shape(home, width), shape(SMALL_ROWS, width, kind=f32)]
    out_shape += [
        shape(LAYERS, hidden // devices, width),
        shape(LAYERS, share, hidden),
        shape(LAYERS, share, width),
        shape(LAYERS, share, 3 * width),
        shape(LAYERS, share, width),
        shape(LAYERS, share, 3 * width),
    ]
    output, grad_tokens, small, *large = pl.pallas_call(
        functools.partial(backward_kernel, devices, patches),
        in_specs=[IN_SMEM if part.ndim == 1 else IN_VMEM for part in near] + [IN_HBM] * len(far),
        out_specs=[IN_VMEM] * len(out_shape),
        out_shape=out_shape,
        scratch_shapes=[
            vmem(away, hidden),
            vmem(away + CLS_ROWS, 3 * width),
            vmem(away + CLS_ROWS, 3 * width),
            vmem(away + CLS_ROWS, width, kind=f32),
            vmem(away, width, kind=f32),
            *[vmem(away, width)] * 5,
            vmem(CLS_ROWS, 3 * width, kind=f32),
            vmem(3, width, width),
            vmem(2, away + CLS_ROWS, width),
            *moving[:2],
            vmem(len(SMALL), SMALL_ROWS, width, kind=f32),
            *[vmem(8, width, kind=f32)] * 6,
            single,
            single,
            single,
            queue(3),
            queue(2),
            *moving[2:],
            queue(len(SMALL)),
            queue(len(SMALL)),
            vmem(RAW_SLOTS, 2, 2, 2, BLOCKS, 2, 2, *PIECE),
            vmem(RAW_SLOTS, 2, 2, BLOCKS, 2, 2, *PIECE),
            vmem(ACC_SLOTS, 2, 2, BLOCKS, 2, 2, *PIECE),
            vmem(ACC_SLOTS, BLOCKS, 2, 2, *PIECE),
            *inbox,
            queue(RAW_SLOTS, 4),
            queue(RAW_SLOTS, 4),
            pltpu.SemaphoreType.REGULAR,
            queue(2, BLOCKS, STAGES - 1),
            queue(2, BLOCKS, STAGES - 1),
        ],
        compiler_params=pltpu.CompilerParams(
            collective_id=1, has_side_effects=True, vmem_limit_bytes=VMEM_MOST
        ),
        name="backward",
    )(*near, *far)
    grad_cls = small[16 : 16 + clip_count]
    small = lax.dynamic_slice_in_dim(small[:16], lax.axis_index("patch") * share, share, 1)
    small = small.reshape(LAYERS, 8, share)
    stacked = [large[i].astype(f32) for i in (5, 4, 3, 2, 1, 0)]
    return (given_order(output), given_order(grad_tokens), grad_cls, *stacked, small[:, 0:3], small[:, 3:6])


def general_local(
    tokens,
    cls_tokens,
    clip_lengths,
    time_proj,
    time_output,
    space_proj,
    space_output,
    up_weight,
    down_weight,
    norm_gains,
    norm_biases,
    cotangent,
):
    frames, patch_rows, width = tokens.shape
    devices = lax.axis_size("patch")
    lay = Layout(devices, frames, patch_rows)
    away_rows = lay.away_rows
    patches = lay.all_patches
    clip_count = cls_tokens.shape[0]

    frame_ids = jnp.arange(frames, dtype=jnp.int32)
    slots = frame_slots(clip_lengths[0], frame_ids)
    bias = time_bias(slots[:, None] == slots[None, :], patch_rows, frames)
    my_frames = lax.axis_index("patch") * lay.away_frames + jnp.arange(lay.away_frames, dtype=jnp.int32)
    my_slots = jnp.where(my_frames < frames, frame_slots(clip_lengths[0], my_frames), -1)
    cls_pick = (my_slots[None, :] == jnp.arange(CLS_ROWS, dtype=jnp.int32)[:, None]).astype(f32)

    def home_order(values):
        return jnp.transpose(values, (1, 0, 2)).reshape(lay.home_rows, width)

    def given_order(values):
        return jnp.transpose(values.reshape(patch_rows, frames, width), (1, 0, 2))

    cls_aug = jnp.pad(cls_tokens.astype(f32), ((0, CLS_ROWS - clip_count), (0, 0)))
    residual = home_order(tokens).astype(f32)
    cotangent_away = lay.to_away(home_order(cotangent))
    stored = []
    for layer in range(LAYERS):
        gains, biases = norm_gains[layer], norm_biases[layer]
        normed, scaled_t, inverse_t = layer_norm(residual, gains[0], biases[0])
        normed_t = normed.astype(bf16)
        qkv_t = project(normed_t, time_proj[layer]).astype(bf16)
        mixed_t = time_forward(bias, qkv_t)
        residual = residual + project(mixed_t, time_output[layer])
        away = lay.to_away(residual.astype(bf16))
        away = away + jnp.pad(cls_aug, ((away_rows, 0), (0, 0)))
        normed, scaled_s, inverse_s = layer_norm(away, gains[1], biases[1])
        normed_s = normed.astype(bf16)
        qkv_s = project(normed_s, space_proj[layer]).astype(bf16)
        mixed_s = space_forward(my_slots, qkv_s, lay.away_frames, patches)
        away = away[:away_rows] + project(mixed_s, space_output[layer])
        normed, scaled_f, inverse_f = layer_norm(away, gains[2], biases[2])
        normed_f = normed.astype(bf16)
        hidden = project(normed_f, up_weight[layer])
        active = gelu_value(hidden).astype(bf16)
        away = away + project(active, down_weight[layer])
        residual = lay.to_home(away.astype(bf16))
        stored.append(
            dict(
                normed_t=normed_t, scaled_t=scaled_t, inverse_t=inverse_t, qkv_t=qkv_t, mixed_t=mixed_t,
                normed_s=normed_s, scaled_s=scaled_s, inverse_s=inverse_s, qkv_s=qkv_s, mixed_s=mixed_s,
                normed_f=normed_f, scaled_f=scaled_f, inverse_f=inverse_f, hidden=hidden, active=active,
            )
        )
    output = given_order(residual.astype(bf16))

    grad_cls = jnp.zeros_like(cls_aug)
    grad_away = cotangent_away[:away_rows]
    results = [None] * LAYERS
    for layer in reversed(range(LAYERS)):
        saved = stored[layer]
        gains = norm_gains[layer]
        branch = grad_away.astype(bf16)
        grad_down = weight_grad(saved["active"], branch)
        grad_active = project_back(branch, down_weight[layer])
        grad_hidden = (grad_active * gelu_slope(saved["hidden"])).astype(bf16)
        grad_up = weight_grad(saved["normed_f"], grad_hidden)
        grad_normed = project_back(grad_hidden, up_weight[layer])
        grad_input, gain_two, bias_two = norm_back(
            grad_normed, saved["scaled_f"], saved["inverse_f"], gains[2]
        )
        grad_away = grad_away + grad_input
        branch = grad_away.astype(bf16)
        grad_space_out = weight_grad(saved["mixed_s"], branch)
        grad_mixed = project_back(branch, space_output[layer]).astype(bf16)
        dq, dk, dv, dck, dcv = space_backward(my_slots, saved["qkv_s"], grad_mixed, lay.away_frames, patches)
        dcls = jnp.concatenate([dck[:, 0], dcv[:, 0]], -1)
        dcls = jnp.dot(cls_pick, dcls, precision=lax.Precision.HIGHEST)
        dcls = jnp.pad(dcls.astype(bf16), ((0, 0), (width, 0)))
        grad_qkv = jnp.concatenate([jnp.concatenate([dq, dk, dv], -1), dcls], 0)
        grad_space_proj = weight_grad(saved["normed_s"], grad_qkv)
        grad_normed = project_back(grad_qkv, space_proj[layer])
        grad_input, gain_one, bias_one = norm_back(
            grad_normed, saved["scaled_s"], saved["inverse_s"], gains[1]
        )
        grad_away = grad_away + grad_input[:away_rows]
        grad_cls = grad_cls + grad_input[away_rows:]
        grad_home = lay.to_home(grad_away.astype(bf16))
        branch = grad_home.astype(bf16)
        grad_time_out = weight_grad(saved["mixed_t"], branch)
        grad_mixed = project_back(branch, time_output[layer]).astype(bf16)
        grad_qkv = time_backward(bias, saved["qkv_t"], grad_mixed)
        grad_time_proj = weight_grad(saved["normed_t"], grad_qkv)
        grad_normed = project_back(grad_qkv, time_proj[layer])
        grad_input, gain_zero, bias_zero = norm_back(
            grad_normed, saved["scaled_t"], saved["inverse_t"], gains[0]
        )
        grad_home = grad_home + grad_input
        if layer > 0:
            grad_away = lay.to_away(grad_home.astype(bf16))[:away_rows]
        large = (grad_time_proj, grad_time_out, grad_space_proj, grad_space_out, grad_up, grad_down)
        large = [lax.psum_scatter(part, "patch", scatter_dimension=0, tiled=True) for part in large]
        large = lax.psum(large, "clip")
        small = (jnp.stack([gain_zero, gain_one, gain_two]), jnp.stack([bias_zero, bias_one, bias_two]))
        results[layer] = [part.astype(f32) for part in large] + list(small)
    grad_tokens = given_order(grad_home.astype(bf16))
    stacked = [jnp.stack([results[layer][i] for layer in range(LAYERS)]) for i in range(8)]
    small = jnp.stack(stacked[6:])
    small = lax.psum(small, ("patch", "clip"))
    share = width // devices
    small = lax.dynamic_slice_in_dim(small, lax.axis_index("patch") * share, share, 3)
    grad_cls = lax.psum(grad_cls[:clip_count], "patch")
    return (output, grad_tokens, grad_cls, *stacked[:6], small[0], small[1])


def solution(mesh):
    in_specs = (
        P("clip", "patch", None),
        P("clip", None),
        P("clip", None),
        P(),
        P(),
        P(),
        P(),
        P(),
        P(),
        P(),
        P(),
        P("clip", "patch", None),
    )
    out_specs = (
        P("clip", "patch", None),
        P("clip", "patch", None),
        P("clip", None),
        P(None, "patch", None),
        P(None, "patch", None),
        P(None, "patch", None),
        P(None, "patch", None),
        P(None, "patch", None),
        P(None, "patch", None),
        P(None, None, "patch"),
        P(None, None, "patch"),
    )
    paired = (mesh.shape["clip"], mesh.shape["patch"]) == (4, 8)
    local = fast_local if paired else general_local
    return jax.shard_map(local, mesh=mesh, in_specs=in_specs, out_specs=out_specs, check_vma=False)
```

```python
import functools

import jax
import jax.numpy as jnp
import numpy as np
from jax import lax
from jax.experimental import pallas as pl
from jax.experimental.pallas import tpu as pltpu
from jax.sharding import PartitionSpec as P

HEADS = 12
HD = 64
LAYERS = 2
REAL_PATCH = 196
QUAD = 4
WIDE = QUAD * HD
QUADS = HEADS // QUAD
CLS_ROWS = 16

EPSILON = 1e-05
NEG_LARGE = -1e30
ROOT_HALF = 0.7071067811865476
INV_ROOT_TWO_PI = 0.3989422804014327
SCALE = HD**-0.5
VMEM_LIMIT = 48 * 1024 * 1024
VMEM_MOST = 62 * 1024 * 1024

f32 = jnp.float32
bf16 = jnp.bfloat16
MESH = pl.DeviceIdType.MESH


def layer_norm(values, norm_gain, norm_bias):
    centered = values - jnp.mean(values, -1, keepdims=True)
    inverse = lax.rsqrt(jnp.mean(centered * centered, -1, keepdims=True) + EPSILON)
    scaled = centered * inverse
    return (scaled * norm_gain + norm_bias, scaled, inverse)


def norm_back(grad_out, scaled, inverse, norm_gain):
    weighted = grad_out * norm_gain
    grad_input = inverse * (
        weighted
        - jnp.mean(weighted, -1, keepdims=True)
        - scaled * jnp.mean(weighted * scaled, -1, keepdims=True)
    )
    return (grad_input, jnp.sum(grad_out * scaled, 0), jnp.sum(grad_out, 0))


def project(left, matrix):
    return jnp.dot(left, matrix, preferred_element_type=f32)


def project_back(grad_out, matrix):
    return lax.dot_general(grad_out, matrix, (((1,), (1,)), ((), ())), preferred_element_type=f32)


def weight_grad(left, grad_out):
    return lax.dot_general(
        left, grad_out, (((0,), (0,)), ((), ())), preferred_element_type=f32
    ).astype(bf16)


def gelu_value(hidden):
    return 0.5 * hidden * (1.0 + lax.erf(hidden * ROOT_HALF))


def gelu_slope(hidden):
    return 0.5 * (1.0 + lax.erf(hidden * ROOT_HALF)) + hidden * INV_ROOT_TWO_PI * jnp.exp(
        -0.5 * hidden * hidden
    )


def dot_nt(left, right):
    return lax.dot_general(left, right, (((1,), (1,)), ((), ())), preferred_element_type=f32)


def dot_nn(left, right):
    return lax.dot_general(left, right, (((1,), (0,)), ((), ())), preferred_element_type=f32)


def dot_tn(left, right):
    return lax.dot_general(left, right, (((0,), (0,)), ((), ())), preferred_element_type=f32)


def spread_heads(rows):
    head = lax.broadcasted_iota(jnp.int32, rows.shape, 1) // HD
    return jnp.concatenate([jnp.where(head == h, rows, jnp.zeros_like(rows)) for h in range(QUAD)], 0)


def merge_heads(stacked):
    count = stacked.shape[0] // QUAD
    head = lax.broadcasted_iota(jnp.int32, (count, WIDE), 1) // HD
    merged = stacked[:count]
    for h in range(1, QUAD):
        merged = jnp.where(head == h, stacked[h * count : (h + 1) * count], merged)
    return merged


def probabilities(scores):
    exponents = [jnp.exp(part - jnp.max(part, 0, keepdims=True)) for part in scores]
    return [part * (1.0 / jnp.sum(part, 0, keepdims=True)) for part in exponents]


def forward_tiles(tiles, bias):
    spreads = [spread_heads(tile[0] * SCALE) for tile in tiles]
    scores = [dot_nt(tile[1], spread) + bias for tile, spread in zip(tiles, spreads)]
    probs = [part.astype(bf16) for part in probabilities(scores)]
    outs = [dot_tn(part, tile[2]) for part, tile in zip(probs, tiles)]
    return [merge_heads(part).astype(bf16) for part in outs]


def backward_tiles(tiles, bias):
    spreads = [spread_heads(tile[0] * SCALE) for tile in tiles]
    grad_spreads = [spread_heads(tile[3]) for tile in tiles]
    scores = [dot_nt(tile[1], spread) + bias for tile, spread in zip(tiles, spreads)]
    grad_probs = [dot_nt(tile[2], spread) for tile, spread in zip(tiles, grad_spreads)]
    probs = probabilities(scores)
    grad_scores = [
        (part * (grad - jnp.sum(part * grad, 0, keepdims=True))).astype(bf16)
        for part, grad in zip(probs, grad_probs)
    ]
    grad_queries = [dot_tn(grad, tile[1]) for grad, tile in zip(grad_scores, tiles)]
    grad_keys = [dot_nn(grad, spread) for grad, spread in zip(grad_scores, spreads)]
    grad_values = [dot_nn(part.astype(bf16), spread) for part, spread in zip(probs, grad_spreads)]
    return [(merge_heads(q) * SCALE, k, v) for q, k, v in zip(grad_queries, grad_keys, grad_values)]


def columns(part, quad, width):
    start = part * width + quad * WIDE
    return slice(start, start + WIDE)


def time_forward_kernel(bias_ref, qkv_ref, out_ref):
    width = out_ref.shape[1]
    bias = bias_ref[...]
    for quad in range(QUADS):
        parts = [qkv_ref[:, columns(part, quad, width)] for part in range(3)]
        out_ref[:, columns(0, quad, width)] = forward_tiles([parts], bias)[0]


def time_backward_kernel(bias_ref, qkv_ref, grad_ref, out_ref):
    width = grad_ref.shape[1]
    bias = bias_ref[...]
    for quad in range(QUADS):
        parts = [qkv_ref[:, columns(part, quad, width)] for part in range(3)]
        grads = backward_tiles([parts + [grad_ref[:, columns(0, quad, width)]]], bias)[0]
        for part in range(3):
            out_ref[:, columns(part, quad, width)] = grads[part].astype(bf16)


def group_rows(patch_count, frames):
    return (2 if patch_count % 2 == 0 else 1) * frames


def time_bias(same_clip, patch_count, frames):
    rows = group_rows(patch_count, frames)
    ids = jnp.arange(rows, dtype=jnp.int32)
    same_patch = (ids[:, None] // frames) == (ids[None, :] // frames)
    tiled = jnp.tile(same_clip, (rows // frames, rows // frames))
    return jnp.tile(jnp.where(same_patch & tiled, 0.0, NEG_LARGE).astype(f32), (1, QUAD))


def params(*semantics):
    return pltpu.CompilerParams(dimension_semantics=semantics, vmem_limit_bytes=VMEM_LIMIT)


def time_forward(bias, qkv):
    rows = bias.shape[0]
    width = qkv.shape[1] // 3
    return pl.pallas_call(
        time_forward_kernel,
        grid=(qkv.shape[0] // rows,),
        in_specs=[
            pl.BlockSpec(bias.shape, lambda i: (0, 0)),
            pl.BlockSpec((rows, 3 * width), lambda i: (i, 0)),
        ],
        out_specs=pl.BlockSpec((rows, width), lambda i: (i, 0)),
        out_shape=jax.ShapeDtypeStruct((qkv.shape[0], width), bf16),
        compiler_params=params("parallel"),
        name="time_forward",
    )(bias, qkv)


def time_backward(bias, qkv, grad_out):
    rows = bias.shape[0]
    width = qkv.shape[1] // 3
    return pl.pallas_call(
        time_backward_kernel,
        grid=(qkv.shape[0] // rows,),
        in_specs=[
            pl.BlockSpec(bias.shape, lambda i: (0, 0)),
            pl.BlockSpec((rows, 3 * width), lambda i: (i, 0)),
            pl.BlockSpec((rows, width), lambda i: (i, 0)),
        ],
        out_specs=pl.BlockSpec((rows, 3 * width), lambda i: (i, 0)),
        out_shape=jax.ShapeDtypeStruct(qkv.shape, bf16),
        compiler_params=params("parallel"),
        name="time_backward",
    )(bias, qkv, grad_out)


def with_class(slot, rows, cls_rows):
    ids = lax.broadcasted_iota(jnp.int32, cls_rows.shape, 0)
    picked = jnp.sum(jnp.where(ids == slot, cls_rows.astype(f32), 0.0), 0, keepdims=True)
    row_ids = lax.broadcasted_iota(jnp.int32, rows.shape, 0)
    return jnp.where(row_ids == REAL_PATCH, picked.astype(bf16), rows)


def key_bias(count):
    key_ids = lax.broadcasted_iota(jnp.int32, (count, 1), 0)
    return jnp.where(key_ids <= REAL_PATCH, 0.0, NEG_LARGE).astype(f32)


def space_forward_kernel(slot_ref, q_ref, k_ref, v_ref, ck_ref, cv_ref, out_ref):
    slot = slot_ref[pl.program_id(0)]
    keys = with_class(slot, k_ref[...], ck_ref[...])
    values = with_class(slot, v_ref[...], cv_ref[...])
    out_ref[...] = forward_tiles([(q_ref[...], keys, values)], key_bias(keys.shape[0]))[0]


def space_backward_kernel(
    slot_ref, q_ref, k_ref, v_ref, ck_ref, cv_ref, g_ref, dq_ref, dk_ref, dv_ref, dck_ref, dcv_ref
):
    slot = slot_ref[pl.program_id(0)]
    keys = with_class(slot, k_ref[...], ck_ref[...])
    values = with_class(slot, v_ref[...], cv_ref[...])
    tile = (q_ref[...], keys, values, g_ref[...])
    grad_q, grad_k, grad_v = backward_tiles([tile], key_bias(keys.shape[0]))[0]
    row_ids = lax.broadcasted_iota(jnp.int32, grad_k.shape, 0)
    dq_ref[...] = grad_q.astype(bf16)
    dk_ref[...] = jnp.where(row_ids < REAL_PATCH, grad_k, 0.0).astype(bf16)
    dv_ref[...] = jnp.where(row_ids < REAL_PATCH, grad_v, 0.0).astype(bf16)
    dck_ref[0] = jnp.sum(jnp.where(row_ids == REAL_PATCH, grad_k, 0.0), 0, keepdims=True)
    dcv_ref[0] = jnp.sum(jnp.where(row_ids == REAL_PATCH, grad_v, 0.0), 0, keepdims=True)


def space_specs(frames, patches):
    cls_block = frames * patches // CLS_ROWS

    def rows(part):
        return pl.BlockSpec((patches, WIDE), lambda f, c, s: (f, part * QUADS + c))

    def cls(part):
        return pl.BlockSpec((CLS_ROWS, WIDE), lambda f, c, s: (cls_block, part * QUADS + c))

    return [rows(0), rows(1), rows(2), cls(1), cls(2)], rows(0)


def space_forward(slots, qkv, frames, patches):
    width = qkv.shape[1] // 3
    in_specs, out_spec = space_specs(frames, patches)
    return pl.pallas_call(
        space_forward_kernel,
        grid_spec=pltpu.PrefetchScalarGridSpec(
            num_scalar_prefetch=1,
            grid=(frames, QUADS),
            in_specs=in_specs,
            out_specs=out_spec,
        ),
        out_shape=jax.ShapeDtypeStruct((frames * patches, width), bf16),
        compiler_params=params("parallel", "parallel"),
        name="space_forward",
    )(slots, qkv, qkv, qkv, qkv, qkv)


def space_backward(slots, qkv, grad_out, frames, patches):
    width = qkv.shape[1] // 3
    in_specs, out_spec = space_specs(frames, patches)
    rows = jax.ShapeDtypeStruct((frames * patches, width), bf16)
    cls_spec = pl.BlockSpec((1, 1, WIDE), lambda f, c, s: (f, 0, c))
    cls = jax.ShapeDtypeStruct((frames, 1, width), f32)
    return pl.pallas_call(
        space_backward_kernel,
        grid_spec=pltpu.PrefetchScalarGridSpec(
            num_scalar_prefetch=1,
            grid=(frames, QUADS),
            in_specs=in_specs + [out_spec],
            out_specs=[out_spec] * 3 + [cls_spec] * 2,
        ),
        out_shape=[rows] * 3 + [cls] * 2,
        compiler_params=params("parallel", "parallel"),
        name="space_backward",
    )(slots, qkv, qkv, qkv, qkv, qkv, grad_out)


def frame_slots(lengths_row, frame_ids):
    clip_ends = jnp.cumsum(lengths_row)
    return jnp.sum((frame_ids[:, None] >= clip_ends[None, :]).astype(jnp.int32), axis=1)


class Layout:
    def __init__(self, devices, frames, patches):
        self.devices = devices
        self.frames = frames
        self.patches = patches
        self.all_patches = patches * devices
        self.away_frames = -(-frames // devices)
        used = self.away_frames * patches
        self.block = -(-used // 16) * 16
        self.home_rows = frames * patches
        self.away_rows = self.away_frames * self.all_patches
        self.sent_rows = devices * self.block

    def home_of_sent(self):
        row = jnp.arange(self.sent_rows, dtype=jnp.int32)
        peer, inner = row // self.block, row % self.block
        frame = peer * self.away_frames + inner // self.patches
        valid = (inner < self.away_frames * self.patches) & (frame < self.frames)
        return jnp.where(valid, (inner % self.patches) * self.frames + frame, -1)

    def sent_of_away(self):
        row = jnp.arange(self.away_rows + CLS_ROWS, dtype=jnp.int32)
        frame, patch = row // self.all_patches, row % self.all_patches
        sent = (patch // self.patches) * self.block + frame * self.patches + patch % self.patches
        return jnp.where(row < self.away_rows, sent, -1)

    def parts(self):
        cuts = (0, self.block // 5 // 16 * 16, self.block // 5 // 16 * 48, self.block)
        return tuple(zip(cuts[:-1], cuts[1:]))

    def orders(self):
        block, patches, near = self.block, self.patches, self.away_frames
        peer, inner = np.meshgrid(range(self.devices), range(block), indexing="ij")
        valid = inner < near * patches
        from_home = np.where(valid, inner // near * self.frames + peer * near + inner % near, -1)
        from_away = np.where(valid, inner // patches * self.all_patches + peer * patches + inner % patches, -1)
        leave = [
            np.concatenate([order[:, low:high].reshape(-1) for low, high in self.parts()])
            for order in (from_home, from_away)
        ]
        row = np.arange(self.away_rows)
        frame, patch = row // self.all_patches, row % self.all_patches
        reach_away = patch // patches * block + patch % patches * near + frame
        row = np.arange(self.home_rows)
        patch, frame = row // self.frames, row % self.frames
        reach_home = frame // near * block + frame % near * patches + patch
        return [np.asarray(part, np.int32)[:, None] for part in (leave[0], reach_away, leave[1], reach_home)]

    def to_away(self, values):
        pick = self.home_of_sent()[:, None] == jnp.arange(self.home_rows, dtype=jnp.int32)[None, :]
        sent = jnp.dot(pick.astype(bf16), values, preferred_element_type=bf16)
        got = lax.all_to_all(sent, "patch", split_axis=0, concat_axis=0, tiled=True)
        pick = self.sent_of_away()[:, None] == jnp.arange(self.sent_rows, dtype=jnp.int32)[None, :]
        return jnp.dot(pick.astype(bf16), got, preferred_element_type=f32)

    def to_home(self, values):
        pick = jnp.arange(self.sent_rows, dtype=jnp.int32)[:, None] == self.sent_of_away()[None, : self.away_rows]
        sent = jnp.dot(pick.astype(bf16), values, preferred_element_type=bf16)
        got = lax.all_to_all(sent, "patch", split_axis=0, concat_axis=0, tiled=True)
        pick = jnp.arange(self.home_rows, dtype=jnp.int32)[:, None] == self.home_of_sent()[None, :]
        return jnp.dot(pick.astype(bf16), got, preferred_element_type=f32)


def norm_rows(values):
    centered = values - jnp.mean(values, -1, keepdims=True)
    inverse = lax.rsqrt(jnp.mean(centered * centered, -1, keepdims=True) + EPSILON)
    return centered, inverse


def norm_forward(values, gain, shift):
    centered, inverse = norm_rows(values)
    return (centered * inverse * gain + shift).astype(bf16)


def norm_backward(values, grad, gain, sums):
    centered, inverse = norm_rows(values)
    weighted = grad * gain
    along = jnp.mean(weighted * centered, -1, keepdims=True) * (inverse * inverse * inverse)

    def fold(part):
        return jnp.sum(part.reshape(part.shape[0] // 8, 8, part.shape[1]), 0)

    sums[0][...] += fold(grad * (centered * inverse))
    sums[1][...] += fold(grad)
    return inverse * (weighted - jnp.mean(weighted, -1, keepdims=True)) - centered * along


class Loads:
    def __init__(self, sources, buffers, sems):
        self.copies = [
            pltpu.make_async_copy(source, buffer, sems.at[i])
            for i, (source, buffer) in enumerate(zip(sources, buffers))
        ]
        for copy in self.copies:
            copy.start()
        self.buffers = buffers
        self.next = 0

    def get(self):
        self.copies[self.next].wait()
        self.next += 1
        return self.buffers[self.next - 1]


class Saves:
    def __init__(self, buffers, targets, sems):
        self.pairs, self.sems = list(zip(buffers, targets)), sems

    def copies(self, part, start, rows):
        here = pl.ds(start, rows)
        return [
            pltpu.make_async_copy(buffer.at[here], target.at[here], self.sems.at[i, part])
            for i, (buffer, target) in enumerate(self.pairs)
        ]

    def put(self, part, start, rows):
        for copy in self.copies(part, start, rows):
            copy.start()

    def finish(self, part, start, rows):
        for copy in self.copies(part, start, rows):
            copy.wait()


class Place:
    AXES = {"core": ("patch", 1), "zl": ("patch", 2), "zh": ("patch", 4), "x": ("clip", 1), "y": ("clip", 2)}

    def __init__(self):
        self.clip, self.patch = lax.axis_index("clip"), lax.axis_index("patch")
        self.me = {
            "core": lax.rem(self.patch, 2),
            "zl": lax.rem(self.patch // 2, 2),
            "zh": self.patch // 4,
            "x": lax.rem(self.clip, 2),
            "y": self.clip // 2,
        }

    def peer(self, dim):
        axis, stride = self.AXES[dim]
        own = self.clip if axis == "clip" else self.patch
        other = own + stride - 2 * stride * self.me[dim]
        return (other, self.patch) if axis == "clip" else (self.clip, other)


class Shuffle:
    def __init__(self, lay, at, sent, got, send_sem, recv_sem):
        self.devices, self.parts, self.at = lay.devices, lay.parts(), at
        self.sent, self.got, self.send_sem, self.recv_sem = sent, got, send_sem, recv_sem
        self.moves = 0

    def greet(self):
        for offset in range(1, self.devices):
            other = (self.at.clip, lax.rem(self.at.patch + offset, self.devices))
            pl.semaphore_signal(pltpu.get_barrier_semaphore(), inc=1, device_id=other, device_id_type=MESH)

    def meet(self, others=0):
        pl.semaphore_wait(pltpu.get_barrier_semaphore(), self.devices - 1 + others)

    def copy(self, offset, part):
        two = self.moves % 2
        other = lax.rem(self.at.patch + offset, self.devices)
        low, high = self.parts[part]
        rows = pl.ds(low, high - low)
        return pltpu.make_async_remote_copy(
            src_ref=self.sent.at[other, rows],
            dst_ref=self.got.at[two, self.at.patch, rows],
            send_sem=self.send_sem.at[part, offset],
            recv_sem=self.recv_sem.at[two, part, offset],
            device_id=(self.at.clip, other),
            device_id_type=MESH,
        )

    def send(self, part, order_ref, source_ref, first, last):
        width = self.sent.shape[-1]
        low, high = self.parts[part]
        rows = (high - low) * self.devices
        start = low * self.devices
        ids = lax.broadcasted_iota(jnp.int32, (rows, last - first), 1) + first
        pick = (order_ref[start : start + rows, :] == ids).astype(f32).astype(bf16)
        picked = dot_nn(pick, source_ref[first:last, :]).astype(bf16)
        self.sent[:, low:high, :] = picked.reshape(self.devices, high - low, width)
        for offset in range(1, self.devices):
            self.copy(offset, part).start()
        self.got[self.moves % 2, self.at.patch, low:high, :] = self.sent[self.at.patch, low:high, :]

    def send_all(self, order_ref, source_ref):
        for part in range(len(self.parts)):
            self.send(part, order_ref, source_ref, 0, source_ref.shape[0])

    def receive(self, order_ref, target_ref):
        for part in range(len(self.parts)):
            for offset in range(1, self.devices):
                self.copy(offset, part).wait()
        devices, block, width = self.got.shape[1:]
        rows = target_ref.shape[0] // 3
        ids = lax.broadcasted_iota(jnp.int32, (rows, devices * block), 1)
        for start in range(0, target_ref.shape[0], rows):
            pick = (order_ref[start : start + rows, :] == ids).astype(f32).astype(bf16)
            got = self.got[self.moves % 2].reshape(devices * block, width)
            target_ref[start : start + rows, :] = dot_nn(pick, got).astype(bf16)
        self.moves += 1


def time_tiles(bias_ref, qkv_ref, width, group, grad_ref=None):
    rows = bias_ref.shape[0]
    here = pl.ds(pl.multiple_of(group * rows, 16), rows)
    tiles = []
    for quad in range(QUADS):
        tile = [qkv_ref[here, columns(part, quad, width)] for part in range(3)]
        if grad_ref is not None:
            tile.append(grad_ref[here, columns(0, quad, width)])
        tiles.append(tile)
    return here, tiles


def space_tiles(patches, total, slot, qkv_ref, width, frame, grad_ref=None):
    here = pl.ds(pl.multiple_of(frame * patches, 16), patches)
    tiles = []
    for quad in range(QUADS):
        tile = [qkv_ref[here, columns(part, quad, width)] for part in range(3)]
        for part in (1, 2):
            tile[part] = with_class(slot, tile[part], qkv_ref[total : total + CLS_ROWS, columns(part, quad, width)])
        if grad_ref is not None:
            tile.append(grad_ref[here, columns(0, quad, width)])
        tiles.append(tile)
    return here, tiles


def group_parts(lay, rows):
    ends = []
    for _, high in lay.parts():
        patches = min(-(-high // lay.away_frames), lay.patches)
        ends.append(-(-patches * lay.frames // rows) * rows)
    return tuple(zip([0] + ends[:-1], ends))


def time_half(layer, lay, *refs):
    x_ref, gain_ref, shift_ref, bias_ref, leave_home, reach_away, proj_hbm, output_hbm = refs[:8]
    away_ref, *saved = refs[8:12]
    normed, qkv, mixed = staged = refs[12:15]
    proj, output, after, load_sem, save_sem, *moving = refs[15:]
    width = x_ref.shape[1]
    rows = bias_ref.shape[0]
    weights = Loads((proj_hbm.at[layer], output_hbm.at[layer]), (proj, output), load_sem)
    saves = Saves(staged, saved, save_sem)
    shuffle = Shuffle(lay, Place(), *moving)
    shuffle.greet()
    gain, shift = gain_ref[layer, 0:1], shift_ref[layer, 0:1]
    parts = group_parts(lay, rows)
    for part, (first, last) in enumerate(parts):
        here = slice(first, last)
        normed[here, :] = norm_forward(x_ref[here, :].astype(f32), gain, shift)
        if part == 0:
            weights.get()
        for start in range(0, 3 * width, width):
            these = slice(start, start + width)
            qkv[here, these] = dot_nn(normed[here, :], proj[:, these]).astype(bf16)

        @pl.loop(first // rows, last // rows)
        def _(group):
            at, tiles = time_tiles(bias_ref, qkv, width, group)
            for quad, done in enumerate(forward_tiles(tiles, bias_ref[...])):
                mixed[at, columns(0, quad, width)] = done

        if part == 0:
            weights.get()
            shuffle.meet()
        after[here, :] = (x_ref[here, :].astype(f32) + dot_nn(mixed[here, :], output[...])).astype(bf16)
        shuffle.send(part, leave_home, after, 0 if part < 2 else first, last)
        saves.put(part, first, last - first)
    shuffle.receive(reach_away, away_ref)
    for part, (first, last) in enumerate(parts):
        saves.finish(part, first, last - first)


def space_half(layer, lay, *refs):
    slot_ref, x_ref, cls_ref, gain_ref, shift_ref, *orders = refs[:10]
    leave_home, reach_away, leave_away, reach_home, grad_ref = orders
    proj_hbm, output_hbm, up_hbm, down_hbm = refs[10:14]
    result_ref, grad_away_ref, *saved = refs[14:23]
    normed, qkv, mixed, middle, normed_f, active, slope = staged = refs[23:30]
    proj, output, up, down, after, load_sem, save_sem, cls_sem, *moving = refs[30:]
    width = x_ref.shape[1]
    total = x_ref.shape[0]
    patches = lay.all_patches
    moves = layer < LAYERS - 1
    sources = [part.at[layer] for part in (proj_hbm, output_hbm, up_hbm, down_hbm)]
    weights = Loads(sources, (proj, output, up, down), load_sem)
    saves = Saves(staged, saved, save_sem)
    cls_saves = Saves(staged[:2], saved[:2], cls_sem)
    if moves:
        shuffle = Shuffle(lay, Place(), *moving)
        shuffle.greet()
    gain, shift = gain_ref[layer, 1:2], shift_ref[layer, 1:2]
    gain_f, shift_f = gain_ref[layer, 2:3], shift_ref[layer, 2:3]
    normed[total:, :] = norm_forward(cls_ref[...], gain, shift)
    if moves:
        shuffle.meet()
        shuffle.send_all(leave_home, grad_ref)
    weights.get()
    for start in range(0, 3 * width, width):
        these = slice(start, start + width)
        qkv[total:, these] = dot_nn(normed[total:, :], proj[:, these]).astype(bf16)
    cls_saves.put(0, total, CLS_ROWS)
    bias = key_bias(patches)
    if moves:
        shuffle.receive(reach_away, grad_away_ref)

    @pl.loop(0, total // patches)
    def _(frame):
        start = pl.multiple_of(frame * patches, 16)
        here = pl.ds(start, patches)
        normed[here, :] = norm_forward(x_ref[here, :].astype(f32), gain, shift)
        for column in range(0, 3 * width, width):
            these = slice(column, column + width)
            qkv[here, these] = dot_nn(normed[here, :], proj[:, these]).astype(bf16)
        _, tiles = space_tiles(patches, total, slot_ref[frame], qkv, width, frame)
        for quad, done in enumerate(forward_tiles(tiles, bias)):
            mixed[here, columns(0, quad, width)] = done

        @pl.when(frame == 0)
        def _():
            for copy in weights.copies[1:]:
                copy.wait()

        residual = x_ref[here, :].astype(f32) + dot_nn(mixed[here, :], output[...])
        middle[here, :] = residual.astype(bf16)
        normed_f[here, :] = norm_forward(residual, gain_f, shift_f)
        for column in range(0, up.shape[1], WIDE):
            these = slice(column, column + WIDE)
            hidden = dot_nn(normed_f[here, :], up[:, these])
            share = 0.5 * (1.0 + lax.erf(hidden * ROOT_HALF))
            active[here, these] = (hidden * share).astype(bf16)
            bend = share + hidden * (INV_ROOT_TWO_PI * jnp.exp(-0.5 * hidden * hidden))
            slope[here, these] = bend.astype(bf16)
        done = (residual + dot_nn(active[here, :], down[...])).astype(bf16)
        if moves:
            after[here, :] = done
            for part in range(2):

                @pl.when(frame == part)
                def _(part=part):
                    shuffle.send(part, leave_away, after, 0, (part + 1) * patches)

        else:
            result_ref[here, :] = done
        saves.put(frame, start, patches)

    if moves:
        shuffle.send(2, leave_away, after, patches, total)
        shuffle.receive(reach_home, result_ref)
    for frame in range(total // patches):
        saves.finish(frame, frame * patches, patches)
    cls_saves.finish(0, total, CLS_ROWS)


CHUNKS = 16
TOTAL = CHUNKS * LAYERS
BLOCKS = 3
PIECE = (48, 128)
ROUTES = (("x", "zl", "zh", "y", "x", "y"), ("y", "zl", "zh", "x", "x", "y"), ("x", "y", "zl", "zh", "x", "y"))
SUMS = 4
STAGES = 7
RAW_SLOTS = 8
ACC_SLOTS = 8
BOX_SLOTS = 4
STRIDE = 2
SEGMENTS = (4, 4, 1, 3, 1, 3)
PLAN = {
    1: dict(early=2, down=1, hidden=1, wide=2, norm=1, frames=(0, 1, 0), up=0, space_out=2, space_proj=1, time_early=0, home=1, time0=1, time1=1, time2=0, time_out=1, time_proj=0),
    0: dict(early=1, down=1, hidden=1, wide=1, norm=0, frames=(1, 2, 2), up=1, space_out=0, space_proj=2, time_early=0, home=1, time0=1, time1=2, time2=0, time_out=1, time_proj=1),
}
SMALL = ("core", "zl", "zh", "x", "y")
SMALL_ROWS = 24


def recv_shape(route, stage):
    left = [dim for dim in ("zh", "zl", "x", "y") if dim not in route[: stage + 1]]
    return (2,) * len(left) + PIECE


class Pump:
    def __init__(self, at, results, scratch):
        self.at, self.results = at, results
        self.raw, self.core_in, self.acc, self.out, *rest = scratch
        self.inboxes = rest[: BLOCKS * SUMS]
        self.core_send, self.core_recv, self.core_free, self.send_sem, self.recv_sem = rest[BLOCKS * SUMS :]
        self.made = self.stepped = 0

    def core_copy(self, c, z):
        slot = lax.rem(c, RAW_SLOTS)
        return pltpu.make_async_remote_copy(
            src_ref=self.raw.at[slot, z // 2, z % 2, 1 - self.at.me["core"]],
            dst_ref=self.core_in.at[slot, z // 2, z % 2],
            send_sem=self.core_send.at[slot, z],
            recv_sem=self.core_recv.at[slot, z],
            device_id=self.at.peer("core"),
            device_id_type=MESH,
        )

    def claim(self, c, known):
        if known >= RAW_SLOTS:
            pl.semaphore_wait(self.core_free, 1)

    def store(self, c, z, core, block, rows):
        slot = lax.rem(c, RAW_SLOTS)
        for xh in range(2):
            for yh in range(2):
                part = rows[xh * 48 : (xh + 1) * 48, yh * 128 : (yh + 1) * 128]
                self.raw[slot, z // 2, z % 2, core, block, xh, yh] = part.astype(bf16)

    def make_chunks(self, count, lhs, rhs):
        first = self.made

        def one(i, c, known):
            self.claim(c, known)
            for half in range(2):
                left = lhs(slice(half * 384, (half + 1) * 384))
                for block in range(BLOCKS):
                    done = dot_tn(left, rhs(i, block * 256))
                    for j in range(4):
                        self.store(c, half * 2 + j // 2, j % 2, block, done[j * 96 : (j + 1) * 96])
            for z in range(4):
                self.core_copy(c, z).start()

        if count == 1:
            one(0, first, first)
        else:
            assert (first >= RAW_SLOTS) == (first + count - 1 >= RAW_SLOTS)

            @pl.loop(0, count)
            def _(i):
                one(i, first + i, first)

        self.made += count
        assert self.made - self.stepped <= RAW_SLOTS

    def make_down(self, lhs, rhs):
        first = self.made

        @pl.loop(0, 4)
        def _(z):
            if first >= RAW_SLOTS:

                @pl.when(z == 0)
                def _():
                    pl.semaphore_wait(self.core_free, 4)

            for core in range(2):
                left = lhs(pl.ds(pl.multiple_of(z * 768 + core * 384, 128), 384))
                for block in range(BLOCKS):
                    done = dot_tn(left, rhs[:, block * 256 : (block + 1) * 256])
                    for c in range(4):
                        self.store_at(first + c, z, core, block, done[c * 96 : (c + 1) * 96])
            for c in range(4):
                slot = (first + c) % RAW_SLOTS
                zh, zl = z // 2, lax.rem(z, 2)
                pltpu.make_async_remote_copy(
                    src_ref=self.raw.at[slot, zh, zl, 1 - self.at.me["core"]],
                    dst_ref=self.core_in.at[slot, zh, zl],
                    send_sem=self.core_send.at[slot, z],
                    recv_sem=self.core_recv.at[slot, z],
                    device_id=self.at.peer("core"),
                    device_id_type=MESH,
                ).start()

        self.made += 4
        assert self.made - self.stepped <= RAW_SLOTS

    def store_at(self, c, z, core, block, rows):
        for xh in range(2):
            for yh in range(2):
                part = rows[xh * 48 : (xh + 1) * 48, yh * 128 : (yh + 1) * 128]
                self.raw[c % RAW_SLOTS, z // 2, lax.rem(z, 2), core, block, xh, yh] = part.astype(bf16)

    def part(self, c, block, stage, value):
        route = ROUTES[block]

        def pick(dim):
            if dim in route[:stage]:
                return self.at.me[dim]
            return value if dim == route[stage] else slice(None)

        return (lax.rem(c, ACC_SLOTS), pick("zh"), pick("zl"), block, pick("x"), pick("y"))

    def exchange(self, c, block, stage):
        me = self.at.me
        dim = ROUTES[block][stage]
        box = lax.rem(c, BOX_SLOTS)
        if stage < SUMS:
            src = self.acc.at[self.part(c, block, stage, 1 - me[dim])]
            dst = self.inboxes[block * SUMS + stage].at[box]
        else:
            slot = lax.rem(c, ACC_SLOTS)
            if stage == SUMS:
                src = dst = self.out.at[slot, block, me["x"], me["y"]]
            elif dim == "x":
                src = dst = self.out.at[slot, block, me["x"]]
            else:
                src = dst = self.out.at[slot, block, :, me["y"]]
        return pltpu.make_async_remote_copy(
            src_ref=src,
            dst_ref=dst,
            send_sem=self.send_sem.at[box, block, stage],
            recv_sem=self.recv_sem.at[box, block, stage],
            device_id=self.at.peer(dim),
            device_id_type=MESH,
        )

    def enter(self, c):
        me = self.at.me
        slot, into = lax.rem(c, RAW_SLOTS), lax.rem(c, ACC_SLOTS)
        for z in range(4):
            self.core_copy(c, z).wait()
        for zh in range(2):
            for zl in range(2):
                both = self.raw[slot, zh, zl, me["core"]].astype(f32) + self.core_in[slot, zh, zl].astype(f32)
                self.acc[into, zh, zl] = both.astype(bf16)

        @pl.when(c < TOTAL - RAW_SLOTS)
        def _():
            pl.semaphore_signal(self.core_free, inc=1, device_id=self.at.peer("core"), device_id_type=MESH)

        for block in range(BLOCKS):
            self.exchange(c, block, 0).start()

    def advance(self, c, stage):
        me = self.at.me
        slot, box = lax.rem(c, ACC_SLOTS), lax.rem(c, BOX_SLOTS)
        for block in range(BLOCKS):
            self.exchange(c, block, stage).wait()
            if stage < SUMS:
                where = self.part(c, block, stage, me[ROUTES[block][stage]])
                both = self.acc[where].astype(f32) + self.inboxes[block * SUMS + stage][box].astype(f32)
                if stage == SUMS - 1:
                    self.out[slot, block, me["x"], me["y"]] = both.astype(bf16)
                else:
                    self.acc[where] = both.astype(bf16)
            if stage + 1 < STAGES - 1:
                self.exchange(c, block, stage + 1).start()
            else:
                self.finish(c, block)

    def finish(self, c, block):
        slot = lax.rem(c, ACC_SLOTS)
        layer = LAYERS - 1 - c // CHUNKS
        inner = lax.rem(c, CHUNKS)
        start = 0
        for which, count in enumerate(SEGMENTS):

            @pl.when((inner >= start) & (inner < start + count))
            def _(which=which, start=start):
                for xh in range(2):
                    for yh in range(2):
                        part = self.out[slot, block, xh, yh]
                        column = block * 256 + yh * 128
                        if which == 0:
                            row = pl.multiple_of((inner - start) * 96 + xh * 48, 16)
                            self.results[which][layer, pl.ds(row, 48), column : column + 128] = part
                        else:
                            at = pl.ds(pl.multiple_of((inner - start) * 768 + column, 128), 128)
                            self.results[which][layer, xh * 48 : (xh + 1) * 48, at] = part

            start += count

    def run_step(self, t):
        for stage in reversed(range(STAGES)):
            c = t - STRIDE * stage

            @pl.when((c >= 0) & (c < TOTAL))
            def _(c=c, stage=stage):
                if stage == 0:
                    self.enter(c)
                else:
                    self.advance(c, stage - 1)

    def step(self, count=1):
        first = self.stepped
        self.stepped += count
        assert min(self.stepped, TOTAL) <= self.made

        @pl.loop(first, first + count)
        def _(t):
            self.run_step(t)

    def inside(self, count):
        first = self.stepped
        self.stepped += count
        assert min(self.stepped, TOTAL) <= self.made
        return first

    def frame_steps(self, counts):
        first = self.inside(sum(counts))
        a, b, c = counts

        def run(frame):
            second, third = (frame + 1) // 2, frame // 2
            low = first + a * second + b * third

            @pl.loop(low, low + a + (b - a) * second + (c - b) * third)
            def _(t):
                self.run_step(t)

        return run


class Small:
    def __init__(self, at, values, boxes, send_sem, recv_sem):
        self.at, self.values, self.boxes, self.send_sem, self.recv_sem = at, values, boxes, send_sem, recv_sem

    def rows(self, i):
        return SMALL_ROWS if i < 3 else 16

    def copy(self, i):
        part = pl.ds(0, self.rows(i))
        return pltpu.make_async_remote_copy(
            src_ref=self.values.at[part],
            dst_ref=self.boxes.at[i, part],
            send_sem=self.send_sem.at[i],
            recv_sem=self.recv_sem.at[i],
            device_id=self.at.peer(SMALL[i]),
            device_id_type=MESH,
        )

    def step(self, i):
        if i > 0:
            rows = slice(0, self.rows(i - 1))
            self.copy(i - 1).wait()
            self.values[rows] += self.boxes[i - 1, rows]
        if i < len(SMALL):
            self.copy(i).start()


class Ring:
    def __init__(self, sources, slots, sems):
        self.sources, self.slots, self.sems = sources, slots, sems
        self.depth = slots.shape[0]
        self.started = self.taken = 0
        for _ in range(self.depth):
            self.start()

    def copy(self, i):
        source = self.sources[i]
        slot = i % self.depth
        return pltpu.make_async_copy(source, self.slots.at[slot, pl.ds(0, source.shape[0])], self.sems.at[slot])

    def start(self):
        if self.started < len(self.sources):
            self.copy(self.started).start()
            self.started += 1

    def take(self):
        i = self.taken
        self.copy(i).wait()
        self.taken += 1
        return self.slots.at[i % self.depth, pl.ds(0, self.sources[i].shape[0])]

    def free(self):
        self.start()


class Single:
    def __init__(self, sources, buffer, sem):
        self.copies = [
            pltpu.make_async_copy(source, buffer.at[pl.ds(0, source.shape[0])], sem) for source in sources
        ]
        self.next = 0
        self.copies[0].start()

    def take(self):
        self.copies[self.next].wait()

    def free(self):
        self.next += 1
        if self.next < len(self.copies):
            self.copies[self.next].start()


def backward_kernel(lay, *refs):
    devices, patches = lay.devices, lay.all_patches
    slot_ref, cls_ref, gain_ref, bias_ref, leave_home, reach_away, leave_away, reach_home = refs[:8]
    weights = dict(zip(("time_proj", "time_output", "space_proj", "space_output", "up", "down"), refs[8:14]))
    grad_hbm, x_out_hbm = refs[14:16]
    names = ("x_home", "normed_t", "qkv_t", "mixed_t", "x_away", "normed_s", "qkv_s", "mixed_s", "middle", "normed_f", "active", "slope")
    refs = refs[16:]
    saved = [dict(zip(names, refs[len(names) * layer : len(names) * (layer + 1)])) for layer in range(LAYERS)]
    refs = refs[len(names) * LAYERS :]
    small_ref, *results, output_hbm, tokens_hbm = refs[:9]
    refs = refs[9:]
    hidden, qkv, dqkv, wide, mixed, branch, x_buf, grad_buf, home_buf, cls_sum = refs[:10]
    weight_slots, lhs_slots, sent, got, small_boxes, *sums = refs[10:21]
    sem_hidden, sem_qkv, sem_x, sem_ends, sem_weight, sem_lhs, sem_sent, sem_got, small_send, small_recv = refs[21:31]
    pump_scratch = refs[31:]
    load_grad = pltpu.make_async_copy(grad_hbm, grad_buf, sem_ends.at[0])
    load_out = pltpu.make_async_copy(x_out_hbm, mixed, sem_ends.at[1])
    save_out = pltpu.make_async_copy(home_buf, output_hbm, sem_ends.at[2])
    save_tokens = pltpu.make_async_copy(mixed, tokens_hbm, sem_ends.at[3])
    load_out.start()
    load_grad.start()

    at = Place()
    shuffle = Shuffle(lay, at, sent, got, sem_sent, sem_got)
    shuffle.greet()
    for dim in ("x", "y"):
        pl.semaphore_signal(pltpu.get_barrier_semaphore(), inc=1, device_id=at.peer(dim), device_id_type=MESH)

    total, width = grad_buf.shape
    parts = range(0, 3 * width, width)
    order = tuple(reversed(range(LAYERS)))
    tiles, lhs = [], []
    for layer in order:
        wide_parts = range(0, weights["up"].shape[2], width)
        tiles += [weights["down"].at[layer, pl.ds(start, width), :] for start in wide_parts]
        tiles += [weights["up"].at[layer, :, pl.ds(start, width)] for start in wide_parts]
        tiles += [weights["space_output"].at[layer]]
        tiles += [weights["space_proj"].at[layer, :, pl.ds(start, width)] for start in parts]
        tiles += [weights["time_output"].at[layer]]
        tiles += [weights["time_proj"].at[layer, :, pl.ds(start, width)] for start in parts]
        here = saved[layer]
        lhs += [here["slope"].at[:, pl.ds(start, width)] for start in wide_parts]
        lhs += [here[name] for name in ("normed_f", "mixed_s", "normed_s", "mixed_t", "normed_t")]
    fill = Single([saved[layer]["active"] for layer in order], hidden, sem_hidden)
    ring = Ring(tiles, weight_slots, sem_weight)
    left = Ring(lhs, lhs_slots, sem_lhs)
    load_qkv = Single([saved[layer][name] for layer in order for name in ("qkv_s", "qkv_t")], qkv, sem_qkv)
    load_x = Single(
        [saved[layer][name] for layer in order for name in ("middle", "x_away", "x_home")], x_buf, sem_x
    )
    pump = Pump(at, results, pump_scratch)
    small = Small(at, small_ref, small_boxes, small_send, small_recv)
    for part in sums:
        part[...] = jnp.zeros_like(part)
    small_ref[...] = jnp.zeros_like(small_ref)
    key_mask = key_bias(patches)

    def back_product(rows, source, count):
        for i in range(count):
            tile = ring.take()
            part = dot_nt(source[:rows, i * width : (i + 1) * width], tile[...])
            if i:
                wide[:rows, :] += part
            else:
                wide[:rows, :] = part
            ring.free()

    frames = total // patches
    group = bias_ref.shape[0]
    groups = group_parts(lay, group)

    def made_of(lhs_tile, source, first=0, rows=None):
        rows = source.shape[0] if rows is None else rows

        def rhs(i, start):
            column = pl.multiple_of((i + first) * width + start, 128) if not isinstance(i, int) else (i + first) * width + start
            return source[:rows, pl.ds(column, WIDE)]

        return (lambda these: lhs_tile[:, these]), rhs

    shuffle.meet(2)
    load_out.wait()
    shuffle.send_all(leave_away, mixed)
    load_grad.wait()
    dy = grad_buf

    for layer in order:
        last = layer == 0
        plan = PLAN[layer]

        def steps(site, plan=plan):
            if plan.get(site, 0):
                pump.step(plan[site])

        fill.take()
        pump.make_down(lambda these: hidden[:, these], dy)
        steps("down")
        for start in range(0, hidden.shape[1], width):
            tile, slope = ring.take(), left.take()
            for block in range(0, width, WIDE):
                grad_active = dot_nt(dy[...], tile[block : block + WIDE, :])
                grad_hidden = grad_active * slope[:, block : block + WIDE].astype(f32)
                hidden[:, start + block : start + block + WIDE] = grad_hidden.astype(bf16)
            ring.free()
            left.free()
        normed_f = left.take()
        if plan["early"]:
            pump.make_chunks(plan["early"], *made_of(normed_f, hidden))
        steps("hidden")
        back_product(total, hidden, hidden.shape[1] // width)
        steps("wide")
        load_x.take()

        @pl.loop(0, frames)
        def _(frame, layer=layer):
            here = pl.ds(pl.multiple_of(frame * patches, 16), patches)
            part = norm_backward(x_buf[here, :].astype(f32), wide[here, :], gain_ref[layer, 2:3], sums[0:2])
            both = dy[here, :].astype(f32) + part
            wide[here, :] = both
            branch[here, :] = both.astype(bf16)

        load_x.free()
        if not last:
            shuffle.receive(reach_home, home_buf)
            save_out.start()
        steps("norm")

        out_tile, *proj_tiles = [ring.take() for _ in range(4)]
        load_qkv.take()
        load_x.take()
        cls_sum[...] = jnp.zeros_like(cls_sum)
        gain = gain_ref[layer, 1:2]
        frame_run = pump.frame_steps(plan["frames"])

        @pl.loop(0, frames)
        def _(frame):
            here = pl.ds(pl.multiple_of(frame * patches, 16), patches)
            mixed[here, :] = dot_nt(branch[here, :], out_tile[...]).astype(bf16)
            slot = slot_ref[frame]
            _, these = space_tiles(patches, total, slot, qkv, width, frame, mixed)
            row_ids = lax.broadcasted_iota(jnp.int32, (patches, WIDE), 0)
            cls_ids = lax.broadcasted_iota(jnp.int32, (CLS_ROWS, WIDE), 0)
            for quad, grads in enumerate(backward_tiles(these, key_mask)):
                dqkv[here, columns(0, quad, width)] = grads[0].astype(bf16)
                for part in (1, 2):
                    where = columns(part, quad, width)
                    dqkv[here, where] = jnp.where(row_ids < REAL_PATCH, grads[part], 0.0).astype(bf16)
                    row = grads[part][REAL_PATCH : REAL_PATCH + 1]
                    cls_sum[:, where] += jnp.where(cls_ids == slot, row, 0.0)
            grad = sum(dot_nt(dqkv[here, i * width : (i + 1) * width], tile[...]) for i, tile in enumerate(proj_tiles))
            part = norm_backward(x_buf[here, :].astype(f32), grad, gain, sums[2:4])
            mixed[here, :] = (wide[here, :] + part).astype(bf16)
            for i in range(2):

                @pl.when(frame == i)
                def _(i=i):
                    shuffle.send(i, leave_away, mixed, 0, (i + 1) * patches)

            frame_run(frame)

        shuffle.send(2, leave_away, mixed, patches, total)
        load_x.free()
        load_qkv.free()
        dqkv[total:, :] = cls_sum[...].astype(bf16)
        grad = sum(dot_nt(dqkv[total:, i * width : (i + 1) * width], tile[...]) for i, tile in enumerate(proj_tiles))
        for _ in range(4):
            ring.free()
        part = norm_backward(cls_ref[...], grad, gain, sums[2:4])
        small_ref[16:24] += part[:8]
        if plan["early"] < 4:
            pump.make_chunks(4 - plan["early"], *made_of(normed_f, hidden, plan["early"]))
        left.free()
        fill.free()
        steps("up")
        pump.make_chunks(1, *made_of(left.take(), branch))
        left.free()
        steps("space_out")
        pump.make_chunks(3, *made_of(left.take(), dqkv))
        left.free()
        steps("space_proj")
        if not last:
            save_out.wait()
        shuffle.receive(reach_home, home_buf)

        out_tile, *proj_tiles = [ring.take() for _ in range(4)]
        load_qkv.take()
        load_x.take()
        mixed_t = left.take()
        if plan["time_early"]:
            pump.make_chunks(1, *made_of(mixed_t, home_buf))
            left.free()
        steps("home")
        for number, (first, end) in enumerate(groups):
            here = slice(first, end)
            mixed[here, :] = dot_nt(home_buf[here, :], out_tile[...]).astype(bf16)

            @pl.loop(first // group, end // group)
            def _(index):
                at_rows, these = time_tiles(bias_ref, qkv, width, index, mixed)
                for quad, grads in enumerate(backward_tiles(these, bias_ref[...])):
                    for part in range(3):
                        dqkv[at_rows, columns(part, quad, width)] = grads[part].astype(bf16)

            grad = sum(dot_nt(dqkv[here, i * width : (i + 1) * width], tile[...]) for i, tile in enumerate(proj_tiles))
            part = norm_backward(x_buf[here, :].astype(f32), grad, gain_ref[layer, 0:1], sums[4:6])
            mixed[here, :] = (home_buf[here, :].astype(f32) + part).astype(bf16)
            if not last:
                shuffle.send(number, leave_home, mixed, 0 if number < 2 else first, end)
            steps("time%d" % number)
        load_qkv.free()
        load_x.free()
        for _ in range(4):
            ring.free()
        for i, part in enumerate(sums):
            row = layer * 8 + (2, 5, 1, 4, 0, 3)[i]
            small_ref[row : row + 1, :] += jnp.sum(part[...], 0, keepdims=True)
            part[...] = jnp.zeros_like(part)
        if last:
            save_tokens.start()
            small.step(0)
        if not plan["time_early"]:
            pump.make_chunks(1, *made_of(mixed_t, home_buf))
            left.free()
        steps("time_out")
        pump.make_chunks(3, *made_of(left.take(), dqkv, rows=total))
        left.free()
        steps("time_proj")
        if last:
            for i in range(1, len(SMALL) + 1):
                pump.step()
                small.step(i)
        else:
            shuffle.receive(reach_away, grad_buf)

    pump.step(TOTAL + STRIDE * (STAGES - 1) - pump.stepped)
    save_tokens.wait()


IN_VMEM = pl.BlockSpec(memory_space=pltpu.VMEM)
IN_SMEM = pl.BlockSpec(memory_space=pltpu.SMEM)
IN_HBM = pl.BlockSpec(memory_space=pl.ANY)


def shape(*dims, kind=bf16):
    return jax.ShapeDtypeStruct(dims, kind)


def half_call(name, body, collective, near, far, out_near, out_far, scratch):
    compiler = dict(vmem_limit_bytes=58 * 1024 * 1024)
    if collective is not None:
        compiler.update(collective_id=collective, has_side_effects=True)
    in_specs = [IN_SMEM if part.ndim == 1 else IN_VMEM for part in near] + [IN_HBM] * len(far)
    return pl.pallas_call(
        body,
        in_specs=in_specs,
        out_specs=[IN_VMEM] * len(out_near) + [IN_HBM] * len(out_far),
        out_shape=[*out_near, *out_far],
        scratch_shapes=[pltpu.VMEM(part.shape, part.dtype) for part in out_far] + scratch,
        compiler_params=pltpu.CompilerParams(**compiler),
        name=name,
    )(*near, *far)


def fast_local(
    tokens,
    cls_tokens,
    clip_lengths,
    time_proj,
    time_output,
    space_proj,
    space_output,
    up_weight,
    down_weight,
    norm_gains,
    norm_biases,
    cotangent,
):
    frames, patch_rows, width = tokens.shape
    devices = lax.axis_size("patch")
    hidden = up_weight.shape[2]
    lay = Layout(devices, frames, patch_rows)
    home, away, block = lay.home_rows, lay.away_rows, lay.block
    patches = lay.all_patches
    clip_count = cls_tokens.shape[0]

    frame_ids = jnp.arange(frames, dtype=jnp.int32)
    slots = frame_slots(clip_lengths[0], frame_ids)
    bias = time_bias(slots[:, None] == slots[None, :], patch_rows, frames)
    my_frames = lax.axis_index("patch") * lay.away_frames + jnp.arange(lay.away_frames, dtype=jnp.int32)
    my_slots = frame_slots(clip_lengths[0], my_frames)
    orders = [jnp.asarray(part) for part in lay.orders()]
    leave_home, reach_away, leave_away, reach_home = orders

    def home_order(values):
        return jnp.transpose(values, (1, 0, 2)).reshape(home, width)

    def given_order(values):
        return jnp.transpose(values.reshape(patch_rows, frames, width), (1, 0, 2))

    def vmem(*dims, kind=bf16):
        return pltpu.VMEM(dims, kind)

    def queue(*counts):
        return pltpu.SemaphoreType.DMA(counts)

    parts = len(lay.parts())
    moving = [vmem(devices, block, width), vmem(2, devices, block, width), queue(parts, devices), queue(2, parts, devices)]
    cls_aug = jnp.pad(cls_tokens.astype(f32), ((0, CLS_ROWS - clip_count), (0, 0)))
    at_home = home_order(tokens)
    grad_home = home_order(cotangent)
    stored = []
    for layer in range(LAYERS):
        x_home = at_home
        x_away, normed_t, qkv_t, mixed_t = half_call(
            "time_half",
            functools.partial(time_half, layer, lay),
            2 + layer,
            (x_home, norm_gains, norm_biases, bias, leave_home, reach_away),
            (time_proj, time_output),
            [shape(away, width)],
            [shape(home, width), shape(home, 3 * width), shape(home, width)],
            [vmem(width, 3 * width), vmem(width, width), vmem(home, width), queue(2), queue(3, parts), *moving],
        )
        moves = layer < LAYERS - 1
        at_home, got_grad, normed_s, qkv_s, mixed_s, middle, normed_f, active, slope = half_call(
            "space_half",
            functools.partial(space_half, layer, lay),
            4 if moves else None,
            (my_slots, x_away, cls_aug, norm_gains, norm_biases, *orders, grad_home),
            (space_proj, space_output, up_weight, down_weight),
            [shape(home if moves else away, width), shape(away, width) if moves else shape(16, width)],
            [
                shape(away + CLS_ROWS, width),
                shape(away + CLS_ROWS, 3 * width),
                *[shape(away, width)] * 3,
                *[shape(away, hidden)] * 2,
            ],
            [
                vmem(width, 3 * width),
                vmem(width, width),
                vmem(width, hidden),
                vmem(hidden, width),
                vmem(away, width),
                queue(4),
                queue(7, lay.away_frames),
                queue(2, 1),
                *(moving if moves else []),
            ],
        )
        grad_away = got_grad if layer == 0 else grad_away
        stored.append((x_home, normed_t, qkv_t, mixed_t, x_away, normed_s, qkv_s, mixed_s, middle, normed_f, active, slope))
    x_out = at_home

    inbox = [vmem(BOX_SLOTS, *recv_shape(ROUTES[b], s)) for b in range(BLOCKS) for s in range(SUMS)]
    single = pltpu.SemaphoreType.DMA
    near = (my_slots, cls_aug, norm_gains, bias, *orders)
    far = (time_proj, time_output, space_proj, space_output, up_weight, down_weight, grad_away, x_out, *stored[0], *stored[1])
    share = width // devices
    out_shape = [
        shape(SMALL_ROWS, width, kind=f32),
        shape(LAYERS, hidden // devices, width),
        shape(LAYERS, share, hidden),
        shape(LAYERS, share, width),
        shape(LAYERS, share, 3 * width),
        shape(LAYERS, share, width),
        shape(LAYERS, share, 3 * width),
        shape(home, width),
        shape(home, width),
    ]
    small, *large, output, grad_tokens = pl.pallas_call(
        functools.partial(backward_kernel, lay),
        in_specs=[IN_SMEM if part.ndim == 1 else IN_VMEM for part in near] + [IN_HBM] * len(far),
        out_specs=[IN_VMEM] * 7 + [IN_HBM] * 2,
        out_shape=out_shape,
        scratch_shapes=[
            vmem(away, hidden),
            vmem(away + CLS_ROWS, 3 * width),
            vmem(away + CLS_ROWS, 3 * width),
            vmem(away, width, kind=f32),
            *[vmem(away, width)] * 5,
            vmem(CLS_ROWS, 3 * width, kind=f32),
            vmem(4, width, width),
            vmem(2, away + CLS_ROWS, width),
            *moving[:2],
            vmem(len(SMALL), SMALL_ROWS, width, kind=f32),
            *[vmem(8, width, kind=f32)] * 6,
            single,
            single,
            single,
            queue(4),
            queue(4),
            queue(2),
            *moving[2:],
            queue(len(SMALL)),
            queue(len(SMALL)),
            vmem(RAW_SLOTS, 2, 2, 2, BLOCKS, 2, 2, *PIECE),
            vmem(RAW_SLOTS, 2, 2, BLOCKS, 2, 2, *PIECE),
            vmem(ACC_SLOTS, 2, 2, BLOCKS, 2, 2, *PIECE),
            vmem(ACC_SLOTS, BLOCKS, 2, 2, *PIECE),
            *inbox,
            queue(RAW_SLOTS, 4),
            queue(RAW_SLOTS, 4),
            pltpu.SemaphoreType.REGULAR,
            queue(BOX_SLOTS, BLOCKS, STAGES - 1),
            queue(BOX_SLOTS, BLOCKS, STAGES - 1),
        ],
        compiler_params=pltpu.CompilerParams(
            collective_id=1, has_side_effects=True, vmem_limit_bytes=VMEM_MOST
        ),
        name="backward",
    )(*near, *far)
    grad_cls = small[16 : 16 + clip_count]
    small = lax.dynamic_slice_in_dim(small[:16], lax.axis_index("patch") * share, share, 1)
    small = small.reshape(LAYERS, 8, share)
    stacked = [large[i].astype(f32) for i in (5, 4, 3, 2, 1, 0)]
    return (given_order(output), given_order(grad_tokens), grad_cls, *stacked, small[:, 0:3], small[:, 3:6])


def general_local(
    tokens,
    cls_tokens,
    clip_lengths,
    time_proj,
    time_output,
    space_proj,
    space_output,
    up_weight,
    down_weight,
    norm_gains,
    norm_biases,
    cotangent,
):
    frames, patch_rows, width = tokens.shape
    devices = lax.axis_size("patch")
    lay = Layout(devices, frames, patch_rows)
    away_rows = lay.away_rows
    patches = lay.all_patches
    clip_count = cls_tokens.shape[0]

    frame_ids = jnp.arange(frames, dtype=jnp.int32)
    slots = frame_slots(clip_lengths[0], frame_ids)
    bias = time_bias(slots[:, None] == slots[None, :], patch_rows, frames)
    my_frames = lax.axis_index("patch") * lay.away_frames + jnp.arange(lay.away_frames, dtype=jnp.int32)
    my_slots = jnp.where(my_frames < frames, frame_slots(clip_lengths[0], my_frames), -1)
    cls_pick = (my_slots[None, :] == jnp.arange(CLS_ROWS, dtype=jnp.int32)[:, None]).astype(f32)

    def home_order(values):
        return jnp.transpose(values, (1, 0, 2)).reshape(lay.home_rows, width)

    def given_order(values):
        return jnp.transpose(values.reshape(patch_rows, frames, width), (1, 0, 2))

    cls_aug = jnp.pad(cls_tokens.astype(f32), ((0, CLS_ROWS - clip_count), (0, 0)))
    residual = home_order(tokens).astype(f32)
    cotangent_away = lay.to_away(home_order(cotangent))
    stored = []
    for layer in range(LAYERS):
        gains, biases = norm_gains[layer], norm_biases[layer]
        normed, scaled_t, inverse_t = layer_norm(residual, gains[0], biases[0])
        normed_t = normed.astype(bf16)
        qkv_t = project(normed_t, time_proj[layer]).astype(bf16)
        mixed_t = time_forward(bias, qkv_t)
        residual = residual + project(mixed_t, time_output[layer])
        away = lay.to_away(residual.astype(bf16))
        away = away + jnp.pad(cls_aug, ((away_rows, 0), (0, 0)))
        normed, scaled_s, inverse_s = layer_norm(away, gains[1], biases[1])
        normed_s = normed.astype(bf16)
        qkv_s = project(normed_s, space_proj[layer]).astype(bf16)
        mixed_s = space_forward(my_slots, qkv_s, lay.away_frames, patches)
        away = away[:away_rows] + project(mixed_s, space_output[layer])
        normed, scaled_f, inverse_f = layer_norm(away, gains[2], biases[2])
        normed_f = normed.astype(bf16)
        hidden = project(normed_f, up_weight[layer])
        active = gelu_value(hidden).astype(bf16)
        away = away + project(active, down_weight[layer])
        residual = lay.to_home(away.astype(bf16))
        stored.append(
            dict(
                normed_t=normed_t, scaled_t=scaled_t, inverse_t=inverse_t, qkv_t=qkv_t, mixed_t=mixed_t,
                normed_s=normed_s, scaled_s=scaled_s, inverse_s=inverse_s, qkv_s=qkv_s, mixed_s=mixed_s,
                normed_f=normed_f, scaled_f=scaled_f, inverse_f=inverse_f, hidden=hidden, active=active,
            )
        )
    output = given_order(residual.astype(bf16))

    grad_cls = jnp.zeros_like(cls_aug)
    grad_away = cotangent_away[:away_rows]
    results = [None] * LAYERS
    for layer in reversed(range(LAYERS)):
        saved = stored[layer]
        gains = norm_gains[layer]
        branch = grad_away.astype(bf16)
        grad_down = weight_grad(saved["active"], branch)
        grad_active = project_back(branch, down_weight[layer])
        grad_hidden = (grad_active * gelu_slope(saved["hidden"])).astype(bf16)
        grad_up = weight_grad(saved["normed_f"], grad_hidden)
        grad_normed = project_back(grad_hidden, up_weight[layer])
        grad_input, gain_two, bias_two = norm_back(
            grad_normed, saved["scaled_f"], saved["inverse_f"], gains[2]
        )
        grad_away = grad_away + grad_input
        branch = grad_away.astype(bf16)
        grad_space_out = weight_grad(saved["mixed_s"], branch)
        grad_mixed = project_back(branch, space_output[layer]).astype(bf16)
        dq, dk, dv, dck, dcv = space_backward(my_slots, saved["qkv_s"], grad_mixed, lay.away_frames, patches)
        dcls = jnp.concatenate([dck[:, 0], dcv[:, 0]], -1)
        dcls = jnp.dot(cls_pick, dcls, precision=lax.Precision.HIGHEST)
        dcls = jnp.pad(dcls.astype(bf16), ((0, 0), (width, 0)))
        grad_qkv = jnp.concatenate([jnp.concatenate([dq, dk, dv], -1), dcls], 0)
        grad_space_proj = weight_grad(saved["normed_s"], grad_qkv)
        grad_normed = project_back(grad_qkv, space_proj[layer])
        grad_input, gain_one, bias_one = norm_back(
            grad_normed, saved["scaled_s"], saved["inverse_s"], gains[1]
        )
        grad_away = grad_away + grad_input[:away_rows]
        grad_cls = grad_cls + grad_input[away_rows:]
        grad_home = lay.to_home(grad_away.astype(bf16))
        branch = grad_home.astype(bf16)
        grad_time_out = weight_grad(saved["mixed_t"], branch)
        grad_mixed = project_back(branch, time_output[layer]).astype(bf16)
        grad_qkv = time_backward(bias, saved["qkv_t"], grad_mixed)
        grad_time_proj = weight_grad(saved["normed_t"], grad_qkv)
        grad_normed = project_back(grad_qkv, time_proj[layer])
        grad_input, gain_zero, bias_zero = norm_back(
            grad_normed, saved["scaled_t"], saved["inverse_t"], gains[0]
        )
        grad_home = grad_home + grad_input
        if layer > 0:
            grad_away = lay.to_away(grad_home.astype(bf16))[:away_rows]
        large = (grad_time_proj, grad_time_out, grad_space_proj, grad_space_out, grad_up, grad_down)
        large = [lax.psum_scatter(part, "patch", scatter_dimension=0, tiled=True) for part in large]
        large = lax.psum(large, "clip")
        small = (jnp.stack([gain_zero, gain_one, gain_two]), jnp.stack([bias_zero, bias_one, bias_two]))
        results[layer] = [part.astype(f32) for part in large] + list(small)
    grad_tokens = given_order(grad_home.astype(bf16))
    stacked = [jnp.stack([results[layer][i] for layer in range(LAYERS)]) for i in range(8)]
    small = jnp.stack(stacked[6:])
    small = lax.psum(small, ("patch", "clip"))
    share = width // devices
    small = lax.dynamic_slice_in_dim(small, lax.axis_index("patch") * share, share, 3)
    grad_cls = lax.psum(grad_cls[:clip_count], "patch")
    return (output, grad_tokens, grad_cls, *stacked[:6], small[0], small[1])


def solution(mesh):
    in_specs = (
        P("clip", "patch", None),
        P("clip", None),
        P("clip", None),
        P(),
        P(),
        P(),
        P(),
        P(),
        P(),
        P(),
        P(),
        P("clip", "patch", None),
    )
    out_specs = (
        P("clip", "patch", None),
        P("clip", "patch", None),
        P("clip", None),
        P(None, "patch", None),
        P(None, "patch", None),
        P(None, "patch", None),
        P(None, "patch", None),
        P(None, "patch", None),
        P(None, "patch", None),
        P(None, None, "patch"),
        P(None, None, "patch"),
    )
    paired = (mesh.shape["clip"], mesh.shape["patch"]) == (4, 8)
    local = fast_local if paired else general_local
    return jax.shard_map(local, mesh=mesh, in_specs=in_specs, out_specs=out_specs, check_vma=False)
```

```python
import functools

import jax
import jax.numpy as jnp
import numpy as np
from jax import lax
from jax.experimental import pallas as pl
from jax.experimental.pallas import tpu as pltpu
from jax.sharding import PartitionSpec as P

HEADS = 12
HD = 64
LAYERS = 2
REAL_PATCH = 196
QUAD = 4
WIDE = QUAD * HD
QUADS = HEADS // QUAD
CLS_ROWS = 16

EPSILON = 1e-05
NEG_LARGE = -1e30
ROOT_HALF = 0.7071067811865476
INV_ROOT_TWO_PI = 0.3989422804014327
SCALE = HD**-0.5
VMEM_LIMIT = 48 * 1024 * 1024
VMEM_MOST = 62 * 1024 * 1024

f32 = jnp.float32
bf16 = jnp.bfloat16
MESH = pl.DeviceIdType.MESH


def layer_norm(values, norm_gain, norm_bias):
    centered = values - jnp.mean(values, -1, keepdims=True)
    inverse = lax.rsqrt(jnp.mean(centered * centered, -1, keepdims=True) + EPSILON)
    scaled = centered * inverse
    return (scaled * norm_gain + norm_bias, scaled, inverse)


def norm_back(grad_out, scaled, inverse, norm_gain):
    weighted = grad_out * norm_gain
    grad_input = inverse * (
        weighted
        - jnp.mean(weighted, -1, keepdims=True)
        - scaled * jnp.mean(weighted * scaled, -1, keepdims=True)
    )
    return (grad_input, jnp.sum(grad_out * scaled, 0), jnp.sum(grad_out, 0))


def project(left, matrix):
    return jnp.dot(left, matrix, preferred_element_type=f32)


def project_back(grad_out, matrix):
    return lax.dot_general(grad_out, matrix, (((1,), (1,)), ((), ())), preferred_element_type=f32)


def weight_grad(left, grad_out):
    return lax.dot_general(
        left, grad_out, (((0,), (0,)), ((), ())), preferred_element_type=f32
    ).astype(bf16)


def gelu_value(hidden):
    return 0.5 * hidden * (1.0 + lax.erf(hidden * ROOT_HALF))


def gelu_slope(hidden):
    return 0.5 * (1.0 + lax.erf(hidden * ROOT_HALF)) + hidden * INV_ROOT_TWO_PI * jnp.exp(
        -0.5 * hidden * hidden
    )


def dot_nt(left, right):
    return lax.dot_general(left, right, (((1,), (1,)), ((), ())), preferred_element_type=f32)


def dot_nn(left, right):
    return lax.dot_general(left, right, (((1,), (0,)), ((), ())), preferred_element_type=f32)


def dot_tn(left, right):
    return lax.dot_general(left, right, (((0,), (0,)), ((), ())), preferred_element_type=f32)


def spread_heads(rows):
    head = lax.broadcasted_iota(jnp.int32, rows.shape, 1) // HD
    return jnp.concatenate([jnp.where(head == h, rows, jnp.zeros_like(rows)) for h in range(QUAD)], 0)


def merge_heads(stacked):
    count = stacked.shape[0] // QUAD
    head = lax.broadcasted_iota(jnp.int32, (count, WIDE), 1) // HD
    merged = stacked[:count]
    for h in range(1, QUAD):
        merged = jnp.where(head == h, stacked[h * count : (h + 1) * count], merged)
    return merged


def probabilities(scores):
    exponents = [jnp.exp(part - jnp.max(part, 0, keepdims=True)) for part in scores]
    return [part * (1.0 / jnp.sum(part, 0, keepdims=True)) for part in exponents]


def forward_tiles(tiles, bias):
    spreads = [spread_heads(tile[0] * SCALE) for tile in tiles]
    scores = [dot_nt(tile[1], spread) + bias for tile, spread in zip(tiles, spreads)]
    probs = [part.astype(bf16) for part in probabilities(scores)]
    outs = [dot_tn(part, tile[2]) for part, tile in zip(probs, tiles)]
    return [merge_heads(part).astype(bf16) for part in outs]


def backward_tiles(tiles, bias):
    spreads = [spread_heads(tile[0] * SCALE) for tile in tiles]
    grad_spreads = [spread_heads(tile[3]) for tile in tiles]
    scores = [dot_nt(tile[1], spread) + bias for tile, spread in zip(tiles, spreads)]
    grad_probs = [dot_nt(tile[2], spread) for tile, spread in zip(tiles, grad_spreads)]
    probs = probabilities(scores)
    grad_scores = [
        (part * (grad - jnp.sum(part * grad, 0, keepdims=True))).astype(bf16)
        for part, grad in zip(probs, grad_probs)
    ]
    grad_queries = [dot_tn(grad, tile[1]) for grad, tile in zip(grad_scores, tiles)]
    grad_keys = [dot_nn(grad, spread) for grad, spread in zip(grad_scores, spreads)]
    grad_values = [dot_nn(part.astype(bf16), spread) for part, spread in zip(probs, grad_spreads)]
    return [(merge_heads(q) * SCALE, k, v) for q, k, v in zip(grad_queries, grad_keys, grad_values)]


def columns(part, quad, width):
    start = part * width + quad * WIDE
    return slice(start, start + WIDE)


def time_forward_kernel(bias_ref, qkv_ref, out_ref):
    width = out_ref.shape[1]
    bias = bias_ref[...]
    for quad in range(QUADS):
        parts = [qkv_ref[:, columns(part, quad, width)] for part in range(3)]
        out_ref[:, columns(0, quad, width)] = forward_tiles([parts], bias)[0]


def time_backward_kernel(bias_ref, qkv_ref, grad_ref, out_ref):
    width = grad_ref.shape[1]
    bias = bias_ref[...]
    for quad in range(QUADS):
        parts = [qkv_ref[:, columns(part, quad, width)] for part in range(3)]
        grads = backward_tiles([parts + [grad_ref[:, columns(0, quad, width)]]], bias)[0]
        for part in range(3):
            out_ref[:, columns(part, quad, width)] = grads[part].astype(bf16)


def group_rows(patch_count, frames):
    return (2 if patch_count % 2 == 0 else 1) * frames


def time_bias(same_clip, patch_count, frames):
    rows = group_rows(patch_count, frames)
    ids = jnp.arange(rows, dtype=jnp.int32)
    same_patch = (ids[:, None] // frames) == (ids[None, :] // frames)
    tiled = jnp.tile(same_clip, (rows // frames, rows // frames))
    return jnp.tile(jnp.where(same_patch & tiled, 0.0, NEG_LARGE).astype(f32), (1, QUAD))


def params(*semantics):
    return pltpu.CompilerParams(dimension_semantics=semantics, vmem_limit_bytes=VMEM_LIMIT)


def time_forward(bias, qkv):
    rows = bias.shape[0]
    width = qkv.shape[1] // 3
    return pl.pallas_call(
        time_forward_kernel,
        grid=(qkv.shape[0] // rows,),
        in_specs=[
            pl.BlockSpec(bias.shape, lambda i: (0, 0)),
            pl.BlockSpec((rows, 3 * width), lambda i: (i, 0)),
        ],
        out_specs=pl.BlockSpec((rows, width), lambda i: (i, 0)),
        out_shape=jax.ShapeDtypeStruct((qkv.shape[0], width), bf16),
        compiler_params=params("parallel"),
        name="time_forward",
    )(bias, qkv)


def time_backward(bias, qkv, grad_out):
    rows = bias.shape[0]
    width = qkv.shape[1] // 3
    return pl.pallas_call(
        time_backward_kernel,
        grid=(qkv.shape[0] // rows,),
        in_specs=[
            pl.BlockSpec(bias.shape, lambda i: (0, 0)),
            pl.BlockSpec((rows, 3 * width), lambda i: (i, 0)),
            pl.BlockSpec((rows, width), lambda i: (i, 0)),
        ],
        out_specs=pl.BlockSpec((rows, 3 * width), lambda i: (i, 0)),
        out_shape=jax.ShapeDtypeStruct(qkv.shape, bf16),
        compiler_params=params("parallel"),
        name="time_backward",
    )(bias, qkv, grad_out)


def with_class(slot, rows, cls_rows):
    ids = lax.broadcasted_iota(jnp.int32, cls_rows.shape, 0)
    picked = jnp.sum(jnp.where(ids == slot, cls_rows.astype(f32), 0.0), 0, keepdims=True)
    row_ids = lax.broadcasted_iota(jnp.int32, rows.shape, 0)
    return jnp.where(row_ids == REAL_PATCH, picked.astype(bf16), rows)


def key_bias(count):
    key_ids = lax.broadcasted_iota(jnp.int32, (count, 1), 0)
    return jnp.where(key_ids <= REAL_PATCH, 0.0, NEG_LARGE).astype(f32)


def space_forward_kernel(slot_ref, q_ref, k_ref, v_ref, ck_ref, cv_ref, out_ref):
    slot = slot_ref[pl.program_id(0)]
    keys = with_class(slot, k_ref[...], ck_ref[...])
    values = with_class(slot, v_ref[...], cv_ref[...])
    out_ref[...] = forward_tiles([(q_ref[...], keys, values)], key_bias(keys.shape[0]))[0]


def space_backward_kernel(
    slot_ref, q_ref, k_ref, v_ref, ck_ref, cv_ref, g_ref, dq_ref, dk_ref, dv_ref, dck_ref, dcv_ref
):
    slot = slot_ref[pl.program_id(0)]
    keys = with_class(slot, k_ref[...], ck_ref[...])
    values = with_class(slot, v_ref[...], cv_ref[...])
    tile = (q_ref[...], keys, values, g_ref[...])
    grad_q, grad_k, grad_v = backward_tiles([tile], key_bias(keys.shape[0]))[0]
    row_ids = lax.broadcasted_iota(jnp.int32, grad_k.shape, 0)
    dq_ref[...] = grad_q.astype(bf16)
    dk_ref[...] = jnp.where(row_ids < REAL_PATCH, grad_k, 0.0).astype(bf16)
    dv_ref[...] = jnp.where(row_ids < REAL_PATCH, grad_v, 0.0).astype(bf16)
    dck_ref[0] = jnp.sum(jnp.where(row_ids == REAL_PATCH, grad_k, 0.0), 0, keepdims=True)
    dcv_ref[0] = jnp.sum(jnp.where(row_ids == REAL_PATCH, grad_v, 0.0), 0, keepdims=True)


def space_specs(frames, patches):
    cls_block = frames * patches // CLS_ROWS

    def rows(part):
        return pl.BlockSpec((patches, WIDE), lambda f, c, s: (f, part * QUADS + c))

    def cls(part):
        return pl.BlockSpec((CLS_ROWS, WIDE), lambda f, c, s: (cls_block, part * QUADS + c))

    return [rows(0), rows(1), rows(2), cls(1), cls(2)], rows(0)


def space_forward(slots, qkv, frames, patches):
    width = qkv.shape[1] // 3
    in_specs, out_spec = space_specs(frames, patches)
    return pl.pallas_call(
        space_forward_kernel,
        grid_spec=pltpu.PrefetchScalarGridSpec(
            num_scalar_prefetch=1,
            grid=(frames, QUADS),
            in_specs=in_specs,
            out_specs=out_spec,
        ),
        out_shape=jax.ShapeDtypeStruct((frames * patches, width), bf16),
        compiler_params=params("parallel", "parallel"),
        name="space_forward",
    )(slots, qkv, qkv, qkv, qkv, qkv)


def space_backward(slots, qkv, grad_out, frames, patches):
    width = qkv.shape[1] // 3
    in_specs, out_spec = space_specs(frames, patches)
    rows = jax.ShapeDtypeStruct((frames * patches, width), bf16)
    cls_spec = pl.BlockSpec((1, 1, WIDE), lambda f, c, s: (f, 0, c))
    cls = jax.ShapeDtypeStruct((frames, 1, width), f32)
    return pl.pallas_call(
        space_backward_kernel,
        grid_spec=pltpu.PrefetchScalarGridSpec(
            num_scalar_prefetch=1,
            grid=(frames, QUADS),
            in_specs=in_specs + [out_spec],
            out_specs=[out_spec] * 3 + [cls_spec] * 2,
        ),
        out_shape=[rows] * 3 + [cls] * 2,
        compiler_params=params("parallel", "parallel"),
        name="space_backward",
    )(slots, qkv, qkv, qkv, qkv, qkv, grad_out)


def frame_slots(lengths_row, frame_ids):
    clip_ends = jnp.cumsum(lengths_row)
    return jnp.sum((frame_ids[:, None] >= clip_ends[None, :]).astype(jnp.int32), axis=1)


class Layout:
    def __init__(self, devices, frames, patches):
        self.devices = devices
        self.frames = frames
        self.patches = patches
        self.all_patches = patches * devices
        self.away_frames = -(-frames // devices)
        used = self.away_frames * patches
        self.block = -(-used // 16) * 16
        self.home_rows = frames * patches
        self.away_rows = self.away_frames * self.all_patches
        self.sent_rows = devices * self.block

    def home_of_sent(self):
        row = jnp.arange(self.sent_rows, dtype=jnp.int32)
        peer, inner = row // self.block, row % self.block
        frame = peer * self.away_frames + inner // self.patches
        valid = (inner < self.away_frames * self.patches) & (frame < self.frames)
        return jnp.where(valid, (inner % self.patches) * self.frames + frame, -1)

    def sent_of_away(self):
        row = jnp.arange(self.away_rows + CLS_ROWS, dtype=jnp.int32)
        frame, patch = row // self.all_patches, row % self.all_patches
        sent = (patch // self.patches) * self.block + frame * self.patches + patch % self.patches
        return jnp.where(row < self.away_rows, sent, -1)

    def parts(self):
        step = self.block // 5 // 16 * 16
        return ((0, step), (step, 3 * step), (3 * step, self.block))

    def frame_parts(self):
        ends = [-(-self.patches * (i + 1) // 16) * 16 for i in range(self.away_frames)]
        return tuple(zip([0] + ends[:-1], ends))

    def frame_rows(self, frame):
        low, high = self.patches * frame, self.patches * (frame + 1)
        return low // 16 * 16, -(-high // 16) * 16

    def leave(self, order, parts):
        order = np.where(np.arange(self.block) < self.away_frames * self.patches, order, -1)
        rows = np.concatenate([order[:, low:high].reshape(-1) for low, high in parts])
        return np.asarray(rows, np.int32)[:, None]

    def orders(self):
        block, patches, near = self.block, self.patches, self.away_frames
        peer, inner = np.meshgrid(range(self.devices), range(block), indexing="ij")
        by_patch = inner // near * self.frames + peer * near + inner % near
        by_frame = inner % patches * self.frames + peer * near + inner // patches
        from_away = inner // patches * self.all_patches + peer * patches + inner % patches
        row = np.arange(self.away_rows)
        frame, patch = row // self.all_patches, row % self.all_patches
        reach_patch = patch // patches * block + patch % patches * near + frame
        low = np.array([self.frame_rows(i)[0] for i in range(near)])[frame]
        high = np.array([self.frame_rows(i)[1] for i in range(near)])[frame]
        reach_frame = patch // patches * (high - low) + frame * patches + patch % patches - low
        row = np.arange(self.home_rows)
        patch, frame = row // self.frames, row % self.frames
        reach_home = frame // near * block + frame % near * patches + patch

        def column(rows):
            return np.asarray(rows, np.int32)[:, None]

        return dict(
            leave_patch=self.leave(by_patch, self.parts()),
            leave_frame=self.leave(by_frame, self.frame_parts()),
            leave_away=self.leave(from_away, self.parts()),
            leave_away_frame=self.leave(from_away, self.frame_parts()),
            reach_patch=column(reach_patch),
            reach_frame=column(reach_frame),
            reach_home=column(reach_home),
        )

    def to_away(self, values):
        pick = self.home_of_sent()[:, None] == jnp.arange(self.home_rows, dtype=jnp.int32)[None, :]
        sent = jnp.dot(pick.astype(bf16), values, preferred_element_type=bf16)
        got = lax.all_to_all(sent, "patch", split_axis=0, concat_axis=0, tiled=True)
        pick = self.sent_of_away()[:, None] == jnp.arange(self.sent_rows, dtype=jnp.int32)[None, :]
        return jnp.dot(pick.astype(bf16), got, preferred_element_type=f32)

    def to_home(self, values):
        pick = jnp.arange(self.sent_rows, dtype=jnp.int32)[:, None] == self.sent_of_away()[None, : self.away_rows]
        sent = jnp.dot(pick.astype(bf16), values, preferred_element_type=bf16)
        got = lax.all_to_all(sent, "patch", split_axis=0, concat_axis=0, tiled=True)
        pick = jnp.arange(self.home_rows, dtype=jnp.int32)[:, None] == self.home_of_sent()[None, :]
        return jnp.dot(pick.astype(bf16), got, preferred_element_type=f32)


def norm_rows(values):
    centered = values - jnp.mean(values, -1, keepdims=True)
    inverse = lax.rsqrt(jnp.mean(centered * centered, -1, keepdims=True) + EPSILON)
    return centered, inverse


def norm_forward(values, gain, shift):
    centered, inverse = norm_rows(values)
    return (centered * inverse * gain + shift).astype(bf16)


def norm_backward(values, grad, gain, sums):
    centered, inverse = norm_rows(values)
    weighted = grad * gain
    along = jnp.mean(weighted * centered, -1, keepdims=True) * (inverse * inverse * inverse)

    def fold(part):
        return jnp.sum(part.reshape(part.shape[0] // 8, 8, part.shape[1]), 0)

    sums[0][...] += fold(grad * (centered * inverse))
    sums[1][...] += fold(grad)
    return inverse * (weighted - jnp.mean(weighted, -1, keepdims=True)) - centered * along


class Loads:
    def __init__(self, sources, buffers, sems):
        self.copies = [
            pltpu.make_async_copy(source, buffer, sems.at[i])
            for i, (source, buffer) in enumerate(zip(sources, buffers))
        ]
        for copy in self.copies:
            copy.start()
        self.buffers = buffers
        self.next = 0

    def get(self):
        self.copies[self.next].wait()
        self.next += 1
        return self.buffers[self.next - 1]


class Saves:
    def __init__(self, buffers, targets, sems):
        self.pairs, self.sems = list(zip(buffers, targets)), sems

    def copies(self, part, start, rows):
        here = pl.ds(start, rows)
        return [
            pltpu.make_async_copy(buffer.at[here], target.at[here], self.sems.at[i, part])
            for i, (buffer, target) in enumerate(self.pairs)
        ]

    def put(self, part, start, rows):
        for copy in self.copies(part, start, rows):
            copy.start()

    def finish(self, part, start, rows):
        for copy in self.copies(part, start, rows):
            copy.wait()


class Place:
    AXES = {"core": ("patch", 1), "zl": ("patch", 2), "zh": ("patch", 4), "x": ("clip", 1), "y": ("clip", 2)}

    def __init__(self):
        self.clip, self.patch = lax.axis_index("clip"), lax.axis_index("patch")
        self.me = {
            "core": lax.rem(self.patch, 2),
            "zl": lax.rem(self.patch // 2, 2),
            "zh": self.patch // 4,
            "x": lax.rem(self.clip, 2),
            "y": self.clip // 2,
        }

    def peer(self, dim):
        axis, stride = self.AXES[dim]
        own = self.clip if axis == "clip" else self.patch
        other = own + stride - 2 * stride * self.me[dim]
        return (other, self.patch) if axis == "clip" else (self.clip, other)


class Shuffle:
    def __init__(self, lay, at, sent, got, send_sem, recv_sem):
        self.lay, self.devices, self.parts, self.at = lay, lay.devices, lay.parts(), at
        self.sent, self.got, self.send_sem, self.recv_sem = sent, got, send_sem, recv_sem
        self.moves = 0

    def greet(self):
        for offset in range(1, self.devices):
            other = (self.at.clip, lax.rem(self.at.patch + offset, self.devices))
            pl.semaphore_signal(pltpu.get_barrier_semaphore(), inc=1, device_id=other, device_id_type=MESH)

    def meet(self, others=0):
        pl.semaphore_wait(pltpu.get_barrier_semaphore(), self.devices - 1 + others)

    def copy(self, offset, part):
        two = self.moves % 2
        other = lax.rem(self.at.patch + offset, self.devices)
        low, high = self.parts[part]
        rows = pl.ds(low, high - low)
        return pltpu.make_async_remote_copy(
            src_ref=self.sent.at[other, rows],
            dst_ref=self.got.at[two, self.at.patch, rows],
            send_sem=self.send_sem.at[part, offset],
            recv_sem=self.recv_sem.at[two, part, offset],
            device_id=(self.at.clip, other),
            device_id_type=MESH,
        )

    def send(self, part, order_ref, source_ref, first, last):
        width = self.sent.shape[-1]
        low, high = self.parts[part]
        rows = (high - low) * self.devices
        start = low * self.devices
        ids = lax.broadcasted_iota(jnp.int32, (rows, last - first), 1) + first
        pick = (order_ref[start : start + rows, :] == ids).astype(f32).astype(bf16)
        picked = dot_nn(pick, source_ref[first:last, :]).astype(bf16)
        self.sent[:, low:high, :] = picked.reshape(self.devices, high - low, width)
        for offset in range(1, self.devices):
            self.copy(offset, part).start()
        self.got[self.moves % 2, self.at.patch, low:high, :] = self.sent[self.at.patch, low:high, :]

    def send_all(self, order_ref, source_ref):
        for part in range(len(self.parts)):
            self.send(part, order_ref, source_ref, 0, source_ref.shape[0])

    def arrive(self, part):
        for offset in range(1, self.devices):
            self.copy(offset, part).wait()

    def receive(self, order_ref, target_ref):
        for part in range(len(self.parts)):
            self.arrive(part)
        devices, block, width = self.got.shape[1:]
        rows = target_ref.shape[0] // 3
        ids = lax.broadcasted_iota(jnp.int32, (rows, devices * block), 1)
        for start in range(0, target_ref.shape[0], rows):
            pick = (order_ref[start : start + rows, :] == ids).astype(f32).astype(bf16)
            got = self.got[self.moves % 2].reshape(devices * block, width)
            target_ref[start : start + rows, :] = dot_nn(pick, got).astype(bf16)
        self.moves += 1

    def receive_frame(self, frame, order_ref, target_ref):
        self.arrive(frame)
        low, high = self.lay.frame_rows(frame)
        patches = self.lay.all_patches
        here = slice(frame * patches, (frame + 1) * patches)
        width = self.got.shape[-1]
        got = self.got[self.moves % 2, :, low:high, :].reshape(self.devices * (high - low), width)
        ids = lax.broadcasted_iota(jnp.int32, (patches, got.shape[0]), 1)
        pick = (order_ref[here, :] == ids).astype(f32).astype(bf16)
        target_ref[here, :] = dot_nn(pick, got).astype(bf16)


def slot_of(lengths_ref, frames):
    end, slot = 0, 0
    for clip in range(lengths_ref.shape[0]):
        end = end + lengths_ref[clip]
        slot = slot + (frames >= end).astype(jnp.int32)
    return slot


def fill_bias(lengths_ref, frames, bias_ref):
    rows = bias_ref.shape[0]

    def split(ids, size, count):
        which = jnp.zeros_like(ids)
        for i in range(1, count):
            which = which + (ids >= i * size).astype(jnp.int32)
        return which, ids - which * size

    key_patch, key_frame = split(lax.broadcasted_iota(jnp.int32, bias_ref.shape, 0), frames, rows // frames)
    _, query = split(lax.broadcasted_iota(jnp.int32, bias_ref.shape, 1), rows, QUAD)
    query_patch, query_frame = split(query, frames, rows // frames)
    same = (key_patch == query_patch) & (slot_of(lengths_ref, key_frame) == slot_of(lengths_ref, query_frame))
    bias_ref[...] = jnp.where(same, 0.0, NEG_LARGE).astype(f32)


def cls_rows_of(cls_ref):
    values = cls_ref[...].astype(f32)
    return jnp.concatenate([values, jnp.zeros((CLS_ROWS - values.shape[0], values.shape[1]), f32)], 0)


def norm_row(norms_ref, layer, which, shift=False):
    row = (3 * LAYERS if shift else 0) + layer * 3 + which
    return norms_ref[row : row + 1, :]


def time_tiles(bias_ref, qkv_ref, width, group, grad_ref=None):
    rows = bias_ref.shape[0]
    here = pl.ds(pl.multiple_of(group * rows, 16), rows)
    tiles = []
    for quad in range(QUADS):
        tile = [qkv_ref[here, columns(part, quad, width)] for part in range(3)]
        if grad_ref is not None:
            tile.append(grad_ref[here, columns(0, quad, width)])
        tiles.append(tile)
    return here, tiles


def space_tiles(patches, total, slot, qkv_ref, width, frame, grad_ref=None):
    here = pl.ds(pl.multiple_of(frame * patches, 16), patches)
    tiles = []
    for quad in range(QUADS):
        tile = [qkv_ref[here, columns(part, quad, width)] for part in range(3)]
        for part in (1, 2):
            tile[part] = with_class(slot, tile[part], qkv_ref[total : total + CLS_ROWS, columns(part, quad, width)])
        if grad_ref is not None:
            tile.append(grad_ref[here, columns(0, quad, width)])
        tiles.append(tile)
    return here, tiles


def group_parts(lay, rows):
    ends = []
    for _, high in lay.parts():
        patches = min(-(-high // lay.away_frames), lay.patches)
        ends.append(-(-patches * lay.frames // rows) * rows)
    return tuple(zip([0] + ends[:-1], ends))


SAVED = ("normed_t", "qkv_t", "mixed_t", "x_away", "normed_s", "qkv_s", "mixed_s", "middle", "normed_f", "active", "slope")
WEIGHTS = ("time_proj", "time_output", "space_proj", "space_output", "up", "down")


def forward_kernel(lay, *refs):
    lengths_ref, norms_ref, cls_ref, leave_frame, reach_frame, leave_away, reach_home = refs[:7]
    sources = dict(zip(WEIGHTS, refs[7:13]))
    tokens_hbm, grad_hbm = refs[13:15]
    home_hbm, grad_away_hbm, result_hbm = refs[15:18]
    saved = [dict(zip(SAVED, refs[18 + len(SAVED) * layer :][: len(SAVED)])) for layer in range(LAYERS)]
    refs = refs[18 + len(SAVED) * LAYERS :]
    weights = dict(zip(WEIGHTS, refs[:6]))
    staged = dict(zip(SAVED, refs[6 : 6 + len(SAVED)]))
    bias_ref, x_home, after, grad, grad_away = refs[6 + len(SAVED) :][:5]
    sem_weight, sem_ends, sem_time, sem_space, sem_cls, *moving = refs[11 + len(SAVED) :]
    normed_t, qkv_t, mixed_t, x_away, normed, qkv, mixed, middle, normed_f, active, slope = (staged[name] for name in SAVED)
    total, width = x_away.shape
    home = x_home.shape[0]
    patches, frames = lay.all_patches, lay.away_frames
    group = bias_ref.shape[0]
    columns_of = [slice(start, start + width) for start in range(0, 3 * width, width)]

    load_x = pltpu.make_async_copy(tokens_hbm, x_home, sem_ends.at[0])
    load_grad = pltpu.make_async_copy(grad_hbm, grad, sem_ends.at[1])
    save_home = pltpu.make_async_copy(x_home, home_hbm, sem_ends.at[2])
    save_result = pltpu.make_async_copy(after, result_hbm, sem_ends.at[3])
    save_grad = pltpu.make_async_copy(grad_away, grad_away_hbm, sem_ends.at[4])
    load_x.start()
    load_grad.start()

    def fetch(layer, i):
        return pltpu.make_async_copy(sources[WEIGHTS[i]].at[layer], weights[WEIGHTS[i]], sem_weight.at[i])

    fetch(0, 0).start()
    at = Place()
    coming, leaving = [Shuffle(lay, at, *moving[:4]) for _ in range(2)]
    extra = Shuffle(lay, at, *moving[4:])
    coming.parts = extra.parts = lay.frame_parts()
    coming.greet()
    fill_bias(lengths_ref, lay.frames, bias_ref)
    key_mask = key_bias(patches)
    cls = cls_rows_of(cls_ref)
    load_grad.wait()
    coming.meet()
    extra.send(0, leave_frame, grad, 0, home)
    load_x.wait()

    for layer in range(LAYERS):
        more = layer < LAYERS - 1
        coming.moves, leaving.moves = 2 * layer, 2 * layer + 1
        if not more:
            extra.send(1, leave_frame, grad, 0, home)
        here = saved[layer]
        time_saves = Saves([staged[name] for name in SAVED[:3]], [here[name] for name in SAVED[:3]], sem_time)
        space_saves = Saves([staged[name] for name in SAVED[3:]], [here[name] for name in SAVED[3:]], sem_space)
        cls_saves = Saves([normed, qkv], [here["normed_s"], here["qkv_s"]], sem_cls)

        gain, shift = norm_row(norms_ref, layer, 0), norm_row(norms_ref, layer, 0, True)
        for start in range(0, home, home // 3):
            rows = slice(start, start + home // 3)
            normed_t[rows, :] = norm_forward(x_home[rows, :].astype(f32), gain, shift)
        fetch(layer, 0).wait()
        if layer == 0:
            for i in range(1, len(WEIGHTS)):
                fetch(0, i).start()
        for these in columns_of:
            qkv_t[:, these] = dot_nn(normed_t[...], weights["time_proj"][:, these]).astype(bf16)
        if more:
            fetch(layer + 1, 0).start()

        @pl.loop(0, home // group)
        def _(index):
            rows, tiles = time_tiles(bias_ref, qkv_t, width, index)
            for quad, done in enumerate(forward_tiles(tiles, bias_ref[...])):
                mixed_t[rows, columns(0, quad, width)] = done

        fetch(layer, 1).wait()
        after[...] = (x_home[...].astype(f32) + dot_nn(mixed_t[...], weights["time_output"][...])).astype(bf16)
        for part in range(frames):
            coming.send(part, leave_frame, after, 0, home)
        if more:
            fetch(layer + 1, 1).start()
        time_saves.put(0, 0, home)

        gain, shift = norm_row(norms_ref, layer, 1), norm_row(norms_ref, layer, 1, True)
        gain_f, shift_f = norm_row(norms_ref, layer, 2), norm_row(norms_ref, layer, 2, True)
        normed[total:, :] = norm_forward(cls, gain, shift)
        fetch(layer, 2).wait()
        for these in columns_of:
            qkv[total:, these] = dot_nn(normed[total:, :], weights["space_proj"][:, these]).astype(bf16)
        cls_saves.put(0, total, CLS_ROWS)
        for i in range(3, len(WEIGHTS)):
            fetch(layer, i).wait()

        @pl.loop(0, frames)
        def _(frame, layer=layer, more=more, space_saves=space_saves, gain=gain, shift=shift, gain_f=gain_f, shift_f=shift_f):
            for number in range(frames):

                @pl.when(frame == number)
                def _(number=number, more=more):
                    coming.receive_frame(number, reach_frame, x_away)
                    if number == frames - 1 and not more:
                        extra.send(2, leave_frame, grad, 0, home)

            start = pl.multiple_of(frame * patches, 16)
            rows = pl.ds(start, patches)
            normed[rows, :] = norm_forward(x_away[rows, :].astype(f32), gain, shift)
            for these in columns_of:
                qkv[rows, these] = dot_nn(normed[rows, :], weights["space_proj"][:, these]).astype(bf16)
            slot = slot_of(lengths_ref, at.patch * frames + frame)
            _, tiles = space_tiles(patches, total, slot, qkv, width, frame)
            for quad, done in enumerate(forward_tiles(tiles, key_mask)):
                mixed[rows, columns(0, quad, width)] = done
            residual = x_away[rows, :].astype(f32) + dot_nn(mixed[rows, :], weights["space_output"][...])
            middle[rows, :] = residual.astype(bf16)
            normed_f[rows, :] = norm_forward(residual, gain_f, shift_f)
            for column in range(0, active.shape[1], WIDE):
                these = slice(column, column + WIDE)
                hidden = dot_nn(normed_f[rows, :], weights["up"][:, these])
                share = 0.5 * (1.0 + lax.erf(hidden * ROOT_HALF))
                active[rows, these] = (hidden * share).astype(bf16)
                bend = share + hidden * (INV_ROOT_TWO_PI * jnp.exp(-0.5 * hidden * hidden))
                slope[rows, these] = bend.astype(bf16)
            after[rows, :] = (residual + dot_nn(active[rows, :], weights["down"][...])).astype(bf16)
            space_saves.put(frame, start, patches)
            for number in range(frames - 1):

                @pl.when(frame == number)
                def _(number=number, more=more):
                    if more:
                        leaving.send(number, leave_away, after, 0, (number + 1) * patches)

        time_saves.finish(0, 0, home)
        if more:
            leaving.send(frames - 1, leave_away, after, (frames - 2) * patches, total)
            for i in range(2, len(WEIGHTS)):
                fetch(layer + 1, i).start()
            leaving.receive(reach_home, x_home)
            save_home.start()
        else:
            save_result.start()
            for frame in range(frames):
                extra.receive_frame(frame, reach_frame, grad_away)
            save_grad.start()
        for frame in range(frames):
            space_saves.finish(frame, frame * patches, patches)
        cls_saves.finish(0, total, CLS_ROWS)
    for copy in (save_home, save_result, save_grad):
        copy.wait()


CHUNKS = 16
TOTAL = CHUNKS * LAYERS
BLOCKS = 3
PIECE = (48, 128)
ROUTES = (("x", "zl", "zh", "y", "x", "y"), ("y", "zl", "zh", "x", "x", "y"), ("x", "y", "zl", "zh", "x", "y"))
SUMS = 4
STAGES = 7
RAW_SLOTS = 8
ACC_SLOTS = 8
BOX_SLOTS = 4
STRIDE = 2
SEGMENTS = (4, 4, 1, 3, 1, 3)
PLAN = {
    1: dict(early=2, down=1, hidden=1, wide=2, norm=1, frames=(0, 1, 0), up=0, space_out=2, space_proj=1, time_early=0, home=1, time0=1, time1=1, time2=0, time_out=1, time_proj=0),
    0: dict(early=1, down=1, hidden=1, wide=1, norm=0, frames=(1, 2, 2), up=1, space_out=0, space_proj=2, time_early=0, home=1, time0=1, time1=2, time2=0, time_out=1, time_proj=1),
}
SMALL = ("core", "zl", "zh", "x", "y")
SMALL_ROWS = 24


def recv_shape(route, stage):
    left = [dim for dim in ("zh", "zl", "x", "y") if dim not in route[: stage + 1]]
    return (2,) * len(left) + PIECE


class Pump:
    def __init__(self, at, results, scratch):
        self.at, self.results = at, results
        self.raw, self.core_in, self.acc, self.out, *rest = scratch
        self.inboxes = rest[: BLOCKS * SUMS]
        self.core_send, self.core_recv, self.core_free, self.send_sem, self.recv_sem = rest[BLOCKS * SUMS :]
        self.made = self.stepped = 0

    def core_copy(self, c, z):
        slot = lax.rem(c, RAW_SLOTS)
        return pltpu.make_async_remote_copy(
            src_ref=self.raw.at[slot, z // 2, z % 2, 1 - self.at.me["core"]],
            dst_ref=self.core_in.at[slot, z // 2, z % 2],
            send_sem=self.core_send.at[slot, z],
            recv_sem=self.core_recv.at[slot, z],
            device_id=self.at.peer("core"),
            device_id_type=MESH,
        )

    def claim(self, c, known):
        if known >= RAW_SLOTS:
            pl.semaphore_wait(self.core_free, 1)

    def store(self, c, z, core, block, rows):
        slot = lax.rem(c, RAW_SLOTS)
        for xh in range(2):
            for yh in range(2):
                part = rows[xh * 48 : (xh + 1) * 48, yh * 128 : (yh + 1) * 128]
                self.raw[slot, z // 2, z % 2, core, block, xh, yh] = part.astype(bf16)

    def make_chunks(self, count, lhs, rhs):
        first = self.made

        def one(i, c, known):
            self.claim(c, known)
            for half in range(2):
                left = lhs(slice(half * 384, (half + 1) * 384))
                for block in range(BLOCKS):
                    done = dot_tn(left, rhs(i, block * 256))
                    for j in range(4):
                        self.store(c, half * 2 + j // 2, j % 2, block, done[j * 96 : (j + 1) * 96])
            for z in range(4):
                self.core_copy(c, z).start()

        if count == 1:
            one(0, first, first)
        else:
            assert (first >= RAW_SLOTS) == (first + count - 1 >= RAW_SLOTS)

            @pl.loop(0, count)
            def _(i):
                one(i, first + i, first)

        self.made += count
        assert self.made - self.stepped <= RAW_SLOTS

    def make_down(self, lhs, rhs):
        first = self.made

        @pl.loop(0, 4)
        def _(z):
            if first >= RAW_SLOTS:

                @pl.when(z == 0)
                def _():
                    pl.semaphore_wait(self.core_free, 4)

            for core in range(2):
                left = lhs(pl.ds(pl.multiple_of(z * 768 + core * 384, 128), 384))
                for block in range(BLOCKS):
                    done = dot_tn(left, rhs[:, block * 256 : (block + 1) * 256])
                    for c in range(4):
                        self.store_at(first + c, z, core, block, done[c * 96 : (c + 1) * 96])
            for c in range(4):
                slot = (first + c) % RAW_SLOTS
                zh, zl = z // 2, lax.rem(z, 2)
                pltpu.make_async_remote_copy(
                    src_ref=self.raw.at[slot, zh, zl, 1 - self.at.me["core"]],
                    dst_ref=self.core_in.at[slot, zh, zl],
                    send_sem=self.core_send.at[slot, z],
                    recv_sem=self.core_recv.at[slot, z],
                    device_id=self.at.peer("core"),
                    device_id_type=MESH,
                ).start()

        self.made += 4
        assert self.made - self.stepped <= RAW_SLOTS

    def store_at(self, c, z, core, block, rows):
        for xh in range(2):
            for yh in range(2):
                part = rows[xh * 48 : (xh + 1) * 48, yh * 128 : (yh + 1) * 128]
                self.raw[c % RAW_SLOTS, z // 2, lax.rem(z, 2), core, block, xh, yh] = part.astype(bf16)

    def part(self, c, block, stage, value):
        route = ROUTES[block]

        def pick(dim):
            if dim in route[:stage]:
                return self.at.me[dim]
            return value if dim == route[stage] else slice(None)

        return (lax.rem(c, ACC_SLOTS), pick("zh"), pick("zl"), block, pick("x"), pick("y"))

    def exchange(self, c, block, stage):
        me = self.at.me
        dim = ROUTES[block][stage]
        box = lax.rem(c, BOX_SLOTS)
        if stage < SUMS:
            src = self.acc.at[self.part(c, block, stage, 1 - me[dim])]
            dst = self.inboxes[block * SUMS + stage].at[box]
        else:
            slot = lax.rem(c, ACC_SLOTS)
            if stage == SUMS:
                src = dst = self.out.at[slot, block, me["x"], me["y"]]
            elif dim == "x":
                src = dst = self.out.at[slot, block, me["x"]]
            else:
                src = dst = self.out.at[slot, block, :, me["y"]]
        return pltpu.make_async_remote_copy(
            src_ref=src,
            dst_ref=dst,
            send_sem=self.send_sem.at[box, block, stage],
            recv_sem=self.recv_sem.at[box, block, stage],
            device_id=self.at.peer(dim),
            device_id_type=MESH,
        )

    def enter(self, c):
        me = self.at.me
        slot, into = lax.rem(c, RAW_SLOTS), lax.rem(c, ACC_SLOTS)
        for z in range(4):
            self.core_copy(c, z).wait()
        for zh in range(2):
            for zl in range(2):
                both = self.raw[slot, zh, zl, me["core"]].astype(f32) + self.core_in[slot, zh, zl].astype(f32)
                self.acc[into, zh, zl] = both.astype(bf16)

        @pl.when(c < TOTAL - RAW_SLOTS)
        def _():
            pl.semaphore_signal(self.core_free, inc=1, device_id=self.at.peer("core"), device_id_type=MESH)

        for block in range(BLOCKS):
            self.exchange(c, block, 0).start()

    def advance(self, c, stage):
        me = self.at.me
        slot, box = lax.rem(c, ACC_SLOTS), lax.rem(c, BOX_SLOTS)
        for block in range(BLOCKS):
            self.exchange(c, block, stage).wait()
            if stage < SUMS:
                where = self.part(c, block, stage, me[ROUTES[block][stage]])
                both = self.acc[where].astype(f32) + self.inboxes[block * SUMS + stage][box].astype(f32)
                if stage == SUMS - 1:
                    self.out[slot, block, me["x"], me["y"]] = both.astype(bf16)
                else:
                    self.acc[where] = both.astype(bf16)
            if stage + 1 < STAGES - 1:
                self.exchange(c, block, stage + 1).start()
            else:
                self.finish(c, block)

    def finish(self, c, block):
        slot = lax.rem(c, ACC_SLOTS)
        layer = LAYERS - 1 - c // CHUNKS
        inner = lax.rem(c, CHUNKS)
        start = 0
        for which, count in enumerate(SEGMENTS):

            @pl.when((inner >= start) & (inner < start + count))
            def _(which=which, start=start):
                for xh in range(2):
                    for yh in range(2):
                        part = self.out[slot, block, xh, yh]
                        column = block * 256 + yh * 128
                        if which == 0:
                            row = pl.multiple_of((inner - start) * 96 + xh * 48, 16)
                            self.results[which][layer, pl.ds(row, 48), column : column + 128] = part
                        else:
                            at = pl.ds(pl.multiple_of((inner - start) * 768 + column, 128), 128)
                            self.results[which][layer, xh * 48 : (xh + 1) * 48, at] = part

            start += count

    def run_step(self, t):
        for stage in reversed(range(STAGES)):
            c = t - STRIDE * stage

            @pl.when((c >= 0) & (c < TOTAL))
            def _(c=c, stage=stage):
                if stage == 0:
                    self.enter(c)
                else:
                    self.advance(c, stage - 1)

    def step(self, count=1):
        first = self.stepped
        self.stepped += count
        assert min(self.stepped, TOTAL) <= self.made

        @pl.loop(first, first + count)
        def _(t):
            self.run_step(t)

    def inside(self, count):
        first = self.stepped
        self.stepped += count
        assert min(self.stepped, TOTAL) <= self.made
        return first

    def frame_steps(self, counts):
        first = self.inside(sum(counts))
        a, b, c = counts

        def run(frame):
            second, third = (frame + 1) // 2, frame // 2
            low = first + a * second + b * third

            @pl.loop(low, low + a + (b - a) * second + (c - b) * third)
            def _(t):
                self.run_step(t)

        return run


class Small:
    def __init__(self, at, values, boxes, send_sem, recv_sem):
        self.at, self.values, self.boxes, self.send_sem, self.recv_sem = at, values, boxes, send_sem, recv_sem

    def rows(self, i):
        return SMALL_ROWS if i < 3 else 16

    def copy(self, i):
        part = pl.ds(0, self.rows(i))
        return pltpu.make_async_remote_copy(
            src_ref=self.values.at[part],
            dst_ref=self.boxes.at[i, part],
            send_sem=self.send_sem.at[i],
            recv_sem=self.recv_sem.at[i],
            device_id=self.at.peer(SMALL[i]),
            device_id_type=MESH,
        )

    def step(self, i):
        if i > 0:
            rows = slice(0, self.rows(i - 1))
            self.copy(i - 1).wait()
            self.values[rows] += self.boxes[i - 1, rows]
        if i < len(SMALL):
            self.copy(i).start()


class Ring:
    def __init__(self, sources, slots, sems):
        self.sources, self.slots, self.sems = sources, slots, sems
        self.depth = slots.shape[0]
        self.started = self.taken = 0
        for _ in range(self.depth):
            self.start()

    def copy(self, i):
        source = self.sources[i]
        slot = i % self.depth
        return pltpu.make_async_copy(source, self.slots.at[slot, pl.ds(0, source.shape[0])], self.sems.at[slot])

    def start(self):
        if self.started < len(self.sources):
            self.copy(self.started).start()
            self.started += 1

    def take(self):
        i = self.taken
        self.copy(i).wait()
        self.taken += 1
        return self.slots.at[i % self.depth, pl.ds(0, self.sources[i].shape[0])]

    def free(self):
        self.start()


class Single:
    def __init__(self, sources, buffer, sem):
        self.copies = [
            pltpu.make_async_copy(source, buffer.at[pl.ds(0, source.shape[0])], sem) for source in sources
        ]
        self.next = 0
        self.copies[0].start()

    def take(self):
        self.copies[self.next].wait()

    def free(self):
        self.next += 1
        if self.next < len(self.copies):
            self.copies[self.next].start()


def backward_kernel(lay, *refs):
    devices, patches = lay.devices, lay.all_patches
    lengths_ref, norms_ref, cls_ref, leave_home, reach_away, leave_away, reach_home = refs[:7]
    weights = dict(zip(WEIGHTS, refs[7:13]))
    grad_hbm, x_out_hbm = refs[13:15]
    names = ("x_home",) + SAVED
    refs = refs[15:]
    saved = [dict(zip(names, refs[len(names) * layer : len(names) * (layer + 1)])) for layer in range(LAYERS)]
    refs = refs[len(names) * LAYERS :]
    small_ref, *results, output_hbm, tokens_hbm = refs[:9]
    refs = refs[9:]
    hidden, qkv, dqkv, wide, mixed, branch, x_buf, grad_buf, home_buf, cls_sum, bias_ref, *refs = refs
    weight_slots, lhs_slots, sent, got, small_boxes, *sums = refs[:11]
    sem_hidden, sem_qkv, sem_x, sem_ends, sem_weight, sem_lhs, sem_sent, sem_got, small_send, small_recv = refs[11:21]
    pump_scratch = refs[21:]
    load_grad = pltpu.make_async_copy(grad_hbm, grad_buf, sem_ends.at[0])
    load_out = pltpu.make_async_copy(x_out_hbm, mixed, sem_ends.at[1])
    save_out = pltpu.make_async_copy(home_buf, output_hbm, sem_ends.at[2])
    save_tokens = pltpu.make_async_copy(mixed, tokens_hbm, sem_ends.at[3])
    load_out.start()
    load_grad.start()

    at = Place()
    shuffle = Shuffle(lay, at, sent, got, sem_sent, sem_got)
    shuffle.greet()
    for dim in ("x", "y"):
        pl.semaphore_signal(pltpu.get_barrier_semaphore(), inc=1, device_id=at.peer(dim), device_id_type=MESH)

    total, width = grad_buf.shape
    parts = range(0, 3 * width, width)
    order = tuple(reversed(range(LAYERS)))
    tiles, lhs = [], []
    for layer in order:
        wide_parts = range(0, weights["up"].shape[2], width)
        tiles += [weights["down"].at[layer, pl.ds(start, width), :] for start in wide_parts]
        tiles += [weights["up"].at[layer, :, pl.ds(start, width)] for start in wide_parts]
        tiles += [weights["space_output"].at[layer]]
        tiles += [weights["space_proj"].at[layer, :, pl.ds(start, width)] for start in parts]
        tiles += [weights["time_output"].at[layer]]
        tiles += [weights["time_proj"].at[layer, :, pl.ds(start, width)] for start in parts]
        here = saved[layer]
        lhs += [here["slope"].at[:, pl.ds(start, width)] for start in wide_parts]
        lhs += [here[name] for name in ("normed_f", "mixed_s", "normed_s", "mixed_t", "normed_t")]
    fill = Single([saved[layer]["active"] for layer in order], hidden, sem_hidden)
    ring = Ring(tiles, weight_slots, sem_weight)
    left = Ring(lhs, lhs_slots, sem_lhs)
    load_qkv = Single([saved[layer][name] for layer in order for name in ("qkv_s", "qkv_t")], qkv, sem_qkv)
    load_x = Single(
        [saved[layer][name] for layer in order for name in ("middle", "x_away", "x_home")], x_buf, sem_x
    )
    pump = Pump(at, results, pump_scratch)
    small = Small(at, small_ref, small_boxes, small_send, small_recv)
    for part in sums:
        part[...] = jnp.zeros_like(part)
    small_ref[...] = jnp.zeros_like(small_ref)
    key_mask = key_bias(patches)
    cls = cls_rows_of(cls_ref)
    fill_bias(lengths_ref, lay.frames, bias_ref)

    def back_product(rows, source, count):
        for i in range(count):
            tile = ring.take()
            part = dot_nt(source[:rows, i * width : (i + 1) * width], tile[...])
            if i:
                wide[:rows, :] += part
            else:
                wide[:rows, :] = part
            ring.free()

    frames = total // patches
    group = bias_ref.shape[0]
    groups = group_parts(lay, group)

    def made_of(lhs_tile, source, first=0, rows=None):
        rows = source.shape[0] if rows is None else rows

        def rhs(i, start):
            column = pl.multiple_of((i + first) * width + start, 128) if not isinstance(i, int) else (i + first) * width + start
            return source[:rows, pl.ds(column, WIDE)]

        return (lambda these: lhs_tile[:, these]), rhs

    shuffle.meet(2)
    load_out.wait()
    shuffle.send_all(leave_away, mixed)
    load_grad.wait()
    dy = grad_buf

    for layer in order:
        last = layer == 0
        plan = PLAN[layer]

        def steps(site, plan=plan):
            if plan.get(site, 0):
                pump.step(plan[site])

        fill.take()
        pump.make_down(lambda these: hidden[:, these], dy)
        steps("down")
        for start in range(0, hidden.shape[1], width):
            tile, slope = ring.take(), left.take()
            for block in range(0, width, WIDE):
                grad_active = dot_nt(dy[...], tile[block : block + WIDE, :])
                grad_hidden = grad_active * slope[:, block : block + WIDE].astype(f32)
                hidden[:, start + block : start + block + WIDE] = grad_hidden.astype(bf16)
            ring.free()
            left.free()
        normed_f = left.take()
        if plan["early"]:
            pump.make_chunks(plan["early"], *made_of(normed_f, hidden))
        steps("hidden")
        back_product(total, hidden, hidden.shape[1] // width)
        steps("wide")
        load_x.take()

        @pl.loop(0, frames)
        def _(frame, layer=layer):
            here = pl.ds(pl.multiple_of(frame * patches, 16), patches)
            part = norm_backward(x_buf[here, :].astype(f32), wide[here, :], norm_row(norms_ref, layer, 2), sums[0:2])
            both = dy[here, :].astype(f32) + part
            wide[here, :] = both
            branch[here, :] = both.astype(bf16)

        load_x.free()
        if not last:
            shuffle.receive(reach_home, home_buf)
            save_out.start()
        steps("norm")

        out_tile, *proj_tiles = [ring.take() for _ in range(4)]
        load_qkv.take()
        load_x.take()
        cls_sum[...] = jnp.zeros_like(cls_sum)
        gain = norm_row(norms_ref, layer, 1)
        frame_run = pump.frame_steps(plan["frames"])

        @pl.loop(0, frames)
        def _(frame):
            here = pl.ds(pl.multiple_of(frame * patches, 16), patches)
            mixed[here, :] = dot_nt(branch[here, :], out_tile[...]).astype(bf16)
            slot = slot_of(lengths_ref, at.patch * frames + frame)
            _, these = space_tiles(patches, total, slot, qkv, width, frame, mixed)
            row_ids = lax.broadcasted_iota(jnp.int32, (patches, WIDE), 0)
            cls_ids = lax.broadcasted_iota(jnp.int32, (CLS_ROWS, WIDE), 0)
            for quad, grads in enumerate(backward_tiles(these, key_mask)):
                dqkv[here, columns(0, quad, width)] = grads[0].astype(bf16)
                for part in (1, 2):
                    where = columns(part, quad, width)
                    dqkv[here, where] = jnp.where(row_ids < REAL_PATCH, grads[part], 0.0).astype(bf16)
                    row = grads[part][REAL_PATCH : REAL_PATCH + 1]
                    cls_sum[:, where] += jnp.where(cls_ids == slot, row, 0.0)
            grad = sum(dot_nt(dqkv[here, i * width : (i + 1) * width], tile[...]) for i, tile in enumerate(proj_tiles))
            part = norm_backward(x_buf[here, :].astype(f32), grad, gain, sums[2:4])
            mixed[here, :] = (wide[here, :] + part).astype(bf16)
            for i in range(2):

                @pl.when(frame == i)
                def _(i=i):
                    shuffle.send(i, leave_away, mixed, 0, (i + 1) * patches)

            frame_run(frame)

        shuffle.send(2, leave_away, mixed, patches, total)
        load_x.free()
        load_qkv.free()
        dqkv[total:, :] = cls_sum[...].astype(bf16)
        grad = sum(dot_nt(dqkv[total:, i * width : (i + 1) * width], tile[...]) for i, tile in enumerate(proj_tiles))
        for _ in range(4):
            ring.free()
        part = norm_backward(cls, grad, gain, sums[2:4])
        small_ref[16:24] += part[:8]
        if plan["early"] < 4:
            pump.make_chunks(4 - plan["early"], *made_of(normed_f, hidden, plan["early"]))
        left.free()
        fill.free()
        steps("up")
        pump.make_chunks(1, *made_of(left.take(), branch))
        left.free()
        steps("space_out")
        pump.make_chunks(3, *made_of(left.take(), dqkv))
        left.free()
        steps("space_proj")
        if not last:
            save_out.wait()
        shuffle.receive(reach_home, home_buf)

        out_tile, *proj_tiles = [ring.take() for _ in range(4)]
        load_qkv.take()
        load_x.take()
        mixed_t = left.take()
        if plan["time_early"]:
            pump.make_chunks(1, *made_of(mixed_t, home_buf))
            left.free()
        steps("home")
        for number, (first, end) in enumerate(groups):
            here = slice(first, end)
            mixed[here, :] = dot_nt(home_buf[here, :], out_tile[...]).astype(bf16)

            @pl.loop(first // group, end // group)
            def _(index):
                at_rows, these = time_tiles(bias_ref, qkv, width, index, mixed)
                for quad, grads in enumerate(backward_tiles(these, bias_ref[...])):
                    for part in range(3):
                        dqkv[at_rows, columns(part, quad, width)] = grads[part].astype(bf16)

            grad = sum(dot_nt(dqkv[here, i * width : (i + 1) * width], tile[...]) for i, tile in enumerate(proj_tiles))
            part = norm_backward(x_buf[here, :].astype(f32), grad, norm_row(norms_ref, layer, 0), sums[4:6])
            mixed[here, :] = (home_buf[here, :].astype(f32) + part).astype(bf16)
            if not last:
                shuffle.send(number, leave_home, mixed, 0 if number < 2 else first, end)
            steps("time%d" % number)
        load_qkv.free()
        load_x.free()
        for _ in range(4):
            ring.free()
        for i, part in enumerate(sums):
            row = layer * 8 + (2, 5, 1, 4, 0, 3)[i]
            small_ref[row : row + 1, :] += jnp.sum(part[...], 0, keepdims=True)
            part[...] = jnp.zeros_like(part)
        if last:
            save_tokens.start()
            small.step(0)
        if not plan["time_early"]:
            pump.make_chunks(1, *made_of(mixed_t, home_buf))
            left.free()
        steps("time_out")
        pump.make_chunks(3, *made_of(left.take(), dqkv, rows=total))
        left.free()
        steps("time_proj")
        if last:
            for i in range(1, len(SMALL) + 1):
                pump.step()
                small.step(i)
        else:
            shuffle.receive(reach_away, grad_buf)

    pump.step(TOTAL + STRIDE * (STAGES - 1) - pump.stepped)
    save_tokens.wait()


IN_VMEM = pl.BlockSpec(memory_space=pltpu.VMEM)
IN_SMEM = pl.BlockSpec(memory_space=pltpu.SMEM)
IN_HBM = pl.BlockSpec(memory_space=pl.ANY)


def shape(*dims, kind=bf16):
    return jax.ShapeDtypeStruct(dims, kind)


def vmem(*dims, kind=bf16):
    return pltpu.VMEM(dims, kind)


def queue(*counts):
    return pltpu.SemaphoreType.DMA(counts)


def whole_call(name, body, collective, near, far, out_near, out_far, scratch):
    return pl.pallas_call(
        body,
        in_specs=[IN_SMEM if part.ndim == 1 else IN_VMEM for part in near] + [IN_HBM] * len(far),
        out_specs=[IN_VMEM] * len(out_near) + [IN_HBM] * len(out_far),
        out_shape=[*out_near, *out_far],
        scratch_shapes=scratch,
        compiler_params=pltpu.CompilerParams(
            collective_id=collective, has_side_effects=True, vmem_limit_bytes=VMEM_MOST
        ),
        name=name,
    )(*near, *far)


def finish_kernel(*refs):
    count = len(refs) // 2
    for source, target in zip(refs[:count], refs[count:]):
        target[...] = source[...].astype(target.dtype)


def finish(parts, kinds, steps=6):
    specs, out = [], []
    for part, kind in zip(parts, kinds):
        cut = part.ndim - 1 if part.shape[-1] % (steps * 128) == 0 else part.ndim - 2
        block = tuple(size // steps if dim == cut else size for dim, size in enumerate(part.shape))

        def index(i, cut=cut, ndim=part.ndim):
            return tuple(i if dim == cut else 0 for dim in range(ndim))

        specs.append(pl.BlockSpec(block, index))
        out.append(jax.ShapeDtypeStruct(part.shape, kind))
    return pl.pallas_call(
        finish_kernel,
        grid=(steps,),
        in_specs=specs,
        out_specs=specs,
        out_shape=out,
        compiler_params=params("arbitrary"),
        name="finish",
    )(*parts)


def fast_local(
    tokens,
    cls_tokens,
    clip_lengths,
    time_proj,
    time_output,
    space_proj,
    space_output,
    up_weight,
    down_weight,
    norm_gains,
    norm_biases,
    cotangent,
):
    frames, patch_rows, width = tokens.shape
    devices = lax.axis_size("patch")
    hidden = up_weight.shape[2]
    lay = Layout(devices, frames, patch_rows)
    home, away, block = lay.home_rows, lay.away_rows, lay.block
    clip_count = cls_tokens.shape[0]
    group = group_rows(patch_rows, frames)
    orders = {name: jnp.asarray(part) for name, part in lay.orders().items()}

    def home_order(values):
        return jnp.transpose(values, (1, 0, 2)).reshape(home, width)

    def given_order(values):
        return jnp.transpose(values.reshape(patch_rows, frames, width), (1, 0, 2))

    parts = len(lay.parts())
    moving = [vmem(devices, block, width), vmem(2, devices, block, width), queue(parts, devices), queue(2, parts, devices)]
    extra = [vmem(devices, block, width), vmem(1, devices, block, width), queue(parts, devices), queue(1, parts, devices)]
    norms = jnp.concatenate([norm_gains.reshape(-1, width), norm_biases.reshape(-1, width)], 0)
    lengths = clip_lengths[0]
    weights = (time_proj, time_output, space_proj, space_output, up_weight, down_weight)
    at_home = home_order(tokens)
    saved_shapes = [
        shape(home, width),
        shape(home, 3 * width),
        shape(home, width),
        shape(away, width),
        shape(away + CLS_ROWS, width),
        shape(away + CLS_ROWS, 3 * width),
        *[shape(away, width)] * 3,
        *[shape(away, hidden)] * 2,
    ]
    bias = vmem(group, QUAD * group, kind=f32)
    home_next, grad_away, x_out, *saved = whole_call(
        "forward",
        functools.partial(forward_kernel, lay),
        2,
        (lengths, norms, cls_tokens, *[orders[name] for name in ("leave_frame", "reach_frame", "leave_away", "reach_home")]),
        (*weights, at_home, home_order(cotangent)),
        [],
        [shape(home, width), shape(away, width), shape(away, width)] + saved_shapes * LAYERS,
        [
            *[vmem(*part.shape[1:]) for part in weights],
            *[vmem(*part.shape) for part in saved_shapes],
            bias,
            vmem(home, width),
            vmem(away, width),
            vmem(home, width),
            vmem(away, width),
            queue(len(weights)),
            queue(5),
            queue(3, 1),
            queue(len(SAVED) - 3, lay.away_frames),
            queue(2, 1),
            *moving,
            *extra,
        ],
    )
    stored = [(at_home, *saved[: len(SAVED)]), (home_next, *saved[len(SAVED) :])]

    inbox = [vmem(BOX_SLOTS, *recv_shape(ROUTES[b], s)) for b in range(BLOCKS) for s in range(SUMS)]
    single = pltpu.SemaphoreType.DMA
    share = width // devices
    small, *large, output, grad_tokens = whole_call(
        "backward",
        functools.partial(backward_kernel, lay),
        1,
        (lengths, norms, cls_tokens, *[orders[name] for name in ("leave_patch", "reach_patch", "leave_away", "reach_home")]),
        (*weights, grad_away, x_out, *stored[0], *stored[1]),
        [
            shape(SMALL_ROWS, width, kind=f32),
            shape(LAYERS, hidden // devices, width),
            shape(LAYERS, share, hidden),
            shape(LAYERS, share, width),
            shape(LAYERS, share, 3 * width),
            shape(LAYERS, share, width),
            shape(LAYERS, share, 3 * width),
        ],
        [shape(home, width), shape(home, width)],
        [
            vmem(away, hidden),
            vmem(away + CLS_ROWS, 3 * width),
            vmem(away + CLS_ROWS, 3 * width),
            vmem(away, width, kind=f32),
            *[vmem(away, width)] * 5,
            vmem(CLS_ROWS, 3 * width, kind=f32),
            bias,
            vmem(4, width, width),
            vmem(2, away + CLS_ROWS, width),
            *moving[:2],
            vmem(len(SMALL), SMALL_ROWS, width, kind=f32),
            *[vmem(8, width, kind=f32)] * 6,
            single,
            single,
            single,
            queue(4),
            queue(4),
            queue(2),
            *moving[2:],
            queue(len(SMALL)),
            queue(len(SMALL)),
            vmem(RAW_SLOTS, 2, 2, 2, BLOCKS, 2, 2, *PIECE),
            vmem(RAW_SLOTS, 2, 2, BLOCKS, 2, 2, *PIECE),
            vmem(ACC_SLOTS, 2, 2, BLOCKS, 2, 2, *PIECE),
            vmem(ACC_SLOTS, BLOCKS, 2, 2, *PIECE),
            *inbox,
            queue(RAW_SLOTS, 4),
            queue(RAW_SLOTS, 4),
            pltpu.SemaphoreType.REGULAR,
            queue(BOX_SLOTS, BLOCKS, STAGES - 1),
            queue(BOX_SLOTS, BLOCKS, STAGES - 1),
        ],
    )
    large = [large[i] for i in (5, 4, 3, 2, 1, 0)]
    *large, output, grad_tokens = finish((*large, output, grad_tokens), (f32,) * len(large) + (bf16,) * 2)
    grad_cls = small[16 : 16 + clip_count]
    small = lax.dynamic_slice_in_dim(small[:16], lax.axis_index("patch") * share, share, 1)
    small = small.reshape(LAYERS, 8, share)
    return (given_order(output), given_order(grad_tokens), grad_cls, *large, small[:, 0:3], small[:, 3:6])


def general_local(
    tokens,
    cls_tokens,
    clip_lengths,
    time_proj,
    time_output,
    space_proj,
    space_output,
    up_weight,
    down_weight,
    norm_gains,
    norm_biases,
    cotangent,
):
    frames, patch_rows, width = tokens.shape
    devices = lax.axis_size("patch")
    lay = Layout(devices, frames, patch_rows)
    away_rows = lay.away_rows
    patches = lay.all_patches
    clip_count = cls_tokens.shape[0]

    frame_ids = jnp.arange(frames, dtype=jnp.int32)
    slots = frame_slots(clip_lengths[0], frame_ids)
    bias = time_bias(slots[:, None] == slots[None, :], patch_rows, frames)
    my_frames = lax.axis_index("patch") * lay.away_frames + jnp.arange(lay.away_frames, dtype=jnp.int32)
    my_slots = jnp.where(my_frames < frames, frame_slots(clip_lengths[0], my_frames), -1)
    cls_pick = (my_slots[None, :] == jnp.arange(CLS_ROWS, dtype=jnp.int32)[:, None]).astype(f32)

    def home_order(values):
        return jnp.transpose(values, (1, 0, 2)).reshape(lay.home_rows, width)

    def given_order(values):
        return jnp.transpose(values.reshape(patch_rows, frames, width), (1, 0, 2))

    cls_aug = jnp.pad(cls_tokens.astype(f32), ((0, CLS_ROWS - clip_count), (0, 0)))
    residual = home_order(tokens).astype(f32)
    cotangent_away = lay.to_away(home_order(cotangent))
    stored = []
    for layer in range(LAYERS):
        gains, biases = norm_gains[layer], norm_biases[layer]
        normed, scaled_t, inverse_t = layer_norm(residual, gains[0], biases[0])
        normed_t = normed.astype(bf16)
        qkv_t = project(normed_t, time_proj[layer]).astype(bf16)
        mixed_t = time_forward(bias, qkv_t)
        residual = residual + project(mixed_t, time_output[layer])
        away = lay.to_away(residual.astype(bf16))
        away = away + jnp.pad(cls_aug, ((away_rows, 0), (0, 0)))
        normed, scaled_s, inverse_s = layer_norm(away, gains[1], biases[1])
        normed_s = normed.astype(bf16)
        qkv_s = project(normed_s, space_proj[layer]).astype(bf16)
        mixed_s = space_forward(my_slots, qkv_s, lay.away_frames, patches)
        away = away[:away_rows] + project(mixed_s, space_output[layer])
        normed, scaled_f, inverse_f = layer_norm(away, gains[2], biases[2])
        normed_f = normed.astype(bf16)
        hidden = project(normed_f, up_weight[layer])
        active = gelu_value(hidden).astype(bf16)
        away = away + project(active, down_weight[layer])
        residual = lay.to_home(away.astype(bf16))
        stored.append(
            dict(
                normed_t=normed_t, scaled_t=scaled_t, inverse_t=inverse_t, qkv_t=qkv_t, mixed_t=mixed_t,
                normed_s=normed_s, scaled_s=scaled_s, inverse_s=inverse_s, qkv_s=qkv_s, mixed_s=mixed_s,
                normed_f=normed_f, scaled_f=scaled_f, inverse_f=inverse_f, hidden=hidden, active=active,
            )
        )
    output = given_order(residual.astype(bf16))

    grad_cls = jnp.zeros_like(cls_aug)
    grad_away = cotangent_away[:away_rows]
    results = [None] * LAYERS
    for layer in reversed(range(LAYERS)):
        saved = stored[layer]
        gains = norm_gains[layer]
        branch = grad_away.astype(bf16)
        grad_down = weight_grad(saved["active"], branch)
        grad_active = project_back(branch, down_weight[layer])
        grad_hidden = (grad_active * gelu_slope(saved["hidden"])).astype(bf16)
        grad_up = weight_grad(saved["normed_f"], grad_hidden)
        grad_normed = project_back(grad_hidden, up_weight[layer])
        grad_input, gain_two, bias_two = norm_back(
            grad_normed, saved["scaled_f"], saved["inverse_f"], gains[2]
        )
        grad_away = grad_away + grad_input
        branch = grad_away.astype(bf16)
        grad_space_out = weight_grad(saved["mixed_s"], branch)
        grad_mixed = project_back(branch, space_output[layer]).astype(bf16)
        dq, dk, dv, dck, dcv = space_backward(my_slots, saved["qkv_s"], grad_mixed, lay.away_frames, patches)
        dcls = jnp.concatenate([dck[:, 0], dcv[:, 0]], -1)
        dcls = jnp.dot(cls_pick, dcls, precision=lax.Precision.HIGHEST)
        dcls = jnp.pad(dcls.astype(bf16), ((0, 0), (width, 0)))
        grad_qkv = jnp.concatenate([jnp.concatenate([dq, dk, dv], -1), dcls], 0)
        grad_space_proj = weight_grad(saved["normed_s"], grad_qkv)
        grad_normed = project_back(grad_qkv, space_proj[layer])
        grad_input, gain_one, bias_one = norm_back(
            grad_normed, saved["scaled_s"], saved["inverse_s"], gains[1]
        )
        grad_away = grad_away + grad_input[:away_rows]
        grad_cls = grad_cls + grad_input[away_rows:]
        grad_home = lay.to_home(grad_away.astype(bf16))
        branch = grad_home.astype(bf16)
        grad_time_out = weight_grad(saved["mixed_t"], branch)
        grad_mixed = project_back(branch, time_output[layer]).astype(bf16)
        grad_qkv = time_backward(bias, saved["qkv_t"], grad_mixed)
        grad_time_proj = weight_grad(saved["normed_t"], grad_qkv)
        grad_normed = project_back(grad_qkv, time_proj[layer])
        grad_input, gain_zero, bias_zero = norm_back(
            grad_normed, saved["scaled_t"], saved["inverse_t"], gains[0]
        )
        grad_home = grad_home + grad_input
        if layer > 0:
            grad_away = lay.to_away(grad_home.astype(bf16))[:away_rows]
        large = (grad_time_proj, grad_time_out, grad_space_proj, grad_space_out, grad_up, grad_down)
        large = [lax.psum_scatter(part, "patch", scatter_dimension=0, tiled=True) for part in large]
        large = lax.psum(large, "clip")
        small = (jnp.stack([gain_zero, gain_one, gain_two]), jnp.stack([bias_zero, bias_one, bias_two]))
        results[layer] = [part.astype(f32) for part in large] + list(small)
    grad_tokens = given_order(grad_home.astype(bf16))
    stacked = [jnp.stack([results[layer][i] for layer in range(LAYERS)]) for i in range(8)]
    small = jnp.stack(stacked[6:])
    small = lax.psum(small, ("patch", "clip"))
    share = width // devices
    small = lax.dynamic_slice_in_dim(small, lax.axis_index("patch") * share, share, 3)
    grad_cls = lax.psum(grad_cls[:clip_count], "patch")
    return (output, grad_tokens, grad_cls, *stacked[:6], small[0], small[1])


def solution(mesh):
    in_specs = (
        P("clip", "patch", None),
        P("clip", None),
        P("clip", None),
        P(),
        P(),
        P(),
        P(),
        P(),
        P(),
        P(),
        P(),
        P("clip", "patch", None),
    )
    out_specs = (
        P("clip", "patch", None),
        P("clip", "patch", None),
        P("clip", None),
        P(None, "patch", None),
        P(None, "patch", None),
        P(None, "patch", None),
        P(None, "patch", None),
        P(None, "patch", None),
        P(None, "patch", None),
        P(None, None, "patch"),
        P(None, None, "patch"),
    )
    paired = (mesh.shape["clip"], mesh.shape["patch"]) == (4, 8)
    local = fast_local if paired else general_local
    return jax.shard_map(local, mesh=mesh, in_specs=in_specs, out_specs=out_specs, check_vma=False)
```

```python
import functools

import jax
import jax.numpy as jnp
import numpy as np
from jax import lax
from jax.experimental import pallas as pl
from jax.experimental.pallas import tpu as pltpu
from jax.sharding import PartitionSpec as P

HEADS = 12
HD = 64
LAYERS = 2
REAL_PATCH = 196
QUAD = 4
WIDE = QUAD * HD
QUADS = HEADS // QUAD
CLS_ROWS = 16

EPSILON = 1e-05
NEG_LARGE = -1e30
ROOT_HALF = 0.7071067811865476
INV_ROOT_TWO_PI = 0.3989422804014327
SCALE = HD**-0.5
VMEM_LIMIT = 48 * 1024 * 1024
VMEM_MOST = 62 * 1024 * 1024

CLIP = "clip"
PATCH = "patch"
f32 = jnp.float32
bf16 = jnp.bfloat16
MESH = pl.DeviceIdType.MESH


def layer_norm(values, norm_gain, norm_bias):
    centered = values - jnp.mean(values, -1, keepdims=True)
    inverse = lax.rsqrt(jnp.mean(centered * centered, -1, keepdims=True) + EPSILON)
    scaled = centered * inverse
    return (scaled * norm_gain + norm_bias, scaled, inverse)


def norm_back(grad_out, scaled, inverse, norm_gain):
    weighted = grad_out * norm_gain
    grad_input = inverse * (
        weighted
        - jnp.mean(weighted, -1, keepdims=True)
        - scaled * jnp.mean(weighted * scaled, -1, keepdims=True)
    )
    return (grad_input, jnp.sum(grad_out * scaled, 0), jnp.sum(grad_out, 0))


def project(left, matrix):
    return jnp.dot(left, matrix, preferred_element_type=f32)


def project_back(grad_out, matrix):
    return lax.dot_general(grad_out, matrix, (((1,), (1,)), ((), ())), preferred_element_type=f32)


def weight_grad(left, grad_out):
    return lax.dot_general(
        left, grad_out, (((0,), (0,)), ((), ())), preferred_element_type=f32
    ).astype(bf16)


def gelu_value(hidden):
    return 0.5 * hidden * (1.0 + lax.erf(hidden * ROOT_HALF))


def gelu_slope(hidden):
    return 0.5 * (1.0 + lax.erf(hidden * ROOT_HALF)) + hidden * INV_ROOT_TWO_PI * jnp.exp(
        -0.5 * hidden * hidden
    )


def dot_nt(left, right):
    return lax.dot_general(left, right, (((1,), (1,)), ((), ())), preferred_element_type=f32)


def dot_nn(left, right):
    return lax.dot_general(left, right, (((1,), (0,)), ((), ())), preferred_element_type=f32)


def dot_tn(left, right):
    return lax.dot_general(left, right, (((0,), (0,)), ((), ())), preferred_element_type=f32)


def spread_heads(rows):
    head = lax.broadcasted_iota(jnp.int32, rows.shape, 1) // HD
    return jnp.concatenate([jnp.where(head == h, rows, jnp.zeros_like(rows)) for h in range(QUAD)], 0)


def merge_heads(stacked):
    count = stacked.shape[0] // QUAD
    head = lax.broadcasted_iota(jnp.int32, (count, WIDE), 1) // HD
    merged = stacked[:count]
    for h in range(1, QUAD):
        merged = jnp.where(head == h, stacked[h * count : (h + 1) * count], merged)
    return merged


def probabilities(scores):
    exponents = [jnp.exp(part - jnp.max(part, 0, keepdims=True)) for part in scores]
    return [part * (1.0 / jnp.sum(part, 0, keepdims=True)) for part in exponents]


def forward_tiles(tiles, bias):
    spreads = [spread_heads(tile[0] * SCALE) for tile in tiles]
    scores = [dot_nt(tile[1], spread) + bias for tile, spread in zip(tiles, spreads)]
    probs = [part.astype(bf16) for part in probabilities(scores)]
    outs = [dot_tn(part, tile[2]) for part, tile in zip(probs, tiles)]
    return [merge_heads(part).astype(bf16) for part in outs]


def backward_tiles(tiles, bias):
    spreads = [spread_heads(tile[0] * SCALE) for tile in tiles]
    grad_spreads = [spread_heads(tile[3]) for tile in tiles]
    scores = [dot_nt(tile[1], spread) + bias for tile, spread in zip(tiles, spreads)]
    grad_probs = [dot_nt(tile[2], spread) for tile, spread in zip(tiles, grad_spreads)]
    probs = probabilities(scores)
    grad_scores = [
        (part * (grad - jnp.sum(part * grad, 0, keepdims=True))).astype(bf16)
        for part, grad in zip(probs, grad_probs)
    ]
    grad_queries = [dot_tn(grad, tile[1]) for grad, tile in zip(grad_scores, tiles)]
    grad_keys = [dot_nn(grad, spread) for grad, spread in zip(grad_scores, spreads)]
    grad_values = [dot_nn(part.astype(bf16), spread) for part, spread in zip(probs, grad_spreads)]
    return [(merge_heads(q) * SCALE, k, v) for q, k, v in zip(grad_queries, grad_keys, grad_values)]


def columns(part, quad, width):
    start = part * width + quad * WIDE
    return slice(start, start + WIDE)


def time_forward_kernel(bias_ref, qkv_ref, out_ref):
    width = out_ref.shape[1]
    bias = bias_ref[...]
    for quad in range(QUADS):
        parts = [qkv_ref[:, columns(part, quad, width)] for part in range(3)]
        out_ref[:, columns(0, quad, width)] = forward_tiles([parts], bias)[0]


def time_backward_kernel(bias_ref, qkv_ref, grad_ref, out_ref):
    width = grad_ref.shape[1]
    bias = bias_ref[...]
    for quad in range(QUADS):
        parts = [qkv_ref[:, columns(part, quad, width)] for part in range(3)]
        grads = backward_tiles([parts + [grad_ref[:, columns(0, quad, width)]]], bias)[0]
        for part in range(3):
            out_ref[:, columns(part, quad, width)] = grads[part].astype(bf16)


def group_rows(patch_count, frames):
    return (2 if patch_count % 2 == 0 else 1) * frames


def time_bias(same_clip, patch_count, frames):
    rows = group_rows(patch_count, frames)
    ids = jnp.arange(rows, dtype=jnp.int32)
    same_patch = (ids[:, None] // frames) == (ids[None, :] // frames)
    tiled = jnp.tile(same_clip, (rows // frames, rows // frames))
    return jnp.tile(jnp.where(same_patch & tiled, 0.0, NEG_LARGE).astype(f32), (1, QUAD))


def params(*semantics):
    return pltpu.CompilerParams(dimension_semantics=semantics, vmem_limit_bytes=VMEM_LIMIT)


def time_forward(bias, qkv):
    rows = bias.shape[0]
    width = qkv.shape[1] // 3
    return pl.pallas_call(
        time_forward_kernel,
        grid=(qkv.shape[0] // rows,),
        in_specs=[
            pl.BlockSpec(bias.shape, lambda i: (0, 0)),
            pl.BlockSpec((rows, 3 * width), lambda i: (i, 0)),
        ],
        out_specs=pl.BlockSpec((rows, width), lambda i: (i, 0)),
        out_shape=jax.ShapeDtypeStruct((qkv.shape[0], width), bf16),
        compiler_params=params("parallel"),
        name="time_forward",
    )(bias, qkv)


def time_backward(bias, qkv, grad_out):
    rows = bias.shape[0]
    width = qkv.shape[1] // 3
    return pl.pallas_call(
        time_backward_kernel,
        grid=(qkv.shape[0] // rows,),
        in_specs=[
            pl.BlockSpec(bias.shape, lambda i: (0, 0)),
            pl.BlockSpec((rows, 3 * width), lambda i: (i, 0)),
            pl.BlockSpec((rows, width), lambda i: (i, 0)),
        ],
        out_specs=pl.BlockSpec((rows, 3 * width), lambda i: (i, 0)),
        out_shape=jax.ShapeDtypeStruct(qkv.shape, bf16),
        compiler_params=params("parallel"),
        name="time_backward",
    )(bias, qkv, grad_out)


def with_class(slot, rows, cls_rows):
    ids = lax.broadcasted_iota(jnp.int32, cls_rows.shape, 0)
    picked = jnp.sum(jnp.where(ids == slot, cls_rows.astype(f32), 0.0), 0, keepdims=True)
    row_ids = lax.broadcasted_iota(jnp.int32, rows.shape, 0)
    return jnp.where(row_ids == REAL_PATCH, picked.astype(bf16), rows)


def key_bias(count):
    key_ids = lax.broadcasted_iota(jnp.int32, (count, 1), 0)
    return jnp.where(key_ids <= REAL_PATCH, 0.0, NEG_LARGE).astype(f32)


def space_forward_kernel(slot_ref, q_ref, k_ref, v_ref, ck_ref, cv_ref, out_ref):
    slot = slot_ref[pl.program_id(0)]
    keys = with_class(slot, k_ref[...], ck_ref[...])
    values = with_class(slot, v_ref[...], cv_ref[...])
    out_ref[...] = forward_tiles([(q_ref[...], keys, values)], key_bias(keys.shape[0]))[0]


def space_backward_kernel(
    slot_ref, q_ref, k_ref, v_ref, ck_ref, cv_ref, g_ref, dq_ref, dk_ref, dv_ref, dck_ref, dcv_ref
):
    slot = slot_ref[pl.program_id(0)]
    keys = with_class(slot, k_ref[...], ck_ref[...])
    values = with_class(slot, v_ref[...], cv_ref[...])
    tile = (q_ref[...], keys, values, g_ref[...])
    grad_q, grad_k, grad_v = backward_tiles([tile], key_bias(keys.shape[0]))[0]
    row_ids = lax.broadcasted_iota(jnp.int32, grad_k.shape, 0)
    dq_ref[...] = grad_q.astype(bf16)
    dk_ref[...] = jnp.where(row_ids < REAL_PATCH, grad_k, 0.0).astype(bf16)
    dv_ref[...] = jnp.where(row_ids < REAL_PATCH, grad_v, 0.0).astype(bf16)
    dck_ref[0] = jnp.sum(jnp.where(row_ids == REAL_PATCH, grad_k, 0.0), 0, keepdims=True)
    dcv_ref[0] = jnp.sum(jnp.where(row_ids == REAL_PATCH, grad_v, 0.0), 0, keepdims=True)


def space_specs(frames, patches):
    cls_block = frames * patches // CLS_ROWS

    def rows(part):
        return pl.BlockSpec((patches, WIDE), lambda f, c, s: (f, part * QUADS + c))

    def cls(part):
        return pl.BlockSpec((CLS_ROWS, WIDE), lambda f, c, s: (cls_block, part * QUADS + c))

    return [rows(0), rows(1), rows(2), cls(1), cls(2)], rows(0)


def space_forward(slots, qkv, frames, patches):
    width = qkv.shape[1] // 3
    in_specs, out_spec = space_specs(frames, patches)
    return pl.pallas_call(
        space_forward_kernel,
        grid_spec=pltpu.PrefetchScalarGridSpec(
            num_scalar_prefetch=1,
            grid=(frames, QUADS),
            in_specs=in_specs,
            out_specs=out_spec,
        ),
        out_shape=jax.ShapeDtypeStruct((frames * patches, width), bf16),
        compiler_params=params("parallel", "parallel"),
        name="space_forward",
    )(slots, qkv, qkv, qkv, qkv, qkv)


def space_backward(slots, qkv, grad_out, frames, patches):
    width = qkv.shape[1] // 3
    in_specs, out_spec = space_specs(frames, patches)
    rows = jax.ShapeDtypeStruct((frames * patches, width), bf16)
    cls_spec = pl.BlockSpec((1, 1, WIDE), lambda f, c, s: (f, 0, c))
    cls = jax.ShapeDtypeStruct((frames, 1, width), f32)
    return pl.pallas_call(
        space_backward_kernel,
        grid_spec=pltpu.PrefetchScalarGridSpec(
            num_scalar_prefetch=1,
            grid=(frames, QUADS),
            in_specs=in_specs + [out_spec],
            out_specs=[out_spec] * 3 + [cls_spec] * 2,
        ),
        out_shape=[rows] * 3 + [cls] * 2,
        compiler_params=params("parallel", "parallel"),
        name="space_backward",
    )(slots, qkv, qkv, qkv, qkv, qkv, grad_out)


def frame_slots(lengths_row, frame_ids):
    clip_ends = jnp.cumsum(lengths_row)
    return jnp.sum((frame_ids[:, None] >= clip_ends[None, :]).astype(jnp.int32), axis=1)


class Layout:
    def __init__(self, devices, frames, patches):
        self.devices = devices
        self.frames = frames
        self.patches = patches
        self.all_patches = patches * devices
        self.away_frames = -(-frames // devices)
        used = self.away_frames * patches
        self.block = -(-used // 16) * 16
        self.home_rows = frames * patches
        self.away_rows = self.away_frames * self.all_patches
        self.sent_rows = devices * self.block

    def home_of_sent(self):
        row = jnp.arange(self.sent_rows, dtype=jnp.int32)
        peer, inner = row // self.block, row % self.block
        frame = peer * self.away_frames + inner // self.patches
        valid = (inner < self.away_frames * self.patches) & (frame < self.frames)
        return jnp.where(valid, (inner % self.patches) * self.frames + frame, -1)

    def sent_of_away(self):
        row = jnp.arange(self.away_rows + CLS_ROWS, dtype=jnp.int32)
        frame, patch = row // self.all_patches, row % self.all_patches
        sent = (patch // self.patches) * self.block + frame * self.patches + patch % self.patches
        return jnp.where(row < self.away_rows, sent, -1)

    def parts(self):
        step = self.block // 5 // 16 * 16
        return ((0, step), (step, 3 * step), (3 * step, self.block))

    def frame_parts(self):
        ends = [-(-self.patches * (i + 1) // 16) * 16 for i in range(self.away_frames)]
        return tuple(zip([0] + ends[:-1], ends))

    def frame_rows(self, frame):
        low, high = self.patches * frame, self.patches * (frame + 1)
        return low // 16 * 16, -(-high // 16) * 16

    def leave(self, order, parts):
        order = np.where(np.arange(self.block) < self.away_frames * self.patches, order, -1)
        rows = np.concatenate([order[:, low:high].reshape(-1) for low, high in parts])
        return np.asarray(rows, np.int32)[:, None]

    def orders(self):
        block, patches, near = self.block, self.patches, self.away_frames
        peer, inner = np.meshgrid(range(self.devices), range(block), indexing="ij")
        by_patch = inner // near * self.frames + peer * near + inner % near
        by_frame = inner % patches * self.frames + peer * near + inner // patches
        from_away = inner // patches * self.all_patches + peer * patches + inner % patches
        row = np.arange(self.away_rows)
        frame, patch = row // self.all_patches, row % self.all_patches
        reach_patch = patch // patches * block + patch % patches * near + frame
        low = np.array([self.frame_rows(i)[0] for i in range(near)])[frame]
        high = np.array([self.frame_rows(i)[1] for i in range(near)])[frame]
        reach_frame = patch // patches * (high - low) + frame * patches + patch % patches - low
        row = np.arange(self.home_rows)
        patch, frame = row // self.frames, row % self.frames
        reach_home = frame // near * block + frame % near * patches + patch

        def column(rows):
            return np.asarray(rows, np.int32)[:, None]

        return dict(
            leave_patch=self.leave(by_patch, self.parts()),
            leave_frame=self.leave(by_frame, self.frame_parts()),
            leave_away=self.leave(from_away, self.parts()),
            reach_patch=column(reach_patch),
            reach_frame=column(reach_frame),
            reach_home=column(reach_home),
        )

    def to_away(self, values):
        pick = self.home_of_sent()[:, None] == jnp.arange(self.home_rows, dtype=jnp.int32)[None, :]
        sent = jnp.dot(pick.astype(bf16), values, preferred_element_type=bf16)
        got = lax.all_to_all(sent, PATCH, split_axis=0, concat_axis=0, tiled=True)
        pick = self.sent_of_away()[:, None] == jnp.arange(self.sent_rows, dtype=jnp.int32)[None, :]
        return jnp.dot(pick.astype(bf16), got, preferred_element_type=f32)

    def to_home(self, values):
        pick = jnp.arange(self.sent_rows, dtype=jnp.int32)[:, None] == self.sent_of_away()[None, : self.away_rows]
        sent = jnp.dot(pick.astype(bf16), values, preferred_element_type=bf16)
        got = lax.all_to_all(sent, PATCH, split_axis=0, concat_axis=0, tiled=True)
        pick = jnp.arange(self.home_rows, dtype=jnp.int32)[:, None] == self.home_of_sent()[None, :]
        return jnp.dot(pick.astype(bf16), got, preferred_element_type=f32)


def norm_rows(values):
    centered = values - jnp.mean(values, -1, keepdims=True)
    inverse = lax.rsqrt(jnp.mean(centered * centered, -1, keepdims=True) + EPSILON)
    return centered, inverse


def norm_forward(values, gain, shift):
    centered, inverse = norm_rows(values)
    return (centered * inverse * gain + shift).astype(bf16)


def norm_backward(values, grad, gain, sums):
    centered, inverse = norm_rows(values)
    weighted = grad * gain
    along = jnp.mean(weighted * centered, -1, keepdims=True) * (inverse * inverse * inverse)

    def fold(part):
        return jnp.sum(part.reshape(part.shape[0] // 8, 8, part.shape[1]), 0)

    sums[0][...] += fold(grad * (centered * inverse))
    sums[1][...] += fold(grad)
    return inverse * (weighted - jnp.mean(weighted, -1, keepdims=True)) - centered * along


class Loads:
    def __init__(self, sources, buffers, sems):
        self.copies = [
            pltpu.make_async_copy(source, buffer, sems.at[i])
            for i, (source, buffer) in enumerate(zip(sources, buffers))
        ]
        for copy in self.copies:
            copy.start()
        self.buffers = buffers
        self.next = 0

    def get(self):
        self.copies[self.next].wait()
        self.next += 1
        return self.buffers[self.next - 1]


class Saves:
    def __init__(self, buffers, targets, sems):
        self.pairs, self.sems = list(zip(buffers, targets)), sems

    def copies(self, part, start, rows):
        here = pl.ds(start, rows)
        return [
            pltpu.make_async_copy(buffer.at[here], target.at[here], self.sems.at[i, part])
            for i, (buffer, target) in enumerate(self.pairs)
        ]

    def put(self, part, start, rows):
        for copy in self.copies(part, start, rows):
            copy.start()

    def finish(self, part, start, rows):
        for copy in self.copies(part, start, rows):
            copy.wait()


class Place:
    AXES = {"core": (PATCH, 1), "zl": (PATCH, 2), "zh": (PATCH, 4), "x": (CLIP, 1), "y": (CLIP, 2)}

    def __init__(self):
        self.clip, self.patch = lax.axis_index(CLIP), lax.axis_index(PATCH)
        self.me = {
            "core": lax.rem(self.patch, 2),
            "zl": lax.rem(self.patch // 2, 2),
            "zh": self.patch // 4,
            "x": lax.rem(self.clip, 2),
            "y": self.clip // 2,
        }

    def peer(self, dim):
        axis, stride = self.AXES[dim]
        own = self.clip if axis == CLIP else self.patch
        other = own + stride - 2 * stride * self.me[dim]
        return (other, self.patch) if axis == CLIP else (self.clip, other)


class Shuffle:
    def __init__(self, lay, at, sent, got, send_sem, recv_sem):
        self.lay, self.devices, self.parts, self.at = lay, lay.devices, lay.parts(), at
        self.sent, self.got, self.send_sem, self.recv_sem = sent, got, send_sem, recv_sem
        self.moves = 0

    def greet(self):
        for offset in range(1, self.devices):
            other = (self.at.clip, lax.rem(self.at.patch + offset, self.devices))
            pl.semaphore_signal(pltpu.get_barrier_semaphore(), inc=1, device_id=other, device_id_type=MESH)

    def meet(self, others=0):
        pl.semaphore_wait(pltpu.get_barrier_semaphore(), self.devices - 1 + others)

    def copy(self, offset, part):
        two = self.moves % 2
        other = lax.rem(self.at.patch + offset, self.devices)
        low, high = self.parts[part]
        rows = pl.ds(low, high - low)
        return pltpu.make_async_remote_copy(
            src_ref=self.sent.at[other, rows],
            dst_ref=self.got.at[two, self.at.patch, rows],
            send_sem=self.send_sem.at[part, offset],
            recv_sem=self.recv_sem.at[two, part, offset],
            device_id=(self.at.clip, other),
            device_id_type=MESH,
        )

    def send(self, part, order_ref, source_ref, first, last):
        width = self.sent.shape[-1]
        low, high = self.parts[part]
        rows = (high - low) * self.devices
        start = low * self.devices
        ids = lax.broadcasted_iota(jnp.int32, (rows, last - first), 1) + first
        pick = (order_ref[start : start + rows, :] == ids).astype(f32).astype(bf16)
        picked = dot_nn(pick, source_ref[first:last, :]).astype(bf16)
        self.sent[:, low:high, :] = picked.reshape(self.devices, high - low, width)
        for offset in range(1, self.devices):
            self.copy(offset, part).start()
        self.got[self.moves % 2, self.at.patch, low:high, :] = self.sent[self.at.patch, low:high, :]

    def send_all(self, order_ref, source_ref):
        for part in range(len(self.parts)):
            self.send(part, order_ref, source_ref, 0, source_ref.shape[0])

    def arrive(self, part):
        for offset in range(1, self.devices):
            self.copy(offset, part).wait()

    def receive(self, order_ref, target_ref):
        for part in range(len(self.parts)):
            self.arrive(part)
        devices, block, width = self.got.shape[1:]
        rows = target_ref.shape[0] // 3
        ids = lax.broadcasted_iota(jnp.int32, (rows, devices * block), 1)
        for start in range(0, target_ref.shape[0], rows):
            pick = (order_ref[start : start + rows, :] == ids).astype(f32).astype(bf16)
            got = self.got[self.moves % 2].reshape(devices * block, width)
            target_ref[start : start + rows, :] = dot_nn(pick, got).astype(bf16)
        self.moves += 1

    def receive_frame(self, frame, order_ref, target_ref):
        self.arrive(frame)
        low, high = self.lay.frame_rows(frame)
        patches = self.lay.all_patches
        here = slice(frame * patches, (frame + 1) * patches)
        width = self.got.shape[-1]
        got = self.got[self.moves % 2, :, low:high, :].reshape(self.devices * (high - low), width)
        ids = lax.broadcasted_iota(jnp.int32, (patches, got.shape[0]), 1)
        pick = (order_ref[here, :] == ids).astype(f32).astype(bf16)
        target_ref[here, :] = dot_nn(pick, got).astype(bf16)


def slot_of(lengths_ref, frames):
    end, slot = 0, 0
    for clip in range(lengths_ref.shape[0]):
        end = end + lengths_ref[clip]
        slot = slot + (frames >= end).astype(jnp.int32)
    return slot


def fill_bias(lengths_ref, frames, bias_ref):
    rows = bias_ref.shape[0]

    def split(ids, size, count):
        which = jnp.zeros_like(ids)
        for i in range(1, count):
            which = which + (ids >= i * size).astype(jnp.int32)
        return which, ids - which * size

    key_patch, key_frame = split(lax.broadcasted_iota(jnp.int32, bias_ref.shape, 0), frames, rows // frames)
    _, query = split(lax.broadcasted_iota(jnp.int32, bias_ref.shape, 1), rows, QUAD)
    query_patch, query_frame = split(query, frames, rows // frames)
    same = (key_patch == query_patch) & (slot_of(lengths_ref, key_frame) == slot_of(lengths_ref, query_frame))
    bias_ref[...] = jnp.where(same, 0.0, NEG_LARGE).astype(f32)


def cls_rows_of(cls_ref):
    values = cls_ref[...].astype(f32)
    return jnp.concatenate([values, jnp.zeros((CLS_ROWS - values.shape[0], values.shape[1]), f32)], 0)


def norm_row(norms_ref, layer, which):
    return norms_ref[which, layer : layer + 1, :]


def time_tiles(bias_ref, qkv_ref, width, group, grad_ref=None):
    rows = bias_ref.shape[0]
    here = pl.ds(pl.multiple_of(group * rows, 16), rows)
    tiles = []
    for quad in range(QUADS):
        tile = [qkv_ref[here, columns(part, quad, width)] for part in range(3)]
        if grad_ref is not None:
            tile.append(grad_ref[here, columns(0, quad, width)])
        tiles.append(tile)
    return here, tiles


def space_tiles(patches, total, slot, qkv_ref, width, frame, grad_ref=None):
    here = pl.ds(pl.multiple_of(frame * patches, 16), patches)
    tiles = []
    for quad in range(QUADS):
        tile = [qkv_ref[here, columns(part, quad, width)] for part in range(3)]
        for part in (1, 2):
            tile[part] = with_class(slot, tile[part], qkv_ref[total : total + CLS_ROWS, columns(part, quad, width)])
        if grad_ref is not None:
            tile.append(grad_ref[here, columns(0, quad, width)])
        tiles.append(tile)
    return here, tiles


def group_parts(lay, rows):
    ends = []
    for _, high in lay.parts():
        patches = min(-(-high // lay.away_frames), lay.patches)
        ends.append(-(-patches * lay.frames // rows) * rows)
    return tuple(zip([0] + ends[:-1], ends))


SAVED = ("normed_t", "qkv_t", "mixed_t", "x_away", "normed_s", "qkv_s", "mixed_s", "middle", "normed_f", "active", "slope")
WEIGHTS = ("time_proj", "time_output", "space_proj", "space_output", "up", "down")


def forward_kernel(lay, *refs):
    lengths_ref, norms_ref, shifts_ref, cls_ref, leave_frame, reach_frame, leave_away, reach_home = refs[:8]
    refs = refs[1:]
    sources = dict(zip(WEIGHTS, refs[7:13]))
    tokens_hbm, grad_hbm = refs[13:15]
    home_hbm, grad_away_hbm, result_hbm = refs[15:18]
    saved = [dict(zip(SAVED, refs[18 + len(SAVED) * layer :][: len(SAVED)])) for layer in range(LAYERS)]
    refs = refs[18 + len(SAVED) * LAYERS :]
    weights = dict(zip(WEIGHTS, refs[:6]))
    staged = dict(zip(SAVED, refs[6 : 6 + len(SAVED)]))
    bias_ref, x_home, after, grad, grad_away = refs[6 + len(SAVED) :][:5]
    sem_weight, sem_ends, sem_time, sem_space, sem_cls, *moving = refs[11 + len(SAVED) :]
    normed_t, qkv_t, mixed_t, x_away, normed, qkv, mixed, middle, normed_f, active, slope = (staged[name] for name in SAVED)
    total, width = x_away.shape
    home = x_home.shape[0]
    patches, frames = lay.all_patches, lay.away_frames
    group = bias_ref.shape[0]
    columns_of = [slice(start, start + width) for start in range(0, 3 * width, width)]

    load_x = pltpu.make_async_copy(tokens_hbm, x_home, sem_ends.at[0])
    load_grad = pltpu.make_async_copy(grad_hbm, grad, sem_ends.at[1])
    save_home = pltpu.make_async_copy(x_home, home_hbm, sem_ends.at[2])
    save_result = pltpu.make_async_copy(after, result_hbm, sem_ends.at[3])
    save_grad = pltpu.make_async_copy(grad_away, grad_away_hbm, sem_ends.at[4])
    load_x.start()
    load_grad.start()

    def fetch(layer, i):
        return pltpu.make_async_copy(sources[WEIGHTS[i]].at[layer], weights[WEIGHTS[i]], sem_weight.at[i])

    fetch(0, 0).start()
    at = Place()
    coming, leaving = [Shuffle(lay, at, *moving[:4]) for _ in range(2)]
    extra = Shuffle(lay, at, *moving[4:])
    coming.parts = extra.parts = lay.frame_parts()
    coming.greet()
    fill_bias(lengths_ref, lay.frames, bias_ref)
    key_mask = key_bias(patches)
    cls = cls_rows_of(cls_ref)
    load_grad.wait()
    coming.meet()
    extra.send(0, leave_frame, grad, 0, home)
    load_x.wait()

    for layer in range(LAYERS):
        more = layer < LAYERS - 1
        coming.moves, leaving.moves = 2 * layer, 2 * layer + 1
        if not more:
            extra.send(1, leave_frame, grad, 0, home)
        here = saved[layer]
        time_saves = Saves([staged[name] for name in SAVED[:3]], [here[name] for name in SAVED[:3]], sem_time)
        space_saves = Saves([staged[name] for name in SAVED[3:]], [here[name] for name in SAVED[3:]], sem_space)
        cls_saves = Saves([normed, qkv], [here["normed_s"], here["qkv_s"]], sem_cls)

        gain, shift = norm_row(norms_ref, layer, 0), norm_row(shifts_ref, layer, 0)
        for start in range(0, home, home // 3):
            rows = slice(start, start + home // 3)
            normed_t[rows, :] = norm_forward(x_home[rows, :].astype(f32), gain, shift)
        fetch(layer, 0).wait()
        if layer == 0:
            for i in range(1, len(WEIGHTS)):
                fetch(0, i).start()
        for these in columns_of:
            qkv_t[:, these] = dot_nn(normed_t[...], weights["time_proj"][:, these]).astype(bf16)
        if more:
            fetch(layer + 1, 0).start()

        @pl.loop(0, home // group)
        def _(index):
            rows, tiles = time_tiles(bias_ref, qkv_t, width, index)
            for quad, done in enumerate(forward_tiles(tiles, bias_ref[...])):
                mixed_t[rows, columns(0, quad, width)] = done

        fetch(layer, 1).wait()
        after[...] = (x_home[...].astype(f32) + dot_nn(mixed_t[...], weights["time_output"][...])).astype(bf16)
        for part in range(frames):
            coming.send(part, leave_frame, after, 0, home)
        if more:
            fetch(layer + 1, 1).start()
        time_saves.put(0, 0, home)

        gain, shift = norm_row(norms_ref, layer, 1), norm_row(shifts_ref, layer, 1)
        gain_f, shift_f = norm_row(norms_ref, layer, 2), norm_row(shifts_ref, layer, 2)
        normed[total:, :] = norm_forward(cls, gain, shift)
        fetch(layer, 2).wait()
        for these in columns_of:
            qkv[total:, these] = dot_nn(normed[total:, :], weights["space_proj"][:, these]).astype(bf16)
        cls_saves.put(0, total, CLS_ROWS)
        for i in range(3, len(WEIGHTS)):
            fetch(layer, i).wait()

        @pl.loop(0, frames)
        def _(frame, layer=layer, more=more, space_saves=space_saves, gain=gain, shift=shift, gain_f=gain_f, shift_f=shift_f):
            for number in range(frames):

                @pl.when(frame == number)
                def _(number=number, more=more):
                    coming.receive_frame(number, reach_frame, x_away)
                    if number == frames - 1 and not more:
                        extra.send(2, leave_frame, grad, 0, home)

            start = pl.multiple_of(frame * patches, 16)
            rows = pl.ds(start, patches)
            normed[rows, :] = norm_forward(x_away[rows, :].astype(f32), gain, shift)
            for these in columns_of:
                qkv[rows, these] = dot_nn(normed[rows, :], weights["space_proj"][:, these]).astype(bf16)
            slot = slot_of(lengths_ref, at.patch * frames + frame)
            _, tiles = space_tiles(patches, total, slot, qkv, width, frame)
            for quad, done in enumerate(forward_tiles(tiles, key_mask)):
                mixed[rows, columns(0, quad, width)] = done
            residual = x_away[rows, :].astype(f32) + dot_nn(mixed[rows, :], weights["space_output"][...])
            middle[rows, :] = residual.astype(bf16)
            normed_f[rows, :] = norm_forward(residual, gain_f, shift_f)
            for column in range(0, active.shape[1], WIDE):
                these = slice(column, column + WIDE)
                hidden = dot_nn(normed_f[rows, :], weights["up"][:, these])
                share = 0.5 * (1.0 + lax.erf(hidden * ROOT_HALF))
                active[rows, these] = (hidden * share).astype(bf16)
                bend = share + hidden * (INV_ROOT_TWO_PI * jnp.exp(-0.5 * hidden * hidden))
                slope[rows, these] = bend.astype(bf16)
            after[rows, :] = (residual + dot_nn(active[rows, :], weights["down"][...])).astype(bf16)
            space_saves.put(frame, start, patches)
            for number in range(frames - 1):

                @pl.when(frame == number)
                def _(number=number, more=more):
                    if more:
                        leaving.send(number, leave_away, after, 0, (number + 1) * patches)

        time_saves.finish(0, 0, home)
        if more:
            leaving.send(frames - 1, leave_away, after, (frames - 2) * patches, total)
            for i in range(2, len(WEIGHTS)):
                fetch(layer + 1, i).start()
            leaving.receive(reach_home, x_home)
            save_home.start()
        else:
            save_result.start()
            for frame in range(frames):
                extra.receive_frame(frame, reach_frame, grad_away)
            save_grad.start()
        for frame in range(frames):
            space_saves.finish(frame, frame * patches, patches)
        cls_saves.finish(0, total, CLS_ROWS)
    for copy in (save_home, save_result, save_grad):
        copy.wait()


CHUNKS = 16
TOTAL = CHUNKS * LAYERS
BLOCKS = 3
PIECE = (48, 128)
ROUTES = (("x", "zl", "zh", "y", "x", "y"), ("y", "zl", "zh", "x", "x", "y"), ("x", "y", "zl", "zh", "x", "y"))
SUMS = 4
STAGES = 7
RAW_SLOTS = 8
ACC_SLOTS = 8
BOX_SLOTS = 4
STRIDE = 2
SEGMENTS = (4, 4, 1, 3, 1, 3)
PLAN = {
    1: dict(early=4, down=2, hidden=2, wide=0, norm=2, frames=(0, 0, 0), up=1, space_out=0, space_proj=0, time_early=0, home=1, time0=1, time1=1, time2=2, time_out=0, time_proj=4),
    0: dict(early=1, down=0, hidden=1, wide=0, norm=2, frames=(0, 1, 1), up=0, space_out=2, space_proj=2, time_early=1, home=2, time0=0, time1=2, time2=0, time_out=0, time_proj=0),
}
SMALL = ("core", "zl", "zh", "x", "y")
SMALL_ROWS = 24


def recv_shape(route, stage):
    left = [dim for dim in ("zh", "zl", "x", "y") if dim not in route[: stage + 1]]
    return (2,) * len(left) + PIECE


class Pump:
    def __init__(self, at, results, scratch):
        self.at, self.results = at, results
        self.raw, self.core_in, self.acc, self.out, *rest = scratch
        self.inboxes = rest[: BLOCKS * SUMS]
        self.core_send, self.core_recv, self.core_free, self.send_sem, self.recv_sem = rest[BLOCKS * SUMS :]
        self.made = self.stepped = 0

    def core_copy(self, c, z):
        slot = lax.rem(c, RAW_SLOTS)
        return pltpu.make_async_remote_copy(
            src_ref=self.raw.at[slot, z // 2, z % 2, 1 - self.at.me["core"]],
            dst_ref=self.core_in.at[slot, z // 2, z % 2],
            send_sem=self.core_send.at[slot, z],
            recv_sem=self.core_recv.at[slot, z],
            device_id=self.at.peer("core"),
            device_id_type=MESH,
        )

    def claim(self, c, known):
        if known >= RAW_SLOTS:
            pl.semaphore_wait(self.core_free, 1)

    def store(self, c, z, core, block, rows):
        slot = lax.rem(c, RAW_SLOTS)
        for xh in range(2):
            for yh in range(2):
                part = rows[xh * 48 : (xh + 1) * 48, yh * 128 : (yh + 1) * 128]
                self.raw[slot, z // 2, z % 2, core, block, xh, yh] = part.astype(bf16)

    def make_chunks(self, count, lhs, rhs):
        first = self.made

        def one(i, c, known):
            self.claim(c, known)
            for half in range(2):
                left = lhs(slice(half * 384, (half + 1) * 384))
                for block in range(BLOCKS):
                    done = dot_tn(left, rhs(i, block * 256))
                    for j in range(4):
                        self.store(c, half * 2 + j // 2, j % 2, block, done[j * 96 : (j + 1) * 96])
            for z in range(4):
                self.core_copy(c, z).start()

        if count == 1:
            one(0, first, first)
        else:
            assert (first >= RAW_SLOTS) == (first + count - 1 >= RAW_SLOTS)

            @pl.loop(0, count)
            def _(i):
                one(i, first + i, first)

        self.made += count
        assert self.made - self.stepped <= RAW_SLOTS

    def make_down(self, lhs, rhs):
        first = self.made

        @pl.loop(0, 4)
        def _(z):
            if first >= RAW_SLOTS:

                @pl.when(z == 0)
                def _():
                    pl.semaphore_wait(self.core_free, 4)

            for core in range(2):
                left = lhs(pl.ds(pl.multiple_of(z * 768 + core * 384, 128), 384))
                for block in range(BLOCKS):
                    done = dot_tn(left, rhs[:, block * 256 : (block + 1) * 256])
                    for c in range(4):
                        self.store_at(first + c, z, core, block, done[c * 96 : (c + 1) * 96])
            for c in range(4):
                slot = (first + c) % RAW_SLOTS
                zh, zl = z // 2, lax.rem(z, 2)
                pltpu.make_async_remote_copy(
                    src_ref=self.raw.at[slot, zh, zl, 1 - self.at.me["core"]],
                    dst_ref=self.core_in.at[slot, zh, zl],
                    send_sem=self.core_send.at[slot, z],
                    recv_sem=self.core_recv.at[slot, z],
                    device_id=self.at.peer("core"),
                    device_id_type=MESH,
                ).start()

        self.made += 4
        assert self.made - self.stepped <= RAW_SLOTS

    def store_at(self, c, z, core, block, rows):
        for xh in range(2):
            for yh in range(2):
                part = rows[xh * 48 : (xh + 1) * 48, yh * 128 : (yh + 1) * 128]
                self.raw[c % RAW_SLOTS, z // 2, lax.rem(z, 2), core, block, xh, yh] = part.astype(bf16)

    def part(self, c, block, stage, value):
        route = ROUTES[block]

        def pick(dim):
            if dim in route[:stage]:
                return self.at.me[dim]
            return value if dim == route[stage] else slice(None)

        return (lax.rem(c, ACC_SLOTS), pick("zh"), pick("zl"), block, pick("x"), pick("y"))

    def exchange(self, c, block, stage):
        me = self.at.me
        dim = ROUTES[block][stage]
        box = lax.rem(c, BOX_SLOTS)
        if stage < SUMS:
            src = self.acc.at[self.part(c, block, stage, 1 - me[dim])]
            dst = self.inboxes[block * SUMS + stage].at[box]
        else:
            slot = lax.rem(c, ACC_SLOTS)
            if stage == SUMS:
                src = dst = self.out.at[slot, block, me["x"], me["y"]]
            elif dim == "x":
                src = dst = self.out.at[slot, block, me["x"]]
            else:
                src = dst = self.out.at[slot, block, :, me["y"]]
        return pltpu.make_async_remote_copy(
            src_ref=src,
            dst_ref=dst,
            send_sem=self.send_sem.at[box, block, stage],
            recv_sem=self.recv_sem.at[box, block, stage],
            device_id=self.at.peer(dim),
            device_id_type=MESH,
        )

    def enter(self, c):
        me = self.at.me
        slot, into = lax.rem(c, RAW_SLOTS), lax.rem(c, ACC_SLOTS)
        for z in range(4):
            self.core_copy(c, z).wait()
        for zh in range(2):
            for zl in range(2):
                both = self.raw[slot, zh, zl, me["core"]].astype(f32) + self.core_in[slot, zh, zl].astype(f32)
                self.acc[into, zh, zl] = both.astype(bf16)

        @pl.when(c < TOTAL - RAW_SLOTS)
        def _():
            pl.semaphore_signal(self.core_free, inc=1, device_id=self.at.peer("core"), device_id_type=MESH)

        for block in range(BLOCKS):
            self.exchange(c, block, 0).start()

    def advance(self, c, stage):
        me = self.at.me
        slot, box = lax.rem(c, ACC_SLOTS), lax.rem(c, BOX_SLOTS)
        for block in range(BLOCKS):
            self.exchange(c, block, stage).wait()
            if stage < SUMS:
                where = self.part(c, block, stage, me[ROUTES[block][stage]])
                both = self.acc[where].astype(f32) + self.inboxes[block * SUMS + stage][box].astype(f32)
                if stage == SUMS - 1:
                    self.out[slot, block, me["x"], me["y"]] = both.astype(bf16)
                else:
                    self.acc[where] = both.astype(bf16)
            if stage + 1 < STAGES - 1:
                self.exchange(c, block, stage + 1).start()
            else:
                self.finish(c, block)

    def finish(self, c, block):
        slot = lax.rem(c, ACC_SLOTS)
        layer = LAYERS - 1 - c // CHUNKS
        inner = lax.rem(c, CHUNKS)
        start = 0
        for which, count in enumerate(SEGMENTS):

            @pl.when((inner >= start) & (inner < start + count))
            def _(which=which, start=start):
                for xh in range(2):
                    for yh in range(2):
                        part = self.out[slot, block, xh, yh]
                        column = block * 256 + yh * 128
                        if which == 0:
                            row = pl.multiple_of((inner - start) * 96 + xh * 48, 16)
                            self.results[which][layer, pl.ds(row, 48), column : column + 128] = part
                        else:
                            at = pl.ds(pl.multiple_of((inner - start) * 768 + column, 128), 128)
                            self.results[which][layer, xh * 48 : (xh + 1) * 48, at] = part

            start += count

    def run_step(self, t):
        for stage in reversed(range(STAGES)):
            c = t - STRIDE * stage

            @pl.when((c >= 0) & (c < TOTAL))
            def _(c=c, stage=stage):
                if stage == 0:
                    self.enter(c)
                else:
                    self.advance(c, stage - 1)

    def step(self, count=1):
        first = self.stepped
        self.stepped += count
        assert min(self.stepped, TOTAL) <= self.made

        @pl.loop(first, first + count)
        def _(t):
            self.run_step(t)

    def inside(self, count):
        first = self.stepped
        self.stepped += count
        assert min(self.stepped, TOTAL) <= self.made
        return first

    def frame_steps(self, counts):
        first = self.inside(sum(counts))
        a, b, c = counts

        def run(frame):
            second, third = (frame + 1) // 2, frame // 2
            low = first + a * second + b * third

            @pl.loop(low, low + a + (b - a) * second + (c - b) * third)
            def _(t):
                self.run_step(t)

        return run


class Small:
    def __init__(self, at, values, boxes, send_sem, recv_sem):
        self.at, self.values, self.boxes, self.send_sem, self.recv_sem = at, values, boxes, send_sem, recv_sem

    def rows(self, i):
        return SMALL_ROWS if i < 3 else 16

    def copy(self, i):
        part = pl.ds(0, self.rows(i))
        return pltpu.make_async_remote_copy(
            src_ref=self.values.at[part],
            dst_ref=self.boxes.at[i, part],
            send_sem=self.send_sem.at[i],
            recv_sem=self.recv_sem.at[i],
            device_id=self.at.peer(SMALL[i]),
            device_id_type=MESH,
        )

    def step(self, i):
        if i > 0:
            rows = slice(0, self.rows(i - 1))
            self.copy(i - 1).wait()
            self.values[rows] += self.boxes[i - 1, rows]
        if i < len(SMALL):
            self.copy(i).start()


class Ring:
    def __init__(self, sources, slots, sems):
        self.sources, self.slots, self.sems = sources, slots, sems
        self.depth = slots.shape[0]
        self.started = self.taken = 0
        for _ in range(self.depth):
            self.start()

    def copy(self, i):
        source = self.sources[i]
        slot = i % self.depth
        return pltpu.make_async_copy(source, self.slots.at[slot, pl.ds(0, source.shape[0])], self.sems.at[slot])

    def start(self):
        if self.started < len(self.sources):
            self.copy(self.started).start()
            self.started += 1

    def take(self):
        i = self.taken
        self.copy(i).wait()
        self.taken += 1
        return self.slots.at[i % self.depth, pl.ds(0, self.sources[i].shape[0])]

    def free(self):
        self.start()


class Single:
    def __init__(self, sources, buffer, sem):
        self.copies = [
            pltpu.make_async_copy(source, buffer.at[pl.ds(0, source.shape[0])], sem) for source in sources
        ]
        self.next = 0
        self.copies[0].start()

    def take(self):
        self.copies[self.next].wait()

    def free(self):
        self.next += 1
        if self.next < len(self.copies):
            self.copies[self.next].start()


def backward_kernel(lay, *refs):
    devices, patches = lay.devices, lay.all_patches
    lengths_ref, norms_ref, cls_ref, leave_home, reach_away, leave_away, reach_home = refs[:7]
    weights = dict(zip(WEIGHTS, refs[7:13]))
    grad_hbm, x_out_hbm = refs[13:15]
    names = ("x_home",) + SAVED
    refs = refs[15:]
    saved = [dict(zip(names, refs[len(names) * layer : len(names) * (layer + 1)])) for layer in range(LAYERS)]
    refs = refs[len(names) * LAYERS :]
    small_ref, *results, output_hbm, tokens_hbm = refs[:9]
    refs = refs[9:]
    hidden, qkv, dqkv, wide, mixed, branch, x_buf, grad_buf, home_buf, cls_sum, bias_ref, *refs = refs
    weight_slots, lhs_slots, sent, got, small_boxes, *sums = refs[:11]
    sem_hidden, sem_qkv, sem_x, sem_ends, sem_weight, sem_lhs, sem_sent, sem_got, small_send, small_recv = refs[11:21]
    pump_scratch = refs[21:]
    load_grad = pltpu.make_async_copy(grad_hbm, grad_buf, sem_ends.at[0])
    load_out = pltpu.make_async_copy(x_out_hbm, mixed, sem_ends.at[1])
    save_out = pltpu.make_async_copy(home_buf, output_hbm, sem_ends.at[2])
    save_tokens = pltpu.make_async_copy(mixed, tokens_hbm, sem_ends.at[3])
    load_out.start()
    load_grad.start()

    at = Place()
    shuffle = Shuffle(lay, at, sent, got, sem_sent, sem_got)
    shuffle.greet()
    for dim in ("x", "y"):
        pl.semaphore_signal(pltpu.get_barrier_semaphore(), inc=1, device_id=at.peer(dim), device_id_type=MESH)

    total, width = grad_buf.shape
    parts = range(0, 3 * width, width)
    order = tuple(reversed(range(LAYERS)))
    tiles, lhs = [], []
    for layer in order:
        wide_parts = range(0, weights["up"].shape[2], width)
        tiles += [weights["down"].at[layer, pl.ds(start, width), :] for start in wide_parts]
        tiles += [weights["up"].at[layer, :, pl.ds(start, width)] for start in wide_parts]
        tiles += [weights["space_output"].at[layer]]
        tiles += [weights["space_proj"].at[layer, :, pl.ds(start, width)] for start in parts]
        tiles += [weights["time_output"].at[layer]]
        tiles += [weights["time_proj"].at[layer, :, pl.ds(start, width)] for start in parts]
        here = saved[layer]
        lhs += [here["slope"].at[:, pl.ds(start, width)] for start in wide_parts]
        lhs += [here[name] for name in ("normed_f", "mixed_s", "normed_s", "mixed_t", "normed_t")]
    fill = Single([saved[layer]["active"] for layer in order], hidden, sem_hidden)
    ring = Ring(tiles, weight_slots, sem_weight)
    left = Ring(lhs, lhs_slots, sem_lhs)
    load_qkv = Single([saved[layer][name] for layer in order for name in ("qkv_s", "qkv_t")], qkv, sem_qkv)
    load_x = Single(
        [saved[layer][name] for layer in order for name in ("middle", "x_away", "x_home")], x_buf, sem_x
    )
    pump = Pump(at, results, pump_scratch)
    small = Small(at, small_ref, small_boxes, small_send, small_recv)
    for part in sums:
        part[...] = jnp.zeros_like(part)
    small_ref[...] = jnp.zeros_like(small_ref)
    key_mask = key_bias(patches)
    cls = cls_rows_of(cls_ref)
    fill_bias(lengths_ref, lay.frames, bias_ref)

    def back_product(rows, source, count):
        for i in range(count):
            tile = ring.take()
            part = dot_nt(source[:rows, i * width : (i + 1) * width], tile[...])
            if i:
                wide[:rows, :] += part
            else:
                wide[:rows, :] = part
            ring.free()

    frames = total // patches
    group = bias_ref.shape[0]
    groups = group_parts(lay, group)

    def made_of(lhs_tile, source, first=0, rows=None):
        rows = source.shape[0] if rows is None else rows

        def rhs(i, start):
            column = pl.multiple_of((i + first) * width + start, 128) if not isinstance(i, int) else (i + first) * width + start
            return source[:rows, pl.ds(column, WIDE)]

        return (lambda these: lhs_tile[:, these]), rhs

    shuffle.meet(2)
    load_out.wait()
    shuffle.send_all(leave_away, mixed)
    load_grad.wait()
    dy = grad_buf

    for layer in order:
        last = layer == 0
        plan = PLAN[layer]

        def steps(site, plan=plan):
            if plan.get(site, 0):
                pump.step(plan[site])

        fill.take()
        pump.make_down(lambda these: hidden[:, these], dy)
        steps("down")
        for start in range(0, hidden.shape[1], width):
            tile, slope = ring.take(), left.take()
            for block in range(0, width, WIDE):
                grad_active = dot_nt(dy[...], tile[block : block + WIDE, :])
                grad_hidden = grad_active * slope[:, block : block + WIDE].astype(f32)
                hidden[:, start + block : start + block + WIDE] = grad_hidden.astype(bf16)
            ring.free()
            left.free()
        normed_f = left.take()
        if plan["early"]:
            pump.make_chunks(plan["early"], *made_of(normed_f, hidden))
        steps("hidden")
        back_product(total, hidden, hidden.shape[1] // width)
        steps("wide")
        load_x.take()

        @pl.loop(0, frames)
        def _(frame, layer=layer):
            here = pl.ds(pl.multiple_of(frame * patches, 16), patches)
            part = norm_backward(x_buf[here, :].astype(f32), wide[here, :], norm_row(norms_ref, layer, 2), sums[0:2])
            both = dy[here, :].astype(f32) + part
            wide[here, :] = both
            branch[here, :] = both.astype(bf16)

        load_x.free()
        if not last:
            shuffle.receive(reach_home, home_buf)
            save_out.start()
        steps("norm")

        out_tile, *proj_tiles = [ring.take() for _ in range(4)]
        load_qkv.take()
        load_x.take()
        cls_sum[...] = jnp.zeros_like(cls_sum)
        gain = norm_row(norms_ref, layer, 1)
        frame_run = pump.frame_steps(plan["frames"]) if sum(plan["frames"]) else None

        @pl.loop(0, frames)
        def _(frame):
            here = pl.ds(pl.multiple_of(frame * patches, 16), patches)
            mixed[here, :] = dot_nt(branch[here, :], out_tile[...]).astype(bf16)
            slot = slot_of(lengths_ref, at.patch * frames + frame)
            _, these = space_tiles(patches, total, slot, qkv, width, frame, mixed)
            row_ids = lax.broadcasted_iota(jnp.int32, (patches, WIDE), 0)
            cls_ids = lax.broadcasted_iota(jnp.int32, (CLS_ROWS, WIDE), 0)
            for quad, grads in enumerate(backward_tiles(these, key_mask)):
                dqkv[here, columns(0, quad, width)] = grads[0].astype(bf16)
                for part in (1, 2):
                    where = columns(part, quad, width)
                    dqkv[here, where] = jnp.where(row_ids < REAL_PATCH, grads[part], 0.0).astype(bf16)
                    row = grads[part][REAL_PATCH : REAL_PATCH + 1]
                    cls_sum[:, where] += jnp.where(cls_ids == slot, row, 0.0)
            grad = sum(dot_nt(dqkv[here, i * width : (i + 1) * width], tile[...]) for i, tile in enumerate(proj_tiles))
            part = norm_backward(x_buf[here, :].astype(f32), grad, gain, sums[2:4])
            mixed[here, :] = (wide[here, :] + part).astype(bf16)
            for i in range(2):

                @pl.when(frame == i)
                def _(i=i):
                    shuffle.send(i, leave_away, mixed, 0, (i + 1) * patches)

            if frame_run is not None:
                frame_run(frame)

        shuffle.send(2, leave_away, mixed, patches, total)
        load_x.free()
        load_qkv.free()
        dqkv[total:, :] = cls_sum[...].astype(bf16)
        grad = sum(dot_nt(dqkv[total:, i * width : (i + 1) * width], tile[...]) for i, tile in enumerate(proj_tiles))
        for _ in range(4):
            ring.free()
        part = norm_backward(cls, grad, gain, sums[2:4])
        small_ref[16:24] += part[:8]
        if plan["early"] < 4:
            pump.make_chunks(4 - plan["early"], *made_of(normed_f, hidden, plan["early"]))
        left.free()
        fill.free()
        steps("up")
        pump.make_chunks(1, *made_of(left.take(), branch))
        left.free()
        steps("space_out")
        pump.make_chunks(3, *made_of(left.take(), dqkv))
        left.free()
        steps("space_proj")
        if not last:
            save_out.wait()
        shuffle.receive(reach_home, home_buf)

        out_tile, *proj_tiles = [ring.take() for _ in range(4)]
        load_qkv.take()
        load_x.take()
        mixed_t = left.take()
        if plan["time_early"]:
            pump.make_chunks(1, *made_of(mixed_t, home_buf))
            left.free()
        steps("home")
        for number, (first, end) in enumerate(groups):
            here = slice(first, end)
            mixed[here, :] = dot_nt(home_buf[here, :], out_tile[...]).astype(bf16)

            @pl.loop(first // group, end // group)
            def _(index):
                at_rows, these = time_tiles(bias_ref, qkv, width, index, mixed)
                for quad, grads in enumerate(backward_tiles(these, bias_ref[...])):
                    for part in range(3):
                        dqkv[at_rows, columns(part, quad, width)] = grads[part].astype(bf16)

            grad = sum(dot_nt(dqkv[here, i * width : (i + 1) * width], tile[...]) for i, tile in enumerate(proj_tiles))
            part = norm_backward(x_buf[here, :].astype(f32), grad, norm_row(norms_ref, layer, 0), sums[4:6])
            mixed[here, :] = (home_buf[here, :].astype(f32) + part).astype(bf16)
            if not last:
                shuffle.send(number, leave_home, mixed, 0 if number < 2 else first, end)
            steps("time%d" % number)
        load_qkv.free()
        load_x.free()
        for _ in range(4):
            ring.free()
        for i, part in enumerate(sums):
            row = layer * 8 + (2, 5, 1, 4, 0, 3)[i]
            small_ref[row : row + 1, :] += jnp.sum(part[...], 0, keepdims=True)
            part[...] = jnp.zeros_like(part)
        if last:
            save_tokens.start()
            small.step(0)
        if not plan["time_early"]:
            pump.make_chunks(1, *made_of(mixed_t, home_buf))
            left.free()
        steps("time_out")
        pump.make_chunks(3, *made_of(left.take(), dqkv, rows=total))
        left.free()
        steps("time_proj")
        if last:
            for i in range(1, len(SMALL) + 1):
                pump.step()
                small.step(i)
        else:
            shuffle.receive(reach_away, grad_buf)

    pump.step(TOTAL + STRIDE * (STAGES - 1) - pump.stepped)
    save_tokens.wait()


IN_VMEM = pl.BlockSpec(memory_space=pltpu.VMEM)
IN_SMEM = pl.BlockSpec(memory_space=pltpu.SMEM)
IN_HBM = pl.BlockSpec(memory_space=pl.ANY)


def shape(*dims, kind=bf16):
    return jax.ShapeDtypeStruct(dims, kind)


def vmem(*dims, kind=bf16):
    return pltpu.VMEM(dims, kind)


def queue(*counts):
    return pltpu.SemaphoreType.DMA(counts)


def whole_call(name, body, collective, near, far, out_near, out_far, scratch):
    return pl.pallas_call(
        body,
        in_specs=[IN_SMEM if part.ndim == 1 else IN_VMEM for part in near] + [IN_HBM] * len(far),
        out_specs=[IN_VMEM] * len(out_near) + [IN_HBM] * len(out_far),
        out_shape=[*out_near, *out_far],
        scratch_shapes=scratch,
        compiler_params=pltpu.CompilerParams(
            collective_id=collective, has_side_effects=True, vmem_limit_bytes=VMEM_MOST
        ),
        name=name,
    )(*near, *far)


def finish_kernel(small_ref, *refs):
    count = len(refs) // 2
    for source, target in zip(refs[:count], refs[count:-1]):
        target[...] = source[...].astype(target.dtype)
    refs[-1][...] = small_ref[16 : 16 + refs[-1].shape[0], :]


def finish(small, clip_count, parts, kinds, steps=6):
    specs, out = [], []
    width = small.shape[1]
    cls = jax.ShapeDtypeStruct((clip_count, width), f32)
    for part, kind in zip(parts, kinds):
        cut = part.ndim - 1 if part.shape[-1] % (steps * 128) == 0 else part.ndim - 2
        block = tuple(size // steps if dim == cut else size for dim, size in enumerate(part.shape))

        def index(i, cut=cut, ndim=part.ndim):
            return tuple(i if dim == cut else 0 for dim in range(ndim))

        specs.append(pl.BlockSpec(block, index))
        out.append(jax.ShapeDtypeStruct(part.shape, kind))
    return pl.pallas_call(
        finish_kernel,
        grid=(steps,),
        in_specs=[pl.BlockSpec(small.shape, lambda i: (0, 0)), *specs],
        out_specs=[*specs, pl.BlockSpec(cls.shape, lambda i: (0, 0))],
        out_shape=[*out, cls],
        compiler_params=pltpu.CompilerParams(vmem_limit_bytes=VMEM_MOST),
        name="finish",
    )(small, *parts)


def fast_local(
    tokens,
    cls_tokens,
    clip_lengths,
    time_proj,
    time_output,
    space_proj,
    space_output,
    up_weight,
    down_weight,
    norm_gains,
    norm_biases,
    cotangent,
):
    frames, patch_rows, width = tokens.shape
    devices = lax.axis_size(PATCH)
    hidden = up_weight.shape[2]
    lay = Layout(devices, frames, patch_rows)
    home, away, block = lay.home_rows, lay.away_rows, lay.block
    clip_count = cls_tokens.shape[0]
    group = group_rows(patch_rows, frames)
    orders = {name: jnp.asarray(part) for name, part in lay.orders().items()}

    def home_order(values):
        return jnp.transpose(values, (1, 0, 2)).reshape(home, width)

    def given_order(values):
        return jnp.transpose(values.reshape(patch_rows, frames, width), (1, 0, 2))

    parts = len(lay.parts())
    moving = [vmem(devices, block, width), vmem(2, devices, block, width), queue(parts, devices), queue(2, parts, devices)]
    extra = [vmem(devices, block, width), vmem(1, devices, block, width), queue(parts, devices), queue(1, parts, devices)]
    gains, shifts = [jnp.transpose(part, (1, 0, 2)) for part in (norm_gains, norm_biases)]
    lengths = clip_lengths[0]
    weights = (time_proj, time_output, space_proj, space_output, up_weight, down_weight)
    at_home = home_order(tokens)
    saved_shapes = [
        shape(home, width),
        shape(home, 3 * width),
        shape(home, width),
        shape(away, width),
        shape(away + CLS_ROWS, width),
        shape(away + CLS_ROWS, 3 * width),
        *[shape(away, width)] * 3,
        *[shape(away, hidden)] * 2,
    ]
    bias = vmem(group, QUAD * group, kind=f32)
    home_next, grad_away, x_out, *saved = whole_call(
        "forward",
        functools.partial(forward_kernel, lay),
        2,
        (lengths, gains, shifts, cls_tokens, *[orders[name] for name in ("leave_frame", "reach_frame", "leave_away", "reach_home")]),
        (*weights, at_home, home_order(cotangent)),
        [],
        [shape(home, width), shape(away, width), shape(away, width)] + saved_shapes * LAYERS,
        [
            *[vmem(*part.shape[1:]) for part in weights],
            *[vmem(*part.shape) for part in saved_shapes],
            bias,
            vmem(home, width),
            vmem(away, width),
            vmem(home, width),
            vmem(away, width),
            queue(len(weights)),
            queue(5),
            queue(3, 1),
            queue(len(SAVED) - 3, lay.away_frames),
            queue(2, 1),
            *moving,
            *extra,
        ],
    )
    stored = [(at_home, *saved[: len(SAVED)]), (home_next, *saved[len(SAVED) :])]

    inbox = [vmem(BOX_SLOTS, *recv_shape(ROUTES[b], s)) for b in range(BLOCKS) for s in range(SUMS)]
    single = pltpu.SemaphoreType.DMA
    share = width // devices
    small, *large, output, grad_tokens = whole_call(
        "backward",
        functools.partial(backward_kernel, lay),
        1,
        (lengths, gains, cls_tokens, *[orders[name] for name in ("leave_patch", "reach_patch", "leave_away", "reach_home")]),
        (*weights, grad_away, x_out, *stored[0], *stored[1]),
        [
            shape(SMALL_ROWS, width, kind=f32),
            shape(LAYERS, hidden // devices, width),
            shape(LAYERS, share, hidden),
            shape(LAYERS, share, width),
            shape(LAYERS, share, 3 * width),
            shape(LAYERS, share, width),
            shape(LAYERS, share, 3 * width),
        ],
        [shape(home, width), shape(home, width)],
        [
            vmem(away, hidden),
            vmem(away + CLS_ROWS, 3 * width),
            vmem(away + CLS_ROWS, 3 * width),
            vmem(away, width, kind=f32),
            *[vmem(away, width)] * 5,
            vmem(CLS_ROWS, 3 * width, kind=f32),
            bias,
            vmem(4, width, width),
            vmem(2, away + CLS_ROWS, width),
            *moving[:2],
            vmem(len(SMALL), SMALL_ROWS, width, kind=f32),
            *[vmem(8, width, kind=f32)] * 6,
            single,
            single,
            single,
            queue(4),
            queue(4),
            queue(2),
            *moving[2:],
            queue(len(SMALL)),
            queue(len(SMALL)),
            vmem(RAW_SLOTS, 2, 2, 2, BLOCKS, 2, 2, *PIECE),
            vmem(RAW_SLOTS, 2, 2, BLOCKS, 2, 2, *PIECE),
            vmem(ACC_SLOTS, 2, 2, BLOCKS, 2, 2, *PIECE),
            vmem(ACC_SLOTS, BLOCKS, 2, 2, *PIECE),
            *inbox,
            queue(RAW_SLOTS, 4),
            queue(RAW_SLOTS, 4),
            pltpu.SemaphoreType.REGULAR,
            queue(BOX_SLOTS, BLOCKS, STAGES - 1),
            queue(BOX_SLOTS, BLOCKS, STAGES - 1),
        ],
    )
    large = [large[i] for i in (5, 4, 3, 2, 1, 0)]
    kinds = (f32,) * len(large) + (bf16,) * 2
    *large, output, grad_tokens, grad_cls = finish(small, clip_count, (*large, output, grad_tokens), kinds)
    small = lax.dynamic_slice_in_dim(small[:16], lax.axis_index(PATCH) * share, share, 1)
    small = small.reshape(LAYERS, 8, share)
    return (given_order(output), given_order(grad_tokens), grad_cls, *large, small[:, 0:3], small[:, 3:6])


def general_local(
    tokens,
    cls_tokens,
    clip_lengths,
    time_proj,
    time_output,
    space_proj,
    space_output,
    up_weight,
    down_weight,
    norm_gains,
    norm_biases,
    cotangent,
):
    frames, patch_rows, width = tokens.shape
    devices = lax.axis_size(PATCH)
    lay = Layout(devices, frames, patch_rows)
    away_rows = lay.away_rows
    patches = lay.all_patches
    clip_count = cls_tokens.shape[0]

    frame_ids = jnp.arange(frames, dtype=jnp.int32)
    slots = frame_slots(clip_lengths[0], frame_ids)
    bias = time_bias(slots[:, None] == slots[None, :], patch_rows, frames)
    my_frames = lax.axis_index(PATCH) * lay.away_frames + jnp.arange(lay.away_frames, dtype=jnp.int32)
    my_slots = jnp.where(my_frames < frames, frame_slots(clip_lengths[0], my_frames), -1)
    cls_pick = (my_slots[None, :] == jnp.arange(CLS_ROWS, dtype=jnp.int32)[:, None]).astype(f32)

    def home_order(values):
        return jnp.transpose(values, (1, 0, 2)).reshape(lay.home_rows, width)

    def given_order(values):
        return jnp.transpose(values.reshape(patch_rows, frames, width), (1, 0, 2))

    cls_aug = jnp.pad(cls_tokens.astype(f32), ((0, CLS_ROWS - clip_count), (0, 0)))
    residual = home_order(tokens).astype(f32)
    cotangent_away = lay.to_away(home_order(cotangent))
    stored = []
    for layer in range(LAYERS):
        gains, biases = norm_gains[layer], norm_biases[layer]
        normed, scaled_t, inverse_t = layer_norm(residual, gains[0], biases[0])
        normed_t = normed.astype(bf16)
        qkv_t = project(normed_t, time_proj[layer]).astype(bf16)
        mixed_t = time_forward(bias, qkv_t)
        residual = residual + project(mixed_t, time_output[layer])
        away = lay.to_away(residual.astype(bf16))
        away = away + jnp.pad(cls_aug, ((away_rows, 0), (0, 0)))
        normed, scaled_s, inverse_s = layer_norm(away, gains[1], biases[1])
        normed_s = normed.astype(bf16)
        qkv_s = project(normed_s, space_proj[layer]).astype(bf16)
        mixed_s = space_forward(my_slots, qkv_s, lay.away_frames, patches)
        away = away[:away_rows] + project(mixed_s, space_output[layer])
        normed, scaled_f, inverse_f = layer_norm(away, gains[2], biases[2])
        normed_f = normed.astype(bf16)
        hidden = project(normed_f, up_weight[layer])
        active = gelu_value(hidden).astype(bf16)
        away = away + project(active, down_weight[layer])
        residual = lay.to_home(away.astype(bf16))
        stored.append(
            dict(
                normed_t=normed_t, scaled_t=scaled_t, inverse_t=inverse_t, qkv_t=qkv_t, mixed_t=mixed_t,
                normed_s=normed_s, scaled_s=scaled_s, inverse_s=inverse_s, qkv_s=qkv_s, mixed_s=mixed_s,
                normed_f=normed_f, scaled_f=scaled_f, inverse_f=inverse_f, hidden=hidden, active=active,
            )
        )
    output = given_order(residual.astype(bf16))

    grad_cls = jnp.zeros_like(cls_aug)
    grad_away = cotangent_away[:away_rows]
    results = [None] * LAYERS
    for layer in reversed(range(LAYERS)):
        saved = stored[layer]
        gains = norm_gains[layer]
        branch = grad_away.astype(bf16)
        grad_down = weight_grad(saved["active"], branch)
        grad_active = project_back(branch, down_weight[layer])
        grad_hidden = (grad_active * gelu_slope(saved["hidden"])).astype(bf16)
        grad_up = weight_grad(saved["normed_f"], grad_hidden)
        grad_normed = project_back(grad_hidden, up_weight[layer])
        grad_input, gain_two, bias_two = norm_back(
            grad_normed, saved["scaled_f"], saved["inverse_f"], gains[2]
        )
        grad_away = grad_away + grad_input
        branch = grad_away.astype(bf16)
        grad_space_out = weight_grad(saved["mixed_s"], branch)
        grad_mixed = project_back(branch, space_output[layer]).astype(bf16)
        dq, dk, dv, dck, dcv = space_backward(my_slots, saved["qkv_s"], grad_mixed, lay.away_frames, patches)
        dcls = jnp.concatenate([dck[:, 0], dcv[:, 0]], -1)
        dcls = jnp.dot(cls_pick, dcls, precision=lax.Precision.HIGHEST)
        dcls = jnp.pad(dcls.astype(bf16), ((0, 0), (width, 0)))
        grad_qkv = jnp.concatenate([jnp.concatenate([dq, dk, dv], -1), dcls], 0)
        grad_space_proj = weight_grad(saved["normed_s"], grad_qkv)
        grad_normed = project_back(grad_qkv, space_proj[layer])
        grad_input, gain_one, bias_one = norm_back(
            grad_normed, saved["scaled_s"], saved["inverse_s"], gains[1]
        )
        grad_away = grad_away + grad_input[:away_rows]
        grad_cls = grad_cls + grad_input[away_rows:]
        grad_home = lay.to_home(grad_away.astype(bf16))
        branch = grad_home.astype(bf16)
        grad_time_out = weight_grad(saved["mixed_t"], branch)
        grad_mixed = project_back(branch, time_output[layer]).astype(bf16)
        grad_qkv = time_backward(bias, saved["qkv_t"], grad_mixed)
        grad_time_proj = weight_grad(saved["normed_t"], grad_qkv)
        grad_normed = project_back(grad_qkv, time_proj[layer])
        grad_input, gain_zero, bias_zero = norm_back(
            grad_normed, saved["scaled_t"], saved["inverse_t"], gains[0]
        )
        grad_home = grad_home + grad_input
        if layer > 0:
            grad_away = lay.to_away(grad_home.astype(bf16))[:away_rows]
        large = (grad_time_proj, grad_time_out, grad_space_proj, grad_space_out, grad_up, grad_down)
        large = [lax.psum_scatter(part, PATCH, scatter_dimension=0, tiled=True) for part in large]
        large = lax.psum(large, CLIP)
        small = (jnp.stack([gain_zero, gain_one, gain_two]), jnp.stack([bias_zero, bias_one, bias_two]))
        results[layer] = [part.astype(f32) for part in large] + list(small)
    grad_tokens = given_order(grad_home.astype(bf16))
    stacked = [jnp.stack([results[layer][i] for layer in range(LAYERS)]) for i in range(8)]
    small = jnp.stack(stacked[6:])
    small = lax.psum(small, (PATCH, CLIP))
    share = width // devices
    small = lax.dynamic_slice_in_dim(small, lax.axis_index(PATCH) * share, share, 3)
    grad_cls = lax.psum(grad_cls[:clip_count], PATCH)
    return (output, grad_tokens, grad_cls, *stacked[:6], small[0], small[1])


def solution(mesh):
    in_specs = (
        P(CLIP, PATCH, None),
        P(CLIP, None),
        P(CLIP, None),
        P(),
        P(),
        P(),
        P(),
        P(),
        P(),
        P(),
        P(),
        P(CLIP, PATCH, None),
    )
    out_specs = (
        P(CLIP, PATCH, None),
        P(CLIP, PATCH, None),
        P(CLIP, None),
        P(None, PATCH, None),
        P(None, PATCH, None),
        P(None, PATCH, None),
        P(None, PATCH, None),
        P(None, PATCH, None),
        P(None, PATCH, None),
        P(None, None, PATCH),
        P(None, None, PATCH),
    )
    paired = (mesh.shape[CLIP], mesh.shape[PATCH]) == (4, 8)
    local = fast_local if paired else general_local
    return jax.shard_map(local, mesh=mesh, in_specs=in_specs, out_specs=out_specs, check_vma=False)
```

```python
import functools

import jax
import jax.numpy as jnp
import numpy as np
from jax import lax
from jax.experimental import pallas as pl
from jax.experimental.pallas import tpu as pltpu
from jax.sharding import PartitionSpec as P

HEADS = 12
HD = 64
LAYERS = 2
REAL_PATCH = 196
QUAD = 4
WIDE = QUAD * HD
QUADS = HEADS // QUAD
CLS_ROWS = 16

EPSILON = 1e-05
NEG_LARGE = -1e30
ROOT_HALF = 0.7071067811865476
INV_ROOT_TWO_PI = 0.3989422804014327
SCALE = HD**-0.5
VMEM_LIMIT = 48 * 1024 * 1024
VMEM_MOST = 62 * 1024 * 1024

CLIP = "clip"
PATCH = "patch"
f32 = jnp.float32
bf16 = jnp.bfloat16
MESH = pl.DeviceIdType.MESH


def layer_norm(values, norm_gain, norm_bias):
    centered = values - jnp.mean(values, -1, keepdims=True)
    inverse = lax.rsqrt(jnp.mean(centered * centered, -1, keepdims=True) + EPSILON)
    scaled = centered * inverse
    return (scaled * norm_gain + norm_bias, scaled, inverse)


def norm_back(grad_out, scaled, inverse, norm_gain):
    weighted = grad_out * norm_gain
    grad_input = inverse * (
        weighted
        - jnp.mean(weighted, -1, keepdims=True)
        - scaled * jnp.mean(weighted * scaled, -1, keepdims=True)
    )
    return (grad_input, jnp.sum(grad_out * scaled, 0), jnp.sum(grad_out, 0))


def project(left, matrix):
    return jnp.dot(left, matrix, preferred_element_type=f32)


def project_back(grad_out, matrix):
    return lax.dot_general(grad_out, matrix, (((1,), (1,)), ((), ())), preferred_element_type=f32)


def weight_grad(left, grad_out):
    return lax.dot_general(
        left, grad_out, (((0,), (0,)), ((), ())), preferred_element_type=f32
    ).astype(bf16)


def gelu_value(hidden):
    return 0.5 * hidden * (1.0 + lax.erf(hidden * ROOT_HALF))


def gelu_slope(hidden):
    return 0.5 * (1.0 + lax.erf(hidden * ROOT_HALF)) + hidden * INV_ROOT_TWO_PI * jnp.exp(
        -0.5 * hidden * hidden
    )


def dot_nt(left, right):
    return lax.dot_general(left, right, (((1,), (1,)), ((), ())), preferred_element_type=f32)


def dot_nn(left, right):
    return lax.dot_general(left, right, (((1,), (0,)), ((), ())), preferred_element_type=f32)


def dot_tn(left, right):
    return lax.dot_general(left, right, (((0,), (0,)), ((), ())), preferred_element_type=f32)


def spread_heads(rows):
    head = lax.broadcasted_iota(jnp.int32, rows.shape, 1) // HD
    return jnp.concatenate([jnp.where(head == h, rows, jnp.zeros_like(rows)) for h in range(QUAD)], 0)


def merge_heads(stacked):
    count = stacked.shape[0] // QUAD
    head = lax.broadcasted_iota(jnp.int32, (count, WIDE), 1) // HD
    merged = stacked[:count]
    for h in range(1, QUAD):
        merged = jnp.where(head == h, stacked[h * count : (h + 1) * count], merged)
    return merged


def probabilities(scores):
    exponents = [jnp.exp(part - jnp.max(part, 0, keepdims=True)) for part in scores]
    return [part * (1.0 / jnp.sum(part, 0, keepdims=True)) for part in exponents]


def forward_tiles(tiles, bias):
    spreads = [spread_heads(tile[0] * SCALE) for tile in tiles]
    scores = [dot_nt(tile[1], spread) + bias for tile, spread in zip(tiles, spreads)]
    probs = [part.astype(bf16) for part in probabilities(scores)]
    outs = [dot_tn(part, tile[2]) for part, tile in zip(probs, tiles)]
    return [merge_heads(part).astype(bf16) for part in outs]


def backward_tiles(tiles, bias):
    spreads = [spread_heads(tile[0] * SCALE) for tile in tiles]
    grad_spreads = [spread_heads(tile[3]) for tile in tiles]
    scores = [dot_nt(tile[1], spread) + bias for tile, spread in zip(tiles, spreads)]
    grad_probs = [dot_nt(tile[2], spread) for tile, spread in zip(tiles, grad_spreads)]
    probs = probabilities(scores)
    grad_scores = [
        (part * (grad - jnp.sum(part * grad, 0, keepdims=True))).astype(bf16)
        for part, grad in zip(probs, grad_probs)
    ]
    grad_queries = [dot_tn(grad, tile[1]) for grad, tile in zip(grad_scores, tiles)]
    grad_keys = [dot_nn(grad, spread) for grad, spread in zip(grad_scores, spreads)]
    grad_values = [dot_nn(part.astype(bf16), spread) for part, spread in zip(probs, grad_spreads)]
    return [(merge_heads(q) * SCALE, k, v) for q, k, v in zip(grad_queries, grad_keys, grad_values)]


def columns(part, quad, width):
    start = part * width + quad * WIDE
    return slice(start, start + WIDE)


def time_forward_kernel(bias_ref, qkv_ref, out_ref):
    width = out_ref.shape[1]
    bias = bias_ref[...]
    for quad in range(QUADS):
        parts = [qkv_ref[:, columns(part, quad, width)] for part in range(3)]
        out_ref[:, columns(0, quad, width)] = forward_tiles([parts], bias)[0]


def time_backward_kernel(bias_ref, qkv_ref, grad_ref, out_ref):
    width = grad_ref.shape[1]
    bias = bias_ref[...]
    for quad in range(QUADS):
        parts = [qkv_ref[:, columns(part, quad, width)] for part in range(3)]
        grads = backward_tiles([parts + [grad_ref[:, columns(0, quad, width)]]], bias)[0]
        for part in range(3):
            out_ref[:, columns(part, quad, width)] = grads[part].astype(bf16)


def group_rows(patch_count, frames):
    return (2 if patch_count % 2 == 0 else 1) * frames


def time_bias(same_clip, patch_count, frames):
    rows = group_rows(patch_count, frames)
    ids = jnp.arange(rows, dtype=jnp.int32)
    same_patch = (ids[:, None] // frames) == (ids[None, :] // frames)
    tiled = jnp.tile(same_clip, (rows // frames, rows // frames))
    return jnp.tile(jnp.where(same_patch & tiled, 0.0, NEG_LARGE).astype(f32), (1, QUAD))


def params(*semantics):
    return pltpu.CompilerParams(dimension_semantics=semantics, vmem_limit_bytes=VMEM_LIMIT)


def time_forward(bias, qkv):
    rows = bias.shape[0]
    width = qkv.shape[1] // 3
    return pl.pallas_call(
        time_forward_kernel,
        grid=(qkv.shape[0] // rows,),
        in_specs=[
            pl.BlockSpec(bias.shape, lambda i: (0, 0)),
            pl.BlockSpec((rows, 3 * width), lambda i: (i, 0)),
        ],
        out_specs=pl.BlockSpec((rows, width), lambda i: (i, 0)),
        out_shape=jax.ShapeDtypeStruct((qkv.shape[0], width), bf16),
        compiler_params=params("parallel"),
        name="time_forward",
    )(bias, qkv)


def time_backward(bias, qkv, grad_out):
    rows = bias.shape[0]
    width = qkv.shape[1] // 3
    return pl.pallas_call(
        time_backward_kernel,
        grid=(qkv.shape[0] // rows,),
        in_specs=[
            pl.BlockSpec(bias.shape, lambda i: (0, 0)),
            pl.BlockSpec((rows, 3 * width), lambda i: (i, 0)),
            pl.BlockSpec((rows, width), lambda i: (i, 0)),
        ],
        out_specs=pl.BlockSpec((rows, 3 * width), lambda i: (i, 0)),
        out_shape=jax.ShapeDtypeStruct(qkv.shape, bf16),
        compiler_params=params("parallel"),
        name="time_backward",
    )(bias, qkv, grad_out)


def with_class(slot, rows, cls_rows):
    ids = lax.broadcasted_iota(jnp.int32, cls_rows.shape, 0)
    picked = jnp.sum(jnp.where(ids == slot, cls_rows.astype(f32), 0.0), 0, keepdims=True)
    row_ids = lax.broadcasted_iota(jnp.int32, rows.shape, 0)
    return jnp.where(row_ids == REAL_PATCH, picked.astype(bf16), rows)


def key_bias(count):
    key_ids = lax.broadcasted_iota(jnp.int32, (count, 1), 0)
    return jnp.where(key_ids <= REAL_PATCH, 0.0, NEG_LARGE).astype(f32)


def space_forward_kernel(slot_ref, q_ref, k_ref, v_ref, ck_ref, cv_ref, out_ref):
    slot = slot_ref[pl.program_id(0)]
    keys = with_class(slot, k_ref[...], ck_ref[...])
    values = with_class(slot, v_ref[...], cv_ref[...])
    out_ref[...] = forward_tiles([(q_ref[...], keys, values)], key_bias(keys.shape[0]))[0]


def space_backward_kernel(
    slot_ref, q_ref, k_ref, v_ref, ck_ref, cv_ref, g_ref, dq_ref, dk_ref, dv_ref, dck_ref, dcv_ref
):
    slot = slot_ref[pl.program_id(0)]
    keys = with_class(slot, k_ref[...], ck_ref[...])
    values = with_class(slot, v_ref[...], cv_ref[...])
    tile = (q_ref[...], keys, values, g_ref[...])
    grad_q, grad_k, grad_v = backward_tiles([tile], key_bias(keys.shape[0]))[0]
    row_ids = lax.broadcasted_iota(jnp.int32, grad_k.shape, 0)
    dq_ref[...] = grad_q.astype(bf16)
    dk_ref[...] = jnp.where(row_ids < REAL_PATCH, grad_k, 0.0).astype(bf16)
    dv_ref[...] = jnp.where(row_ids < REAL_PATCH, grad_v, 0.0).astype(bf16)
    dck_ref[0] = jnp.sum(jnp.where(row_ids == REAL_PATCH, grad_k, 0.0), 0, keepdims=True)
    dcv_ref[0] = jnp.sum(jnp.where(row_ids == REAL_PATCH, grad_v, 0.0), 0, keepdims=True)


def space_specs(frames, patches):
    cls_block = frames * patches // CLS_ROWS

    def rows(part):
        return pl.BlockSpec((patches, WIDE), lambda f, c, s: (f, part * QUADS + c))

    def cls(part):
        return pl.BlockSpec((CLS_ROWS, WIDE), lambda f, c, s: (cls_block, part * QUADS + c))

    return [rows(0), rows(1), rows(2), cls(1), cls(2)], rows(0)


def space_forward(slots, qkv, frames, patches):
    width = qkv.shape[1] // 3
    in_specs, out_spec = space_specs(frames, patches)
    return pl.pallas_call(
        space_forward_kernel,
        grid_spec=pltpu.PrefetchScalarGridSpec(
            num_scalar_prefetch=1,
            grid=(frames, QUADS),
            in_specs=in_specs,
            out_specs=out_spec,
        ),
        out_shape=jax.ShapeDtypeStruct((frames * patches, width), bf16),
        compiler_params=params("parallel", "parallel"),
        name="space_forward",
    )(slots, qkv, qkv, qkv, qkv, qkv)


def space_backward(slots, qkv, grad_out, frames, patches):
    width = qkv.shape[1] // 3
    in_specs, out_spec = space_specs(frames, patches)
    rows = jax.ShapeDtypeStruct((frames * patches, width), bf16)
    cls_spec = pl.BlockSpec((1, 1, WIDE), lambda f, c, s: (f, 0, c))
    cls = jax.ShapeDtypeStruct((frames, 1, width), f32)
    return pl.pallas_call(
        space_backward_kernel,
        grid_spec=pltpu.PrefetchScalarGridSpec(
            num_scalar_prefetch=1,
            grid=(frames, QUADS),
            in_specs=in_specs + [out_spec],
            out_specs=[out_spec] * 3 + [cls_spec] * 2,
        ),
        out_shape=[rows] * 3 + [cls] * 2,
        compiler_params=params("parallel", "parallel"),
        name="space_backward",
    )(slots, qkv, qkv, qkv, qkv, qkv, grad_out)


def frame_slots(lengths_row, frame_ids):
    clip_ends = jnp.cumsum(lengths_row)
    return jnp.sum((frame_ids[:, None] >= clip_ends[None, :]).astype(jnp.int32), axis=1)


class Layout:
    def __init__(self, devices, frames, patches):
        self.devices = devices
        self.frames = frames
        self.patches = patches
        self.all_patches = patches * devices
        self.away_frames = -(-frames // devices)
        used = self.away_frames * patches
        self.block = -(-used // 16) * 16
        self.home_rows = frames * patches
        self.away_rows = self.away_frames * self.all_patches
        self.sent_rows = devices * self.block

    def home_of_sent(self):
        row = jnp.arange(self.sent_rows, dtype=jnp.int32)
        peer, inner = row // self.block, row % self.block
        frame = peer * self.away_frames + inner // self.patches
        valid = (inner < self.away_frames * self.patches) & (frame < self.frames)
        return jnp.where(valid, (inner % self.patches) * self.frames + frame, -1)

    def sent_of_away(self):
        row = jnp.arange(self.away_rows + CLS_ROWS, dtype=jnp.int32)
        frame, patch = row // self.all_patches, row % self.all_patches
        sent = (patch // self.patches) * self.block + frame * self.patches + patch % self.patches
        return jnp.where(row < self.away_rows, sent, -1)

    def parts(self):
        step = self.block // 5 // 16 * 16
        return ((0, step), (step, 3 * step), (3 * step, self.block))

    def frame_parts(self):
        ends = [-(-self.patches * (i + 1) // 16) * 16 for i in range(self.away_frames)]
        return tuple(zip([0] + ends[:-1], ends))

    def frame_rows(self, frame):
        low, high = self.patches * frame, self.patches * (frame + 1)
        return low // 16 * 16, -(-high // 16) * 16

    def leave(self, order, parts):
        order = np.where(np.arange(self.block) < self.away_frames * self.patches, order, -1)
        rows = np.concatenate([order[:, low:high].reshape(-1) for low, high in parts])
        return np.asarray(rows, np.int32)[:, None]

    def orders(self):
        block, patches, near = self.block, self.patches, self.away_frames
        peer, inner = np.meshgrid(range(self.devices), range(block), indexing="ij")
        by_patch = inner // near * self.frames + peer * near + inner % near
        by_frame = inner % patches * self.frames + peer * near + inner // patches
        from_away = inner // patches * self.all_patches + peer * patches + inner % patches
        row = np.arange(self.away_rows)
        frame, patch = row // self.all_patches, row % self.all_patches
        reach_patch = patch // patches * block + patch % patches * near + frame
        low = np.array([self.frame_rows(i)[0] for i in range(near)])[frame]
        high = np.array([self.frame_rows(i)[1] for i in range(near)])[frame]
        reach_frame = patch // patches * (high - low) + frame * patches + patch % patches - low
        row = np.arange(self.home_rows)
        patch, frame = row // self.frames, row % self.frames
        reach_home = frame // near * block + frame % near * patches + patch

        def column(rows):
            return np.asarray(rows, np.int32)[:, None]

        return dict(
            leave_patch=self.leave(by_patch, self.parts()),
            leave_frame=self.leave(by_frame, self.frame_parts()),
            leave_away=self.leave(from_away, self.parts()),
            reach_patch=column(reach_patch),
            reach_frame=column(reach_frame),
            reach_home=column(reach_home),
        )

    def to_away(self, values):
        pick = self.home_of_sent()[:, None] == jnp.arange(self.home_rows, dtype=jnp.int32)[None, :]
        sent = jnp.dot(pick.astype(bf16), values, preferred_element_type=bf16)
        got = lax.all_to_all(sent, PATCH, split_axis=0, concat_axis=0, tiled=True)
        pick = self.sent_of_away()[:, None] == jnp.arange(self.sent_rows, dtype=jnp.int32)[None, :]
        return jnp.dot(pick.astype(bf16), got, preferred_element_type=f32)

    def to_home(self, values):
        pick = jnp.arange(self.sent_rows, dtype=jnp.int32)[:, None] == self.sent_of_away()[None, : self.away_rows]
        sent = jnp.dot(pick.astype(bf16), values, preferred_element_type=bf16)
        got = lax.all_to_all(sent, PATCH, split_axis=0, concat_axis=0, tiled=True)
        pick = jnp.arange(self.home_rows, dtype=jnp.int32)[:, None] == self.home_of_sent()[None, :]
        return jnp.dot(pick.astype(bf16), got, preferred_element_type=f32)


def norm_rows(values):
    centered = values - jnp.mean(values, -1, keepdims=True)
    inverse = lax.rsqrt(jnp.mean(centered * centered, -1, keepdims=True) + EPSILON)
    return centered, inverse


def norm_forward(values, gain, shift):
    centered, inverse = norm_rows(values)
    return (centered * inverse * gain + shift).astype(bf16)


def norm_backward(values, grad, gain, sums):
    centered, inverse = norm_rows(values)
    weighted = grad * gain
    along = jnp.mean(weighted * centered, -1, keepdims=True) * (inverse * inverse * inverse)

    def fold(part):
        return jnp.sum(part.reshape(part.shape[0] // 8, 8, part.shape[1]), 0)

    sums[0][...] += fold(grad * (centered * inverse))
    sums[1][...] += fold(grad)
    return inverse * (weighted - jnp.mean(weighted, -1, keepdims=True)) - centered * along


class Loads:
    def __init__(self, sources, buffers, sems):
        self.copies = [
            pltpu.make_async_copy(source, buffer, sems.at[i])
            for i, (source, buffer) in enumerate(zip(sources, buffers))
        ]
        for copy in self.copies:
            copy.start()
        self.buffers = buffers
        self.next = 0

    def get(self):
        self.copies[self.next].wait()
        self.next += 1
        return self.buffers[self.next - 1]


class Saves:
    def __init__(self, buffers, targets, sems):
        self.pairs, self.sems = list(zip(buffers, targets)), sems

    def copies(self, part, start, rows):
        here = pl.ds(start, rows)
        return [
            pltpu.make_async_copy(buffer.at[here], target.at[here], self.sems.at[i, part])
            for i, (buffer, target) in enumerate(self.pairs)
        ]

    def put(self, part, start, rows):
        for copy in self.copies(part, start, rows):
            copy.start()

    def finish(self, part, start, rows):
        for copy in self.copies(part, start, rows):
            copy.wait()


class Place:
    AXES = {"core": (PATCH, 1), "zl": (PATCH, 2), "zh": (PATCH, 4), "x": (CLIP, 1), "y": (CLIP, 2)}

    def __init__(self):
        self.clip, self.patch = lax.axis_index(CLIP), lax.axis_index(PATCH)
        self.me = {
            "core": lax.rem(self.patch, 2),
            "zl": lax.rem(self.patch // 2, 2),
            "zh": self.patch // 4,
            "x": lax.rem(self.clip, 2),
            "y": self.clip // 2,
        }

    def peer(self, dim):
        axis, stride = self.AXES[dim]
        own = self.clip if axis == CLIP else self.patch
        other = own + stride - 2 * stride * self.me[dim]
        return (other, self.patch) if axis == CLIP else (self.clip, other)


class Shuffle:
    def __init__(self, lay, at, sent, got, send_sem, recv_sem):
        self.lay, self.devices, self.parts, self.at = lay, lay.devices, lay.parts(), at
        self.sent, self.got, self.send_sem, self.recv_sem = sent, got, send_sem, recv_sem
        self.moves = 0

    def greet(self):
        for offset in range(1, self.devices):
            other = (self.at.clip, lax.rem(self.at.patch + offset, self.devices))
            pl.semaphore_signal(pltpu.get_barrier_semaphore(), inc=1, device_id=other, device_id_type=MESH)

    def meet(self, others=0):
        pl.semaphore_wait(pltpu.get_barrier_semaphore(), self.devices - 1 + others)

    def copy(self, offset, part):
        two = self.moves % 2
        other = lax.rem(self.at.patch + offset, self.devices)
        low, high = self.parts[part]
        rows = pl.ds(low, high - low)
        return pltpu.make_async_remote_copy(
            src_ref=self.sent.at[other, rows],
            dst_ref=self.got.at[two, self.at.patch, rows],
            send_sem=self.send_sem.at[part, offset],
            recv_sem=self.recv_sem.at[two, part, offset],
            device_id=(self.at.clip, other),
            device_id_type=MESH,
        )

    def send(self, part, order_ref, source_ref, first, last):
        width = self.sent.shape[-1]
        low, high = self.parts[part]
        rows = (high - low) * self.devices
        start = low * self.devices
        ids = lax.broadcasted_iota(jnp.int32, (rows, last - first), 1) + first
        pick = (order_ref[start : start + rows, :] == ids).astype(f32).astype(bf16)
        picked = dot_nn(pick, source_ref[first:last, :]).astype(bf16)
        self.sent[:, low:high, :] = picked.reshape(self.devices, high - low, width)
        for offset in range(1, self.devices):
            self.copy(offset, part).start()
        self.got[self.moves % 2, self.at.patch, low:high, :] = self.sent[self.at.patch, low:high, :]

    def send_all(self, order_ref, source_ref):
        for part in range(len(self.parts)):
            self.send(part, order_ref, source_ref, 0, source_ref.shape[0])

    def arrive(self, part):
        for offset in range(1, self.devices):
            self.copy(offset, part).wait()

    def receive(self, order_ref, target_ref):
        for part in range(len(self.parts)):
            self.arrive(part)
        devices, block, width = self.got.shape[1:]
        rows = target_ref.shape[0] // 3
        ids = lax.broadcasted_iota(jnp.int32, (rows, devices * block), 1)
        for start in range(0, target_ref.shape[0], rows):
            pick = (order_ref[start : start + rows, :] == ids).astype(f32).astype(bf16)
            got = self.got[self.moves % 2].reshape(devices * block, width)
            target_ref[start : start + rows, :] = dot_nn(pick, got).astype(bf16)
        self.moves += 1

    def receive_frame(self, frame, order_ref, target_ref):
        self.arrive(frame)
        low, high = self.lay.frame_rows(frame)
        patches = self.lay.all_patches
        here = slice(frame * patches, (frame + 1) * patches)
        width = self.got.shape[-1]
        got = self.got[self.moves % 2, :, low:high, :].reshape(self.devices * (high - low), width)
        ids = lax.broadcasted_iota(jnp.int32, (patches, got.shape[0]), 1)
        pick = (order_ref[here, :] == ids).astype(f32).astype(bf16)
        target_ref[here, :] = dot_nn(pick, got).astype(bf16)


def slot_of(lengths_ref, frames):
    end, slot = 0, 0
    for clip in range(lengths_ref.shape[0]):
        end = end + lengths_ref[clip]
        slot = slot + (frames >= end).astype(jnp.int32)
    return slot


def fill_bias(lengths_ref, frames, bias_ref):
    rows = bias_ref.shape[0]

    def split(ids, size, count):
        which = jnp.zeros_like(ids)
        for i in range(1, count):
            which = which + (ids >= i * size).astype(jnp.int32)
        return which, ids - which * size

    key_patch, key_frame = split(lax.broadcasted_iota(jnp.int32, bias_ref.shape, 0), frames, rows // frames)
    _, query = split(lax.broadcasted_iota(jnp.int32, bias_ref.shape, 1), rows, QUAD)
    query_patch, query_frame = split(query, frames, rows // frames)
    same = (key_patch == query_patch) & (slot_of(lengths_ref, key_frame) == slot_of(lengths_ref, query_frame))
    bias_ref[...] = jnp.where(same, 0.0, NEG_LARGE).astype(f32)


def cls_rows_of(cls_ref):
    values = cls_ref[...].astype(f32)
    return jnp.concatenate([values, jnp.zeros((CLS_ROWS - values.shape[0], values.shape[1]), f32)], 0)


def norm_row(norms_ref, layer, which):
    return norms_ref[which, layer : layer + 1, :]


def time_tiles(bias_ref, qkv_ref, width, group, grad_ref=None):
    rows = bias_ref.shape[0]
    here = pl.ds(pl.multiple_of(group * rows, 16), rows)
    tiles = []
    for quad in range(QUADS):
        tile = [qkv_ref[here, columns(part, quad, width)] for part in range(3)]
        if grad_ref is not None:
            tile.append(grad_ref[here, columns(0, quad, width)])
        tiles.append(tile)
    return here, tiles


def space_tiles(patches, total, slot, qkv_ref, width, frame, grad_ref=None):
    here = pl.ds(pl.multiple_of(frame * patches, 16), patches)
    tiles = []
    for quad in range(QUADS):
        tile = [qkv_ref[here, columns(part, quad, width)] for part in range(3)]
        for part in (1, 2):
            tile[part] = with_class(slot, tile[part], qkv_ref[total : total + CLS_ROWS, columns(part, quad, width)])
        if grad_ref is not None:
            tile.append(grad_ref[here, columns(0, quad, width)])
        tiles.append(tile)
    return here, tiles


def group_parts(lay, rows):
    ends = []
    for _, high in lay.parts():
        patches = min(-(-high // lay.away_frames), lay.patches)
        ends.append(-(-patches * lay.frames // rows) * rows)
    return tuple(zip([0] + ends[:-1], ends))


SAVED = ("normed_t", "qkv_t", "mixed_t", "x_away", "normed_s", "qkv_s", "mixed_s", "middle", "normed_f", "active", "slope")
WEIGHTS = ("time_proj", "time_output", "space_proj", "space_output", "up", "down")


def forward_kernel(lay, *refs):
    lengths_ref, norms_ref, shifts_ref, cls_ref, leave_frame, reach_frame, leave_away, reach_home = refs[:8]
    refs = refs[1:]
    sources = dict(zip(WEIGHTS, refs[7:13]))
    tokens_hbm, grad_hbm = refs[13:15]
    home_hbm, grad_away_hbm, result_hbm = refs[15:18]
    saved = [dict(zip(SAVED, refs[18 + len(SAVED) * layer :][: len(SAVED)])) for layer in range(LAYERS)]
    refs = refs[18 + len(SAVED) * LAYERS :]
    weights = dict(zip(WEIGHTS, refs[:6]))
    staged = dict(zip(SAVED, refs[6 : 6 + len(SAVED)]))
    bias_ref, x_home, after, grad, grad_away = refs[6 + len(SAVED) :][:5]
    sem_weight, sem_ends, sem_time, sem_space, sem_cls, *moving = refs[11 + len(SAVED) :]
    normed_t, qkv_t, mixed_t, x_away, normed, qkv, mixed, middle, normed_f, active, slope = (staged[name] for name in SAVED)
    total, width = x_away.shape
    home = x_home.shape[0]
    patches, frames = lay.all_patches, lay.away_frames
    group = bias_ref.shape[0]
    columns_of = [slice(start, start + width) for start in range(0, 3 * width, width)]

    load_x = pltpu.make_async_copy(tokens_hbm, x_home, sem_ends.at[0])
    load_grad = pltpu.make_async_copy(grad_hbm, grad, sem_ends.at[1])
    save_home = pltpu.make_async_copy(x_home, home_hbm, sem_ends.at[2])
    save_result = pltpu.make_async_copy(after, result_hbm, sem_ends.at[3])
    save_grad = pltpu.make_async_copy(grad_away, grad_away_hbm, sem_ends.at[4])
    load_x.start()
    load_grad.start()

    def fetch(layer, i):
        return pltpu.make_async_copy(sources[WEIGHTS[i]].at[layer], weights[WEIGHTS[i]], sem_weight.at[i])

    fetch(0, 0).start()
    at = Place()
    coming, leaving = [Shuffle(lay, at, *moving[:4]) for _ in range(2)]
    extra = Shuffle(lay, at, *moving[4:])
    coming.parts = extra.parts = lay.frame_parts()
    coming.greet()
    fill_bias(lengths_ref, lay.frames, bias_ref)
    key_mask = key_bias(patches)
    cls = cls_rows_of(cls_ref)
    load_grad.wait()
    coming.meet()
    extra.send(0, leave_frame, grad, 0, home)
    load_x.wait()

    for layer in range(LAYERS):
        more = layer < LAYERS - 1
        coming.moves, leaving.moves = 2 * layer, 2 * layer + 1
        if not more:
            extra.send(1, leave_frame, grad, 0, home)
        here = saved[layer]
        time_saves = Saves([staged[name] for name in SAVED[:3]], [here[name] for name in SAVED[:3]], sem_time)
        space_saves = Saves([staged[name] for name in SAVED[3:]], [here[name] for name in SAVED[3:]], sem_space)
        cls_saves = Saves([normed, qkv], [here["normed_s"], here["qkv_s"]], sem_cls)

        gain, shift = norm_row(norms_ref, layer, 0), norm_row(shifts_ref, layer, 0)
        for start in range(0, home, home // 3):
            rows = slice(start, start + home // 3)
            normed_t[rows, :] = norm_forward(x_home[rows, :].astype(f32), gain, shift)
        fetch(layer, 0).wait()
        if layer == 0:
            for i in range(1, len(WEIGHTS)):
                fetch(0, i).start()
        for these in columns_of:
            qkv_t[:, these] = dot_nn(normed_t[...], weights["time_proj"][:, these]).astype(bf16)
        if more:
            fetch(layer + 1, 0).start()

        @pl.loop(0, home // group)
        def _(index):
            rows, tiles = time_tiles(bias_ref, qkv_t, width, index)
            for quad, done in enumerate(forward_tiles(tiles, bias_ref[...])):
                mixed_t[rows, columns(0, quad, width)] = done

        fetch(layer, 1).wait()
        after[...] = (x_home[...].astype(f32) + dot_nn(mixed_t[...], weights["time_output"][...])).astype(bf16)
        for part in range(frames):
            coming.send(part, leave_frame, after, 0, home)
        if more:
            fetch(layer + 1, 1).start()
        time_saves.put(0, 0, home)

        gain, shift = norm_row(norms_ref, layer, 1), norm_row(shifts_ref, layer, 1)
        gain_f, shift_f = norm_row(norms_ref, layer, 2), norm_row(shifts_ref, layer, 2)
        normed[total:, :] = norm_forward(cls, gain, shift)
        fetch(layer, 2).wait()
        for these in columns_of:
            qkv[total:, these] = dot_nn(normed[total:, :], weights["space_proj"][:, these]).astype(bf16)
        cls_saves.put(0, total, CLS_ROWS)
        for i in range(3, len(WEIGHTS)):
            fetch(layer, i).wait()

        @pl.loop(0, frames)
        def _(frame, layer=layer, more=more, space_saves=space_saves, gain=gain, shift=shift, gain_f=gain_f, shift_f=shift_f):
            for number in range(frames):

                @pl.when(frame == number)
                def _(number=number, more=more):
                    coming.receive_frame(number, reach_frame, x_away)
                    if number == frames - 1 and not more:
                        extra.send(2, leave_frame, grad, 0, home)

            start = pl.multiple_of(frame * patches, 16)
            rows = pl.ds(start, patches)
            normed[rows, :] = norm_forward(x_away[rows, :].astype(f32), gain, shift)
            for these in columns_of:
                qkv[rows, these] = dot_nn(normed[rows, :], weights["space_proj"][:, these]).astype(bf16)
            slot = slot_of(lengths_ref, at.patch * frames + frame)
            _, tiles = space_tiles(patches, total, slot, qkv, width, frame)
            for quad, done in enumerate(forward_tiles(tiles, key_mask)):
                mixed[rows, columns(0, quad, width)] = done
            residual = x_away[rows, :].astype(f32) + dot_nn(mixed[rows, :], weights["space_output"][...])
            middle[rows, :] = residual.astype(bf16)
            normed_f[rows, :] = norm_forward(residual, gain_f, shift_f)
            for column in range(0, active.shape[1], WIDE):
                these = slice(column, column + WIDE)
                hidden = dot_nn(normed_f[rows, :], weights["up"][:, these])
                share = 0.5 * (1.0 + lax.erf(hidden * ROOT_HALF))
                active[rows, these] = (hidden * share).astype(bf16)
                bend = share + hidden * (INV_ROOT_TWO_PI * jnp.exp(-0.5 * hidden * hidden))
                slope[rows, these] = bend.astype(bf16)
            after[rows, :] = (residual + dot_nn(active[rows, :], weights["down"][...])).astype(bf16)
            space_saves.put(frame, start, patches)
            for number in range(frames - 1):

                @pl.when(frame == number)
                def _(number=number, more=more):
                    if more:
                        leaving.send(number, leave_away, after, 0, (number + 1) * patches)

        time_saves.finish(0, 0, home)
        if more:
            leaving.send(frames - 1, leave_away, after, (frames - 2) * patches, total)
            for i in range(2, len(WEIGHTS)):
                fetch(layer + 1, i).start()
            leaving.receive(reach_home, x_home)
            save_home.start()
        else:
            save_result.start()
            for frame in range(frames):
                extra.receive_frame(frame, reach_frame, grad_away)
            save_grad.start()
        for frame in range(frames):
            space_saves.finish(frame, frame * patches, patches)
        cls_saves.finish(0, total, CLS_ROWS)
    for copy in (save_home, save_result, save_grad):
        copy.wait()


CHUNKS = 16
TOTAL = CHUNKS * LAYERS
BLOCKS = 3
PIECE = (48, 128)
ROUTES = (("x", "zl", "zh", "y", "x", "y"), ("y", "x", "zl", "zh", "y", "x"), ("y", "x", "zl", "zh", "x", "y"))
SUMS = 4
STAGES = 7
RAW_SLOTS = 8
ACC_SLOTS = 8
BOX_SLOTS = 4
STRIDE = 2
SEGMENTS = (4, 4, 1, 3, 1, 3)
PLAN = {
    1: dict(early=3, down=2, hidden=1, wide=2, norm=0, frames=(0, 0, 0), up=0, space_out=2, space_proj=1, time_early=0, home=1, time0=1, time1=2, time2=0, time_out=1, time_proj=2),
    0: dict(early=1, down=1, hidden=1, wide=0, norm=1, frames=(1, 1, 1), up=0, space_out=2, space_proj=1, time_early=0, home=1, time0=1, time1=1, time2=1, time_out=0, time_proj=0),
}
SMALL = ("core", "zl", "zh", "x", "y")
SMALL_ROWS = 24


def recv_shape(route, stage):
    left = [dim for dim in ("zh", "zl", "x", "y") if dim not in route[: stage + 1]]
    return (2,) * len(left) + PIECE


class Pump:
    def __init__(self, at, results, scratch):
        self.at, self.results = at, results
        self.raw, self.core_in, self.acc, self.out, *rest = scratch
        self.inboxes = rest[: BLOCKS * SUMS]
        self.core_send, self.core_recv, self.core_free, self.send_sem, self.recv_sem = rest[BLOCKS * SUMS :]
        self.made = self.stepped = 0

    def core_copy(self, c, z):
        slot = lax.rem(c, RAW_SLOTS)
        return pltpu.make_async_remote_copy(
            src_ref=self.raw.at[slot, z // 2, z % 2, 1 - self.at.me["core"]],
            dst_ref=self.core_in.at[slot, z // 2, z % 2],
            send_sem=self.core_send.at[slot, z],
            recv_sem=self.core_recv.at[slot, z],
            device_id=self.at.peer("core"),
            device_id_type=MESH,
        )

    def claim(self, c, known):
        if known >= RAW_SLOTS:
            pl.semaphore_wait(self.core_free, 1)

    def store(self, c, z, core, block, rows):
        slot = lax.rem(c, RAW_SLOTS)
        for xh in range(2):
            for yh in range(2):
                part = rows[xh * 48 : (xh + 1) * 48, yh * 128 : (yh + 1) * 128]
                self.raw[slot, z // 2, z % 2, core, block, xh, yh] = part.astype(bf16)

    def make_chunks(self, count, lhs, rhs):
        first = self.made

        def one(i, c, known):
            self.claim(c, known)
            for half in range(2):
                left = lhs(slice(half * 384, (half + 1) * 384))
                for block in range(BLOCKS):
                    done = dot_tn(left, rhs(i, block * 256))
                    for j in range(4):
                        self.store(c, half * 2 + j // 2, j % 2, block, done[j * 96 : (j + 1) * 96])
            for z in range(4):
                self.core_copy(c, z).start()

        if count == 1:
            one(0, first, first)
        else:
            assert (first >= RAW_SLOTS) == (first + count - 1 >= RAW_SLOTS)

            @pl.loop(0, count)
            def _(i):
                one(i, first + i, first)

        self.made += count
        assert self.made - self.stepped <= RAW_SLOTS

    def make_down(self, lhs, rhs):
        first = self.made

        @pl.loop(0, 4)
        def _(z):
            if first >= RAW_SLOTS:

                @pl.when(z == 0)
                def _():
                    pl.semaphore_wait(self.core_free, 4)

            for core in range(2):
                left = lhs(pl.ds(pl.multiple_of(z * 768 + core * 384, 128), 384))
                for block in range(BLOCKS):
                    done = dot_tn(left, rhs[:, block * 256 : (block + 1) * 256])
                    for c in range(4):
                        self.store_at(first + c, z, core, block, done[c * 96 : (c + 1) * 96])
            for c in range(4):
                slot = (first + c) % RAW_SLOTS
                zh, zl = z // 2, lax.rem(z, 2)
                pltpu.make_async_remote_copy(
                    src_ref=self.raw.at[slot, zh, zl, 1 - self.at.me["core"]],
                    dst_ref=self.core_in.at[slot, zh, zl],
                    send_sem=self.core_send.at[slot, z],
                    recv_sem=self.core_recv.at[slot, z],
                    device_id=self.at.peer("core"),
                    device_id_type=MESH,
                ).start()

        self.made += 4
        assert self.made - self.stepped <= RAW_SLOTS

    def store_at(self, c, z, core, block, rows):
        for xh in range(2):
            for yh in range(2):
                part = rows[xh * 48 : (xh + 1) * 48, yh * 128 : (yh + 1) * 128]
                self.raw[c % RAW_SLOTS, z // 2, lax.rem(z, 2), core, block, xh, yh] = part.astype(bf16)

    def part(self, c, block, stage, value):
        route = ROUTES[block]

        def pick(dim):
            if dim in route[:stage]:
                return self.at.me[dim]
            return value if dim == route[stage] else slice(None)

        return (lax.rem(c, ACC_SLOTS), pick("zh"), pick("zl"), block, pick("x"), pick("y"))

    def exchange(self, c, block, stage):
        me = self.at.me
        dim = ROUTES[block][stage]
        box = lax.rem(c, BOX_SLOTS)
        if stage < SUMS:
            src = self.acc.at[self.part(c, block, stage, 1 - me[dim])]
            dst = self.inboxes[block * SUMS + stage].at[box]
        else:
            slot = lax.rem(c, ACC_SLOTS)
            if stage == SUMS:
                src = dst = self.out.at[slot, block, me["x"], me["y"]]
            elif dim == "x":
                src = dst = self.out.at[slot, block, me["x"]]
            else:
                src = dst = self.out.at[slot, block, :, me["y"]]
        return pltpu.make_async_remote_copy(
            src_ref=src,
            dst_ref=dst,
            send_sem=self.send_sem.at[box, block, stage],
            recv_sem=self.recv_sem.at[box, block, stage],
            device_id=self.at.peer(dim),
            device_id_type=MESH,
        )

    def enter(self, c):
        me = self.at.me
        slot, into = lax.rem(c, RAW_SLOTS), lax.rem(c, ACC_SLOTS)
        for z in range(4):
            self.core_copy(c, z).wait()
        for zh in range(2):
            for zl in range(2):
                both = self.raw[slot, zh, zl, me["core"]].astype(f32) + self.core_in[slot, zh, zl].astype(f32)
                self.acc[into, zh, zl] = both.astype(bf16)

        @pl.when(c < TOTAL - RAW_SLOTS)
        def _():
            pl.semaphore_signal(self.core_free, inc=1, device_id=self.at.peer("core"), device_id_type=MESH)

        for block in range(BLOCKS):
            self.exchange(c, block, 0).start()

    def advance(self, c, stage):
        me = self.at.me
        slot, box = lax.rem(c, ACC_SLOTS), lax.rem(c, BOX_SLOTS)
        for block in range(BLOCKS):
            self.exchange(c, block, stage).wait()
            if stage < SUMS:
                where = self.part(c, block, stage, me[ROUTES[block][stage]])
                both = self.acc[where].astype(f32) + self.inboxes[block * SUMS + stage][box].astype(f32)
                if stage == SUMS - 1:
                    self.out[slot, block, me["x"], me["y"]] = both.astype(bf16)
                else:
                    self.acc[where] = both.astype(bf16)
            if stage + 1 < STAGES - 1:
                self.exchange(c, block, stage + 1).start()
            else:
                self.finish(c, block)

    def finish(self, c, block):
        slot = lax.rem(c, ACC_SLOTS)
        layer = LAYERS - 1 - c // CHUNKS
        inner = lax.rem(c, CHUNKS)
        start = 0
        for which, count in enumerate(SEGMENTS):

            @pl.when((inner >= start) & (inner < start + count))
            def _(which=which, start=start):
                for xh in range(2):
                    for yh in range(2):
                        part = self.out[slot, block, xh, yh]
                        column = block * 256 + yh * 128
                        if which == 0:
                            row = pl.multiple_of((inner - start) * 96 + xh * 48, 16)
                            self.results[which][layer, pl.ds(row, 48), column : column + 128] = part
                        else:
                            at = pl.ds(pl.multiple_of((inner - start) * 768 + column, 128), 128)
                            self.results[which][layer, xh * 48 : (xh + 1) * 48, at] = part

            start += count

    def run_step(self, t):
        for stage in reversed(range(STAGES)):
            c = t - STRIDE * stage

            @pl.when((c >= 0) & (c < TOTAL))
            def _(c=c, stage=stage):
                if stage == 0:
                    self.enter(c)
                else:
                    self.advance(c, stage - 1)

    def step(self, count=1):
        first = self.stepped
        self.stepped += count
        assert min(self.stepped, TOTAL) <= self.made

        @pl.loop(first, first + count)
        def _(t):
            self.run_step(t)

    def inside(self, count):
        first = self.stepped
        self.stepped += count
        assert min(self.stepped, TOTAL) <= self.made
        return first

    def frame_steps(self, counts):
        first = self.inside(sum(counts))
        a, b, c = counts

        def run(frame):
            second, third = (frame + 1) // 2, frame // 2
            low = first + a * second + b * third

            @pl.loop(low, low + a + (b - a) * second + (c - b) * third)
            def _(t):
                self.run_step(t)

        return run


class Small:
    def __init__(self, at, values, boxes, send_sem, recv_sem):
        self.at, self.values, self.boxes, self.send_sem, self.recv_sem = at, values, boxes, send_sem, recv_sem

    def rows(self, i):
        return SMALL_ROWS if i < 3 else 16

    def copy(self, i):
        part = pl.ds(0, self.rows(i))
        return pltpu.make_async_remote_copy(
            src_ref=self.values.at[part],
            dst_ref=self.boxes.at[i, part],
            send_sem=self.send_sem.at[i],
            recv_sem=self.recv_sem.at[i],
            device_id=self.at.peer(SMALL[i]),
            device_id_type=MESH,
        )

    def step(self, i):
        if i > 0:
            rows = slice(0, self.rows(i - 1))
            self.copy(i - 1).wait()
            self.values[rows] += self.boxes[i - 1, rows]
        if i < len(SMALL):
            self.copy(i).start()


class Ring:
    def __init__(self, sources, slots, sems):
        self.sources, self.slots, self.sems = sources, slots, sems
        self.depth = slots.shape[0]
        self.started = self.taken = 0
        for _ in range(self.depth):
            self.start()

    def copy(self, i):
        source = self.sources[i]
        slot = i % self.depth
        return pltpu.make_async_copy(source, self.slots.at[slot, pl.ds(0, source.shape[0])], self.sems.at[slot])

    def start(self):
        if self.started < len(self.sources):
            self.copy(self.started).start()
            self.started += 1

    def take(self):
        i = self.taken
        self.copy(i).wait()
        self.taken += 1
        return self.slots.at[i % self.depth, pl.ds(0, self.sources[i].shape[0])]

    def free(self):
        self.start()


class Single:
    def __init__(self, sources, buffer, sem):
        self.copies = [
            pltpu.make_async_copy(source, buffer.at[pl.ds(0, source.shape[0])], sem) for source in sources
        ]
        self.next = 0
        self.copies[0].start()

    def take(self):
        self.copies[self.next].wait()

    def free(self):
        self.next += 1
        if self.next < len(self.copies):
            self.copies[self.next].start()


def backward_kernel(lay, *refs):
    devices, patches = lay.devices, lay.all_patches
    lengths_ref, norms_ref, cls_ref, leave_home, reach_away, leave_away, reach_home = refs[:7]
    weights = dict(zip(WEIGHTS, refs[7:13]))
    grad_hbm, x_out_hbm = refs[13:15]
    names = ("x_home",) + SAVED
    refs = refs[15:]
    saved = [dict(zip(names, refs[len(names) * layer : len(names) * (layer + 1)])) for layer in range(LAYERS)]
    refs = refs[len(names) * LAYERS :]
    small_ref, *results, output_hbm, tokens_hbm = refs[:9]
    refs = refs[9:]
    hidden, qkv, dqkv, wide, mixed, branch, x_buf, grad_buf, home_buf, cls_sum, bias_ref, *refs = refs
    weight_slots, lhs_slots, sent, got, small_boxes, *sums = refs[:11]
    sem_hidden, sem_qkv, sem_x, sem_ends, sem_weight, sem_lhs, sem_sent, sem_got, small_send, small_recv = refs[11:21]
    pump_scratch = refs[21:]
    load_grad = pltpu.make_async_copy(grad_hbm, grad_buf, sem_ends.at[0])
    load_out = pltpu.make_async_copy(x_out_hbm, mixed, sem_ends.at[1])
    save_out = pltpu.make_async_copy(home_buf, output_hbm, sem_ends.at[2])
    save_tokens = pltpu.make_async_copy(mixed, tokens_hbm, sem_ends.at[3])
    load_out.start()
    load_grad.start()

    at = Place()
    shuffle = Shuffle(lay, at, sent, got, sem_sent, sem_got)
    shuffle.greet()
    for dim in ("x", "y"):
        pl.semaphore_signal(pltpu.get_barrier_semaphore(), inc=1, device_id=at.peer(dim), device_id_type=MESH)

    total, width = grad_buf.shape
    parts = range(0, 3 * width, width)
    order = tuple(reversed(range(LAYERS)))
    tiles, lhs = [], []
    for layer in order:
        wide_parts = range(0, weights["up"].shape[2], width)
        tiles += [weights["down"].at[layer, pl.ds(start, width), :] for start in wide_parts]
        tiles += [weights["up"].at[layer, :, pl.ds(start, width)] for start in wide_parts]
        tiles += [weights["space_output"].at[layer]]
        tiles += [weights["space_proj"].at[layer, :, pl.ds(start, width)] for start in parts]
        tiles += [weights["time_output"].at[layer]]
        tiles += [weights["time_proj"].at[layer, :, pl.ds(start, width)] for start in parts]
        here = saved[layer]
        lhs += [here["slope"].at[:, pl.ds(start, width)] for start in wide_parts]
        lhs += [here[name] for name in ("normed_f", "mixed_s", "normed_s", "mixed_t", "normed_t")]
    fill = Single([saved[layer]["active"] for layer in order], hidden, sem_hidden)
    ring = Ring(tiles, weight_slots, sem_weight)
    left = Ring(lhs, lhs_slots, sem_lhs)
    load_qkv = Single([saved[layer][name] for layer in order for name in ("qkv_s", "qkv_t")], qkv, sem_qkv)
    load_x = Single(
        [saved[layer][name] for layer in order for name in ("middle", "x_away", "x_home")], x_buf, sem_x
    )
    pump = Pump(at, results, pump_scratch)
    small = Small(at, small_ref, small_boxes, small_send, small_recv)
    for part in sums:
        part[...] = jnp.zeros_like(part)
    small_ref[...] = jnp.zeros_like(small_ref)
    key_mask = key_bias(patches)
    cls = cls_rows_of(cls_ref)
    fill_bias(lengths_ref, lay.frames, bias_ref)

    def back_product(rows, source, count):
        for i in range(count):
            tile = ring.take()
            part = dot_nt(source[:rows, i * width : (i + 1) * width], tile[...])
            if i:
                wide[:rows, :] += part
            else:
                wide[:rows, :] = part
            ring.free()

    frames = total // patches
    group = bias_ref.shape[0]
    groups = group_parts(lay, group)

    def made_of(lhs_tile, source, first=0, rows=None):
        rows = source.shape[0] if rows is None else rows

        def rhs(i, start):
            column = pl.multiple_of((i + first) * width + start, 128) if not isinstance(i, int) else (i + first) * width + start
            return source[:rows, pl.ds(column, WIDE)]

        return (lambda these: lhs_tile[:, these]), rhs

    shuffle.meet(2)
    load_out.wait()
    shuffle.send_all(leave_away, mixed)
    load_grad.wait()
    dy = grad_buf

    for layer in order:
        last = layer == 0
        plan = PLAN[layer]

        def steps(site, plan=plan):
            if plan.get(site, 0):
                pump.step(plan[site])

        fill.take()
        pump.make_down(lambda these: hidden[:, these], dy)
        steps("down")
        for start in range(0, hidden.shape[1], width):
            tile, slope = ring.take(), left.take()
            for block in range(0, width, WIDE):
                grad_active = dot_nt(dy[...], tile[block : block + WIDE, :])
                grad_hidden = grad_active * slope[:, block : block + WIDE].astype(f32)
                hidden[:, start + block : start + block + WIDE] = grad_hidden.astype(bf16)
            ring.free()
            left.free()
        normed_f = left.take()
        if plan["early"]:
            pump.make_chunks(plan["early"], *made_of(normed_f, hidden))
        steps("hidden")
        back_product(total, hidden, hidden.shape[1] // width)
        steps("wide")
        load_x.take()

        @pl.loop(0, frames)
        def _(frame, layer=layer):
            here = pl.ds(pl.multiple_of(frame * patches, 16), patches)
            part = norm_backward(x_buf[here, :].astype(f32), wide[here, :], norm_row(norms_ref, layer, 2), sums[0:2])
            both = dy[here, :].astype(f32) + part
            wide[here, :] = both
            branch[here, :] = both.astype(bf16)

        load_x.free()
        if not last:
            shuffle.receive(reach_home, home_buf)
            save_out.start()
        steps("norm")

        out_tile, *proj_tiles = [ring.take() for _ in range(4)]
        load_qkv.take()
        load_x.take()
        cls_sum[...] = jnp.zeros_like(cls_sum)
        gain = norm_row(norms_ref, layer, 1)
        frame_run = pump.frame_steps(plan["frames"]) if sum(plan["frames"]) else None

        @pl.loop(0, frames)
        def _(frame):
            here = pl.ds(pl.multiple_of(frame * patches, 16), patches)
            mixed[here, :] = dot_nt(branch[here, :], out_tile[...]).astype(bf16)
            slot = slot_of(lengths_ref, at.patch * frames + frame)
            _, these = space_tiles(patches, total, slot, qkv, width, frame, mixed)
            row_ids = lax.broadcasted_iota(jnp.int32, (patches, WIDE), 0)
            cls_ids = lax.broadcasted_iota(jnp.int32, (CLS_ROWS, WIDE), 0)
            for quad, grads in enumerate(backward_tiles(these, key_mask)):
                dqkv[here, columns(0, quad, width)] = grads[0].astype(bf16)
                for part in (1, 2):
                    where = columns(part, quad, width)
                    dqkv[here, where] = jnp.where(row_ids < REAL_PATCH, grads[part], 0.0).astype(bf16)
                    row = grads[part][REAL_PATCH : REAL_PATCH + 1]
                    cls_sum[:, where] += jnp.where(cls_ids == slot, row, 0.0)
            grad = sum(dot_nt(dqkv[here, i * width : (i + 1) * width], tile[...]) for i, tile in enumerate(proj_tiles))
            part = norm_backward(x_buf[here, :].astype(f32), grad, gain, sums[2:4])
            mixed[here, :] = (wide[here, :] + part).astype(bf16)
            for i in range(2):

                @pl.when(frame == i)
                def _(i=i):
                    shuffle.send(i, leave_away, mixed, 0, (i + 1) * patches)

            if frame_run is not None:
                frame_run(frame)

        shuffle.send(2, leave_away, mixed, patches, total)
        load_x.free()
        load_qkv.free()
        dqkv[total:, :] = cls_sum[...].astype(bf16)
        grad = sum(dot_nt(dqkv[total:, i * width : (i + 1) * width], tile[...]) for i, tile in enumerate(proj_tiles))
        for _ in range(4):
            ring.free()
        part = norm_backward(cls, grad, gain, sums[2:4])
        small_ref[16:24] += part[:8]
        if plan["early"] < 4:
            pump.make_chunks(4 - plan["early"], *made_of(normed_f, hidden, plan["early"]))
        left.free()
        fill.free()
        steps("up")
        pump.make_chunks(1, *made_of(left.take(), branch))
        left.free()
        steps("space_out")
        pump.make_chunks(3, *made_of(left.take(), dqkv))
        left.free()
        steps("space_proj")
        if not last:
            save_out.wait()
        shuffle.receive(reach_home, home_buf)

        out_tile, *proj_tiles = [ring.take() for _ in range(4)]
        load_qkv.take()
        load_x.take()
        mixed_t = left.take()
        if plan["time_early"]:
            pump.make_chunks(1, *made_of(mixed_t, home_buf))
            left.free()
        steps("home")

        def close_part(number, layer=layer, last=last, proj_tiles=proj_tiles):
            first, end = groups[number]
            here = slice(first, end)
            grad = sum(dot_nt(dqkv[here, i * width : (i + 1) * width], tile[...]) for i, tile in enumerate(proj_tiles))
            part = norm_backward(x_buf[here, :].astype(f32), grad, norm_row(norms_ref, layer, 0), sums[4:6])
            mixed[here, :] = (home_buf[here, :].astype(f32) + part).astype(bf16)
            if not last:
                shuffle.send(number, leave_home, mixed, 0 if number < 2 else first, end)

        for number, (first, end) in enumerate(groups):
            here = slice(first, end)
            mixed[here, :] = dot_nt(home_buf[here, :], out_tile[...]).astype(bf16)

            @pl.loop(first // group, end // group)
            def _(index):
                at_rows, these = time_tiles(bias_ref, qkv, width, index, mixed)
                for quad, grads in enumerate(backward_tiles(these, bias_ref[...])):
                    for part in range(3):
                        dqkv[at_rows, columns(part, quad, width)] = grads[part].astype(bf16)

            if not last:
                close_part(number)
            steps("time%d" % number)
        if not last:
            load_qkv.free()
            load_x.free()
            for _ in range(4):
                ring.free()
        if not plan["time_early"]:
            pump.make_chunks(1, *made_of(mixed_t, home_buf))
            left.free()
        steps("time_out")
        pump.make_chunks(3, *made_of(left.take(), dqkv, rows=total))
        left.free()
        steps("time_proj")
        if last:
            for number in range(len(groups)):
                pump.step()
                close_part(number)
            save_tokens.start()
        for i, part in enumerate(sums):
            row = layer * 8 + (2, 5, 1, 4, 0, 3)[i]
            small_ref[row : row + 1, :] += jnp.sum(part[...], 0, keepdims=True)
            part[...] = jnp.zeros_like(part)
        if last:
            small.step(0)
            for i in range(1, len(SMALL) + 1):
                pump.step()
                small.step(i)
        else:
            shuffle.receive(reach_away, grad_buf)

    pump.step(TOTAL + STRIDE * (STAGES - 1) - pump.stepped)
    save_tokens.wait()


IN_VMEM = pl.BlockSpec(memory_space=pltpu.VMEM)
IN_SMEM = pl.BlockSpec(memory_space=pltpu.SMEM)
IN_HBM = pl.BlockSpec(memory_space=pl.ANY)


def shape(*dims, kind=bf16):
    return jax.ShapeDtypeStruct(dims, kind)


def vmem(*dims, kind=bf16):
    return pltpu.VMEM(dims, kind)


def queue(*counts):
    return pltpu.SemaphoreType.DMA(counts)


def whole_call(name, body, collective, near, far, out_near, out_far, scratch):
    return pl.pallas_call(
        body,
        in_specs=[IN_SMEM if part.ndim == 1 else IN_VMEM for part in near] + [IN_HBM] * len(far),
        out_specs=[IN_VMEM] * len(out_near) + [IN_HBM] * len(out_far),
        out_shape=[*out_near, *out_far],
        scratch_shapes=scratch,
        compiler_params=pltpu.CompilerParams(
            collective_id=collective, has_side_effects=True, vmem_limit_bytes=VMEM_MOST
        ),
        name=name,
    )(*near, *far)


def finish_kernel(small_ref, *refs):
    count = len(refs) // 2
    for source, target in zip(refs[:count], refs[count:-1]):
        target[...] = source[...].astype(target.dtype)
    refs[-1][...] = small_ref[16 : 16 + refs[-1].shape[0], :]


def finish(small, clip_count, parts, kinds, steps=6):
    specs, out = [], []
    width = small.shape[1]
    cls = jax.ShapeDtypeStruct((clip_count, width), f32)
    for part, kind in zip(parts, kinds):
        cut = part.ndim - 2 if part.shape[-2] % (steps * 16) == 0 else part.ndim - 1
        block = tuple(size // steps if dim == cut else size for dim, size in enumerate(part.shape))

        def index(i, cut=cut, ndim=part.ndim):
            return tuple(i if dim == cut else 0 for dim in range(ndim))

        specs.append(pl.BlockSpec(block, index))
        out.append(jax.ShapeDtypeStruct(part.shape, kind))
    return pl.pallas_call(
        finish_kernel,
        grid=(steps,),
        in_specs=[pl.BlockSpec(small.shape, lambda i: (0, 0)), *specs],
        out_specs=[*specs, pl.BlockSpec(cls.shape, lambda i: (0, 0))],
        out_shape=[*out, cls],
        compiler_params=pltpu.CompilerParams(vmem_limit_bytes=VMEM_MOST),
        name="finish",
    )(small, *parts)


def fast_local(
    tokens,
    cls_tokens,
    clip_lengths,
    time_proj,
    time_output,
    space_proj,
    space_output,
    up_weight,
    down_weight,
    norm_gains,
    norm_biases,
    cotangent,
):
    frames, patch_rows, width = tokens.shape
    devices = lax.axis_size(PATCH)
    hidden = up_weight.shape[2]
    lay = Layout(devices, frames, patch_rows)
    home, away, block = lay.home_rows, lay.away_rows, lay.block
    clip_count = cls_tokens.shape[0]
    group = group_rows(patch_rows, frames)
    orders = {name: jnp.asarray(part) for name, part in lay.orders().items()}

    def home_order(values):
        return jnp.transpose(values, (1, 0, 2)).reshape(home, width)

    def given_order(values):
        return jnp.transpose(values.reshape(patch_rows, frames, width), (1, 0, 2))

    parts = len(lay.parts())
    moving = [vmem(devices, block, width), vmem(2, devices, block, width), queue(parts, devices), queue(2, parts, devices)]
    extra = [vmem(devices, block, width), vmem(1, devices, block, width), queue(parts, devices), queue(1, parts, devices)]
    gains, shifts = [jnp.transpose(part, (1, 0, 2)) for part in (norm_gains, norm_biases)]
    lengths = clip_lengths[0]
    weights = (time_proj, time_output, space_proj, space_output, up_weight, down_weight)
    at_home = home_order(tokens)
    saved_shapes = [
        shape(home, width),
        shape(home, 3 * width),
        shape(home, width),
        shape(away, width),
        shape(away + CLS_ROWS, width),
        shape(away + CLS_ROWS, 3 * width),
        *[shape(away, width)] * 3,
        *[shape(away, hidden)] * 2,
    ]
    bias = vmem(group, QUAD * group, kind=f32)
    home_next, grad_away, x_out, *saved = whole_call(
        "forward",
        functools.partial(forward_kernel, lay),
        2,
        (lengths, gains, shifts, cls_tokens, *[orders[name] for name in ("leave_frame", "reach_frame", "leave_away", "reach_home")]),
        (*weights, at_home, home_order(cotangent)),
        [],
        [shape(home, width), shape(away, width), shape(away, width)] + saved_shapes * LAYERS,
        [
            *[vmem(*part.shape[1:]) for part in weights],
            *[vmem(*part.shape) for part in saved_shapes],
            bias,
            vmem(home, width),
            vmem(away, width),
            vmem(home, width),
            vmem(away, width),
            queue(len(weights)),
            queue(5),
            queue(3, 1),
            queue(len(SAVED) - 3, lay.away_frames),
            queue(2, 1),
            *moving,
            *extra,
        ],
    )
    stored = [(at_home, *saved[: len(SAVED)]), (home_next, *saved[len(SAVED) :])]

    inbox = [vmem(BOX_SLOTS, *recv_shape(ROUTES[b], s)) for b in range(BLOCKS) for s in range(SUMS)]
    single = pltpu.SemaphoreType.DMA
    share = width // devices
    small, *large, output, grad_tokens = whole_call(
        "backward",
        functools.partial(backward_kernel, lay),
        1,
        (lengths, gains, cls_tokens, *[orders[name] for name in ("leave_patch", "reach_patch", "leave_away", "reach_home")]),
        (*weights, grad_away, x_out, *stored[0], *stored[1]),
        [
            shape(SMALL_ROWS, width, kind=f32),
            shape(LAYERS, hidden // devices, width),
            shape(LAYERS, share, hidden),
            shape(LAYERS, share, width),
            shape(LAYERS, share, 3 * width),
            shape(LAYERS, share, width),
            shape(LAYERS, share, 3 * width),
        ],
        [shape(home, width), shape(home, width)],
        [
            vmem(away, hidden),
            vmem(away + CLS_ROWS, 3 * width),
            vmem(away + CLS_ROWS, 3 * width),
            vmem(away, width, kind=f32),
            *[vmem(away, width)] * 5,
            vmem(CLS_ROWS, 3 * width, kind=f32),
            bias,
            vmem(4, width, width),
            vmem(2, away + CLS_ROWS, width),
            *moving[:2],
            vmem(len(SMALL), SMALL_ROWS, width, kind=f32),
            *[vmem(8, width, kind=f32)] * 6,
            single,
            single,
            single,
            queue(4),
            queue(4),
            queue(2),
            *moving[2:],
            queue(len(SMALL)),
            queue(len(SMALL)),
            vmem(RAW_SLOTS, 2, 2, 2, BLOCKS, 2, 2, *PIECE),
            vmem(RAW_SLOTS, 2, 2, BLOCKS, 2, 2, *PIECE),
            vmem(ACC_SLOTS, 2, 2, BLOCKS, 2, 2, *PIECE),
            vmem(ACC_SLOTS, BLOCKS, 2, 2, *PIECE),
            *inbox,
            queue(RAW_SLOTS, 4),
            queue(RAW_SLOTS, 4),
            pltpu.SemaphoreType.REGULAR,
            queue(BOX_SLOTS, BLOCKS, STAGES - 1),
            queue(BOX_SLOTS, BLOCKS, STAGES - 1),
        ],
    )
    large = [large[i] for i in (5, 4, 3, 2, 1, 0)]
    kinds = (f32,) * len(large) + (bf16,) * 2
    *large, output, grad_tokens, grad_cls = finish(small, clip_count, (*large, output, grad_tokens), kinds)
    small = lax.dynamic_slice_in_dim(small[:16], lax.axis_index(PATCH) * share, share, 1)
    small = small.reshape(LAYERS, 8, share)
    return (given_order(output), given_order(grad_tokens), grad_cls, *large, small[:, 0:3], small[:, 3:6])


def general_local(
    tokens,
    cls_tokens,
    clip_lengths,
    time_proj,
    time_output,
    space_proj,
    space_output,
    up_weight,
    down_weight,
    norm_gains,
    norm_biases,
    cotangent,
):
    frames, patch_rows, width = tokens.shape
    devices = lax.axis_size(PATCH)
    lay = Layout(devices, frames, patch_rows)
    away_rows = lay.away_rows
    patches = lay.all_patches
    clip_count = cls_tokens.shape[0]

    frame_ids = jnp.arange(frames, dtype=jnp.int32)
    slots = frame_slots(clip_lengths[0], frame_ids)
    bias = time_bias(slots[:, None] == slots[None, :], patch_rows, frames)
    my_frames = lax.axis_index(PATCH) * lay.away_frames + jnp.arange(lay.away_frames, dtype=jnp.int32)
    my_slots = jnp.where(my_frames < frames, frame_slots(clip_lengths[0], my_frames), -1)
    cls_pick = (my_slots[None, :] == jnp.arange(CLS_ROWS, dtype=jnp.int32)[:, None]).astype(f32)

    def home_order(values):
        return jnp.transpose(values, (1, 0, 2)).reshape(lay.home_rows, width)

    def given_order(values):
        return jnp.transpose(values.reshape(patch_rows, frames, width), (1, 0, 2))

    cls_aug = jnp.pad(cls_tokens.astype(f32), ((0, CLS_ROWS - clip_count), (0, 0)))
    residual = home_order(tokens).astype(f32)
    cotangent_away = lay.to_away(home_order(cotangent))
    stored = []
    for layer in range(LAYERS):
        gains, biases = norm_gains[layer], norm_biases[layer]
        normed, scaled_t, inverse_t = layer_norm(residual, gains[0], biases[0])
        normed_t = normed.astype(bf16)
        qkv_t = project(normed_t, time_proj[layer]).astype(bf16)
        mixed_t = time_forward(bias, qkv_t)
        residual = residual + project(mixed_t, time_output[layer])
        away = lay.to_away(residual.astype(bf16))
        away = away + jnp.pad(cls_aug, ((away_rows, 0), (0, 0)))
        normed, scaled_s, inverse_s = layer_norm(away, gains[1], biases[1])
        normed_s = normed.astype(bf16)
        qkv_s = project(normed_s, space_proj[layer]).astype(bf16)
        mixed_s = space_forward(my_slots, qkv_s, lay.away_frames, patches)
        away = away[:away_rows] + project(mixed_s, space_output[layer])
        normed, scaled_f, inverse_f = layer_norm(away, gains[2], biases[2])
        normed_f = normed.astype(bf16)
        hidden = project(normed_f, up_weight[layer])
        active = gelu_value(hidden).astype(bf16)
        away = away + project(active, down_weight[layer])
        residual = lay.to_home(away.astype(bf16))
        stored.append(
            dict(
                normed_t=normed_t, scaled_t=scaled_t, inverse_t=inverse_t, qkv_t=qkv_t, mixed_t=mixed_t,
                normed_s=normed_s, scaled_s=scaled_s, inverse_s=inverse_s, qkv_s=qkv_s, mixed_s=mixed_s,
                normed_f=normed_f, scaled_f=scaled_f, inverse_f=inverse_f, hidden=hidden, active=active,
            )
        )
    output = given_order(residual.astype(bf16))

    grad_cls = jnp.zeros_like(cls_aug)
    grad_away = cotangent_away[:away_rows]
    results = [None] * LAYERS
    for layer in reversed(range(LAYERS)):
        saved = stored[layer]
        gains = norm_gains[layer]
        branch = grad_away.astype(bf16)
        grad_down = weight_grad(saved["active"], branch)
        grad_active = project_back(branch, down_weight[layer])
        grad_hidden = (grad_active * gelu_slope(saved["hidden"])).astype(bf16)
        grad_up = weight_grad(saved["normed_f"], grad_hidden)
        grad_normed = project_back(grad_hidden, up_weight[layer])
        grad_input, gain_two, bias_two = norm_back(
            grad_normed, saved["scaled_f"], saved["inverse_f"], gains[2]
        )
        grad_away = grad_away + grad_input
        branch = grad_away.astype(bf16)
        grad_space_out = weight_grad(saved["mixed_s"], branch)
        grad_mixed = project_back(branch, space_output[layer]).astype(bf16)
        dq, dk, dv, dck, dcv = space_backward(my_slots, saved["qkv_s"], grad_mixed, lay.away_frames, patches)
        dcls = jnp.concatenate([dck[:, 0], dcv[:, 0]], -1)
        dcls = jnp.dot(cls_pick, dcls, precision=lax.Precision.HIGHEST)
        dcls = jnp.pad(dcls.astype(bf16), ((0, 0), (width, 0)))
        grad_qkv = jnp.concatenate([jnp.concatenate([dq, dk, dv], -1), dcls], 0)
        grad_space_proj = weight_grad(saved["normed_s"], grad_qkv)
        grad_normed = project_back(grad_qkv, space_proj[layer])
        grad_input, gain_one, bias_one = norm_back(
            grad_normed, saved["scaled_s"], saved["inverse_s"], gains[1]
        )
        grad_away = grad_away + grad_input[:away_rows]
        grad_cls = grad_cls + grad_input[away_rows:]
        grad_home = lay.to_home(grad_away.astype(bf16))
        branch = grad_home.astype(bf16)
        grad_time_out = weight_grad(saved["mixed_t"], branch)
        grad_mixed = project_back(branch, time_output[layer]).astype(bf16)
        grad_qkv = time_backward(bias, saved["qkv_t"], grad_mixed)
        grad_time_proj = weight_grad(saved["normed_t"], grad_qkv)
        grad_normed = project_back(grad_qkv, time_proj[layer])
        grad_input, gain_zero, bias_zero = norm_back(
            grad_normed, saved["scaled_t"], saved["inverse_t"], gains[0]
        )
        grad_home = grad_home + grad_input
        if layer > 0:
            grad_away = lay.to_away(grad_home.astype(bf16))[:away_rows]
        large = (grad_time_proj, grad_time_out, grad_space_proj, grad_space_out, grad_up, grad_down)
        large = [lax.psum_scatter(part, PATCH, scatter_dimension=0, tiled=True) for part in large]
        large = lax.psum(large, CLIP)
        small = (jnp.stack([gain_zero, gain_one, gain_two]), jnp.stack([bias_zero, bias_one, bias_two]))
        results[layer] = [part.astype(f32) for part in large] + list(small)
    grad_tokens = given_order(grad_home.astype(bf16))
    stacked = [jnp.stack([results[layer][i] for layer in range(LAYERS)]) for i in range(8)]
    small = jnp.stack(stacked[6:])
    small = lax.psum(small, (PATCH, CLIP))
    share = width // devices
    small = lax.dynamic_slice_in_dim(small, lax.axis_index(PATCH) * share, share, 3)
    grad_cls = lax.psum(grad_cls[:clip_count], PATCH)
    return (output, grad_tokens, grad_cls, *stacked[:6], small[0], small[1])


def solution(mesh):
    in_specs = (
        P(CLIP, PATCH, None),
        P(CLIP, None),
        P(CLIP, None),
        P(),
        P(),
        P(),
        P(),
        P(),
        P(),
        P(),
        P(),
        P(CLIP, PATCH, None),
    )
    out_specs = (
        P(CLIP, PATCH, None),
        P(CLIP, PATCH, None),
        P(CLIP, None),
        P(None, PATCH, None),
        P(None, PATCH, None),
        P(None, PATCH, None),
        P(None, PATCH, None),
        P(None, PATCH, None),
        P(None, PATCH, None),
        P(None, None, PATCH),
        P(None, None, PATCH),
    )
    paired = (mesh.shape[CLIP], mesh.shape[PATCH]) == (4, 8)
    local = fast_local if paired else general_local
    return jax.shard_map(local, mesh=mesh, in_specs=in_specs, out_specs=out_specs, check_vma=False)
```

```python
import functools

import jax
import jax.numpy as jnp
import numpy as np
from jax import lax
from jax.experimental import pallas as pl
from jax.experimental.pallas import tpu as pltpu
from jax.sharding import PartitionSpec as P

HEADS = 12
HD = 64
LAYERS = 2
REAL_PATCH = 196
QUAD = 4
WIDE = QUAD * HD
QUADS = HEADS // QUAD
CLS_ROWS = 16

EPSILON = 1e-05
NEG_LARGE = -1e30
ROOT_HALF = 0.7071067811865476
INV_ROOT_TWO_PI = 0.3989422804014327
SCALE = HD**-0.5
VMEM_LIMIT = 48 * 1024 * 1024
VMEM_MOST = 62 * 1024 * 1024

CLIP = "clip"
PATCH = "patch"
f32 = jnp.float32
bf16 = jnp.bfloat16
MESH = pl.DeviceIdType.MESH


def layer_norm(values, norm_gain, norm_bias):
    centered = values - jnp.mean(values, -1, keepdims=True)
    inverse = lax.rsqrt(jnp.mean(centered * centered, -1, keepdims=True) + EPSILON)
    scaled = centered * inverse
    return (scaled * norm_gain + norm_bias, scaled, inverse)


def norm_back(grad_out, scaled, inverse, norm_gain):
    weighted = grad_out * norm_gain
    grad_input = inverse * (
        weighted
        - jnp.mean(weighted, -1, keepdims=True)
        - scaled * jnp.mean(weighted * scaled, -1, keepdims=True)
    )
    return (grad_input, jnp.sum(grad_out * scaled, 0), jnp.sum(grad_out, 0))


def project(left, matrix):
    return jnp.dot(left, matrix, preferred_element_type=f32)


def project_back(grad_out, matrix):
    return lax.dot_general(grad_out, matrix, (((1,), (1,)), ((), ())), preferred_element_type=f32)


def weight_grad(left, grad_out):
    return lax.dot_general(
        left, grad_out, (((0,), (0,)), ((), ())), preferred_element_type=f32
    ).astype(bf16)


def gelu_value(hidden):
    return 0.5 * hidden * (1.0 + lax.erf(hidden * ROOT_HALF))


def gelu_slope(hidden):
    return 0.5 * (1.0 + lax.erf(hidden * ROOT_HALF)) + hidden * INV_ROOT_TWO_PI * jnp.exp(
        -0.5 * hidden * hidden
    )


def dot_nt(left, right):
    return lax.dot_general(left, right, (((1,), (1,)), ((), ())), preferred_element_type=f32)


def dot_nn(left, right):
    return lax.dot_general(left, right, (((1,), (0,)), ((), ())), preferred_element_type=f32)


def dot_tn(left, right):
    return lax.dot_general(left, right, (((0,), (0,)), ((), ())), preferred_element_type=f32)


def spread_heads(rows):
    head = lax.broadcasted_iota(jnp.int32, rows.shape, 1) // HD
    return jnp.concatenate([jnp.where(head == h, rows, jnp.zeros_like(rows)) for h in range(QUAD)], 0)


def merge_heads(stacked):
    count = stacked.shape[0] // QUAD
    head = lax.broadcasted_iota(jnp.int32, (count, WIDE), 1) // HD
    merged = stacked[:count]
    for h in range(1, QUAD):
        merged = jnp.where(head == h, stacked[h * count : (h + 1) * count], merged)
    return merged


def probabilities(scores):
    exponents = [jnp.exp(part - jnp.max(part, 0, keepdims=True)) for part in scores]
    return [part * (1.0 / jnp.sum(part, 0, keepdims=True)) for part in exponents]


def forward_tiles(tiles, bias):
    spreads = [spread_heads(tile[0] * SCALE) for tile in tiles]
    scores = [dot_nt(tile[1], spread) + bias for tile, spread in zip(tiles, spreads)]
    probs = [part.astype(bf16) for part in probabilities(scores)]
    outs = [dot_tn(part, tile[2]) for part, tile in zip(probs, tiles)]
    return [merge_heads(part).astype(bf16) for part in outs]


def backward_tiles(tiles, bias):
    spreads = [spread_heads(tile[0] * SCALE) for tile in tiles]
    grad_spreads = [spread_heads(tile[3]) for tile in tiles]
    scores = [dot_nt(tile[1], spread) + bias for tile, spread in zip(tiles, spreads)]
    grad_probs = [dot_nt(tile[2], spread) for tile, spread in zip(tiles, grad_spreads)]
    probs = probabilities(scores)
    grad_scores = [
        (part * (grad - jnp.sum(part * grad, 0, keepdims=True))).astype(bf16)
        for part, grad in zip(probs, grad_probs)
    ]
    grad_queries = [dot_tn(grad, tile[1]) for grad, tile in zip(grad_scores, tiles)]
    grad_keys = [dot_nn(grad, spread) for grad, spread in zip(grad_scores, spreads)]
    grad_values = [dot_nn(part.astype(bf16), spread) for part, spread in zip(probs, grad_spreads)]
    return [(merge_heads(q) * SCALE, k, v) for q, k, v in zip(grad_queries, grad_keys, grad_values)]


def columns(part, quad, width):
    start = part * width + quad * WIDE
    return slice(start, start + WIDE)


def time_forward_kernel(bias_ref, qkv_ref, out_ref):
    width = out_ref.shape[1]
    bias = bias_ref[...]
    for quad in range(QUADS):
        parts = [qkv_ref[:, columns(part, quad, width)] for part in range(3)]
        out_ref[:, columns(0, quad, width)] = forward_tiles([parts], bias)[0]


def time_backward_kernel(bias_ref, qkv_ref, grad_ref, out_ref):
    width = grad_ref.shape[1]
    bias = bias_ref[...]
    for quad in range(QUADS):
        parts = [qkv_ref[:, columns(part, quad, width)] for part in range(3)]
        grads = backward_tiles([parts + [grad_ref[:, columns(0, quad, width)]]], bias)[0]
        for part in range(3):
            out_ref[:, columns(part, quad, width)] = grads[part].astype(bf16)


def group_rows(patch_count, frames):
    return (2 if patch_count % 2 == 0 else 1) * frames


def time_bias(same_clip, patch_count, frames):
    rows = group_rows(patch_count, frames)
    ids = jnp.arange(rows, dtype=jnp.int32)
    same_patch = (ids[:, None] // frames) == (ids[None, :] // frames)
    tiled = jnp.tile(same_clip, (rows // frames, rows // frames))
    return jnp.tile(jnp.where(same_patch & tiled, 0.0, NEG_LARGE).astype(f32), (1, QUAD))


def params(*semantics):
    return pltpu.CompilerParams(dimension_semantics=semantics, vmem_limit_bytes=VMEM_LIMIT)


def time_forward(bias, qkv):
    rows = bias.shape[0]
    width = qkv.shape[1] // 3
    return pl.pallas_call(
        time_forward_kernel,
        grid=(qkv.shape[0] // rows,),
        in_specs=[
            pl.BlockSpec(bias.shape, lambda i: (0, 0)),
            pl.BlockSpec((rows, 3 * width), lambda i: (i, 0)),
        ],
        out_specs=pl.BlockSpec((rows, width), lambda i: (i, 0)),
        out_shape=jax.ShapeDtypeStruct((qkv.shape[0], width), bf16),
        compiler_params=params("parallel"),
        name="time_forward",
    )(bias, qkv)


def time_backward(bias, qkv, grad_out):
    rows = bias.shape[0]
    width = qkv.shape[1] // 3
    return pl.pallas_call(
        time_backward_kernel,
        grid=(qkv.shape[0] // rows,),
        in_specs=[
            pl.BlockSpec(bias.shape, lambda i: (0, 0)),
            pl.BlockSpec((rows, 3 * width), lambda i: (i, 0)),
            pl.BlockSpec((rows, width), lambda i: (i, 0)),
        ],
        out_specs=pl.BlockSpec((rows, 3 * width), lambda i: (i, 0)),
        out_shape=jax.ShapeDtypeStruct(qkv.shape, bf16),
        compiler_params=params("parallel"),
        name="time_backward",
    )(bias, qkv, grad_out)


def with_class(slot, rows, cls_rows):
    ids = lax.broadcasted_iota(jnp.int32, cls_rows.shape, 0)
    picked = jnp.sum(jnp.where(ids == slot, cls_rows.astype(f32), 0.0), 0, keepdims=True)
    row_ids = lax.broadcasted_iota(jnp.int32, rows.shape, 0)
    return jnp.where(row_ids == REAL_PATCH, picked.astype(bf16), rows)


def key_bias(count):
    key_ids = lax.broadcasted_iota(jnp.int32, (count, 1), 0)
    return jnp.where(key_ids <= REAL_PATCH, 0.0, NEG_LARGE).astype(f32)


def space_forward_kernel(slot_ref, q_ref, k_ref, v_ref, ck_ref, cv_ref, out_ref):
    slot = slot_ref[pl.program_id(0)]
    keys = with_class(slot, k_ref[...], ck_ref[...])
    values = with_class(slot, v_ref[...], cv_ref[...])
    out_ref[...] = forward_tiles([(q_ref[...], keys, values)], key_bias(keys.shape[0]))[0]


def space_backward_kernel(
    slot_ref, q_ref, k_ref, v_ref, ck_ref, cv_ref, g_ref, dq_ref, dk_ref, dv_ref, dck_ref, dcv_ref
):
    slot = slot_ref[pl.program_id(0)]
    keys = with_class(slot, k_ref[...], ck_ref[...])
    values = with_class(slot, v_ref[...], cv_ref[...])
    tile = (q_ref[...], keys, values, g_ref[...])
    grad_q, grad_k, grad_v = backward_tiles([tile], key_bias(keys.shape[0]))[0]
    row_ids = lax.broadcasted_iota(jnp.int32, grad_k.shape, 0)
    dq_ref[...] = grad_q.astype(bf16)
    dk_ref[...] = jnp.where(row_ids < REAL_PATCH, grad_k, 0.0).astype(bf16)
    dv_ref[...] = jnp.where(row_ids < REAL_PATCH, grad_v, 0.0).astype(bf16)
    dck_ref[0] = jnp.sum(jnp.where(row_ids == REAL_PATCH, grad_k, 0.0), 0, keepdims=True)
    dcv_ref[0] = jnp.sum(jnp.where(row_ids == REAL_PATCH, grad_v, 0.0), 0, keepdims=True)


def space_specs(frames, patches):
    cls_block = frames * patches // CLS_ROWS

    def rows(part):
        return pl.BlockSpec((patches, WIDE), lambda f, c, s: (f, part * QUADS + c))

    def cls(part):
        return pl.BlockSpec((CLS_ROWS, WIDE), lambda f, c, s: (cls_block, part * QUADS + c))

    return [rows(0), rows(1), rows(2), cls(1), cls(2)], rows(0)


def space_forward(slots, qkv, frames, patches):
    width = qkv.shape[1] // 3
    in_specs, out_spec = space_specs(frames, patches)
    return pl.pallas_call(
        space_forward_kernel,
        grid_spec=pltpu.PrefetchScalarGridSpec(
            num_scalar_prefetch=1,
            grid=(frames, QUADS),
            in_specs=in_specs,
            out_specs=out_spec,
        ),
        out_shape=jax.ShapeDtypeStruct((frames * patches, width), bf16),
        compiler_params=params("parallel", "parallel"),
        name="space_forward",
    )(slots, qkv, qkv, qkv, qkv, qkv)


def space_backward(slots, qkv, grad_out, frames, patches):
    width = qkv.shape[1] // 3
    in_specs, out_spec = space_specs(frames, patches)
    rows = jax.ShapeDtypeStruct((frames * patches, width), bf16)
    cls_spec = pl.BlockSpec((1, 1, WIDE), lambda f, c, s: (f, 0, c))
    cls = jax.ShapeDtypeStruct((frames, 1, width), f32)
    return pl.pallas_call(
        space_backward_kernel,
        grid_spec=pltpu.PrefetchScalarGridSpec(
            num_scalar_prefetch=1,
            grid=(frames, QUADS),
            in_specs=in_specs + [out_spec],
            out_specs=[out_spec] * 3 + [cls_spec] * 2,
        ),
        out_shape=[rows] * 3 + [cls] * 2,
        compiler_params=params("parallel", "parallel"),
        name="space_backward",
    )(slots, qkv, qkv, qkv, qkv, qkv, grad_out)


def frame_slots(lengths_row, frame_ids):
    clip_ends = jnp.cumsum(lengths_row)
    return jnp.sum((frame_ids[:, None] >= clip_ends[None, :]).astype(jnp.int32), axis=1)


class Layout:
    def __init__(self, devices, frames, patches):
        self.devices = devices
        self.frames = frames
        self.patches = patches
        self.all_patches = patches * devices
        self.away_frames = -(-frames // devices)
        used = self.away_frames * patches
        self.block = -(-used // 16) * 16
        self.home_rows = frames * patches
        self.away_rows = self.away_frames * self.all_patches
        self.sent_rows = devices * self.block

    def home_of_sent(self):
        row = jnp.arange(self.sent_rows, dtype=jnp.int32)
        peer, inner = row // self.block, row % self.block
        frame = peer * self.away_frames + inner // self.patches
        valid = (inner < self.away_frames * self.patches) & (frame < self.frames)
        return jnp.where(valid, (inner % self.patches) * self.frames + frame, -1)

    def sent_of_away(self):
        row = jnp.arange(self.away_rows + CLS_ROWS, dtype=jnp.int32)
        frame, patch = row // self.all_patches, row % self.all_patches
        sent = (patch // self.patches) * self.block + frame * self.patches + patch % self.patches
        return jnp.where(row < self.away_rows, sent, -1)

    def parts(self):
        step = self.block // 5 // 16 * 16
        return ((0, step), (step, 3 * step), (3 * step, self.block))

    def frame_parts(self):
        ends = [-(-self.patches * (i + 1) // 16) * 16 for i in range(self.away_frames)]
        return tuple(zip([0] + ends[:-1], ends))

    def frame_rows(self, frame):
        low, high = self.patches * frame, self.patches * (frame + 1)
        return low // 16 * 16, -(-high // 16) * 16

    def leave(self, order, parts):
        order = np.where(np.arange(self.block) < self.away_frames * self.patches, order, -1)
        rows = np.concatenate([order[:, low:high].reshape(-1) for low, high in parts])
        return np.asarray(rows, np.int32)[:, None]

    def orders(self):
        block, patches, near = self.block, self.patches, self.away_frames
        peer, inner = np.meshgrid(range(self.devices), range(block), indexing="ij")
        by_patch = inner // near * self.frames + peer * near + inner % near
        by_frame = inner % patches * self.frames + peer * near + inner // patches
        from_away = inner // patches * self.all_patches + peer * patches + inner % patches
        row = np.arange(self.away_rows)
        frame, patch = row // self.all_patches, row % self.all_patches
        reach_patch = patch // patches * block + patch % patches * near + frame
        low = np.array([self.frame_rows(i)[0] for i in range(near)])[frame]
        high = np.array([self.frame_rows(i)[1] for i in range(near)])[frame]
        reach_frame = patch // patches * (high - low) + frame * patches + patch % patches - low
        row = np.arange(self.home_rows)
        patch, frame = row // self.frames, row % self.frames
        reach_home = frame // near * block + frame % near * patches + patch

        def column(rows):
            return np.asarray(rows, np.int32)[:, None]

        return dict(
            leave_patch=self.leave(by_patch, self.parts()),
            leave_frame=self.leave(by_frame, self.frame_parts()),
            leave_away=self.leave(from_away, self.parts()),
            reach_patch=column(reach_patch),
            reach_frame=column(reach_frame),
            reach_home=column(reach_home),
        )

    def to_away(self, values):
        pick = self.home_of_sent()[:, None] == jnp.arange(self.home_rows, dtype=jnp.int32)[None, :]
        sent = jnp.dot(pick.astype(bf16), values, preferred_element_type=bf16)
        got = lax.all_to_all(sent, PATCH, split_axis=0, concat_axis=0, tiled=True)
        pick = self.sent_of_away()[:, None] == jnp.arange(self.sent_rows, dtype=jnp.int32)[None, :]
        return jnp.dot(pick.astype(bf16), got, preferred_element_type=f32)

    def to_home(self, values):
        pick = jnp.arange(self.sent_rows, dtype=jnp.int32)[:, None] == self.sent_of_away()[None, : self.away_rows]
        sent = jnp.dot(pick.astype(bf16), values, preferred_element_type=bf16)
        got = lax.all_to_all(sent, PATCH, split_axis=0, concat_axis=0, tiled=True)
        pick = jnp.arange(self.home_rows, dtype=jnp.int32)[:, None] == self.home_of_sent()[None, :]
        return jnp.dot(pick.astype(bf16), got, preferred_element_type=f32)


def norm_rows(values):
    centered = values - jnp.mean(values, -1, keepdims=True)
    inverse = lax.rsqrt(jnp.mean(centered * centered, -1, keepdims=True) + EPSILON)
    return centered, inverse


def norm_forward(values, gain, shift):
    centered, inverse = norm_rows(values)
    return (centered * inverse * gain + shift).astype(bf16)


def norm_backward(values, grad, gain, sums):
    centered, inverse = norm_rows(values)
    weighted = grad * gain
    along = jnp.mean(weighted * centered, -1, keepdims=True) * (inverse * inverse * inverse)

    def fold(part):
        return jnp.sum(part.reshape(part.shape[0] // 8, 8, part.shape[1]), 0)

    sums[0][...] += fold(grad * (centered * inverse))
    sums[1][...] += fold(grad)
    return inverse * (weighted - jnp.mean(weighted, -1, keepdims=True)) - centered * along


class Loads:
    def __init__(self, sources, buffers, sems):
        self.copies = [
            pltpu.make_async_copy(source, buffer, sems.at[i])
            for i, (source, buffer) in enumerate(zip(sources, buffers))
        ]
        for copy in self.copies:
            copy.start()
        self.buffers = buffers
        self.next = 0

    def get(self):
        self.copies[self.next].wait()
        self.next += 1
        return self.buffers[self.next - 1]


class Saves:
    def __init__(self, buffers, targets, sems):
        self.pairs, self.sems = list(zip(buffers, targets)), sems

    def copies(self, part, start, rows):
        here = pl.ds(start, rows)
        return [
            pltpu.make_async_copy(buffer.at[here], target.at[here], self.sems.at[i, part])
            for i, (buffer, target) in enumerate(self.pairs)
        ]

    def put(self, part, start, rows):
        for copy in self.copies(part, start, rows):
            copy.start()

    def finish(self, part, start, rows):
        for copy in self.copies(part, start, rows):
            copy.wait()


class Place:
    AXES = {"core": (PATCH, 1), "zl": (PATCH, 2), "zh": (PATCH, 4), "x": (CLIP, 1), "y": (CLIP, 2)}

    def __init__(self):
        self.clip, self.patch = lax.axis_index(CLIP), lax.axis_index(PATCH)
        self.me = {
            "core": lax.rem(self.patch, 2),
            "zl": lax.rem(self.patch // 2, 2),
            "zh": self.patch // 4,
            "x": lax.rem(self.clip, 2),
            "y": self.clip // 2,
        }

    def peer(self, dim):
        axis, stride = self.AXES[dim]
        own = self.clip if axis == CLIP else self.patch
        other = own + stride - 2 * stride * self.me[dim]
        return (other, self.patch) if axis == CLIP else (self.clip, other)


class Shuffle:
    def __init__(self, lay, at, sent, got, send_sem, recv_sem):
        self.lay, self.devices, self.parts, self.at = lay, lay.devices, lay.parts(), at
        self.sent, self.got, self.send_sem, self.recv_sem = sent, got, send_sem, recv_sem
        self.moves = 0

    def greet(self):
        for offset in range(1, self.devices):
            other = (self.at.clip, lax.rem(self.at.patch + offset, self.devices))
            pl.semaphore_signal(pltpu.get_barrier_semaphore(), inc=1, device_id=other, device_id_type=MESH)

    def meet(self, others=0):
        pl.semaphore_wait(pltpu.get_barrier_semaphore(), self.devices - 1 + others)

    def copy(self, offset, part):
        two = self.moves % 2
        other = lax.rem(self.at.patch + offset, self.devices)
        low, high = self.parts[part]
        rows = pl.ds(low, high - low)
        return pltpu.make_async_remote_copy(
            src_ref=self.sent.at[other, rows],
            dst_ref=self.got.at[two, self.at.patch, rows],
            send_sem=self.send_sem.at[part, offset],
            recv_sem=self.recv_sem.at[two, part, offset],
            device_id=(self.at.clip, other),
            device_id_type=MESH,
        )

    def send(self, part, order_ref, source_ref, first, last):
        width = self.sent.shape[-1]
        low, high = self.parts[part]
        rows = (high - low) * self.devices
        start = low * self.devices
        ids = lax.broadcasted_iota(jnp.int32, (rows, last - first), 1) + first
        pick = (order_ref[start : start + rows, :] == ids).astype(f32).astype(bf16)
        picked = dot_nn(pick, source_ref[first:last, :]).astype(bf16)
        self.sent[:, low:high, :] = picked.reshape(self.devices, high - low, width)
        for offset in range(1, self.devices):
            self.copy(offset, part).start()
        self.got[self.moves % 2, self.at.patch, low:high, :] = self.sent[self.at.patch, low:high, :]

    def send_all(self, order_ref, source_ref):
        for part in range(len(self.parts)):
            self.send(part, order_ref, source_ref, 0, source_ref.shape[0])

    def arrive(self, part):
        for offset in range(1, self.devices):
            self.copy(offset, part).wait()

    def receive(self, order_ref, target_ref):
        for part in range(len(self.parts)):
            self.arrive(part)
        devices, block, width = self.got.shape[1:]
        rows = target_ref.shape[0] // 3
        ids = lax.broadcasted_iota(jnp.int32, (rows, devices * block), 1)
        for start in range(0, target_ref.shape[0], rows):
            pick = (order_ref[start : start + rows, :] == ids).astype(f32).astype(bf16)
            got = self.got[self.moves % 2].reshape(devices * block, width)
            target_ref[start : start + rows, :] = dot_nn(pick, got).astype(bf16)
        self.moves += 1

    def receive_frame(self, frame, order_ref, target_ref):
        self.arrive(frame)
        low, high = self.lay.frame_rows(frame)
        patches = self.lay.all_patches
        here = slice(frame * patches, (frame + 1) * patches)
        width = self.got.shape[-1]
        got = self.got[self.moves % 2, :, low:high, :].reshape(self.devices * (high - low), width)
        ids = lax.broadcasted_iota(jnp.int32, (patches, got.shape[0]), 1)
        pick = (order_ref[here, :] == ids).astype(f32).astype(bf16)
        target_ref[here, :] = dot_nn(pick, got).astype(bf16)


def slot_of(lengths_ref, frames):
    end, slot = 0, 0
    for clip in range(lengths_ref.shape[0]):
        end = end + lengths_ref[clip]
        slot = slot + (frames >= end).astype(jnp.int32)
    return slot


def fill_bias(lengths_ref, frames, bias_ref):
    rows = bias_ref.shape[0]

    def split(ids, size, count):
        which = jnp.zeros_like(ids)
        for i in range(1, count):
            which = which + (ids >= i * size).astype(jnp.int32)
        return which, ids - which * size

    key_patch, key_frame = split(lax.broadcasted_iota(jnp.int32, bias_ref.shape, 0), frames, rows // frames)
    _, query = split(lax.broadcasted_iota(jnp.int32, bias_ref.shape, 1), rows, QUAD)
    query_patch, query_frame = split(query, frames, rows // frames)
    same = (key_patch == query_patch) & (slot_of(lengths_ref, key_frame) == slot_of(lengths_ref, query_frame))
    bias_ref[...] = jnp.where(same, 0.0, NEG_LARGE).astype(f32)


def cls_rows_of(cls_ref):
    values = cls_ref[...].astype(f32)
    return jnp.concatenate([values, jnp.zeros((CLS_ROWS - values.shape[0], values.shape[1]), f32)], 0)


def norm_row(norms_ref, layer, which):
    return norms_ref[which, layer : layer + 1, :]


def time_tiles(bias_ref, qkv_ref, width, group, grad_ref=None):
    rows = bias_ref.shape[0]
    here = pl.ds(pl.multiple_of(group * rows, 16), rows)
    tiles = []
    for quad in range(QUADS):
        tile = [qkv_ref[here, columns(part, quad, width)] for part in range(3)]
        if grad_ref is not None:
            tile.append(grad_ref[here, columns(0, quad, width)])
        tiles.append(tile)
    return here, tiles


def space_tiles(patches, total, slot, qkv_ref, width, frame, grad_ref=None):
    here = pl.ds(pl.multiple_of(frame * patches, 16), patches)
    tiles = []
    for quad in range(QUADS):
        tile = [qkv_ref[here, columns(part, quad, width)] for part in range(3)]
        for part in (1, 2):
            tile[part] = with_class(slot, tile[part], qkv_ref[total : total + CLS_ROWS, columns(part, quad, width)])
        if grad_ref is not None:
            tile.append(grad_ref[here, columns(0, quad, width)])
        tiles.append(tile)
    return here, tiles


def group_parts(lay, rows):
    ends = []
    for _, high in lay.parts():
        patches = min(-(-high // lay.away_frames), lay.patches)
        ends.append(-(-patches * lay.frames // rows) * rows)
    return tuple(zip([0] + ends[:-1], ends))


SAVED = ("normed_t", "qkv_t", "mixed_t", "x_away", "normed_s", "qkv_s", "mixed_s", "middle", "normed_f", "active", "slope")
WEIGHTS = ("time_proj", "time_output", "space_proj", "space_output", "up", "down")


def forward_kernel(lay, *refs):
    lengths_ref, norms_ref, shifts_ref, cls_ref, leave_frame, reach_frame, leave_away, reach_home = refs[:8]
    refs = refs[1:]
    sources = dict(zip(WEIGHTS, refs[7:13]))
    tokens_hbm, grad_hbm = refs[13:15]
    home_hbm, grad_away_hbm, result_hbm = refs[15:18]
    saved = [dict(zip(SAVED, refs[18 + len(SAVED) * layer :][: len(SAVED)])) for layer in range(LAYERS)]
    refs = refs[18 + len(SAVED) * LAYERS :]
    weights = dict(zip(WEIGHTS, refs[:6]))
    staged = dict(zip(SAVED, refs[6 : 6 + len(SAVED)]))
    bias_ref, x_home, after, grad, grad_away = refs[6 + len(SAVED) :][:5]
    sem_weight, sem_ends, sem_time, sem_space, sem_cls, *moving = refs[11 + len(SAVED) :]
    normed_t, qkv_t, mixed_t, x_away, normed, qkv, mixed, middle, normed_f, active, slope = (staged[name] for name in SAVED)
    total, width = x_away.shape
    home = x_home.shape[0]
    patches, frames = lay.all_patches, lay.away_frames
    group = bias_ref.shape[0]
    columns_of = [slice(start, start + width) for start in range(0, 3 * width, width)]

    load_x = pltpu.make_async_copy(tokens_hbm, x_home, sem_ends.at[0])
    load_grad = pltpu.make_async_copy(grad_hbm, grad, sem_ends.at[1])
    save_home = pltpu.make_async_copy(x_home, home_hbm, sem_ends.at[2])
    save_result = pltpu.make_async_copy(after, result_hbm, sem_ends.at[3])
    save_grad = pltpu.make_async_copy(grad_away, grad_away_hbm, sem_ends.at[4])
    load_x.start()
    load_grad.start()

    def fetch(layer, i):
        return pltpu.make_async_copy(sources[WEIGHTS[i]].at[layer], weights[WEIGHTS[i]], sem_weight.at[i])

    fetch(0, 0).start()
    at = Place()
    coming, leaving = [Shuffle(lay, at, *moving[:4]) for _ in range(2)]
    extra = Shuffle(lay, at, *moving[4:])
    coming.parts = extra.parts = lay.frame_parts()
    coming.greet()
    fill_bias(lengths_ref, lay.frames, bias_ref)
    key_mask = key_bias(patches)
    cls = cls_rows_of(cls_ref)
    load_grad.wait()
    coming.meet()
    extra.send(0, leave_frame, grad, 0, home)
    load_x.wait()

    for layer in range(LAYERS):
        more = layer < LAYERS - 1
        coming.moves, leaving.moves = 2 * layer, 2 * layer + 1
        if not more:
            extra.send(1, leave_frame, grad, 0, home)
        here = saved[layer]
        time_saves = Saves([staged[name] for name in SAVED[:3]], [here[name] for name in SAVED[:3]], sem_time)
        space_saves = Saves([staged[name] for name in SAVED[3:]], [here[name] for name in SAVED[3:]], sem_space)
        cls_saves = Saves([normed, qkv], [here["normed_s"], here["qkv_s"]], sem_cls)

        gain, shift = norm_row(norms_ref, layer, 0), norm_row(shifts_ref, layer, 0)
        for start in range(0, home, home // 3):
            rows = slice(start, start + home // 3)
            normed_t[rows, :] = norm_forward(x_home[rows, :].astype(f32), gain, shift)
        fetch(layer, 0).wait()
        if layer == 0:
            for i in range(1, len(WEIGHTS)):
                fetch(0, i).start()
        for these in columns_of:
            qkv_t[:, these] = dot_nn(normed_t[...], weights["time_proj"][:, these]).astype(bf16)
        if more:
            fetch(layer + 1, 0).start()

        @pl.loop(0, home // group)
        def _(index):
            rows, tiles = time_tiles(bias_ref, qkv_t, width, index)
            for quad, done in enumerate(forward_tiles(tiles, bias_ref[...])):
                mixed_t[rows, columns(0, quad, width)] = done

        fetch(layer, 1).wait()
        after[...] = (x_home[...].astype(f32) + dot_nn(mixed_t[...], weights["time_output"][...])).astype(bf16)
        for part in range(frames):
            coming.send(part, leave_frame, after, 0, home)
        if more:
            fetch(layer + 1, 1).start()
        time_saves.put(0, 0, home)

        gain, shift = norm_row(norms_ref, layer, 1), norm_row(shifts_ref, layer, 1)
        gain_f, shift_f = norm_row(norms_ref, layer, 2), norm_row(shifts_ref, layer, 2)
        normed[total:, :] = norm_forward(cls, gain, shift)
        fetch(layer, 2).wait()
        for these in columns_of:
            qkv[total:, these] = dot_nn(normed[total:, :], weights["space_proj"][:, these]).astype(bf16)
        cls_saves.put(0, total, CLS_ROWS)
        for i in range(3, len(WEIGHTS)):
            fetch(layer, i).wait()

        @pl.loop(0, frames)
        def _(frame, layer=layer, more=more, space_saves=space_saves, gain=gain, shift=shift, gain_f=gain_f, shift_f=shift_f):
            for number in range(frames):

                @pl.when(frame == number)
                def _(number=number, more=more):
                    coming.receive_frame(number, reach_frame, x_away)
                    if number == frames - 1 and not more:
                        extra.send(2, leave_frame, grad, 0, home)

            start = pl.multiple_of(frame * patches, 16)
            rows = pl.ds(start, patches)
            normed[rows, :] = norm_forward(x_away[rows, :].astype(f32), gain, shift)
            for these in columns_of:
                qkv[rows, these] = dot_nn(normed[rows, :], weights["space_proj"][:, these]).astype(bf16)
            slot = slot_of(lengths_ref, at.patch * frames + frame)
            _, tiles = space_tiles(patches, total, slot, qkv, width, frame)
            for quad, done in enumerate(forward_tiles(tiles, key_mask)):
                mixed[rows, columns(0, quad, width)] = done
            residual = x_away[rows, :].astype(f32) + dot_nn(mixed[rows, :], weights["space_output"][...])
            middle[rows, :] = residual.astype(bf16)
            normed_f[rows, :] = norm_forward(residual, gain_f, shift_f)
            for column in range(0, active.shape[1], WIDE):
                these = slice(column, column + WIDE)
                hidden = dot_nn(normed_f[rows, :], weights["up"][:, these])
                share = 0.5 * (1.0 + lax.erf(hidden * ROOT_HALF))
                active[rows, these] = (hidden * share).astype(bf16)
                bend = share + hidden * (INV_ROOT_TWO_PI * jnp.exp(-0.5 * hidden * hidden))
                slope[rows, these] = bend.astype(bf16)
            after[rows, :] = (residual + dot_nn(active[rows, :], weights["down"][...])).astype(bf16)
            space_saves.put(frame, start, patches)
            for number in range(frames - 1):

                @pl.when(frame == number)
                def _(number=number, more=more):
                    if more:
                        leaving.send(number, leave_away, after, 0, (number + 1) * patches)

        time_saves.finish(0, 0, home)
        if more:
            leaving.send(frames - 1, leave_away, after, (frames - 2) * patches, total)
            for i in range(2, len(WEIGHTS)):
                fetch(layer + 1, i).start()
            leaving.receive(reach_home, x_home)
            save_home.start()
        else:
            save_result.start()
            for frame in range(frames):
                extra.receive_frame(frame, reach_frame, grad_away)
            save_grad.start()
        for frame in range(frames):
            space_saves.finish(frame, frame * patches, patches)
        cls_saves.finish(0, total, CLS_ROWS)
    for copy in (save_home, save_result, save_grad):
        copy.wait()


CHUNKS = 16
TOTAL = CHUNKS * LAYERS
BLOCKS = 3
PIECE = (48, 128)
ROUTES = (("x", "zl", "zh", "y", "x", "y"), ("y", "x", "zl", "zh", "y", "x"), ("y", "x", "zl", "zh", "x", "y"))
SUMS = 4
STAGES = 7
RAW_SLOTS = 8
ACC_SLOTS = 8
BOX_SLOTS = 4
STRIDE = 2
SEGMENTS = (4, 4, 1, 3, 1, 3)
PLAN = {
    1: dict(early=3, down=2, hidden=1, wide=1, norm=0, frames=(2, 0, 0), up=1, space_out=2, space_proj=1, time_early=0, home=0, time0=1, time1=1, time2=0, time_out=1, time_proj=3),
    0: dict(early=2, down=1, hidden=1, wide=1, norm=0, frames=(2, 0, 1), up=2, space_out=0, space_proj=1, time_early=0, home=1, time0=0, time1=1, time2=1, time_out=1, time_proj=3),
}
SMALL = ("core", "zl", "zh", "x", "y")
SMALL_ROWS = 24


def recv_shape(route, stage):
    left = [dim for dim in ("zh", "zl", "x", "y") if dim not in route[: stage + 1]]
    return (2,) * len(left) + PIECE


class Pump:
    def __init__(self, at, results, scratch):
        self.at, self.results = at, results
        self.raw, self.core_in, self.acc, self.out, *rest = scratch
        self.inboxes = rest[: BLOCKS * SUMS]
        self.core_send, self.core_recv, self.core_free, self.send_sem, self.recv_sem = rest[BLOCKS * SUMS :]
        self.made = self.stepped = 0

    def core_copy(self, c, z):
        slot = lax.rem(c, RAW_SLOTS)
        return pltpu.make_async_remote_copy(
            src_ref=self.raw.at[slot, z // 2, z % 2, 1 - self.at.me["core"]],
            dst_ref=self.core_in.at[slot, z // 2, z % 2],
            send_sem=self.core_send.at[slot, z],
            recv_sem=self.core_recv.at[slot, z],
            device_id=self.at.peer("core"),
            device_id_type=MESH,
        )

    def claim(self, c, known):
        if known >= RAW_SLOTS:
            pl.semaphore_wait(self.core_free, 1)

    def store(self, c, z, core, block, rows):
        slot = lax.rem(c, RAW_SLOTS)
        for xh in range(2):
            for yh in range(2):
                part = rows[xh * 48 : (xh + 1) * 48, yh * 128 : (yh + 1) * 128]
                self.raw[slot, z // 2, z % 2, core, block, xh, yh] = part.astype(bf16)

    def make_chunks(self, count, lhs, rhs):
        first = self.made

        def one(i, c, known):
            self.claim(c, known)
            for half in range(2):
                left = lhs(slice(half * 384, (half + 1) * 384))
                for block in range(BLOCKS):
                    done = dot_tn(left, rhs(i, block * 256))
                    for j in range(4):
                        self.store(c, half * 2 + j // 2, j % 2, block, done[j * 96 : (j + 1) * 96])
            for z in range(4):
                self.core_copy(c, z).start()

        if count == 1:
            one(0, first, first)
        else:
            assert (first >= RAW_SLOTS) == (first + count - 1 >= RAW_SLOTS)

            @pl.loop(0, count)
            def _(i):
                one(i, first + i, first)

        self.made += count
        assert self.made - self.stepped <= RAW_SLOTS

    def make_down(self, lhs, rhs):
        first = self.made

        @pl.loop(0, 4)
        def _(z):
            if first >= RAW_SLOTS:

                @pl.when(z == 0)
                def _():
                    pl.semaphore_wait(self.core_free, 4)

            for core in range(2):
                left = lhs(pl.ds(pl.multiple_of(z * 768 + core * 384, 128), 384))
                for block in range(BLOCKS):
                    done = dot_tn(left, rhs[:, block * 256 : (block + 1) * 256])
                    for c in range(4):
                        self.store_at(first + c, z, core, block, done[c * 96 : (c + 1) * 96])
            for c in range(4):
                slot = (first + c) % RAW_SLOTS
                zh, zl = z // 2, lax.rem(z, 2)
                pltpu.make_async_remote_copy(
                    src_ref=self.raw.at[slot, zh, zl, 1 - self.at.me["core"]],
                    dst_ref=self.core_in.at[slot, zh, zl],
                    send_sem=self.core_send.at[slot, z],
                    recv_sem=self.core_recv.at[slot, z],
                    device_id=self.at.peer("core"),
                    device_id_type=MESH,
                ).start()

        self.made += 4
        assert self.made - self.stepped <= RAW_SLOTS

    def store_at(self, c, z, core, block, rows):
        for xh in range(2):
            for yh in range(2):
                part = rows[xh * 48 : (xh + 1) * 48, yh * 128 : (yh + 1) * 128]
                self.raw[c % RAW_SLOTS, z // 2, lax.rem(z, 2), core, block, xh, yh] = part.astype(bf16)

    def part(self, c, block, stage, value):
        route = ROUTES[block]

        def pick(dim):
            if dim in route[:stage]:
                return self.at.me[dim]
            return value if dim == route[stage] else slice(None)

        return (lax.rem(c, ACC_SLOTS), pick("zh"), pick("zl"), block, pick("x"), pick("y"))

    def exchange(self, c, block, stage):
        me = self.at.me
        dim = ROUTES[block][stage]
        box = lax.rem(c, BOX_SLOTS)
        if stage < SUMS:
            src = self.acc.at[self.part(c, block, stage, 1 - me[dim])]
            dst = self.inboxes[block * SUMS + stage].at[box]
        else:
            slot = lax.rem(c, ACC_SLOTS)
            if stage == SUMS:
                src = dst = self.out.at[slot, block, me["x"], me["y"]]
            elif dim == "x":
                src = dst = self.out.at[slot, block, me["x"]]
            else:
                src = dst = self.out.at[slot, block, :, me["y"]]
        return pltpu.make_async_remote_copy(
            src_ref=src,
            dst_ref=dst,
            send_sem=self.send_sem.at[box, block, stage],
            recv_sem=self.recv_sem.at[box, block, stage],
            device_id=self.at.peer(dim),
            device_id_type=MESH,
        )

    def enter(self, c):
        me = self.at.me
        slot, into = lax.rem(c, RAW_SLOTS), lax.rem(c, ACC_SLOTS)
        for z in range(4):
            self.core_copy(c, z).wait()
        for zh in range(2):
            for zl in range(2):
                both = self.raw[slot, zh, zl, me["core"]].astype(f32) + self.core_in[slot, zh, zl].astype(f32)
                self.acc[into, zh, zl] = both.astype(bf16)

        @pl.when(c < TOTAL - RAW_SLOTS)
        def _():
            pl.semaphore_signal(self.core_free, inc=1, device_id=self.at.peer("core"), device_id_type=MESH)

        for block in range(BLOCKS):
            self.exchange(c, block, 0).start()

    def advance(self, c, stage):
        me = self.at.me
        slot, box = lax.rem(c, ACC_SLOTS), lax.rem(c, BOX_SLOTS)
        for block in range(BLOCKS):
            self.exchange(c, block, stage).wait()
            if stage < SUMS:
                where = self.part(c, block, stage, me[ROUTES[block][stage]])
                both = self.acc[where].astype(f32) + self.inboxes[block * SUMS + stage][box].astype(f32)
                if stage == SUMS - 1:
                    self.out[slot, block, me["x"], me["y"]] = both.astype(bf16)
                else:
                    self.acc[where] = both.astype(bf16)
            if stage + 1 < STAGES - 1:
                self.exchange(c, block, stage + 1).start()
            else:
                self.finish(c, block)

    def finish(self, c, block):
        slot = lax.rem(c, ACC_SLOTS)
        layer = LAYERS - 1 - c // CHUNKS
        inner = lax.rem(c, CHUNKS)
        start = 0
        for which, count in enumerate(SEGMENTS):

            @pl.when((inner >= start) & (inner < start + count))
            def _(which=which, start=start):
                for xh in range(2):
                    for yh in range(2):
                        part = self.out[slot, block, xh, yh]
                        column = block * 256 + yh * 128
                        if which == 0:
                            row = pl.multiple_of((inner - start) * 96 + xh * 48, 16)
                            self.results[which][layer, pl.ds(row, 48), column : column + 128] = part
                        else:
                            at = pl.ds(pl.multiple_of((inner - start) * 768 + column, 128), 128)
                            self.results[which][layer, xh * 48 : (xh + 1) * 48, at] = part

            start += count

    def run_step(self, t):
        for stage in reversed(range(STAGES)):
            c = t - STRIDE * stage

            @pl.when((c >= 0) & (c < TOTAL))
            def _(c=c, stage=stage):
                if stage == 0:
                    self.enter(c)
                else:
                    self.advance(c, stage - 1)

    def step(self, count=1):
        first = self.stepped
        self.stepped += count
        assert min(self.stepped, TOTAL) <= self.made

        @pl.loop(first, first + count)
        def _(t):
            self.run_step(t)

    def inside(self, count):
        first = self.stepped
        self.stepped += count
        assert min(self.stepped, TOTAL) <= self.made
        return first

    def frame_steps(self, counts):
        first = self.inside(sum(counts))
        a, b, c = counts

        def run(frame):
            second, third = (frame + 1) // 2, frame // 2
            low = first + a * second + b * third

            @pl.loop(low, low + a + (b - a) * second + (c - b) * third)
            def _(t):
                self.run_step(t)

        return run


class Small:
    def __init__(self, at, values, boxes, send_sem, recv_sem):
        self.at, self.values, self.boxes, self.send_sem, self.recv_sem = at, values, boxes, send_sem, recv_sem

    def rows(self, i):
        return SMALL_ROWS if i < 3 else 16

    def copy(self, i):
        part = pl.ds(0, self.rows(i))
        return pltpu.make_async_remote_copy(
            src_ref=self.values.at[part],
            dst_ref=self.boxes.at[i, part],
            send_sem=self.send_sem.at[i],
            recv_sem=self.recv_sem.at[i],
            device_id=self.at.peer(SMALL[i]),
            device_id_type=MESH,
        )

    def step(self, i):
        if i > 0:
            rows = slice(0, self.rows(i - 1))
            self.copy(i - 1).wait()
            self.values[rows] += self.boxes[i - 1, rows]
        if i < len(SMALL):
            self.copy(i).start()


class Ring:
    def __init__(self, sources, slots, sems):
        self.sources, self.slots, self.sems = sources, slots, sems
        self.depth = slots.shape[0]
        self.started = self.taken = 0
        for _ in range(self.depth):
            self.start()

    def copy(self, i):
        source = self.sources[i]
        slot = i % self.depth
        return pltpu.make_async_copy(source, self.slots.at[slot, pl.ds(0, source.shape[0])], self.sems.at[slot])

    def start(self):
        if self.started < len(self.sources):
            self.copy(self.started).start()
            self.started += 1

    def take(self):
        i = self.taken
        self.copy(i).wait()
        self.taken += 1
        return self.slots.at[i % self.depth, pl.ds(0, self.sources[i].shape[0])]

    def free(self):
        self.start()


class Single:
    def __init__(self, sources, buffer, sem):
        self.copies = [
            pltpu.make_async_copy(source, buffer.at[pl.ds(0, source.shape[0])], sem) for source in sources
        ]
        self.next = 0
        self.copies[0].start()

    def take(self):
        self.copies[self.next].wait()

    def free(self):
        self.next += 1
        if self.next < len(self.copies):
            self.copies[self.next].start()


def backward_kernel(lay, *refs):
    devices, patches = lay.devices, lay.all_patches
    lengths_ref, norms_ref, cls_ref, leave_home, reach_away, leave_away, reach_home = refs[:7]
    weights = dict(zip(WEIGHTS, refs[7:13]))
    grad_hbm, x_out_hbm = refs[13:15]
    names = ("x_home",) + SAVED
    refs = refs[15:]
    saved = [dict(zip(names, refs[len(names) * layer : len(names) * (layer + 1)])) for layer in range(LAYERS)]
    refs = refs[len(names) * LAYERS :]
    small_ref, *results, output_hbm, tokens_hbm = refs[:9]
    refs = refs[9:]
    hidden, qkv, dqkv, wide, mixed, branch, x_buf, grad_buf, home_buf, cls_sum, bias_ref, *refs = refs
    weight_slots, lhs_slots, sent, got, small_boxes, *sums = refs[:11]
    sem_hidden, sem_qkv, sem_x, sem_ends, sem_weight, sem_lhs, sem_sent, sem_got, small_send, small_recv = refs[11:21]
    pump_scratch = refs[21:]
    load_grad = pltpu.make_async_copy(grad_hbm, grad_buf, sem_ends.at[0])
    load_out = pltpu.make_async_copy(x_out_hbm, mixed, sem_ends.at[1])
    save_out = pltpu.make_async_copy(home_buf, output_hbm, sem_ends.at[2])
    save_tokens = pltpu.make_async_copy(mixed, tokens_hbm, sem_ends.at[3])
    load_out.start()
    load_grad.start()

    at = Place()
    shuffle = Shuffle(lay, at, sent, got, sem_sent, sem_got)
    shuffle.greet()
    for dim in ("x", "y"):
        pl.semaphore_signal(pltpu.get_barrier_semaphore(), inc=1, device_id=at.peer(dim), device_id_type=MESH)

    total, width = grad_buf.shape
    parts = range(0, 3 * width, width)
    order = tuple(reversed(range(LAYERS)))
    tiles, lhs = [], []
    for layer in order:
        wide_parts = range(0, weights["up"].shape[2], width)
        tiles += [weights["down"].at[layer, pl.ds(start, width), :] for start in wide_parts]
        tiles += [weights["up"].at[layer, :, pl.ds(start, width)] for start in wide_parts]
        tiles += [weights["space_output"].at[layer]]
        tiles += [weights["space_proj"].at[layer, :, pl.ds(start, width)] for start in parts]
        tiles += [weights["time_output"].at[layer]]
        tiles += [weights["time_proj"].at[layer, :, pl.ds(start, width)] for start in parts]
        here = saved[layer]
        lhs += [here["slope"].at[:, pl.ds(start, width)] for start in wide_parts]
        lhs += [here[name] for name in ("normed_f", "mixed_s", "normed_s", "mixed_t", "normed_t")]
    fill = Single([saved[layer]["active"] for layer in order], hidden, sem_hidden)
    pump = Pump(at, results, pump_scratch)
    small = Small(at, small_ref, small_boxes, small_send, small_recv)
    for part in sums:
        part[...] = jnp.zeros_like(part)
    small_ref[...] = jnp.zeros_like(small_ref)
    key_mask = key_bias(patches)
    cls = cls_rows_of(cls_ref)
    fill_bias(lengths_ref, lay.frames, bias_ref)

    def back_product(rows, source, count):
        for i in range(count):
            tile = ring.take()
            part = dot_nt(source[:rows, i * width : (i + 1) * width], tile[...])
            if i:
                wide[:rows, :] += part
            else:
                wide[:rows, :] = part
            ring.free()

    frames = total // patches
    group = bias_ref.shape[0]
    groups = group_parts(lay, group)

    def made_of(lhs_tile, source, first=0, rows=None):
        rows = source.shape[0] if rows is None else rows

        def rhs(i, start):
            column = pl.multiple_of((i + first) * width + start, 128) if not isinstance(i, int) else (i + first) * width + start
            return source[:rows, pl.ds(column, WIDE)]

        return (lambda these: lhs_tile[:, these]), rhs

    shuffle.meet(2)
    load_out.wait()
    shuffle.send_all(leave_away, mixed)
    load_grad.wait()
    dy = grad_buf
    fill.take()
    ring = Ring(tiles, weight_slots, sem_weight)
    left = Ring(lhs, lhs_slots, sem_lhs)
    load_qkv = Single([saved[layer][name] for layer in order for name in ("qkv_s", "qkv_t")], qkv, sem_qkv)
    load_x = Single(
        [saved[layer][name] for layer in order for name in ("middle", "x_away", "x_home")], x_buf, sem_x
    )

    for layer in order:
        last = layer == 0
        plan = PLAN[layer]

        def steps(site, plan=plan):
            if plan.get(site, 0):
                pump.step(plan[site])

        if last:
            fill.take()
        pump.make_down(lambda these: hidden[:, these], dy)
        steps("down")
        for start in range(0, hidden.shape[1], width):
            tile, slope = ring.take(), left.take()
            for block in range(0, width, WIDE):
                grad_active = dot_nt(dy[...], tile[block : block + WIDE, :])
                grad_hidden = grad_active * slope[:, block : block + WIDE].astype(f32)
                hidden[:, start + block : start + block + WIDE] = grad_hidden.astype(bf16)
            ring.free()
            left.free()
        normed_f = left.take()
        if plan["early"]:
            pump.make_chunks(plan["early"], *made_of(normed_f, hidden))
        steps("hidden")
        back_product(total, hidden, hidden.shape[1] // width)
        steps("wide")
        load_x.take()

        @pl.loop(0, frames)
        def _(frame, layer=layer):
            here = pl.ds(pl.multiple_of(frame * patches, 16), patches)
            part = norm_backward(x_buf[here, :].astype(f32), wide[here, :], norm_row(norms_ref, layer, 2), sums[0:2])
            both = dy[here, :].astype(f32) + part
            wide[here, :] = both
            branch[here, :] = both.astype(bf16)

        load_x.free()
        steps("norm")

        out_tile, *proj_tiles = [ring.take() for _ in range(4)]
        load_qkv.take()
        load_x.take()
        cls_sum[...] = jnp.zeros_like(cls_sum)
        gain = norm_row(norms_ref, layer, 1)
        frame_run = pump.frame_steps(plan["frames"]) if sum(plan["frames"]) else None

        @pl.loop(0, frames)
        def _(frame):
            here = pl.ds(pl.multiple_of(frame * patches, 16), patches)
            mixed[here, :] = dot_nt(branch[here, :], out_tile[...]).astype(bf16)
            slot = slot_of(lengths_ref, at.patch * frames + frame)
            _, these = space_tiles(patches, total, slot, qkv, width, frame, mixed)
            row_ids = lax.broadcasted_iota(jnp.int32, (patches, WIDE), 0)
            cls_ids = lax.broadcasted_iota(jnp.int32, (CLS_ROWS, WIDE), 0)
            for quad, grads in enumerate(backward_tiles(these, key_mask)):
                dqkv[here, columns(0, quad, width)] = grads[0].astype(bf16)
                for part in (1, 2):
                    where = columns(part, quad, width)
                    dqkv[here, where] = jnp.where(row_ids < REAL_PATCH, grads[part], 0.0).astype(bf16)
                    row = grads[part][REAL_PATCH : REAL_PATCH + 1]
                    cls_sum[:, where] += jnp.where(cls_ids == slot, row, 0.0)
            grad = sum(dot_nt(dqkv[here, i * width : (i + 1) * width], tile[...]) for i, tile in enumerate(proj_tiles))
            part = norm_backward(x_buf[here, :].astype(f32), grad, gain, sums[2:4])
            mixed[here, :] = (wide[here, :] + part).astype(bf16)
            for i in range(2):

                @pl.when(frame == i)
                def _(i=i, last=last):
                    if i == 0 and not last:
                        shuffle.receive(reach_home, home_buf)
                        save_out.start()
                    shuffle.send(i, leave_away, mixed, 0, (i + 1) * patches)

            if frame_run is not None:
                frame_run(frame)

        shuffle.send(2, leave_away, mixed, patches, total)
        load_x.free()
        load_qkv.free()
        dqkv[total:, :] = cls_sum[...].astype(bf16)
        grad = sum(dot_nt(dqkv[total:, i * width : (i + 1) * width], tile[...]) for i, tile in enumerate(proj_tiles))
        for _ in range(4):
            ring.free()
        part = norm_backward(cls, grad, gain, sums[2:4])
        small_ref[16:24] += part[:8]
        if plan["early"] < 4:
            pump.make_chunks(4 - plan["early"], *made_of(normed_f, hidden, plan["early"]))
        left.free()
        fill.free()
        steps("up")
        pump.make_chunks(1, *made_of(left.take(), branch))
        left.free()
        steps("space_out")
        pump.make_chunks(3, *made_of(left.take(), dqkv))
        left.free()
        steps("space_proj")
        if not last:
            save_out.wait()
        shuffle.receive(reach_home, home_buf)

        out_tile, *proj_tiles = [ring.take() for _ in range(4)]
        load_qkv.take()
        load_x.take()
        mixed_t = left.take()
        if plan["time_early"]:
            pump.make_chunks(1, *made_of(mixed_t, home_buf))
            left.free()
        steps("home")

        def close_part(number, layer=layer, last=last, proj_tiles=proj_tiles):
            first, end = groups[number]
            here = slice(first, end)
            grad = sum(dot_nt(dqkv[here, i * width : (i + 1) * width], tile[...]) for i, tile in enumerate(proj_tiles))
            part = norm_backward(x_buf[here, :].astype(f32), grad, norm_row(norms_ref, layer, 0), sums[4:6])
            mixed[here, :] = (home_buf[here, :].astype(f32) + part).astype(bf16)
            if not last:
                shuffle.send(number, leave_home, mixed, 0 if number < 2 else first, end)

        for number, (first, end) in enumerate(groups):
            here = slice(first, end)
            mixed[here, :] = dot_nt(home_buf[here, :], out_tile[...]).astype(bf16)

            @pl.loop(first // group, end // group)
            def _(index):
                at_rows, these = time_tiles(bias_ref, qkv, width, index, mixed)
                for quad, grads in enumerate(backward_tiles(these, bias_ref[...])):
                    for part in range(3):
                        dqkv[at_rows, columns(part, quad, width)] = grads[part].astype(bf16)

            if not last:
                close_part(number)
            steps("time%d" % number)
        if not last:
            load_qkv.free()
            load_x.free()
            for _ in range(4):
                ring.free()
        if not plan["time_early"]:
            pump.make_chunks(1, *made_of(mixed_t, home_buf))
            left.free()
        steps("time_out")
        pump.make_chunks(3, *made_of(left.take(), dqkv, rows=total))
        left.free()
        steps("time_proj")
        if last:
            for number in range(len(groups)):
                pump.step()
                close_part(number)
            save_tokens.start()
        for i, part in enumerate(sums):
            row = layer * 8 + (2, 5, 1, 4, 0, 3)[i]
            small_ref[row : row + 1, :] += jnp.sum(part[...], 0, keepdims=True)
            part[...] = jnp.zeros_like(part)
        if last:
            small.step(0)
            for i in range(1, len(SMALL) + 1):
                pump.step()
                small.step(i)
        else:
            shuffle.receive(reach_away, grad_buf)

    pump.step(TOTAL + STRIDE * (STAGES - 1) - pump.stepped)
    save_tokens.wait()


IN_VMEM = pl.BlockSpec(memory_space=pltpu.VMEM)
IN_SMEM = pl.BlockSpec(memory_space=pltpu.SMEM)
IN_HBM = pl.BlockSpec(memory_space=pl.ANY)


def shape(*dims, kind=bf16):
    return jax.ShapeDtypeStruct(dims, kind)


def vmem(*dims, kind=bf16):
    return pltpu.VMEM(dims, kind)


def queue(*counts):
    return pltpu.SemaphoreType.DMA(counts)


def whole_call(name, body, collective, near, far, out_near, out_far, scratch):
    return pl.pallas_call(
        body,
        in_specs=[IN_SMEM if part.ndim == 1 else IN_VMEM for part in near] + [IN_HBM] * len(far),
        out_specs=[IN_VMEM] * len(out_near) + [IN_HBM] * len(out_far),
        out_shape=[*out_near, *out_far],
        scratch_shapes=scratch,
        compiler_params=pltpu.CompilerParams(
            collective_id=collective, has_side_effects=True, vmem_limit_bytes=VMEM_MOST
        ),
        name=name,
    )(*near, *far)


def finish_kernel(small_ref, *refs):
    count = len(refs) // 2
    for source, target in zip(refs[:count], refs[count:-1]):
        target[...] = source[...].astype(target.dtype)
    refs[-1][...] = small_ref[16 : 16 + refs[-1].shape[0], :]


def finish(small, clip_count, parts, kinds, steps=3):
    specs, out = [], []
    width = small.shape[1]
    cls = jax.ShapeDtypeStruct((clip_count, width), f32)
    for part, kind in zip(parts, kinds):
        cut = part.ndim - 2 if part.shape[-2] % (steps * 16) == 0 else part.ndim - 1
        block = tuple(size // steps if dim == cut else size for dim, size in enumerate(part.shape))

        def index(i, cut=cut, ndim=part.ndim):
            return tuple(i if dim == cut else 0 for dim in range(ndim))

        specs.append(pl.BlockSpec(block, index))
        out.append(jax.ShapeDtypeStruct(part.shape, kind))
    return pl.pallas_call(
        finish_kernel,
        grid=(steps,),
        in_specs=[pl.BlockSpec(small.shape, lambda i: (0, 0)), *specs],
        out_specs=[*specs, pl.BlockSpec(cls.shape, lambda i: (0, 0))],
        out_shape=[*out, cls],
        compiler_params=pltpu.CompilerParams(vmem_limit_bytes=VMEM_MOST),
        name="finish",
    )(small, *parts)


def fast_local(
    tokens,
    cls_tokens,
    clip_lengths,
    time_proj,
    time_output,
    space_proj,
    space_output,
    up_weight,
    down_weight,
    norm_gains,
    norm_biases,
    cotangent,
):
    frames, patch_rows, width = tokens.shape
    devices = lax.axis_size(PATCH)
    hidden = up_weight.shape[2]
    lay = Layout(devices, frames, patch_rows)
    home, away, block = lay.home_rows, lay.away_rows, lay.block
    clip_count = cls_tokens.shape[0]
    group = group_rows(patch_rows, frames)
    orders = {name: jnp.asarray(part) for name, part in lay.orders().items()}

    def home_order(values):
        return jnp.transpose(values, (1, 0, 2)).reshape(home, width)

    def given_order(values):
        return jnp.transpose(values.reshape(patch_rows, frames, width), (1, 0, 2))

    parts = len(lay.parts())
    moving = [vmem(devices, block, width), vmem(2, devices, block, width), queue(parts, devices), queue(2, parts, devices)]
    extra = [vmem(devices, block, width), vmem(1, devices, block, width), queue(parts, devices), queue(1, parts, devices)]
    gains, shifts = [jnp.transpose(part, (1, 0, 2)) for part in (norm_gains, norm_biases)]
    lengths = clip_lengths[0]
    weights = (time_proj, time_output, space_proj, space_output, up_weight, down_weight)
    at_home = home_order(tokens)
    saved_shapes = [
        shape(home, width),
        shape(home, 3 * width),
        shape(home, width),
        shape(away, width),
        shape(away + CLS_ROWS, width),
        shape(away + CLS_ROWS, 3 * width),
        *[shape(away, width)] * 3,
        *[shape(away, hidden)] * 2,
    ]
    bias = vmem(group, QUAD * group, kind=f32)
    home_next, grad_away, x_out, *saved = whole_call(
        "forward",
        functools.partial(forward_kernel, lay),
        2,
        (lengths, gains, shifts, cls_tokens, *[orders[name] for name in ("leave_frame", "reach_frame", "leave_away", "reach_home")]),
        (*weights, at_home, home_order(cotangent)),
        [],
        [shape(home, width), shape(away, width), shape(away, width)] + saved_shapes * LAYERS,
        [
            *[vmem(*part.shape[1:]) for part in weights],
            *[vmem(*part.shape) for part in saved_shapes],
            bias,
            vmem(home, width),
            vmem(away, width),
            vmem(home, width),
            vmem(away, width),
            queue(len(weights)),
            queue(5),
            queue(3, 1),
            queue(len(SAVED) - 3, lay.away_frames),
            queue(2, 1),
            *moving,
            *extra,
        ],
    )
    stored = [(at_home, *saved[: len(SAVED)]), (home_next, *saved[len(SAVED) :])]

    inbox = [vmem(BOX_SLOTS, *recv_shape(ROUTES[b], s)) for b in range(BLOCKS) for s in range(SUMS)]
    single = pltpu.SemaphoreType.DMA
    share = width // devices
    small, *large, output, grad_tokens = whole_call(
        "backward",
        functools.partial(backward_kernel, lay),
        1,
        (lengths, gains, cls_tokens, *[orders[name] for name in ("leave_patch", "reach_patch", "leave_away", "reach_home")]),
        (*weights, grad_away, x_out, *stored[0], *stored[1]),
        [
            shape(SMALL_ROWS, width, kind=f32),
            shape(LAYERS, hidden // devices, width),
            shape(LAYERS, share, hidden),
            shape(LAYERS, share, width),
            shape(LAYERS, share, 3 * width),
            shape(LAYERS, share, width),
            shape(LAYERS, share, 3 * width),
        ],
        [shape(home, width), shape(home, width)],
        [
            vmem(away, hidden),
            vmem(away + CLS_ROWS, 3 * width),
            vmem(away + CLS_ROWS, 3 * width),
            vmem(away, width, kind=f32),
            *[vmem(away, width)] * 5,
            vmem(CLS_ROWS, 3 * width, kind=f32),
            bias,
            vmem(4, width, width),
            vmem(2, away + CLS_ROWS, width),
            *moving[:2],
            vmem(len(SMALL), SMALL_ROWS, width, kind=f32),
            *[vmem(8, width, kind=f32)] * 6,
            single,
            single,
            single,
            queue(4),
            queue(4),
            queue(2),
            *moving[2:],
            queue(len(SMALL)),
            queue(len(SMALL)),
            vmem(RAW_SLOTS, 2, 2, 2, BLOCKS, 2, 2, *PIECE),
            vmem(RAW_SLOTS, 2, 2, BLOCKS, 2, 2, *PIECE),
            vmem(ACC_SLOTS, 2, 2, BLOCKS, 2, 2, *PIECE),
            vmem(ACC_SLOTS, BLOCKS, 2, 2, *PIECE),
            *inbox,
            queue(RAW_SLOTS, 4),
            queue(RAW_SLOTS, 4),
            pltpu.SemaphoreType.REGULAR,
            queue(BOX_SLOTS, BLOCKS, STAGES - 1),
            queue(BOX_SLOTS, BLOCKS, STAGES - 1),
        ],
    )
    large = [large[i] for i in (5, 4, 3, 2, 1, 0)]
    kinds = (f32,) * len(large) + (bf16,) * 2
    *large, output, grad_tokens, grad_cls = finish(small, clip_count, (*large, output, grad_tokens), kinds)
    small = lax.dynamic_slice_in_dim(small[:16], lax.axis_index(PATCH) * share, share, 1)
    small = small.reshape(LAYERS, 8, share)
    return (given_order(output), given_order(grad_tokens), grad_cls, *large, small[:, 0:3], small[:, 3:6])


def general_local(
    tokens,
    cls_tokens,
    clip_lengths,
    time_proj,
    time_output,
    space_proj,
    space_output,
    up_weight,
    down_weight,
    norm_gains,
    norm_biases,
    cotangent,
):
    frames, patch_rows, width = tokens.shape
    devices = lax.axis_size(PATCH)
    lay = Layout(devices, frames, patch_rows)
    away_rows = lay.away_rows
    patches = lay.all_patches
    clip_count = cls_tokens.shape[0]

    frame_ids = jnp.arange(frames, dtype=jnp.int32)
    slots = frame_slots(clip_lengths[0], frame_ids)
    bias = time_bias(slots[:, None] == slots[None, :], patch_rows, frames)
    my_frames = lax.axis_index(PATCH) * lay.away_frames + jnp.arange(lay.away_frames, dtype=jnp.int32)
    my_slots = jnp.where(my_frames < frames, frame_slots(clip_lengths[0], my_frames), -1)
    cls_pick = (my_slots[None, :] == jnp.arange(CLS_ROWS, dtype=jnp.int32)[:, None]).astype(f32)

    def home_order(values):
        return jnp.transpose(values, (1, 0, 2)).reshape(lay.home_rows, width)

    def given_order(values):
        return jnp.transpose(values.reshape(patch_rows, frames, width), (1, 0, 2))

    cls_aug = jnp.pad(cls_tokens.astype(f32), ((0, CLS_ROWS - clip_count), (0, 0)))
    residual = home_order(tokens).astype(f32)
    cotangent_away = lay.to_away(home_order(cotangent))
    stored = []
    for layer in range(LAYERS):
        gains, biases = norm_gains[layer], norm_biases[layer]
        normed, scaled_t, inverse_t = layer_norm(residual, gains[0], biases[0])
        normed_t = normed.astype(bf16)
        qkv_t = project(normed_t, time_proj[layer]).astype(bf16)
        mixed_t = time_forward(bias, qkv_t)
        residual = residual + project(mixed_t, time_output[layer])
        away = lay.to_away(residual.astype(bf16))
        away = away + jnp.pad(cls_aug, ((away_rows, 0), (0, 0)))
        normed, scaled_s, inverse_s = layer_norm(away, gains[1], biases[1])
        normed_s = normed.astype(bf16)
        qkv_s = project(normed_s, space_proj[layer]).astype(bf16)
        mixed_s = space_forward(my_slots, qkv_s, lay.away_frames, patches)
        away = away[:away_rows] + project(mixed_s, space_output[layer])
        normed, scaled_f, inverse_f = layer_norm(away, gains[2], biases[2])
        normed_f = normed.astype(bf16)
        hidden = project(normed_f, up_weight[layer])
        active = gelu_value(hidden).astype(bf16)
        away = away + project(active, down_weight[layer])
        residual = lay.to_home(away.astype(bf16))
        stored.append(
            dict(
                normed_t=normed_t, scaled_t=scaled_t, inverse_t=inverse_t, qkv_t=qkv_t, mixed_t=mixed_t,
                normed_s=normed_s, scaled_s=scaled_s, inverse_s=inverse_s, qkv_s=qkv_s, mixed_s=mixed_s,
                normed_f=normed_f, scaled_f=scaled_f, inverse_f=inverse_f, hidden=hidden, active=active,
            )
        )
    output = given_order(residual.astype(bf16))

    grad_cls = jnp.zeros_like(cls_aug)
    grad_away = cotangent_away[:away_rows]
    results = [None] * LAYERS
    for layer in reversed(range(LAYERS)):
        saved = stored[layer]
        gains = norm_gains[layer]
        branch = grad_away.astype(bf16)
        grad_down = weight_grad(saved["active"], branch)
        grad_active = project_back(branch, down_weight[layer])
        grad_hidden = (grad_active * gelu_slope(saved["hidden"])).astype(bf16)
        grad_up = weight_grad(saved["normed_f"], grad_hidden)
        grad_normed = project_back(grad_hidden, up_weight[layer])
        grad_input, gain_two, bias_two = norm_back(
            grad_normed, saved["scaled_f"], saved["inverse_f"], gains[2]
        )
        grad_away = grad_away + grad_input
        branch = grad_away.astype(bf16)
        grad_space_out = weight_grad(saved["mixed_s"], branch)
        grad_mixed = project_back(branch, space_output[layer]).astype(bf16)
        dq, dk, dv, dck, dcv = space_backward(my_slots, saved["qkv_s"], grad_mixed, lay.away_frames, patches)
        dcls = jnp.concatenate([dck[:, 0], dcv[:, 0]], -1)
        dcls = jnp.dot(cls_pick, dcls, precision=lax.Precision.HIGHEST)
        dcls = jnp.pad(dcls.astype(bf16), ((0, 0), (width, 0)))
        grad_qkv = jnp.concatenate([jnp.concatenate([dq, dk, dv], -1), dcls], 0)
        grad_space_proj = weight_grad(saved["normed_s"], grad_qkv)
        grad_normed = project_back(grad_qkv, space_proj[layer])
        grad_input, gain_one, bias_one = norm_back(
            grad_normed, saved["scaled_s"], saved["inverse_s"], gains[1]
        )
        grad_away = grad_away + grad_input[:away_rows]
        grad_cls = grad_cls + grad_input[away_rows:]
        grad_home = lay.to_home(grad_away.astype(bf16))
        branch = grad_home.astype(bf16)
        grad_time_out = weight_grad(saved["mixed_t"], branch)
        grad_mixed = project_back(branch, time_output[layer]).astype(bf16)
        grad_qkv = time_backward(bias, saved["qkv_t"], grad_mixed)
        grad_time_proj = weight_grad(saved["normed_t"], grad_qkv)
        grad_normed = project_back(grad_qkv, time_proj[layer])
        grad_input, gain_zero, bias_zero = norm_back(
            grad_normed, saved["scaled_t"], saved["inverse_t"], gains[0]
        )
        grad_home = grad_home + grad_input
        if layer > 0:
            grad_away = lay.to_away(grad_home.astype(bf16))[:away_rows]
        large = (grad_time_proj, grad_time_out, grad_space_proj, grad_space_out, grad_up, grad_down)
        large = [lax.psum_scatter(part, PATCH, scatter_dimension=0, tiled=True) for part in large]
        large = lax.psum(large, CLIP)
        small = (jnp.stack([gain_zero, gain_one, gain_two]), jnp.stack([bias_zero, bias_one, bias_two]))
        results[layer] = [part.astype(f32) for part in large] + list(small)
    grad_tokens = given_order(grad_home.astype(bf16))
    stacked = [jnp.stack([results[layer][i] for layer in range(LAYERS)]) for i in range(8)]
    small = jnp.stack(stacked[6:])
    small = lax.psum(small, (PATCH, CLIP))
    share = width // devices
    small = lax.dynamic_slice_in_dim(small, lax.axis_index(PATCH) * share, share, 3)
    grad_cls = lax.psum(grad_cls[:clip_count], PATCH)
    return (output, grad_tokens, grad_cls, *stacked[:6], small[0], small[1])


def solution(mesh):
    in_specs = (
        P(CLIP, PATCH, None),
        P(CLIP, None),
        P(CLIP, None),
        P(),
        P(),
        P(),
        P(),
        P(),
        P(),
        P(),
        P(),
        P(CLIP, PATCH, None),
    )
    out_specs = (
        P(CLIP, PATCH, None),
        P(CLIP, PATCH, None),
        P(CLIP, None),
        P(None, PATCH, None),
        P(None, PATCH, None),
        P(None, PATCH, None),
        P(None, PATCH, None),
        P(None, PATCH, None),
        P(None, PATCH, None),
        P(None, None, PATCH),
        P(None, None, PATCH),
    )
    paired = (mesh.shape[CLIP], mesh.shape[PATCH]) == (4, 8)
    local = fast_local if paired else general_local
    return jax.shard_map(local, mesh=mesh, in_specs=in_specs, out_specs=out_specs, check_vma=False)
```

```python
import functools

import jax
import jax.numpy as jnp
import numpy as np
from jax import lax
from jax.experimental import pallas as pl
from jax.experimental.pallas import tpu as pltpu
from jax.sharding import PartitionSpec as P

HEADS = 12
HD = 64
LAYERS = 2
REAL_PATCH = 196
QUAD = 4
WIDE = QUAD * HD
QUADS = HEADS // QUAD
CLS_ROWS = 16

EPSILON = 1e-05
NEG_LARGE = -1e30
ROOT_HALF = 0.7071067811865476
INV_ROOT_TWO_PI = 0.3989422804014327
SCALE = HD**-0.5
VMEM_LIMIT = 48 * 1024 * 1024
VMEM_MOST = 62 * 1024 * 1024

CLIP = "clip"
PATCH = "patch"
f32 = jnp.float32
bf16 = jnp.bfloat16
MESH = pl.DeviceIdType.MESH


def layer_norm(values, norm_gain, norm_bias):
    centered = values - jnp.mean(values, -1, keepdims=True)
    inverse = lax.rsqrt(jnp.mean(centered * centered, -1, keepdims=True) + EPSILON)
    scaled = centered * inverse
    return (scaled * norm_gain + norm_bias, scaled, inverse)


def norm_back(grad_out, scaled, inverse, norm_gain):
    weighted = grad_out * norm_gain
    grad_input = inverse * (
        weighted
        - jnp.mean(weighted, -1, keepdims=True)
        - scaled * jnp.mean(weighted * scaled, -1, keepdims=True)
    )
    return (grad_input, jnp.sum(grad_out * scaled, 0), jnp.sum(grad_out, 0))


def project(left, matrix):
    return jnp.dot(left, matrix, preferred_element_type=f32)


def project_back(grad_out, matrix):
    return lax.dot_general(grad_out, matrix, (((1,), (1,)), ((), ())), preferred_element_type=f32)


def weight_grad(left, grad_out):
    return lax.dot_general(
        left, grad_out, (((0,), (0,)), ((), ())), preferred_element_type=f32
    ).astype(bf16)


def gelu_value(hidden):
    return 0.5 * hidden * (1.0 + lax.erf(hidden * ROOT_HALF))


def gelu_slope(hidden):
    return 0.5 * (1.0 + lax.erf(hidden * ROOT_HALF)) + hidden * INV_ROOT_TWO_PI * jnp.exp(
        -0.5 * hidden * hidden
    )


def dot_nt(left, right):
    return lax.dot_general(left, right, (((1,), (1,)), ((), ())), preferred_element_type=f32)


def dot_nn(left, right):
    return lax.dot_general(left, right, (((1,), (0,)), ((), ())), preferred_element_type=f32)


def dot_tn(left, right):
    return lax.dot_general(left, right, (((0,), (0,)), ((), ())), preferred_element_type=f32)


def spread_heads(rows):
    head = lax.broadcasted_iota(jnp.int32, rows.shape, 1) // HD
    return jnp.concatenate([jnp.where(head == h, rows, jnp.zeros_like(rows)) for h in range(QUAD)], 0)


def merge_heads(stacked):
    count = stacked.shape[0] // QUAD
    head = lax.broadcasted_iota(jnp.int32, (count, WIDE), 1) // HD
    merged = stacked[:count]
    for h in range(1, QUAD):
        merged = jnp.where(head == h, stacked[h * count : (h + 1) * count], merged)
    return merged


def probabilities(scores):
    exponents = [jnp.exp(part - jnp.max(part, 0, keepdims=True)) for part in scores]
    return [part * (1.0 / jnp.sum(part, 0, keepdims=True)) for part in exponents]


def forward_tiles(tiles, bias):
    spreads = [spread_heads(tile[0] * SCALE) for tile in tiles]
    scores = [dot_nt(tile[1], spread) + bias for tile, spread in zip(tiles, spreads)]
    probs = [part.astype(bf16) for part in probabilities(scores)]
    outs = [dot_tn(part, tile[2]) for part, tile in zip(probs, tiles)]
    return [merge_heads(part).astype(bf16) for part in outs]


def backward_tiles(tiles, bias):
    spreads = [spread_heads(tile[0] * SCALE) for tile in tiles]
    grad_spreads = [spread_heads(tile[3]) for tile in tiles]
    scores = [dot_nt(tile[1], spread) + bias for tile, spread in zip(tiles, spreads)]
    grad_probs = [dot_nt(tile[2], spread) for tile, spread in zip(tiles, grad_spreads)]
    probs = probabilities(scores)
    grad_scores = [
        (part * (grad - jnp.sum(part * grad, 0, keepdims=True))).astype(bf16)
        for part, grad in zip(probs, grad_probs)
    ]
    grad_queries = [dot_tn(grad, tile[1]) for grad, tile in zip(grad_scores, tiles)]
    grad_keys = [dot_nn(grad, spread) for grad, spread in zip(grad_scores, spreads)]
    grad_values = [dot_nn(part.astype(bf16), spread) for part, spread in zip(probs, grad_spreads)]
    return [(merge_heads(q) * SCALE, k, v) for q, k, v in zip(grad_queries, grad_keys, grad_values)]


def columns(part, quad, width):
    start = part * width + quad * WIDE
    return slice(start, start + WIDE)


def time_forward_kernel(bias_ref, qkv_ref, out_ref):
    width = out_ref.shape[1]
    bias = bias_ref[...]
    for quad in range(QUADS):
        parts = [qkv_ref[:, columns(part, quad, width)] for part in range(3)]
        out_ref[:, columns(0, quad, width)] = forward_tiles([parts], bias)[0]


def time_backward_kernel(bias_ref, qkv_ref, grad_ref, out_ref):
    width = grad_ref.shape[1]
    bias = bias_ref[...]
    for quad in range(QUADS):
        parts = [qkv_ref[:, columns(part, quad, width)] for part in range(3)]
        grads = backward_tiles([parts + [grad_ref[:, columns(0, quad, width)]]], bias)[0]
        for part in range(3):
            out_ref[:, columns(part, quad, width)] = grads[part].astype(bf16)


def group_rows(patch_count, frames):
    return (2 if patch_count % 2 == 0 else 1) * frames


def time_bias(same_clip, patch_count, frames):
    rows = group_rows(patch_count, frames)
    ids = jnp.arange(rows, dtype=jnp.int32)
    same_patch = (ids[:, None] // frames) == (ids[None, :] // frames)
    tiled = jnp.tile(same_clip, (rows // frames, rows // frames))
    return jnp.tile(jnp.where(same_patch & tiled, 0.0, NEG_LARGE).astype(f32), (1, QUAD))


def params(*semantics):
    return pltpu.CompilerParams(dimension_semantics=semantics, vmem_limit_bytes=VMEM_LIMIT)


def time_forward(bias, qkv):
    rows = bias.shape[0]
    width = qkv.shape[1] // 3
    return pl.pallas_call(
        time_forward_kernel,
        grid=(qkv.shape[0] // rows,),
        in_specs=[
            pl.BlockSpec(bias.shape, lambda i: (0, 0)),
            pl.BlockSpec((rows, 3 * width), lambda i: (i, 0)),
        ],
        out_specs=pl.BlockSpec((rows, width), lambda i: (i, 0)),
        out_shape=jax.ShapeDtypeStruct((qkv.shape[0], width), bf16),
        compiler_params=params("parallel"),
        name="time_forward",
    )(bias, qkv)


def time_backward(bias, qkv, grad_out):
    rows = bias.shape[0]
    width = qkv.shape[1] // 3
    return pl.pallas_call(
        time_backward_kernel,
        grid=(qkv.shape[0] // rows,),
        in_specs=[
            pl.BlockSpec(bias.shape, lambda i: (0, 0)),
            pl.BlockSpec((rows, 3 * width), lambda i: (i, 0)),
            pl.BlockSpec((rows, width), lambda i: (i, 0)),
        ],
        out_specs=pl.BlockSpec((rows, 3 * width), lambda i: (i, 0)),
        out_shape=jax.ShapeDtypeStruct(qkv.shape, bf16),
        compiler_params=params("parallel"),
        name="time_backward",
    )(bias, qkv, grad_out)


def with_class(slot, rows, cls_rows):
    ids = lax.broadcasted_iota(jnp.int32, cls_rows.shape, 0)
    picked = jnp.sum(jnp.where(ids == slot, cls_rows.astype(f32), 0.0), 0, keepdims=True)
    row_ids = lax.broadcasted_iota(jnp.int32, rows.shape, 0)
    return jnp.where(row_ids == REAL_PATCH, picked.astype(bf16), rows)


def key_bias(count):
    key_ids = lax.broadcasted_iota(jnp.int32, (count, 1), 0)
    return jnp.where(key_ids <= REAL_PATCH, 0.0, NEG_LARGE).astype(f32)


def space_forward_kernel(slot_ref, q_ref, k_ref, v_ref, ck_ref, cv_ref, out_ref):
    slot = slot_ref[pl.program_id(0)]
    keys = with_class(slot, k_ref[...], ck_ref[...])
    values = with_class(slot, v_ref[...], cv_ref[...])
    out_ref[...] = forward_tiles([(q_ref[...], keys, values)], key_bias(keys.shape[0]))[0]


def space_backward_kernel(
    slot_ref, q_ref, k_ref, v_ref, ck_ref, cv_ref, g_ref, dq_ref, dk_ref, dv_ref, dck_ref, dcv_ref
):
    slot = slot_ref[pl.program_id(0)]
    keys = with_class(slot, k_ref[...], ck_ref[...])
    values = with_class(slot, v_ref[...], cv_ref[...])
    tile = (q_ref[...], keys, values, g_ref[...])
    grad_q, grad_k, grad_v = backward_tiles([tile], key_bias(keys.shape[0]))[0]
    row_ids = lax.broadcasted_iota(jnp.int32, grad_k.shape, 0)
    dq_ref[...] = grad_q.astype(bf16)
    dk_ref[...] = jnp.where(row_ids < REAL_PATCH, grad_k, 0.0).astype(bf16)
    dv_ref[...] = jnp.where(row_ids < REAL_PATCH, grad_v, 0.0).astype(bf16)
    dck_ref[0] = jnp.sum(jnp.where(row_ids == REAL_PATCH, grad_k, 0.0), 0, keepdims=True)
    dcv_ref[0] = jnp.sum(jnp.where(row_ids == REAL_PATCH, grad_v, 0.0), 0, keepdims=True)


def space_specs(frames, patches):
    cls_block = frames * patches // CLS_ROWS

    def rows(part):
        return pl.BlockSpec((patches, WIDE), lambda f, c, s: (f, part * QUADS + c))

    def cls(part):
        return pl.BlockSpec((CLS_ROWS, WIDE), lambda f, c, s: (cls_block, part * QUADS + c))

    return [rows(0), rows(1), rows(2), cls(1), cls(2)], rows(0)


def space_forward(slots, qkv, frames, patches):
    width = qkv.shape[1] // 3
    in_specs, out_spec = space_specs(frames, patches)
    return pl.pallas_call(
        space_forward_kernel,
        grid_spec=pltpu.PrefetchScalarGridSpec(
            num_scalar_prefetch=1,
            grid=(frames, QUADS),
            in_specs=in_specs,
            out_specs=out_spec,
        ),
        out_shape=jax.ShapeDtypeStruct((frames * patches, width), bf16),
        compiler_params=params("parallel", "parallel"),
        name="space_forward",
    )(slots, qkv, qkv, qkv, qkv, qkv)


def space_backward(slots, qkv, grad_out, frames, patches):
    width = qkv.shape[1] // 3
    in_specs, out_spec = space_specs(frames, patches)
    rows = jax.ShapeDtypeStruct((frames * patches, width), bf16)
    cls_spec = pl.BlockSpec((1, 1, WIDE), lambda f, c, s: (f, 0, c))
    cls = jax.ShapeDtypeStruct((frames, 1, width), f32)
    return pl.pallas_call(
        space_backward_kernel,
        grid_spec=pltpu.PrefetchScalarGridSpec(
            num_scalar_prefetch=1,
            grid=(frames, QUADS),
            in_specs=in_specs + [out_spec],
            out_specs=[out_spec] * 3 + [cls_spec] * 2,
        ),
        out_shape=[rows] * 3 + [cls] * 2,
        compiler_params=params("parallel", "parallel"),
        name="space_backward",
    )(slots, qkv, qkv, qkv, qkv, qkv, grad_out)


def frame_slots(lengths_row, frame_ids):
    clip_ends = jnp.cumsum(lengths_row)
    return jnp.sum((frame_ids[:, None] >= clip_ends[None, :]).astype(jnp.int32), axis=1)


class Layout:
    def __init__(self, devices, frames, patches):
        self.devices = devices
        self.frames = frames
        self.patches = patches
        self.all_patches = patches * devices
        self.away_frames = -(-frames // devices)
        used = self.away_frames * patches
        self.block = -(-used // 16) * 16
        self.home_rows = frames * patches
        self.away_rows = self.away_frames * self.all_patches
        self.sent_rows = devices * self.block

    def home_of_sent(self):
        row = jnp.arange(self.sent_rows, dtype=jnp.int32)
        peer, inner = row // self.block, row % self.block
        frame = peer * self.away_frames + inner // self.patches
        valid = (inner < self.away_frames * self.patches) & (frame < self.frames)
        return jnp.where(valid, (inner % self.patches) * self.frames + frame, -1)

    def sent_of_away(self):
        row = jnp.arange(self.away_rows + CLS_ROWS, dtype=jnp.int32)
        frame, patch = row // self.all_patches, row % self.all_patches
        sent = (patch // self.patches) * self.block + frame * self.patches + patch % self.patches
        return jnp.where(row < self.away_rows, sent, -1)

    def parts(self):
        step = self.block // 5 // 16 * 16
        return ((0, step), (step, 3 * step), (3 * step, self.block))

    def frame_parts(self):
        ends = [-(-self.patches * (i + 1) // 16) * 16 for i in range(self.away_frames)]
        return tuple(zip([0] + ends[:-1], ends))

    def frame_rows(self, frame):
        low, high = self.patches * frame, self.patches * (frame + 1)
        return low // 16 * 16, -(-high // 16) * 16

    def leave(self, order, parts):
        order = np.where(np.arange(self.block) < self.away_frames * self.patches, order, -1)
        rows = np.concatenate([order[:, low:high].reshape(-1) for low, high in parts])
        return np.asarray(rows, np.int32)[:, None]

    def orders(self):
        block, patches, near = self.block, self.patches, self.away_frames
        peer, inner = np.meshgrid(range(self.devices), range(block), indexing="ij")
        by_patch = inner // near * self.frames + peer * near + inner % near
        by_frame = inner % patches * self.frames + peer * near + inner // patches
        from_away = inner // patches * self.all_patches + peer * patches + inner % patches
        row = np.arange(self.away_rows)
        frame, patch = row // self.all_patches, row % self.all_patches
        reach_patch = patch // patches * block + patch % patches * near + frame
        low = np.array([self.frame_rows(i)[0] for i in range(near)])[frame]
        high = np.array([self.frame_rows(i)[1] for i in range(near)])[frame]
        reach_frame = patch // patches * (high - low) + frame * patches + patch % patches - low
        row = np.arange(self.home_rows)
        patch, frame = row // self.frames, row % self.frames
        reach_home = frame // near * block + frame % near * patches + patch

        def column(rows):
            return np.asarray(rows, np.int32)[:, None]

        return dict(
            leave_patch=self.leave(by_patch, self.parts()),
            leave_frame=self.leave(by_frame, self.frame_parts()),
            leave_away=self.leave(from_away, self.parts()),
            reach_patch=column(reach_patch),
            reach_frame=column(reach_frame),
            reach_home=column(reach_home),
        )

    def to_away(self, values):
        pick = self.home_of_sent()[:, None] == jnp.arange(self.home_rows, dtype=jnp.int32)[None, :]
        sent = jnp.dot(pick.astype(bf16), values, preferred_element_type=bf16)
        got = lax.all_to_all(sent, PATCH, split_axis=0, concat_axis=0, tiled=True)
        pick = self.sent_of_away()[:, None] == jnp.arange(self.sent_rows, dtype=jnp.int32)[None, :]
        return jnp.dot(pick.astype(bf16), got, preferred_element_type=f32)

    def to_home(self, values):
        pick = jnp.arange(self.sent_rows, dtype=jnp.int32)[:, None] == self.sent_of_away()[None, : self.away_rows]
        sent = jnp.dot(pick.astype(bf16), values, preferred_element_type=bf16)
        got = lax.all_to_all(sent, PATCH, split_axis=0, concat_axis=0, tiled=True)
        pick = jnp.arange(self.home_rows, dtype=jnp.int32)[:, None] == self.home_of_sent()[None, :]
        return jnp.dot(pick.astype(bf16), got, preferred_element_type=f32)


def norm_rows(values):
    centered = values - jnp.mean(values, -1, keepdims=True)
    inverse = lax.rsqrt(jnp.mean(centered * centered, -1, keepdims=True) + EPSILON)
    return centered, inverse


def norm_forward(values, gain, shift):
    centered, inverse = norm_rows(values)
    return (centered * inverse * gain + shift).astype(bf16)


def norm_backward(values, grad, gain, sums):
    centered, inverse = norm_rows(values)
    weighted = grad * gain
    along = jnp.mean(weighted * centered, -1, keepdims=True) * (inverse * inverse * inverse)

    def fold(part):
        return jnp.sum(part.reshape(part.shape[0] // 8, 8, part.shape[1]), 0)

    sums[0][...] += fold(grad * (centered * inverse))
    sums[1][...] += fold(grad)
    return inverse * (weighted - jnp.mean(weighted, -1, keepdims=True)) - centered * along


class Loads:
    def __init__(self, sources, buffers, sems):
        self.copies = [
            pltpu.make_async_copy(source, buffer, sems.at[i])
            for i, (source, buffer) in enumerate(zip(sources, buffers))
        ]
        for copy in self.copies:
            copy.start()
        self.buffers = buffers
        self.next = 0

    def get(self):
        self.copies[self.next].wait()
        self.next += 1
        return self.buffers[self.next - 1]


class Saves:
    def __init__(self, buffers, targets, sems):
        self.pairs, self.sems = list(zip(buffers, targets)), sems

    def copies(self, part, start, rows):
        here = pl.ds(start, rows)
        return [
            pltpu.make_async_copy(buffer.at[here], target.at[here], self.sems.at[i, part])
            for i, (buffer, target) in enumerate(self.pairs)
        ]

    def put(self, part, start, rows):
        for copy in self.copies(part, start, rows):
            copy.start()

    def finish(self, part, start, rows):
        for copy in self.copies(part, start, rows):
            copy.wait()


class Place:
    AXES = {"core": (PATCH, 1), "zl": (PATCH, 2), "zh": (PATCH, 4), "x": (CLIP, 1), "y": (CLIP, 2)}

    def __init__(self):
        self.clip, self.patch = lax.axis_index(CLIP), lax.axis_index(PATCH)
        self.me = {
            "core": lax.rem(self.patch, 2),
            "zl": lax.rem(self.patch // 2, 2),
            "zh": self.patch // 4,
            "x": lax.rem(self.clip, 2),
            "y": self.clip // 2,
        }

    def peer(self, dim):
        axis, stride = self.AXES[dim]
        own = self.clip if axis == CLIP else self.patch
        other = own + stride - 2 * stride * self.me[dim]
        return (other, self.patch) if axis == CLIP else (self.clip, other)


class Shuffle:
    def __init__(self, lay, at, sent, got, send_sem, recv_sem):
        self.lay, self.devices, self.parts, self.at = lay, lay.devices, lay.parts(), at
        self.sent, self.got, self.send_sem, self.recv_sem = sent, got, send_sem, recv_sem
        self.moves = 0

    def greet(self):
        for offset in range(1, self.devices):
            other = (self.at.clip, lax.rem(self.at.patch + offset, self.devices))
            pl.semaphore_signal(pltpu.get_barrier_semaphore(), inc=1, device_id=other, device_id_type=MESH)

    def meet(self, others=0):
        pl.semaphore_wait(pltpu.get_barrier_semaphore(), self.devices - 1 + others)

    def copy(self, offset, part):
        two = self.moves % 2
        other = lax.rem(self.at.patch + offset, self.devices)
        low, high = self.parts[part]
        rows = pl.ds(low, high - low)
        return pltpu.make_async_remote_copy(
            src_ref=self.sent.at[other, rows],
            dst_ref=self.got.at[two, self.at.patch, rows],
            send_sem=self.send_sem.at[part, offset],
            recv_sem=self.recv_sem.at[two, part, offset],
            device_id=(self.at.clip, other),
            device_id_type=MESH,
        )

    def send(self, part, order_ref, source_ref, first, last):
        width = self.sent.shape[-1]
        low, high = self.parts[part]
        rows = (high - low) * self.devices
        start = low * self.devices
        ids = lax.broadcasted_iota(jnp.int32, (rows, last - first), 1) + first
        pick = (order_ref[start : start + rows, :] == ids).astype(f32).astype(bf16)
        picked = dot_nn(pick, source_ref[first:last, :]).astype(bf16)
        self.sent[:, low:high, :] = picked.reshape(self.devices, high - low, width)
        for offset in range(1, self.devices):
            self.copy(offset, part).start()
        self.got[self.moves % 2, self.at.patch, low:high, :] = self.sent[self.at.patch, low:high, :]

    def send_all(self, order_ref, source_ref):
        for part in range(len(self.parts)):
            self.send(part, order_ref, source_ref, 0, source_ref.shape[0])

    def arrive(self, part):
        for offset in range(1, self.devices):
            self.copy(offset, part).wait()

    def receive(self, order_ref, target_ref):
        for part in range(len(self.parts)):
            self.arrive(part)
        devices, block, width = self.got.shape[1:]
        rows = target_ref.shape[0] // 3
        ids = lax.broadcasted_iota(jnp.int32, (rows, devices * block), 1)
        for start in range(0, target_ref.shape[0], rows):
            pick = (order_ref[start : start + rows, :] == ids).astype(f32).astype(bf16)
            got = self.got[self.moves % 2].reshape(devices * block, width)
            target_ref[start : start + rows, :] = dot_nn(pick, got).astype(bf16)
        self.moves += 1

    def receive_frame(self, frame, order_ref, target_ref):
        self.arrive(frame)
        low, high = self.lay.frame_rows(frame)
        patches = self.lay.all_patches
        here = slice(frame * patches, (frame + 1) * patches)
        width = self.got.shape[-1]
        got = self.got[self.moves % 2, :, low:high, :].reshape(self.devices * (high - low), width)
        ids = lax.broadcasted_iota(jnp.int32, (patches, got.shape[0]), 1)
        pick = (order_ref[here, :] == ids).astype(f32).astype(bf16)
        target_ref[here, :] = dot_nn(pick, got).astype(bf16)


def slot_of(lengths_ref, frames):
    end, slot = 0, 0
    for clip in range(lengths_ref.shape[0]):
        end = end + lengths_ref[clip]
        slot = slot + (frames >= end).astype(jnp.int32)
    return slot


def fill_bias(lengths_ref, frames, bias_ref):
    rows = bias_ref.shape[0]

    def split(ids, size, count):
        which = jnp.zeros_like(ids)
        for i in range(1, count):
            which = which + (ids >= i * size).astype(jnp.int32)
        return which, ids - which * size

    key_patch, key_frame = split(lax.broadcasted_iota(jnp.int32, bias_ref.shape, 0), frames, rows // frames)
    _, query = split(lax.broadcasted_iota(jnp.int32, bias_ref.shape, 1), rows, QUAD)
    query_patch, query_frame = split(query, frames, rows // frames)
    same = (key_patch == query_patch) & (slot_of(lengths_ref, key_frame) == slot_of(lengths_ref, query_frame))
    bias_ref[...] = jnp.where(same, 0.0, NEG_LARGE).astype(f32)


def cls_rows_of(cls_ref):
    values = cls_ref[...].astype(f32)
    return jnp.concatenate([values, jnp.zeros((CLS_ROWS - values.shape[0], values.shape[1]), f32)], 0)


def norm_row(norms_ref, layer, which):
    return norms_ref[which, layer : layer + 1, :]


def time_tiles(bias_ref, qkv_ref, width, group, grad_ref=None):
    rows = bias_ref.shape[0]
    here = pl.ds(pl.multiple_of(group * rows, 16), rows)
    tiles = []
    for quad in range(QUADS):
        tile = [qkv_ref[here, columns(part, quad, width)] for part in range(3)]
        if grad_ref is not None:
            tile.append(grad_ref[here, columns(0, quad, width)])
        tiles.append(tile)
    return here, tiles


def space_tiles(patches, total, slot, qkv_ref, width, frame, grad_ref=None):
    here = pl.ds(pl.multiple_of(frame * patches, 16), patches)
    tiles = []
    for quad in range(QUADS):
        tile = [qkv_ref[here, columns(part, quad, width)] for part in range(3)]
        for part in (1, 2):
            tile[part] = with_class(slot, tile[part], qkv_ref[total : total + CLS_ROWS, columns(part, quad, width)])
        if grad_ref is not None:
            tile.append(grad_ref[here, columns(0, quad, width)])
        tiles.append(tile)
    return here, tiles


def group_parts(lay, rows):
    ends = []
    for _, high in lay.parts():
        patches = min(-(-high // lay.away_frames), lay.patches)
        ends.append(-(-patches * lay.frames // rows) * rows)
    return tuple(zip([0] + ends[:-1], ends))


SAVED = ("normed_t", "qkv_t", "mixed_t", "x_away", "normed_s", "qkv_s", "mixed_s", "middle", "normed_f", "active", "slope")
WEIGHTS = ("time_proj", "time_output", "space_proj", "space_output", "up", "down")


def forward_kernel(lay, *refs):
    lengths_ref, norms_ref, shifts_ref, cls_ref, leave_frame, reach_frame, leave_away, reach_home = refs[:8]
    refs = refs[1:]
    sources = dict(zip(WEIGHTS, refs[7:13]))
    tokens_hbm, grad_hbm = refs[13:15]
    home_hbm, grad_away_hbm, result_hbm = refs[15:18]
    saved = [dict(zip(SAVED, refs[18 + len(SAVED) * layer :][: len(SAVED)])) for layer in range(LAYERS)]
    refs = refs[18 + len(SAVED) * LAYERS :]
    weights = dict(zip(WEIGHTS, refs[:6]))
    staged = dict(zip(SAVED, refs[6 : 6 + len(SAVED)]))
    bias_ref, x_home, after, grad, grad_away = refs[6 + len(SAVED) :][:5]
    sem_weight, sem_ends, sem_time, sem_space, sem_cls, *moving = refs[11 + len(SAVED) :]
    normed_t, qkv_t, mixed_t, x_away, normed, qkv, mixed, middle, normed_f, active, slope = (staged[name] for name in SAVED)
    total, width = x_away.shape
    home = x_home.shape[0]
    patches, frames = lay.all_patches, lay.away_frames
    group = bias_ref.shape[0]
    columns_of = [slice(start, start + width) for start in range(0, 3 * width, width)]

    load_x = pltpu.make_async_copy(tokens_hbm, x_home, sem_ends.at[0])
    load_grad = pltpu.make_async_copy(grad_hbm, grad, sem_ends.at[1])
    save_home = pltpu.make_async_copy(x_home, home_hbm, sem_ends.at[2])
    save_result = pltpu.make_async_copy(after, result_hbm, sem_ends.at[3])
    save_grad = pltpu.make_async_copy(grad_away, grad_away_hbm, sem_ends.at[4])
    load_x.start()
    load_grad.start()

    def fetch(layer, i):
        return pltpu.make_async_copy(sources[WEIGHTS[i]].at[layer], weights[WEIGHTS[i]], sem_weight.at[i])

    fetch(0, 0).start()
    at = Place()
    coming, leaving = [Shuffle(lay, at, *moving[:4]) for _ in range(2)]
    extra = Shuffle(lay, at, *moving[4:])
    coming.parts = extra.parts = lay.frame_parts()
    coming.greet()
    fill_bias(lengths_ref, lay.frames, bias_ref)
    key_mask = key_bias(patches)
    cls = cls_rows_of(cls_ref)
    load_grad.wait()
    coming.meet()
    extra.send(0, leave_frame, grad, 0, home)
    load_x.wait()

    for layer in range(LAYERS):
        more = layer < LAYERS - 1
        coming.moves, leaving.moves = 2 * layer, 2 * layer + 1
        if not more:
            extra.send(1, leave_frame, grad, 0, home)
        here = saved[layer]
        time_saves = Saves([staged[name] for name in SAVED[:3]], [here[name] for name in SAVED[:3]], sem_time)
        space_saves = Saves([staged[name] for name in SAVED[3:]], [here[name] for name in SAVED[3:]], sem_space)
        cls_saves = Saves([normed, qkv], [here["normed_s"], here["qkv_s"]], sem_cls)

        gain, shift = norm_row(norms_ref, layer, 0), norm_row(shifts_ref, layer, 0)
        for start in range(0, home, home // 3):
            rows = slice(start, start + home // 3)
            normed_t[rows, :] = norm_forward(x_home[rows, :].astype(f32), gain, shift)
        fetch(layer, 0).wait()
        if layer == 0:
            for i in range(1, len(WEIGHTS)):
                fetch(0, i).start()
        for these in columns_of:
            qkv_t[:, these] = dot_nn(normed_t[...], weights["time_proj"][:, these]).astype(bf16)
        if more:
            fetch(layer + 1, 0).start()

        @pl.loop(0, home // group)
        def _(index):
            rows, tiles = time_tiles(bias_ref, qkv_t, width, index)
            for quad, done in enumerate(forward_tiles(tiles, bias_ref[...])):
                mixed_t[rows, columns(0, quad, width)] = done

        fetch(layer, 1).wait()
        after[...] = (x_home[...].astype(f32) + dot_nn(mixed_t[...], weights["time_output"][...])).astype(bf16)
        for part in range(frames):
            coming.send(part, leave_frame, after, 0, home)
        if more:
            fetch(layer + 1, 1).start()
        time_saves.put(0, 0, home)

        gain, shift = norm_row(norms_ref, layer, 1), norm_row(shifts_ref, layer, 1)
        gain_f, shift_f = norm_row(norms_ref, layer, 2), norm_row(shifts_ref, layer, 2)
        normed[total:, :] = norm_forward(cls, gain, shift)
        fetch(layer, 2).wait()
        for these in columns_of:
            qkv[total:, these] = dot_nn(normed[total:, :], weights["space_proj"][:, these]).astype(bf16)
        cls_saves.put(0, total, CLS_ROWS)
        for i in range(3, len(WEIGHTS)):
            fetch(layer, i).wait()

        @pl.loop(0, frames)
        def _(frame, layer=layer, more=more, space_saves=space_saves, gain=gain, shift=shift, gain_f=gain_f, shift_f=shift_f):
            for number in range(frames):

                @pl.when(frame == number)
                def _(number=number, more=more):
                    coming.receive_frame(number, reach_frame, x_away)
                    if number == frames - 1 and not more:
                        extra.send(2, leave_frame, grad, 0, home)

            start = pl.multiple_of(frame * patches, 16)
            rows = pl.ds(start, patches)
            normed[rows, :] = norm_forward(x_away[rows, :].astype(f32), gain, shift)
            for these in columns_of:
                qkv[rows, these] = dot_nn(normed[rows, :], weights["space_proj"][:, these]).astype(bf16)
            slot = slot_of(lengths_ref, at.patch * frames + frame)
            _, tiles = space_tiles(patches, total, slot, qkv, width, frame)
            for quad, done in enumerate(forward_tiles(tiles, key_mask)):
                mixed[rows, columns(0, quad, width)] = done
            residual = x_away[rows, :].astype(f32) + dot_nn(mixed[rows, :], weights["space_output"][...])
            middle[rows, :] = residual.astype(bf16)
            normed_f[rows, :] = norm_forward(residual, gain_f, shift_f)
            for column in range(0, active.shape[1], WIDE):
                these = slice(column, column + WIDE)
                hidden = dot_nn(normed_f[rows, :], weights["up"][:, these])
                share = 0.5 * (1.0 + lax.erf(hidden * ROOT_HALF))
                active[rows, these] = (hidden * share).astype(bf16)
                bend = share + hidden * (INV_ROOT_TWO_PI * jnp.exp(-0.5 * hidden * hidden))
                slope[rows, these] = bend.astype(bf16)
            after[rows, :] = (residual + dot_nn(active[rows, :], weights["down"][...])).astype(bf16)
            space_saves.put(frame, start, patches)
            for number in range(frames - 1):

                @pl.when(frame == number)
                def _(number=number, more=more):
                    if more:
                        leaving.send(number, leave_away, after, 0, (number + 1) * patches)

        time_saves.finish(0, 0, home)
        if more:
            leaving.send(frames - 1, leave_away, after, (frames - 2) * patches, total)
            for i in range(2, len(WEIGHTS)):
                fetch(layer + 1, i).start()
            leaving.receive(reach_home, x_home)
            save_home.start()
        else:
            save_result.start()
            for frame in range(frames):
                extra.receive_frame(frame, reach_frame, grad_away)
            save_grad.start()
        for frame in range(frames):
            space_saves.finish(frame, frame * patches, patches)
        cls_saves.finish(0, total, CLS_ROWS)
    for copy in (save_home, save_result, save_grad):
        copy.wait()


CHUNKS = 16
TOTAL = CHUNKS * LAYERS
BLOCKS = 3
PIECE = (48, 128)
ROUTES = (("x", "zl", "zh", "y", "x", "y"), ("y", "x", "zl", "zh", "y", "x"), ("y", "x", "zl", "zh", "x", "y"))
SUMS = 4
STAGES = 7
RAW_SLOTS = 8
ACC_SLOTS = 8
BOX_SLOTS = 4
STRIDE = 2
SEGMENTS = (4, 4, 1, 3, 1, 3)
PLAN = {
    1: dict(early=3, down=2, hidden=1, wide=2, norm=0, frames=(0, 0, 0), up=0, space_out=2, space_proj=1, time_early=0, home=1, time0=1, time1=2, time2=0, time_out=1, time_proj=2),
    0: dict(early=1, down=1, hidden=1, wide=0, norm=1, frames=(1, 1, 1), up=0, space_out=2, space_proj=1, time_early=0, home=1, time0=1, time1=1, time2=1, time_out=0, time_proj=0),
}
SMALL = ("core", "zl", "zh", "x", "y")
SMALL_ROWS = 24


def recv_shape(route, stage):
    left = [dim for dim in ("zh", "zl", "x", "y") if dim not in route[: stage + 1]]
    return (2,) * len(left) + PIECE


class Pump:
    def __init__(self, at, results, scratch):
        self.at, self.results = at, results
        self.raw, self.core_in, self.acc, self.out, *rest = scratch
        self.inboxes = rest[: BLOCKS * SUMS]
        self.core_send, self.core_recv, self.core_free, self.send_sem, self.recv_sem = rest[BLOCKS * SUMS :]
        self.made = self.stepped = 0

    def core_copy(self, c, z):
        slot = lax.rem(c, RAW_SLOTS)
        return pltpu.make_async_remote_copy(
            src_ref=self.raw.at[slot, z // 2, z % 2, 1 - self.at.me["core"]],
            dst_ref=self.core_in.at[slot, z // 2, z % 2],
            send_sem=self.core_send.at[slot, z],
            recv_sem=self.core_recv.at[slot, z],
            device_id=self.at.peer("core"),
            device_id_type=MESH,
        )

    def claim(self, c, known):
        if known >= RAW_SLOTS:
            pl.semaphore_wait(self.core_free, 1)

    def store(self, c, z, core, block, rows):
        slot = lax.rem(c, RAW_SLOTS)
        for xh in range(2):
            for yh in range(2):
                part = rows[xh * 48 : (xh + 1) * 48, yh * 128 : (yh + 1) * 128]
                self.raw[slot, z // 2, z % 2, core, block, xh, yh] = part.astype(bf16)

    def make_chunks(self, count, lhs, rhs):
        first = self.made

        def one(i, c, known):
            self.claim(c, known)
            for half in range(2):
                left = lhs(slice(half * 384, (half + 1) * 384))
                for block in range(BLOCKS):
                    done = dot_tn(left, rhs(i, block * 256))
                    for j in range(4):
                        self.store(c, half * 2 + j // 2, j % 2, block, done[j * 96 : (j + 1) * 96])
            for z in range(4):
                self.core_copy(c, z).start()

        if count == 1:
            one(0, first, first)
        else:
            assert (first >= RAW_SLOTS) == (first + count - 1 >= RAW_SLOTS)

            @pl.loop(0, count)
            def _(i):
                one(i, first + i, first)

        self.made += count
        assert self.made - self.stepped <= RAW_SLOTS

    def make_down(self, lhs, rhs):
        first = self.made

        @pl.loop(0, 4)
        def _(z):
            if first >= RAW_SLOTS:

                @pl.when(z == 0)
                def _():
                    pl.semaphore_wait(self.core_free, 4)

            for core in range(2):
                left = lhs(pl.ds(pl.multiple_of(z * 768 + core * 384, 128), 384))
                for block in range(BLOCKS):
                    done = dot_tn(left, rhs[:, block * 256 : (block + 1) * 256])
                    for c in range(4):
                        self.store_at(first + c, z, core, block, done[c * 96 : (c + 1) * 96])
            for c in range(4):
                slot = (first + c) % RAW_SLOTS
                zh, zl = z // 2, lax.rem(z, 2)
                pltpu.make_async_remote_copy(
                    src_ref=self.raw.at[slot, zh, zl, 1 - self.at.me["core"]],
                    dst_ref=self.core_in.at[slot, zh, zl],
                    send_sem=self.core_send.at[slot, z],
                    recv_sem=self.core_recv.at[slot, z],
                    device_id=self.at.peer("core"),
                    device_id_type=MESH,
                ).start()

        self.made += 4
        assert self.made - self.stepped <= RAW_SLOTS

    def store_at(self, c, z, core, block, rows):
        for xh in range(2):
            for yh in range(2):
                part = rows[xh * 48 : (xh + 1) * 48, yh * 128 : (yh + 1) * 128]
                self.raw[c % RAW_SLOTS, z // 2, lax.rem(z, 2), core, block, xh, yh] = part.astype(bf16)

    def part(self, c, block, stage, value):
        route = ROUTES[block]

        def pick(dim):
            if dim in route[:stage]:
                return self.at.me[dim]
            return value if dim == route[stage] else slice(None)

        return (lax.rem(c, ACC_SLOTS), pick("zh"), pick("zl"), block, pick("x"), pick("y"))

    def exchange(self, c, block, stage):
        me = self.at.me
        dim = ROUTES[block][stage]
        box = lax.rem(c, BOX_SLOTS)
        if stage < SUMS:
            src = self.acc.at[self.part(c, block, stage, 1 - me[dim])]
            dst = self.inboxes[block * SUMS + stage].at[box]
        else:
            slot = lax.rem(c, ACC_SLOTS)
            if stage == SUMS:
                src = dst = self.out.at[slot, block, me["x"], me["y"]]
            elif dim == "x":
                src = dst = self.out.at[slot, block, me["x"]]
            else:
                src = dst = self.out.at[slot, block, :, me["y"]]
        return pltpu.make_async_remote_copy(
            src_ref=src,
            dst_ref=dst,
            send_sem=self.send_sem.at[box, block, stage],
            recv_sem=self.recv_sem.at[box, block, stage],
            device_id=self.at.peer(dim),
            device_id_type=MESH,
        )

    def enter(self, c):
        me = self.at.me
        slot, into = lax.rem(c, RAW_SLOTS), lax.rem(c, ACC_SLOTS)
        for z in range(4):
            self.core_copy(c, z).wait()
        for zh in range(2):
            for zl in range(2):
                both = self.raw[slot, zh, zl, me["core"]].astype(f32) + self.core_in[slot, zh, zl].astype(f32)
                self.acc[into, zh, zl] = both.astype(bf16)

        @pl.when(c < TOTAL - RAW_SLOTS)
        def _():
            pl.semaphore_signal(self.core_free, inc=1, device_id=self.at.peer("core"), device_id_type=MESH)

        for block in range(BLOCKS):
            self.exchange(c, block, 0).start()

    def advance(self, c, stage):
        me = self.at.me
        slot, box = lax.rem(c, ACC_SLOTS), lax.rem(c, BOX_SLOTS)
        for block in range(BLOCKS):
            self.exchange(c, block, stage).wait()
            if stage < SUMS:
                where = self.part(c, block, stage, me[ROUTES[block][stage]])
                both = self.acc[where].astype(f32) + self.inboxes[block * SUMS + stage][box].astype(f32)
                if stage == SUMS - 1:
                    self.out[slot, block, me["x"], me["y"]] = both.astype(bf16)
                else:
                    self.acc[where] = both.astype(bf16)
            if stage + 1 < STAGES - 1:
                self.exchange(c, block, stage + 1).start()
            else:
                self.finish(c, block)

    def finish(self, c, block):
        slot = lax.rem(c, ACC_SLOTS)
        layer = LAYERS - 1 - c // CHUNKS
        inner = lax.rem(c, CHUNKS)
        start = 0
        for which, count in enumerate(SEGMENTS):

            @pl.when((inner >= start) & (inner < start + count))
            def _(which=which, start=start):
                for xh in range(2):
                    for yh in range(2):
                        part = self.out[slot, block, xh, yh]
                        column = block * 256 + yh * 128
                        if which == 0:
                            row = pl.multiple_of((inner - start) * 96 + xh * 48, 16)
                            self.results[which][layer, pl.ds(row, 48), column : column + 128] = part
                        else:
                            at = pl.ds(pl.multiple_of((inner - start) * 768 + column, 128), 128)
                            self.results[which][layer, xh * 48 : (xh + 1) * 48, at] = part

            start += count

    def run_step(self, t):
        for stage in reversed(range(STAGES)):
            c = t - STRIDE * stage

            @pl.when((c >= 0) & (c < TOTAL))
            def _(c=c, stage=stage):
                if stage == 0:
                    self.enter(c)
                else:
                    self.advance(c, stage - 1)

    def step(self, count=1):
        first = self.stepped
        self.stepped += count
        assert min(self.stepped, TOTAL) <= self.made

        @pl.loop(first, first + count)
        def _(t):
            self.run_step(t)

    def inside(self, count):
        first = self.stepped
        self.stepped += count
        assert min(self.stepped, TOTAL) <= self.made
        return first

    def frame_steps(self, counts):
        first = self.inside(sum(counts))
        a, b, c = counts

        def run(frame):
            second, third = (frame + 1) // 2, frame // 2
            low = first + a * second + b * third

            @pl.loop(low, low + a + (b - a) * second + (c - b) * third)
            def _(t):
                self.run_step(t)

        return run


class Small:
    def __init__(self, at, values, boxes, send_sem, recv_sem):
        self.at, self.values, self.boxes, self.send_sem, self.recv_sem = at, values, boxes, send_sem, recv_sem

    def rows(self, i):
        return SMALL_ROWS if i < 3 else 16

    def copy(self, i):
        part = pl.ds(0, self.rows(i))
        return pltpu.make_async_remote_copy(
            src_ref=self.values.at[part],
            dst_ref=self.boxes.at[i, part],
            send_sem=self.send_sem.at[i],
            recv_sem=self.recv_sem.at[i],
            device_id=self.at.peer(SMALL[i]),
            device_id_type=MESH,
        )

    def step(self, i):
        if i > 0:
            rows = slice(0, self.rows(i - 1))
            self.copy(i - 1).wait()
            self.values[rows] += self.boxes[i - 1, rows]
        if i < len(SMALL):
            self.copy(i).start()


class Ring:
    def __init__(self, sources, slots, sems):
        self.sources, self.slots, self.sems = sources, slots, sems
        self.depth = slots.shape[0]
        self.started = self.taken = 0
        for _ in range(self.depth):
            self.start()

    def copy(self, i):
        source = self.sources[i]
        slot = i % self.depth
        return pltpu.make_async_copy(source, self.slots.at[slot, pl.ds(0, source.shape[0])], self.sems.at[slot])

    def start(self):
        if self.started < len(self.sources):
            self.copy(self.started).start()
            self.started += 1

    def take(self):
        i = self.taken
        self.copy(i).wait()
        self.taken += 1
        return self.slots.at[i % self.depth, pl.ds(0, self.sources[i].shape[0])]

    def free(self):
        self.start()


class Single:
    def __init__(self, sources, buffer, sem):
        self.copies = [
            pltpu.make_async_copy(source, buffer.at[pl.ds(0, source.shape[0])], sem) for source in sources
        ]
        self.next = 0
        self.copies[0].start()

    def take(self):
        self.copies[self.next].wait()

    def free(self):
        self.next += 1
        if self.next < len(self.copies):
            self.copies[self.next].start()


def backward_kernel(lay, *refs):
    devices, patches = lay.devices, lay.all_patches
    lengths_ref, norms_ref, cls_ref, leave_home, reach_away, leave_away, reach_home = refs[:7]
    weights = dict(zip(WEIGHTS, refs[7:13]))
    grad_hbm, x_out_hbm = refs[13:15]
    names = ("x_home",) + SAVED
    refs = refs[15:]
    saved = [dict(zip(names, refs[len(names) * layer : len(names) * (layer + 1)])) for layer in range(LAYERS)]
    refs = refs[len(names) * LAYERS :]
    small_ref, *results, output_hbm, tokens_hbm = refs[:9]
    refs = refs[9:]
    hidden, qkv, dqkv, wide, mixed, branch, x_buf, grad_buf, home_buf, cls_sum, bias_ref, *refs = refs
    weight_slots, lhs_slots, sent, got, small_boxes, *sums = refs[:11]
    sem_hidden, sem_qkv, sem_x, sem_ends, sem_weight, sem_lhs, sem_sent, sem_got, small_send, small_recv = refs[11:21]
    pump_scratch = refs[21:]
    load_grad = pltpu.make_async_copy(grad_hbm, grad_buf, sem_ends.at[0])
    load_out = pltpu.make_async_copy(x_out_hbm, mixed, sem_ends.at[1])
    save_out = pltpu.make_async_copy(home_buf, output_hbm, sem_ends.at[2])
    save_tokens = pltpu.make_async_copy(mixed, tokens_hbm, sem_ends.at[3])
    load_out.start()
    load_grad.start()

    at = Place()
    shuffle = Shuffle(lay, at, sent, got, sem_sent, sem_got)
    shuffle.greet()
    for dim in ("x", "y"):
        pl.semaphore_signal(pltpu.get_barrier_semaphore(), inc=1, device_id=at.peer(dim), device_id_type=MESH)

    total, width = grad_buf.shape
    parts = range(0, 3 * width, width)
    order = tuple(reversed(range(LAYERS)))
    tiles, lhs = [], []
    for layer in order:
        wide_parts = range(0, weights["up"].shape[2], width)
        tiles += [weights["down"].at[layer, pl.ds(start, width), :] for start in wide_parts]
        tiles += [weights["up"].at[layer, :, pl.ds(start, width)] for start in wide_parts]
        tiles += [weights["space_output"].at[layer]]
        tiles += [weights["space_proj"].at[layer, :, pl.ds(start, width)] for start in parts]
        tiles += [weights["time_output"].at[layer]]
        tiles += [weights["time_proj"].at[layer, :, pl.ds(start, width)] for start in parts]
        here = saved[layer]
        lhs += [here["slope"].at[:, pl.ds(start, width)] for start in wide_parts]
        lhs += [here[name] for name in ("normed_f", "mixed_s", "normed_s", "mixed_t", "normed_t")]
    fill = Single([saved[layer]["active"] for layer in order], hidden, sem_hidden)
    pump = Pump(at, results, pump_scratch)
    small = Small(at, small_ref, small_boxes, small_send, small_recv)
    for part in sums:
        part[...] = jnp.zeros_like(part)
    small_ref[...] = jnp.zeros_like(small_ref)
    key_mask = key_bias(patches)
    cls = cls_rows_of(cls_ref)
    fill_bias(lengths_ref, lay.frames, bias_ref)

    def back_product(rows, source, count):
        for i in range(count):
            tile = ring.take()
            part = dot_nt(source[:rows, i * width : (i + 1) * width], tile[...])
            if i:
                wide[:rows, :] += part
            else:
                wide[:rows, :] = part
            ring.free()

    frames = total // patches
    group = bias_ref.shape[0]
    groups = group_parts(lay, group)

    def made_of(lhs_tile, source, first=0, rows=None):
        rows = source.shape[0] if rows is None else rows

        def rhs(i, start):
            column = pl.multiple_of((i + first) * width + start, 128) if not isinstance(i, int) else (i + first) * width + start
            return source[:rows, pl.ds(column, WIDE)]

        return (lambda these: lhs_tile[:, these]), rhs

    shuffle.meet(2)
    load_out.wait()
    shuffle.send_all(leave_away, mixed)
    load_grad.wait()
    dy = grad_buf
    fill.take()
    ring = Ring(tiles, weight_slots, sem_weight)
    left = Ring(lhs, lhs_slots, sem_lhs)
    load_qkv = Single([saved[layer][name] for layer in order for name in ("qkv_s", "qkv_t")], qkv, sem_qkv)
    load_x = Single(
        [saved[layer][name] for layer in order for name in ("middle", "x_away", "x_home")], x_buf, sem_x
    )

    for layer in order:
        last = layer == 0
        plan = PLAN[layer]

        def steps(site, plan=plan):
            if plan.get(site, 0):
                pump.step(plan[site])

        if last:
            fill.take()
        pump.make_down(lambda these: hidden[:, these], dy)
        steps("down")
        for start in range(0, hidden.shape[1], width):
            tile, slope = ring.take(), left.take()
            for block in range(0, width, WIDE):
                grad_active = dot_nt(dy[...], tile[block : block + WIDE, :])
                grad_hidden = grad_active * slope[:, block : block + WIDE].astype(f32)
                hidden[:, start + block : start + block + WIDE] = grad_hidden.astype(bf16)
            ring.free()
            left.free()
        normed_f = left.take()
        if plan["early"]:
            pump.make_chunks(plan["early"], *made_of(normed_f, hidden))
        steps("hidden")
        back_product(total, hidden, hidden.shape[1] // width)
        steps("wide")
        load_x.take()

        @pl.loop(0, frames)
        def _(frame, layer=layer):
            here = pl.ds(pl.multiple_of(frame * patches, 16), patches)
            part = norm_backward(x_buf[here, :].astype(f32), wide[here, :], norm_row(norms_ref, layer, 2), sums[0:2])
            both = dy[here, :].astype(f32) + part
            wide[here, :] = both
            branch[here, :] = both.astype(bf16)

        load_x.free()
        steps("norm")

        out_tile, *proj_tiles = [ring.take() for _ in range(4)]
        load_qkv.take()
        load_x.take()
        cls_sum[...] = jnp.zeros_like(cls_sum)
        gain = norm_row(norms_ref, layer, 1)
        frame_run = pump.frame_steps(plan["frames"]) if sum(plan["frames"]) else None

        @pl.loop(0, frames)
        def _(frame):
            here = pl.ds(pl.multiple_of(frame * patches, 16), patches)
            mixed[here, :] = dot_nt(branch[here, :], out_tile[...]).astype(bf16)
            slot = slot_of(lengths_ref, at.patch * frames + frame)
            _, these = space_tiles(patches, total, slot, qkv, width, frame, mixed)
            row_ids = lax.broadcasted_iota(jnp.int32, (patches, WIDE), 0)
            cls_ids = lax.broadcasted_iota(jnp.int32, (CLS_ROWS, WIDE), 0)
            for quad, grads in enumerate(backward_tiles(these, key_mask)):
                dqkv[here, columns(0, quad, width)] = grads[0].astype(bf16)
                for part in (1, 2):
                    where = columns(part, quad, width)
                    dqkv[here, where] = jnp.where(row_ids < REAL_PATCH, grads[part], 0.0).astype(bf16)
                    row = grads[part][REAL_PATCH : REAL_PATCH + 1]
                    cls_sum[:, where] += jnp.where(cls_ids == slot, row, 0.0)
            grad = sum(dot_nt(dqkv[here, i * width : (i + 1) * width], tile[...]) for i, tile in enumerate(proj_tiles))
            part = norm_backward(x_buf[here, :].astype(f32), grad, gain, sums[2:4])
            mixed[here, :] = (wide[here, :] + part).astype(bf16)
            for i in range(2):

                @pl.when(frame == i)
                def _(i=i, last=last):
                    if i == 0 and not last:
                        shuffle.receive(reach_home, home_buf)
                        save_out.start()
                    shuffle.send(i, leave_away, mixed, 0, (i + 1) * patches)

            if frame_run is not None:
                frame_run(frame)

        shuffle.send(2, leave_away, mixed, patches, total)
        load_x.free()
        load_qkv.free()
        dqkv[total:, :] = cls_sum[...].astype(bf16)
        grad = sum(dot_nt(dqkv[total:, i * width : (i + 1) * width], tile[...]) for i, tile in enumerate(proj_tiles))
        for _ in range(4):
            ring.free()
        part = norm_backward(cls, grad, gain, sums[2:4])
        small_ref[16:24] += part[:8]
        if plan["early"] < 4:
            pump.make_chunks(4 - plan["early"], *made_of(normed_f, hidden, plan["early"]))
        left.free()
        fill.free()
        steps("up")
        pump.make_chunks(1, *made_of(left.take(), branch))
        left.free()
        steps("space_out")
        pump.make_chunks(3, *made_of(left.take(), dqkv))
        left.free()
        steps("space_proj")
        if not last:
            save_out.wait()
        shuffle.receive(reach_home, home_buf)

        out_tile, *proj_tiles = [ring.take() for _ in range(4)]
        load_qkv.take()
        load_x.take()
        mixed_t = left.take()
        if plan["time_early"]:
            pump.make_chunks(1, *made_of(mixed_t, home_buf))
            left.free()
        steps("home")

        def close_part(number, layer=layer, last=last, proj_tiles=proj_tiles):
            first, end = groups[number]
            here = slice(first, end)
            grad = sum(dot_nt(dqkv[here, i * width : (i + 1) * width], tile[...]) for i, tile in enumerate(proj_tiles))
            part = norm_backward(x_buf[here, :].astype(f32), grad, norm_row(norms_ref, layer, 0), sums[4:6])
            mixed[here, :] = (home_buf[here, :].astype(f32) + part).astype(bf16)
            if not last:
                shuffle.send(number, leave_home, mixed, 0 if number < 2 else first, end)

        for number, (first, end) in enumerate(groups):
            here = slice(first, end)
            mixed[here, :] = dot_nt(home_buf[here, :], out_tile[...]).astype(bf16)

            @pl.loop(first // group, end // group)
            def _(index):
                at_rows, these = time_tiles(bias_ref, qkv, width, index, mixed)
                for quad, grads in enumerate(backward_tiles(these, bias_ref[...])):
                    for part in range(3):
                        dqkv[at_rows, columns(part, quad, width)] = grads[part].astype(bf16)

            if not last:
                close_part(number)
            steps("time%d" % number)
        if not last:
            load_qkv.free()
            load_x.free()
            for _ in range(4):
                ring.free()
        if not plan["time_early"]:
            pump.make_chunks(1, *made_of(mixed_t, home_buf))
            left.free()
        steps("time_out")
        pump.make_chunks(3, *made_of(left.take(), dqkv, rows=total))
        left.free()
        steps("time_proj")
        if last:
            for number in range(len(groups)):
                pump.step()
                close_part(number)
            save_tokens.start()
        for i, part in enumerate(sums):
            row = layer * 8 + (2, 5, 1, 4, 0, 3)[i]
            small_ref[row : row + 1, :] += jnp.sum(part[...], 0, keepdims=True)
            part[...] = jnp.zeros_like(part)
        if last:
            small.step(0)
            for i in range(1, len(SMALL) + 1):
                pump.step()
                small.step(i)
        else:
            shuffle.receive(reach_away, grad_buf)

    pump.step(TOTAL + STRIDE * (STAGES - 1) - pump.stepped)
    save_tokens.wait()


IN_VMEM = pl.BlockSpec(memory_space=pltpu.VMEM)
IN_SMEM = pl.BlockSpec(memory_space=pltpu.SMEM)
IN_HBM = pl.BlockSpec(memory_space=pl.ANY)


def shape(*dims, kind=bf16):
    return jax.ShapeDtypeStruct(dims, kind)


def vmem(*dims, kind=bf16):
    return pltpu.VMEM(dims, kind)


def queue(*counts):
    return pltpu.SemaphoreType.DMA(counts)


def whole_call(name, body, collective, near, far, out_near, out_far, scratch):
    return pl.pallas_call(
        body,
        in_specs=[IN_SMEM if part.ndim == 1 else IN_VMEM for part in near] + [IN_HBM] * len(far),
        out_specs=[IN_VMEM] * len(out_near) + [IN_HBM] * len(out_far),
        out_shape=[*out_near, *out_far],
        scratch_shapes=scratch,
        compiler_params=pltpu.CompilerParams(
            collective_id=collective, has_side_effects=True, vmem_limit_bytes=VMEM_MOST
        ),
        name=name,
    )(*near, *far)


def finish_kernel(small_ref, *refs):
    count = len(refs) // 2
    for source, target in zip(refs[:count], refs[count:-1]):
        target[...] = source[...].astype(target.dtype)
    refs[-1][...] = small_ref[16 : 16 + refs[-1].shape[0], :]


def finish(small, clip_count, parts, kinds, steps=3):
    specs, out = [], []
    width = small.shape[1]
    cls = jax.ShapeDtypeStruct((clip_count, width), f32)
    for part, kind in zip(parts, kinds):
        cut = part.ndim - 2 if part.shape[-2] % (steps * 16) == 0 else part.ndim - 1
        block = tuple(size // steps if dim == cut else size for dim, size in enumerate(part.shape))

        def index(i, cut=cut, ndim=part.ndim):
            return tuple(i if dim == cut else 0 for dim in range(ndim))

        specs.append(pl.BlockSpec(block, index))
        out.append(jax.ShapeDtypeStruct(part.shape, kind))
    return pl.pallas_call(
        finish_kernel,
        grid=(steps,),
        in_specs=[pl.BlockSpec(small.shape, lambda i: (0, 0)), *specs],
        out_specs=[*specs, pl.BlockSpec(cls.shape, lambda i: (0, 0))],
        out_shape=[*out, cls],
        compiler_params=pltpu.CompilerParams(vmem_limit_bytes=VMEM_MOST),
        name="finish",
    )(small, *parts)


def fast_local(
    tokens,
    cls_tokens,
    clip_lengths,
    time_proj,
    time_output,
    space_proj,
    space_output,
    up_weight,
    down_weight,
    norm_gains,
    norm_biases,
    cotangent,
):
    frames, patch_rows, width = tokens.shape
    devices = lax.axis_size(PATCH)
    hidden = up_weight.shape[2]
    lay = Layout(devices, frames, patch_rows)
    home, away, block = lay.home_rows, lay.away_rows, lay.block
    clip_count = cls_tokens.shape[0]
    group = group_rows(patch_rows, frames)
    orders = {name: jnp.asarray(part) for name, part in lay.orders().items()}

    def home_order(values):
        return jnp.transpose(values, (1, 0, 2)).reshape(home, width)

    def given_order(values):
        return jnp.transpose(values.reshape(patch_rows, frames, width), (1, 0, 2))

    parts = len(lay.parts())
    moving = [vmem(devices, block, width), vmem(2, devices, block, width), queue(parts, devices), queue(2, parts, devices)]
    extra = [vmem(devices, block, width), vmem(1, devices, block, width), queue(parts, devices), queue(1, parts, devices)]
    gains, shifts = [jnp.transpose(part, (1, 0, 2)) for part in (norm_gains, norm_biases)]
    lengths = clip_lengths[0]
    weights = (time_proj, time_output, space_proj, space_output, up_weight, down_weight)
    at_home = home_order(tokens)
    saved_shapes = [
        shape(home, width),
        shape(home, 3 * width),
        shape(home, width),
        shape(away, width),
        shape(away + CLS_ROWS, width),
        shape(away + CLS_ROWS, 3 * width),
        *[shape(away, width)] * 3,
        *[shape(away, hidden)] * 2,
    ]
    bias = vmem(group, QUAD * group, kind=f32)
    home_next, grad_away, x_out, *saved = whole_call(
        "forward",
        functools.partial(forward_kernel, lay),
        2,
        (lengths, gains, shifts, cls_tokens, *[orders[name] for name in ("leave_frame", "reach_frame", "leave_away", "reach_home")]),
        (*weights, at_home, home_order(cotangent)),
        [],
        [shape(home, width), shape(away, width), shape(away, width)] + saved_shapes * LAYERS,
        [
            *[vmem(*part.shape[1:]) for part in weights],
            *[vmem(*part.shape) for part in saved_shapes],
            bias,
            vmem(home, width),
            vmem(away, width),
            vmem(home, width),
            vmem(away, width),
            queue(len(weights)),
            queue(5),
            queue(3, 1),
            queue(len(SAVED) - 3, lay.away_frames),
            queue(2, 1),
            *moving,
            *extra,
        ],
    )
    stored = [(at_home, *saved[: len(SAVED)]), (home_next, *saved[len(SAVED) :])]

    inbox = [vmem(BOX_SLOTS, *recv_shape(ROUTES[b], s)) for b in range(BLOCKS) for s in range(SUMS)]
    single = pltpu.SemaphoreType.DMA
    share = width // devices
    small, *large, output, grad_tokens = whole_call(
        "backward",
        functools.partial(backward_kernel, lay),
        1,
        (lengths, gains, cls_tokens, *[orders[name] for name in ("leave_patch", "reach_patch", "leave_away", "reach_home")]),
        (*weights, grad_away, x_out, *stored[0], *stored[1]),
        [
            shape(SMALL_ROWS, width, kind=f32),
            shape(LAYERS, hidden // devices, width),
            shape(LAYERS, share, hidden),
            shape(LAYERS, share, width),
            shape(LAYERS, share, 3 * width),
            shape(LAYERS, share, width),
            shape(LAYERS, share, 3 * width),
        ],
        [shape(home, width), shape(home, width)],
        [
            vmem(away, hidden),
            vmem(away + CLS_ROWS, 3 * width),
            vmem(away + CLS_ROWS, 3 * width),
            vmem(away, width, kind=f32),
            *[vmem(away, width)] * 5,
            vmem(CLS_ROWS, 3 * width, kind=f32),
            bias,
            vmem(4, width, width),
            vmem(2, away + CLS_ROWS, width),
            *moving[:2],
            vmem(len(SMALL), SMALL_ROWS, width, kind=f32),
            *[vmem(8, width, kind=f32)] * 6,
            single,
            single,
            single,
            queue(4),
            queue(4),
            queue(2),
            *moving[2:],
            queue(len(SMALL)),
            queue(len(SMALL)),
            vmem(RAW_SLOTS, 2, 2, 2, BLOCKS, 2, 2, *PIECE),
            vmem(RAW_SLOTS, 2, 2, BLOCKS, 2, 2, *PIECE),
            vmem(ACC_SLOTS, 2, 2, BLOCKS, 2, 2, *PIECE),
            vmem(ACC_SLOTS, BLOCKS, 2, 2, *PIECE),
            *inbox,
            queue(RAW_SLOTS, 4),
            queue(RAW_SLOTS, 4),
            pltpu.SemaphoreType.REGULAR,
            queue(BOX_SLOTS, BLOCKS, STAGES - 1),
            queue(BOX_SLOTS, BLOCKS, STAGES - 1),
        ],
    )
    large = [large[i] for i in (5, 4, 3, 2, 1, 0)]
    kinds = (f32,) * len(large) + (bf16,) * 2
    *large, output, grad_tokens, grad_cls = finish(small, clip_count, (*large, output, grad_tokens), kinds)
    small = lax.dynamic_slice_in_dim(small[:16], lax.axis_index(PATCH) * share, share, 1)
    small = small.reshape(LAYERS, 8, share)
    return (given_order(output), given_order(grad_tokens), grad_cls, *large, small[:, 0:3], small[:, 3:6])


def general_local(
    tokens,
    cls_tokens,
    clip_lengths,
    time_proj,
    time_output,
    space_proj,
    space_output,
    up_weight,
    down_weight,
    norm_gains,
    norm_biases,
    cotangent,
):
    frames, patch_rows, width = tokens.shape
    devices = lax.axis_size(PATCH)
    lay = Layout(devices, frames, patch_rows)
    away_rows = lay.away_rows
    patches = lay.all_patches
    clip_count = cls_tokens.shape[0]

    frame_ids = jnp.arange(frames, dtype=jnp.int32)
    slots = frame_slots(clip_lengths[0], frame_ids)
    bias = time_bias(slots[:, None] == slots[None, :], patch_rows, frames)
    my_frames = lax.axis_index(PATCH) * lay.away_frames + jnp.arange(lay.away_frames, dtype=jnp.int32)
    my_slots = jnp.where(my_frames < frames, frame_slots(clip_lengths[0], my_frames), -1)
    cls_pick = (my_slots[None, :] == jnp.arange(CLS_ROWS, dtype=jnp.int32)[:, None]).astype(f32)

    def home_order(values):
        return jnp.transpose(values, (1, 0, 2)).reshape(lay.home_rows, width)

    def given_order(values):
        return jnp.transpose(values.reshape(patch_rows, frames, width), (1, 0, 2))

    cls_aug = jnp.pad(cls_tokens.astype(f32), ((0, CLS_ROWS - clip_count), (0, 0)))
    residual = home_order(tokens).astype(f32)
    cotangent_away = lay.to_away(home_order(cotangent))
    stored = []
    for layer in range(LAYERS):
        gains, biases = norm_gains[layer], norm_biases[layer]
        normed, scaled_t, inverse_t = layer_norm(residual, gains[0], biases[0])
        normed_t = normed.astype(bf16)
        qkv_t = project(normed_t, time_proj[layer]).astype(bf16)
        mixed_t = time_forward(bias, qkv_t)
        residual = residual + project(mixed_t, time_output[layer])
        away = lay.to_away(residual.astype(bf16))
        away = away + jnp.pad(cls_aug, ((away_rows, 0), (0, 0)))
        normed, scaled_s, inverse_s = layer_norm(away, gains[1], biases[1])
        normed_s = normed.astype(bf16)
        qkv_s = project(normed_s, space_proj[layer]).astype(bf16)
        mixed_s = space_forward(my_slots, qkv_s, lay.away_frames, patches)
        away = away[:away_rows] + project(mixed_s, space_output[layer])
        normed, scaled_f, inverse_f = layer_norm(away, gains[2], biases[2])
        normed_f = normed.astype(bf16)
        hidden = project(normed_f, up_weight[layer])
        active = gelu_value(hidden).astype(bf16)
        away = away + project(active, down_weight[layer])
        residual = lay.to_home(away.astype(bf16))
        stored.append(
            dict(
                normed_t=normed_t, scaled_t=scaled_t, inverse_t=inverse_t, qkv_t=qkv_t, mixed_t=mixed_t,
                normed_s=normed_s, scaled_s=scaled_s, inverse_s=inverse_s, qkv_s=qkv_s, mixed_s=mixed_s,
                normed_f=normed_f, scaled_f=scaled_f, inverse_f=inverse_f, hidden=hidden, active=active,
            )
        )
    output = given_order(residual.astype(bf16))

    grad_cls = jnp.zeros_like(cls_aug)
    grad_away = cotangent_away[:away_rows]
    results = [None] * LAYERS
    for layer in reversed(range(LAYERS)):
        saved = stored[layer]
        gains = norm_gains[layer]
        branch = grad_away.astype(bf16)
        grad_down = weight_grad(saved["active"], branch)
        grad_active = project_back(branch, down_weight[layer])
        grad_hidden = (grad_active * gelu_slope(saved["hidden"])).astype(bf16)
        grad_up = weight_grad(saved["normed_f"], grad_hidden)
        grad_normed = project_back(grad_hidden, up_weight[layer])
        grad_input, gain_two, bias_two = norm_back(
            grad_normed, saved["scaled_f"], saved["inverse_f"], gains[2]
        )
        grad_away = grad_away + grad_input
        branch = grad_away.astype(bf16)
        grad_space_out = weight_grad(saved["mixed_s"], branch)
        grad_mixed = project_back(branch, space_output[layer]).astype(bf16)
        dq, dk, dv, dck, dcv = space_backward(my_slots, saved["qkv_s"], grad_mixed, lay.away_frames, patches)
        dcls = jnp.concatenate([dck[:, 0], dcv[:, 0]], -1)
        dcls = jnp.dot(cls_pick, dcls, precision=lax.Precision.HIGHEST)
        dcls = jnp.pad(dcls.astype(bf16), ((0, 0), (width, 0)))
        grad_qkv = jnp.concatenate([jnp.concatenate([dq, dk, dv], -1), dcls], 0)
        grad_space_proj = weight_grad(saved["normed_s"], grad_qkv)
        grad_normed = project_back(grad_qkv, space_proj[layer])
        grad_input, gain_one, bias_one = norm_back(
            grad_normed, saved["scaled_s"], saved["inverse_s"], gains[1]
        )
        grad_away = grad_away + grad_input[:away_rows]
        grad_cls = grad_cls + grad_input[away_rows:]
        grad_home = lay.to_home(grad_away.astype(bf16))
        branch = grad_home.astype(bf16)
        grad_time_out = weight_grad(saved["mixed_t"], branch)
        grad_mixed = project_back(branch, time_output[layer]).astype(bf16)
        grad_qkv = time_backward(bias, saved["qkv_t"], grad_mixed)
        grad_time_proj = weight_grad(saved["normed_t"], grad_qkv)
        grad_normed = project_back(grad_qkv, time_proj[layer])
        grad_input, gain_zero, bias_zero = norm_back(
            grad_normed, saved["scaled_t"], saved["inverse_t"], gains[0]
        )
        grad_home = grad_home + grad_input
        if layer > 0:
            grad_away = lay.to_away(grad_home.astype(bf16))[:away_rows]
        large = (grad_time_proj, grad_time_out, grad_space_proj, grad_space_out, grad_up, grad_down)
        large = [lax.psum_scatter(part, PATCH, scatter_dimension=0, tiled=True) for part in large]
        large = lax.psum(large, CLIP)
        small = (jnp.stack([gain_zero, gain_one, gain_two]), jnp.stack([bias_zero, bias_one, bias_two]))
        results[layer] = [part.astype(f32) for part in large] + list(small)
    grad_tokens = given_order(grad_home.astype(bf16))
    stacked = [jnp.stack([results[layer][i] for layer in range(LAYERS)]) for i in range(8)]
    small = jnp.stack(stacked[6:])
    small = lax.psum(small, (PATCH, CLIP))
    share = width // devices
    small = lax.dynamic_slice_in_dim(small, lax.axis_index(PATCH) * share, share, 3)
    grad_cls = lax.psum(grad_cls[:clip_count], PATCH)
    return (output, grad_tokens, grad_cls, *stacked[:6], small[0], small[1])


def solution(mesh):
    in_specs = (
        P(CLIP, PATCH, None),
        P(CLIP, None),
        P(CLIP, None),
        P(),
        P(),
        P(),
        P(),
        P(),
        P(),
        P(),
        P(),
        P(CLIP, PATCH, None),
    )
    out_specs = (
        P(CLIP, PATCH, None),
        P(CLIP, PATCH, None),
        P(CLIP, None),
        P(None, PATCH, None),
        P(None, PATCH, None),
        P(None, PATCH, None),
        P(None, PATCH, None),
        P(None, PATCH, None),
        P(None, PATCH, None),
        P(None, None, PATCH),
        P(None, None, PATCH),
    )
    paired = (mesh.shape[CLIP], mesh.shape[PATCH]) == (4, 8)
    local = fast_local if paired else general_local
    return jax.shard_map(local, mesh=mesh, in_specs=in_specs, out_specs=out_specs, check_vma=False)
```
